32 devices in a mesh: fsdp: 2 (over x), ctx: 4 (over z), tp: 4 (over y, core).
Axes of the slice: x: 2, y: 2, z: 4, core: 2. Of those that a mesh axis runs over, the one named last changes fastest.
Arguments:
- hidden_in: bfloat16 [2048, 2048], P(('fsdp', 'ctx'), 'tp'), may hold values from -6 to 6
- positions: int32 [2048], P(('fsdp', 'ctx')), may hold values from 0 to 2046, as said below
- chosen: int32 [2048, 6], P(('fsdp', 'ctx')), may hold values from 0 to 15, all different within a row; in each aligned block of 256 rows (0 to 255, 256 to 511, ...) at most 160 rows name the same one
- out_grad: bfloat16 [2048, 2048], P(('fsdp', 'ctx'), 'tp'), may hold values from -6 to 6
- attn_gain: bfloat16 [2048], P(('fsdp', 'ctx')), may hold values from 0.5 to 1.5
- w_query: bfloat16 [2048, 2048], P(('fsdp', 'ctx'), 'tp'), may hold values from -0.125 to 0.125
- w_key: bfloat16 [2048, 2048], P(('fsdp', 'ctx'), 'tp'), may hold values from -0.125 to 0.125
- w_value: bfloat16 [2048, 2048], P(('fsdp', 'ctx'), 'tp'), may hold values from -0.125 to 0.125
- w_out: bfloat16 [2048, 2048], P('tp', ('fsdp', 'ctx')), may hold values from -0.75 to 0.75
- moe_gain: bfloat16 [2048], P(('fsdp', 'ctx')), may hold values from 0.5 to 1.5
- router: bfloat16 [2048, 16], P(('fsdp', 'ctx')), may hold values from -0.0625 to 0.0625
- shared_gate: bfloat16 [2048, 2816], P(('fsdp', 'ctx'), 'tp'), may hold values from -0.125 to 0.125
- shared_up: bfloat16 [2048, 2816], P(('fsdp', 'ctx'), 'tp'), may hold values from -0.125 to 0.125
- shared_down: bfloat16 [2816, 2048], P('tp', ('fsdp', 'ctx')), may hold values from -0.109375 to 0.109375
- expert_gate: bfloat16 [16, 2048, 1408], P('ctx', 'fsdp', 'tp'), may hold values from -0.125 to 0.125
- expert_up: bfloat16 [16, 2048, 1408], P('ctx', 'fsdp', 'tp'), may hold values from -0.125 to 0.125
- expert_down: bfloat16 [16, 1408, 2048], P('ctx', 'tp', 'fsdp'), may hold values from -1 to 1
Outputs:
- layer_out: bfloat16 [2048, 2048], P(('fsdp', 'ctx'), 'tp')
- input_grad: float32 [2048, 2048], P(('fsdp', 'ctx'), 'tp')
- attn_gain_grad: float32 [2048], P(('fsdp', 'ctx'))
- w_query_grad: float32 [2048, 2048], P(('fsdp', 'ctx'), 'tp')
- w_key_grad: float32 [2048, 2048], P(('fsdp', 'ctx'), 'tp')
- w_value_grad: float32 [2048, 2048], P(('fsdp', 'ctx'), 'tp')
- w_out_grad: float32 [2048, 2048], P('tp', ('fsdp', 'ctx'))
- moe_gain_grad: float32 [2048], P(('fsdp', 'ctx'))
- router_grad: float32 [2048, 16], P(('fsdp', 'ctx'))
- shared_gate_grad: float32 [2048, 2816], P(('fsdp', 'ctx'), 'tp')
- shared_up_grad: float32 [2048, 2816], P(('fsdp', 'ctx'), 'tp')
- shared_down_grad: float32 [2816, 2048], P('tp', ('fsdp', 'ctx'))
- expert_gate_grad: float32 [16, 2048, 1408], P('ctx', 'fsdp', 'tp')
- expert_up_grad: float32 [16, 2048, 1408], P('ctx', 'fsdp', 'tp')
- expert_down_grad: float32 [16, 1408, 2048], P('ctx', 'tp', 'fsdp')
The draws below stay inside these ranges and needn't reach their ends.
Inputs may be any that keep to these rules, and one draw needn't show every extreme that they name: `chosen`: each row names 6 different experts; among the 256 rows of one device no expert is named more than 160 times, a bound that some block reaches. `positions`: within each sequence of 1024 tokens the first position is 0, each later one exceeds the one before it by 1, 2 or 3, and the last one is 2046.
All inputs are finite; a program needn't handle non-finite values.
Results may differ from the reference program's by a relative error of at most 0.025.
Values may be sent and summed in bfloat16 or wider, within the bound.
A program may use at most 320 MiB of HBM per device.

```python
import math
import jax
import jax.numpy as jnp
import numpy as np
from jax import lax

D = 2048
H = 16
HD = 128
FFE = 1408
FFS = 2816
TOPK = 6
TOK = 256
EXPERTS = 16
SEQS = 2
LEN = 1024
TOKENS = 2048
CAP = 160


def draw_positions(key, part):
    key = jax.random.fold_in(key, 11)
    jitter = jax.random.randint(key, (SEQS, LEN), 0, 2).astype(jnp.int32)
    jitter = jitter.at[:, 0].set(0)
    jitter = jitter.at[:, LEN - 1].set(0)
    places = 2 * jnp.arange(LEN, dtype=jnp.int32)[None, :] + jitter
    return places.astype(jnp.int32).reshape(-1)


def steps_of(key, extent, cuts, least, high):
    factor_of, own = 1.0, jax.random.fold_in(key, 6)
    for axis_at, parts in cuts:
        draws = jnp.exp(jax.random.uniform(jax.random.fold_in(own, axis_at), (parts,), jnp.float32, least / len(cuts), high / len(cuts)))
        factor_of = factor_of * jnp.repeat(draws, extent[axis_at] // parts).reshape([-1 if axis == axis_at else 1 for axis in range(len(extent))])
    return factor_of


def assign_block(key, own, number, rows, amount, top, most, slope):
    ranking = jax.random.permutation(key, amount)
    packed, common = load_shares(amount, rows * top, most, slope, True), load_shares(amount, rows * top, most, slope, False)
    places = jnp.arange(amount)

    def named(lengths, turn):
        used = int((lengths > 0).sum())
        fixed = max(1, used // 4)
        moved = fixed + (places - fixed + turn * (used - fixed)) % max(1, amount - fixed)
        return jnp.zeros((amount,), jnp.int32).at[ranking[jnp.where(places < fixed, places, moved)]].set(jnp.asarray(lengths, jnp.int32))

    lengths = jnp.where(number % 4 == 0, named(packed, number // 4), named(common, number - number // 4 - 1))
    mixed = jax.random.permutation(jax.random.fold_in(own, 3), amount)
    giver, sink = mixed[0:amount // 2 * 2:2], mixed[1:amount // 2 * 2:2]
    slack = jnp.minimum(lengths[giver] - 1, most - lengths[sink]) // 2
    slack = jnp.where((giver == ranking[0]) | (sink == ranking[0]) | (lengths[sink] == 0), 0, jnp.maximum(slack, 0))
    moved = jax.random.randint(jax.random.fold_in(own, 4), (amount // 2,), 0, 1 << 20) % (slack + 1)
    lengths = lengths.at[giver].add(-moved).at[sink].add(moved)
    members = jnp.searchsorted(jnp.cumsum(lengths), jnp.arange(rows * top), side="right").astype(jnp.int32)
    table = members.reshape(top, rows).T
    table = table[jax.random.permutation(jax.random.fold_in(own, 1), rows)]
    turn = jax.random.randint(jax.random.fold_in(own, 2), (rows, 1), 0, top)
    return jnp.take_along_axis(table, (jnp.arange(top)[None, :] + turn) % top, axis=1)


def load_shares(number_of, total, reach, slope, full):
    weights = [(1 << 20) // math.isqrt(rank ** slope) + 1 for rank in range(1, number_of + 1)]
    largest = reach if full else min(reach, max(-(-total // number_of), total * weights[0] // sum(weights)))
    least = 1 if total - largest >= number_of - 1 else 0
    given, surplus = [largest] + [least] * (number_of - 1), total - largest - least * (number_of - 1)
    while surplus > 0:
        free = [i for i in range(1, number_of) if given[i] < largest] or [i for i in range(1, number_of) if given[i] < reach]
        pool, budget = sum([weights[i] for i in free]), surplus
        for i in free:
            extra = min(reach - given[i], max(1, budget * weights[i] // pool), surplus)
            given[i] = given[i] + extra
            surplus = surplus - extra
    return np.array(given)


def scatter_about(key, extent, deviation, bound, cuts=(), held_as=jnp.bfloat16):
    values = deviation * jax.random.normal(key, extent, jnp.float32)
    if cuts:
        values = values * steps_of(key, extent, cuts, -0.22, 0.18)
    return jnp.clip(values, -bound, bound).astype(held_as)


def setup_inputs(seed: int = 0) -> dict:
    streams_of = jax.random.split(jax.random.key(seed), 18)
    hidden_in = scatter_about(streams_of[0], (TOKENS, D), 1.0, 6.0, ((0, 8), (1, 4)))
    positions = draw_positions(jax.random.fold_in(streams_of[17], 71), 0)
    chosen_keys = jax.random.split(jax.random.fold_in(streams_of[2], 1), TOKENS // TOK)
    chosen_turns = jax.random.permutation(jax.random.fold_in(streams_of[2], 3), TOKENS // TOK)
    chosen = jax.vmap(lambda own, number: assign_block(jax.random.fold_in(streams_of[2], 2), own, number, TOK, EXPERTS, TOPK, CAP, 2))(chosen_keys, chosen_turns).reshape((TOKENS, TOPK))
    out_grad = scatter_about(streams_of[3], (TOKENS, D), 1.0, 6.0, ((0, 8), (1, 4)))
    attn_gain = jnp.clip(1.0 + 0.1 * jax.random.normal(streams_of[4], (D,), jnp.float32), 0.5, 1.5).astype(jnp.bfloat16)
    w_query = scatter_about(streams_of[5], (D, H * HD), D ** -0.5, 0.125, ((0, 8), (1, 4)))
    w_key = scatter_about(streams_of[6], (D, H * HD), D ** -0.5, 0.125, ((0, 8), (1, 4)))
    w_value = scatter_about(streams_of[7], (D, H * HD), D ** -0.5, 0.125, ((0, 8), (1, 4)))
    w_out = scatter_about(streams_of[8], (H * HD, D), (HD // 2) ** -0.5, 0.75, ((0, 4), (1, 8)))
    moe_gain = jnp.clip(1.0 + 0.1 * jax.random.normal(streams_of[9], (D,), jnp.float32), 0.5, 1.5).astype(jnp.bfloat16)
    router = scatter_about(streams_of[10], (D, EXPERTS), (4 * D) ** -0.5, 0.0625, ((0, 8),))
    shared_gate = scatter_about(streams_of[11], (D, FFS), D ** -0.5, 0.125, ((0, 8), (1, 4)))
    shared_up = scatter_about(streams_of[12], (D, FFS), D ** -0.5, 0.125, ((0, 8), (1, 4)))
    shared_down = scatter_about(streams_of[13], (FFS, D), FFS ** -0.5, 0.109375, ((0, 4), (1, 8)))
    expert_gate = scatter_about(streams_of[14], (EXPERTS, D, FFE), D ** -0.5, 0.125, ((0, 4), (1, 2), (2, 4)))
    expert_up = scatter_about(streams_of[15], (EXPERTS, D, FFE), D ** -0.5, 0.125, ((0, 4), (1, 2), (2, 4)))
    expert_down = scatter_about(streams_of[16], (EXPERTS, FFE, D), (max(1, FFE * 6 // (EXPERTS * EXPERTS))) ** -0.5, 1.0, ((0, 4), (1, 4), (2, 2)))
    return dict(hidden_in=hidden_in, positions=positions, chosen=chosen, out_grad=out_grad, attn_gain=attn_gain, w_query=w_query, w_key=w_key, w_value=w_value, w_out=w_out, moe_gain=moe_gain, router=router, shared_gate=shared_gate, shared_up=shared_up, shared_down=shared_down, expert_gate=expert_gate, expert_up=expert_up, expert_down=expert_down)


EPS = 1e-06
NEG_BIG = -1e+30

@jax.custom_vjp
def low(v):
    return lax.optimization_barrier(v.astype(jnp.bfloat16)).astype(jnp.float32)

@jax.custom_vjp
def low_back(v):
    return v

def low_keep(v):
    return (low(v), None)

def low_pass(kept, grad):
    return (grad,)

def back_keep(v):
    return (v, None)

def back_low(kept, grad):
    return (low(grad),)
low.defvjp(low_keep, low_pass)
low_back.defvjp(back_keep, back_low)

def mat_high(left, right):
    return jnp.dot(left, right, precision=lax.Precision.HIGHEST, preferred_element_type=jnp.float32)

def rms_norm(values, gain):
    return values * lax.rsqrt(lax.optimization_barrier(jnp.mean(values * values, axis=1, keepdims=True)) + EPS) * gain[None, :]

def rotary(values, positions):
    half_dim = HD // 2
    inverse = 10000.0 ** (-jnp.arange(half_dim, dtype=jnp.float32) * 2.0 / HD)
    angles = positions.astype(jnp.float32)[:, None] * inverse[None, :]
    cosine = jnp.cos(angles)[:, None, :]
    sine_val = jnp.sin(angles)[:, None, :]
    lower_half = values[..., :half_dim]
    upper_half = values[..., half_dim:]
    return jnp.concatenate([lower_half * cosine - upper_half * sine_val, upper_half * cosine + lower_half * sine_val], axis=-1)

def attention(query_b, key_b, value_b):
    block = min(512, LEN)
    per_seq = LEN // block
    keys_all = key_b.reshape(SEQS, LEN, H, HD)
    vals_all = value_b.reshape(SEQS, LEN, H, HD)
    queries = query_b.reshape(SEQS * per_seq, block, H, HD)
    block_ids = jnp.arange(SEQS * per_seq, dtype=jnp.int32)
    seq_ids = block_ids // per_seq
    starts = block_ids % per_seq * block

    def one_block(inputs):
        query_blk, seq_id, first_row = inputs
        key_seq = keys_all[seq_id]
        val_seq = vals_all[seq_id]
        scores = low_back(jnp.einsum('qhd,khd->qhk', query_blk, key_seq, precision=lax.Precision.HIGHEST) * HD ** (-0.5))
        visible = jnp.arange(LEN, dtype=jnp.int32)[None, :] <= (first_row + jnp.arange(block, dtype=jnp.int32))[:, None]
        scores = jnp.where(visible[:, None, :], scores, NEG_BIG)
        probs_all = jax.nn.softmax(scores, axis=2)
        return jnp.einsum('qhk,khd->qhd', low(probs_all), val_seq, precision=lax.Precision.HIGHEST)
    outs = lax.map(jax.checkpoint(one_block), (queries, seq_ids, starts))
    return outs.reshape(SEQS * LEN, H * HD)

def forward(params, hidden, positions, chosen):
    attn_gain, w_query, w_key, w_value, w_out, moe_gain, router, shared_gate, shared_up, shared_down, expert_gate, expert_up, expert_down = params
    tokens = hidden.shape[0]
    normed_in = low(rms_norm(hidden, attn_gain))
    query_pre = low_back(mat_high(normed_in, w_query)).reshape(tokens, H, HD)
    key_pre = low_back(mat_high(normed_in, w_key)).reshape(tokens, H, HD)
    value_b = low(low_back(mat_high(normed_in, w_value))).reshape(tokens, H, HD)
    query_b = low(rotary(query_pre, positions))
    key_b = low(rotary(key_pre, positions))
    heads_b = low(low_back(attention(query_b, key_b, value_b)))
    resid_mid = hidden + low_back(mat_high(heads_b, w_out))
    moe_in = low(rms_norm(resid_mid, moe_gain))
    logits = low_back(mat_high(moe_in, router))
    router_p = jax.nn.softmax(logits, axis=1)
    picked = lax.optimization_barrier(jnp.sum((chosen[:, :, None] == jnp.arange(EXPERTS, dtype=jnp.int32)[None, None, :]).astype(jnp.float32), axis=1))
    mixing = router_p * picked
    shared_a = low_back(mat_high(moe_in, shared_gate))
    shared_b = low_back(mat_high(moe_in, shared_up))
    shared_out = low_back(mat_high(low(jax.nn.silu(shared_a) * shared_b), shared_down))

    def expert_step(running, inputs):
        gate_w, up_w, down_w, column = inputs
        expert_a = low_back(mat_high(moe_in, gate_w))
        expert_up_proj = low_back(mat_high(moe_in, up_w))
        expert_y = low_back(mat_high(low(jax.nn.silu(expert_a) * expert_up_proj), down_w))
        return (running + column[:, None] * expert_y, None)
    routed = lax.scan(jax.checkpoint(expert_step), jnp.zeros((tokens, D), jnp.float32), (expert_gate, expert_up, expert_down, mixing.T))[0]
    return resid_mid + shared_out + routed

def reference(hidden_in, positions, chosen, out_grad, attn_gain, w_query, w_key, w_value, w_out, moe_gain, router, shared_gate, shared_up, shared_down, expert_gate, expert_up, expert_down):
    params = tuple((weight_arr.astype(jnp.float32) for weight_arr in (attn_gain, w_query, w_key, w_value, w_out, moe_gain, router, shared_gate, shared_up, shared_down, expert_gate, expert_up, expert_down)))
    hidden = hidden_in.astype(jnp.float32)

    def closed(hidden_val, params_val):
        return forward(params_val, hidden_val, positions, chosen)
    result, pullback = jax.vjp(closed, hidden, params)
    input_grad, param_grads = pullback(out_grad.astype(jnp.float32))
    return (result.astype(jnp.bfloat16), input_grad, param_grads[0], param_grads[1], param_grads[2], param_grads[3], param_grads[4], param_grads[5], param_grads[6], param_grads[7], param_grads[8], param_grads[9], param_grads[10], param_grads[11], param_grads[12])
```

```python
import jax
import jax.numpy as jnp
from jax import lax
from jax.sharding import PartitionSpec as P

HD = 128
TOPK = 6


EPS = 1e-06
NEG_BIG = -1e30


def as_sent(value):
    return jax.tree.map(lambda a: a.astype(jnp.bfloat16) if a.dtype == jnp.float32 else a, value)


def features(local_part):
    return lax.all_gather(local_part, "tp", axis=1, tiled=True)


def row_stats(partial_terms):
    return lax.psum(partial_terms, "tp")


def partial_sums(partial_terms):
    return jax.tree.map(
        lambda part: part.astype(jnp.float32),
        lax.psum_scatter(as_sent(partial_terms), "tp", scatter_dimension=1, tiled=True),
    )


def to_owners(slot_rows):
    return lax.all_to_all(slot_rows, "ctx", split_axis=0, concat_axis=2, tiled=True)


def to_sources(slot_rows):
    return lax.all_to_all(
        slot_rows.astype(jnp.bfloat16), "ctx", split_axis=2, concat_axis=0, tiled=True
    ).astype(slot_rows.dtype)


def rotary(values, positions, rotate_sign):
    half_dim = values.shape[-1] // 2
    inverse = 10000.0 ** (-jnp.arange(half_dim, dtype=jnp.float32) * 2.0 / values.shape[-1])
    angles = positions.astype(jnp.float32)[:, None] * inverse[None, :]
    cosine = jnp.cos(angles)[:, None, :]
    sine_val = rotate_sign * jnp.sin(angles)[:, None, :]
    lower_half = values[..., :half_dim]
    upper_half = values[..., half_dim:]
    return jnp.concatenate(
        [lower_half * cosine - upper_half * sine_val, upper_half * cosine + lower_half * sine_val],
        axis=-1,
    )


def norm_rows(values, gain_part, model_width):
    square_sum = row_stats(jnp.sum(values * values, axis=1))
    row_scale = lax.rsqrt(square_sum / model_width + EPS)
    return (values * row_scale[:, None] * gain_part[None, :], row_scale)


def norm_back(values, row_scale, gain_part, grad_normed, model_width, tp_rank):
    quarter = values.shape[1]
    local_sum = jnp.sum(grad_normed * gain_part[None, :] * values, axis=1)
    gain_local = jnp.sum(grad_normed * values * row_scale[:, None], axis=0)
    gain_whole = lax.dynamic_update_slice_in_dim(
        jnp.zeros((model_width,), jnp.float32), gain_local, tp_rank * quarter, 0
    )
    row_total, gain_grad = row_stats((local_sum, gain_whole))
    back = (
        row_scale[:, None] * gain_part[None, :] * grad_normed
        - values * (row_scale**3 * row_total / model_width)[:, None]
    )
    return (back, gain_grad)


def scatter_slots(assign_rows, flat_exp, slot_of, n_exp, capacity):
    buffer = jnp.zeros((n_exp, capacity, assign_rows.shape[1]), assign_rows.dtype)
    return buffer.at[flat_exp, slot_of].set(assign_rows)


def silu_grad(pre_act):
    sigmoid_val = jax.nn.sigmoid(pre_act)
    return sigmoid_val * (1.0 + pre_act * (1.0 - sigmoid_val))


def keep_state(carried):
    return carried


def per_device(
    hidden_in,
    positions,
    chosen,
    out_grad,
    attn_gain,
    w_query,
    w_key,
    w_value,
    w_out,
    moe_gain,
    router,
    shared_gate,
    shared_up,
    shared_down,
    expert_gate,
    expert_up,
    expert_down,
):
    tp_rank = lax.axis_index("tp")
    ctx_rank = lax.axis_index("ctx")
    n_ctx = lax.axis_size("ctx")
    tok_rows, quarter = hidden_in.shape
    model_width = quarter * lax.axis_size("tp")
    gain_one, wq_all, wk_all, wv_all, gain_two, router_all, gate_all, up_all, wo_all, down_all = (
        lax.all_gather(attn_gain, ("fsdp", "ctx"), axis=0, tiled=True),
        lax.all_gather(w_query, ("fsdp", "ctx"), axis=0, tiled=True),
        lax.all_gather(w_key, ("fsdp", "ctx"), axis=0, tiled=True),
        lax.all_gather(w_value, ("fsdp", "ctx"), axis=0, tiled=True),
        lax.all_gather(moe_gain, ("fsdp", "ctx"), axis=0, tiled=True),
        lax.all_gather(router, ("fsdp", "ctx"), axis=0, tiled=True),
        lax.all_gather(shared_gate, ("fsdp", "ctx"), axis=0, tiled=True),
        lax.all_gather(shared_up, ("fsdp", "ctx"), axis=0, tiled=True),
        lax.all_gather(w_out, ("fsdp", "ctx"), axis=1, tiled=True),
        lax.all_gather(shared_down, ("fsdp", "ctx"), axis=1, tiled=True),
    )
    expert_gate_weights, expert_up_weights, expert_down_weights = (
        lax.all_gather(expert_gate, "fsdp", axis=1, tiled=True),
        lax.all_gather(expert_up, "fsdp", axis=1, tiled=True),
        lax.all_gather(expert_down, "fsdp", axis=2, tiled=True),
    )
    gain_q1 = lax.dynamic_slice_in_dim(gain_one, tp_rank * quarter, quarter).astype(jnp.float32)
    gain_q2 = lax.dynamic_slice_in_dim(gain_two, tp_rank * quarter, quarter).astype(jnp.float32)
    router_rows = lax.dynamic_slice_in_dim(router_all, tp_rank * quarter, quarter, 0)
    head_count = wq_all.shape[1] // HD
    scale_att = HD ** (-0.5)
    resid_in = hidden_in.astype(jnp.float32)
    normed_one, scale_one = norm_rows(resid_in, gain_q1, model_width)
    normed_in = features(normed_one.astype(jnp.bfloat16))
    query_pre = jnp.dot(normed_in, wq_all, preferred_element_type=jnp.float32).reshape(
        tok_rows, head_count, HD
    )
    key_pre = jnp.dot(normed_in, wk_all, preferred_element_type=jnp.float32).reshape(
        tok_rows, head_count, HD
    )
    value_b = (
        jnp.dot(normed_in, wv_all, preferred_element_type=jnp.float32)
        .astype(jnp.bfloat16)
        .reshape(tok_rows, head_count, HD)
    )
    query_b = rotary(query_pre, positions, 1.0).astype(jnp.bfloat16)
    key_b = rotary(key_pre, positions, 1.0).astype(jnp.bfloat16)
    q_start = ctx_rank * tok_rows
    row_pos = q_start + jnp.arange(tok_rows)
    start_state = (
        jnp.full((tok_rows, head_count), NEG_BIG, jnp.float32),
        jnp.zeros((tok_rows, head_count), jnp.float32),
        jnp.zeros((tok_rows, head_count, HD), jnp.float32),
    )
    keys_blk = lax.all_gather(key_b, "ctx", axis=0, tiled=True)
    vals_blk = lax.all_gather(value_b, "ctx", axis=0, tiled=True)
    key_count = keys_blk.shape[0]

    def compute(state_in):
        run_max, run_sum, run_acc = state_in
        scores = (
            jnp.einsum("qhd,khd->qhk", query_b, keys_blk, preferred_element_type=jnp.float32)
            * scale_att
        )
        visible = jnp.arange(key_count)[None, :] <= row_pos[:, None]
        scores = jnp.where(visible[:, None, :], scores, NEG_BIG)
        new_max = jnp.maximum(run_max, jnp.max(scores, axis=2))
        weights = jnp.exp(scores - new_max[:, :, None])
        new_sum = jnp.sum(weights, axis=2)
        new_acc = jnp.einsum(
            "qhk,khd->qhd",
            weights.astype(jnp.bfloat16),
            vals_blk,
            preferred_element_type=jnp.float32,
        )
        return (new_max, new_sum, new_acc)

    run_max, run_sum, run_acc = lax.cond(
        jnp.int32(0) <= q_start + tok_rows - 1, compute, keep_state, start_state
    )
    heads_f = run_acc / run_sum[:, :, None]
    log_sum = run_max + jnp.log(run_sum)
    heads_b = heads_f.astype(jnp.bfloat16).reshape(tok_rows, head_count * HD)
    resid_mid = resid_in + partial_sums(
        jnp.dot(heads_b, wo_all, preferred_element_type=jnp.float32)
    )
    normed_two, scale_two = norm_rows(resid_mid, gain_q2, model_width)
    moe_part = normed_two.astype(jnp.bfloat16)
    moe_in = features(moe_part)
    n_exp = router_all.shape[1]
    exp_dev = n_exp // n_ctx
    capacity = min(tok_rows, 5 * TOPK * tok_rows // (3 * n_exp))
    logits = jnp.dot(moe_in, router_all, preferred_element_type=jnp.float32)
    probs_all = jax.nn.softmax(logits, axis=1)
    picked = (chosen[:, :, None] == jnp.arange(n_exp)[None, None, :]).astype(jnp.float32)
    gate_vals = jnp.sum(picked * probs_all[:, None, :], axis=2)
    shared_a = jnp.dot(moe_in, gate_all, preferred_element_type=jnp.float32)
    shared_b = jnp.dot(moe_in, up_all, preferred_element_type=jnp.float32)
    shared_act = (jax.nn.silu(shared_a) * shared_b).astype(jnp.bfloat16)
    shared_out = jnp.dot(shared_act, down_all, preferred_element_type=jnp.float32)
    flat_exp = chosen.reshape(-1)
    flat_hot = (flat_exp[:, None] == jnp.arange(n_exp)[None, :]).astype(jnp.int32)
    slot_of = jnp.sum((jnp.cumsum(flat_hot, axis=0) - flat_hot) * flat_hot, axis=1)
    token_of = jnp.arange(tok_rows * TOPK) // TOPK
    slot_count = n_ctx * capacity
    outgoing = scatter_slots(moe_in[token_of], flat_exp, slot_of, n_exp, capacity)
    received_rows = to_owners(outgoing.reshape(n_ctx, exp_dev, capacity, model_width)).reshape(
        exp_dev, slot_count, model_width
    )
    expert_a = jnp.einsum(
        "bmw,bwv->bmv", received_rows, expert_gate_weights, preferred_element_type=jnp.float32
    )
    expert_up_proj = jnp.einsum(
        "bmw,bwv->bmv", received_rows, expert_up_weights, preferred_element_type=jnp.float32
    )
    expert_act = (jax.nn.silu(expert_a) * expert_up_proj).astype(jnp.bfloat16)
    expert_out = jnp.einsum(
        "erf,efd->erd", expert_act, expert_down_weights, preferred_element_type=jnp.float32
    )
    returned = to_sources(expert_out.reshape(1, exp_dev, slot_count, model_width))
    shared_q, slot_q = partial_sums((shared_out, returned.reshape(n_exp * capacity, model_width)))
    slot_rows = slot_q.reshape(n_exp, capacity, quarter)[flat_exp, slot_of].reshape(
        tok_rows, TOPK, quarter
    )
    result = resid_mid + shared_q + jnp.sum(gate_vals[:, :, None] * slot_rows, axis=1)
    layer_out = result.astype(jnp.bfloat16)
    grad_out = out_grad.astype(jnp.float32)
    gate_grad = row_stats(jnp.sum(grad_out[:, None, :] * slot_rows, axis=2))
    prob_grad = jnp.sum(gate_grad[:, :, None] * picked, axis=1)
    logit_grad = (
        probs_all * (prob_grad - jnp.sum(probs_all * prob_grad, axis=1, keepdims=True))
    ).astype(jnp.bfloat16)
    router_grad = jnp.einsum("td,te->de", moe_in, logit_grad, preferred_element_type=jnp.float32)
    router_back_q = jnp.einsum(
        "te,de->td", logit_grad, router_rows, preferred_element_type=jnp.float32
    )
    grad_full = features(out_grad)
    shared_dact = jnp.einsum("td,fd->tf", grad_full, down_all, preferred_element_type=jnp.float32)
    shared_da = (shared_dact * shared_b * silu_grad(shared_a)).astype(jnp.bfloat16)
    shared_db = (shared_dact * jax.nn.silu(shared_a)).astype(jnp.bfloat16)
    shared_down_grad = jnp.einsum(
        "tf,td->fd", shared_act, grad_full, preferred_element_type=jnp.float32
    )
    shared_gate_grad = jnp.einsum(
        "td,tf->df", moe_in, shared_da, preferred_element_type=jnp.float32
    )
    shared_up_grad = jnp.einsum("td,tf->df", moe_in, shared_db, preferred_element_type=jnp.float32)
    shared_back = jnp.einsum(
        "tf,df->td", shared_da, gate_all, preferred_element_type=jnp.float32
    ) + jnp.einsum("tf,df->td", shared_db, up_all, preferred_element_type=jnp.float32)
    assign_grad = (
        (gate_vals[:, :, None] * grad_full[:, None, :])
        .astype(jnp.bfloat16)
        .reshape(tok_rows * TOPK, model_width)
    )
    grad_slots = scatter_slots(assign_grad, flat_exp, slot_of, n_exp, capacity)
    grad_arrived = to_owners(grad_slots.reshape(n_ctx, exp_dev, capacity, model_width)).reshape(
        exp_dev, slot_count, model_width
    )
    expert_dact = jnp.einsum(
        "erd,efd->erf", grad_arrived, expert_down_weights, preferred_element_type=jnp.float32
    )
    expert_da = (expert_dact * expert_up_proj * silu_grad(expert_a)).astype(jnp.bfloat16)
    expert_up_proj_grad = (expert_dact * jax.nn.silu(expert_a)).astype(jnp.bfloat16)
    edown_grad = jnp.einsum(
        "erf,erd->efd", expert_act, grad_arrived, preferred_element_type=jnp.float32
    )
    egate_grad = jnp.einsum(
        "qgo,qgz->qoz", received_rows, expert_da, preferred_element_type=jnp.float32
    )
    expert_up_weight_grad = jnp.einsum(
        "qgo,qgz->qoz", received_rows, expert_up_proj_grad, preferred_element_type=jnp.float32
    )
    expert_back = jnp.einsum(
        "iac,igc->iag", expert_da, expert_gate_weights, preferred_element_type=jnp.float32
    ) + jnp.einsum(
        "iac,igc->iag", expert_up_proj_grad, expert_up_weights, preferred_element_type=jnp.float32
    )
    back_slots = to_sources(expert_back.reshape(1, exp_dev, slot_count, model_width)).reshape(
        n_exp, capacity, model_width
    )
    token_back = jnp.sum(back_slots[flat_exp, slot_of].reshape(tok_rows, TOPK, model_width), axis=1)
    moe_back_q = partial_sums(shared_back + token_back)
    mid_back, gain_two_grad = norm_back(
        resid_mid, scale_two, gain_q2, moe_back_q + router_back_q, model_width, tp_rank
    )
    mid_grad = grad_out + mid_back
    branch_full = features(mid_grad.astype(jnp.bfloat16))
    wo_grad = jnp.einsum("tf,td->fd", heads_b, branch_full, preferred_element_type=jnp.float32)
    heads_grad = (
        jnp.einsum("td,fd->tf", branch_full, wo_all, preferred_element_type=jnp.float32)
        .astype(jnp.bfloat16)
        .reshape(tok_rows, head_count, HD)
    )
    row_delta = jnp.sum(heads_grad.astype(jnp.float32) * heads_f, axis=2)
    seq_len = tok_rows * n_ctx
    back_state = (
        jnp.zeros((tok_rows, head_count, HD), jnp.float32),
        jnp.zeros((seq_len, head_count, HD), jnp.float32),
        jnp.zeros((seq_len, head_count, HD), jnp.float32),
    )
    attend_keys_blk = lax.all_gather(key_b, "ctx", axis=0, tiled=True)
    attend_vals_blk = lax.all_gather(value_b, "ctx", axis=0, tiled=True)
    attend_key_count = attend_keys_blk.shape[0]

    def compute(state_in):
        scores = (
            jnp.einsum("qhd,khd->qhk", query_b, attend_keys_blk, preferred_element_type=jnp.float32)
            * scale_att
        )
        visible = jnp.arange(attend_key_count)[None, :] <= row_pos[:, None]
        probs_blk = jnp.where(visible[:, None, :], jnp.exp(scores - log_sum[:, :, None]), 0.0)
        value_part = jnp.einsum(
            "qhk,qhd->khd",
            probs_blk.astype(jnp.bfloat16),
            heads_grad,
            preferred_element_type=jnp.float32,
        )
        dot_grad = jnp.einsum(
            "qhd,khd->qhk", heads_grad, attend_vals_blk, preferred_element_type=jnp.float32
        )
        score_grad = (probs_blk * (dot_grad - row_delta[:, :, None])).astype(jnp.bfloat16)
        query_acc = (
            jnp.einsum(
                "qhk,khd->qhd", score_grad, attend_keys_blk, preferred_element_type=jnp.float32
            )
            * scale_att
        )
        key_part = (
            jnp.einsum("qhk,qhd->khd", score_grad, query_b, preferred_element_type=jnp.float32)
            * scale_att
        )
        return (query_acc, key_part, value_part)

    query_grad, key_grad_all, value_grad_all = lax.cond(
        jnp.int32(0) <= q_start + tok_rows - 1, compute, keep_state, back_state
    )
    key_grad, value_grad = (
        lax.psum_scatter(
            key_grad_all.astype(jnp.bfloat16), "ctx", scatter_dimension=0, tiled=True
        ).astype(jnp.float32),
        lax.psum_scatter(
            value_grad_all.astype(jnp.bfloat16), "ctx", scatter_dimension=0, tiled=True
        ).astype(jnp.float32),
    )
    query_pre_grad = (
        rotary(query_grad, positions, -1.0).astype(jnp.bfloat16).reshape(tok_rows, head_count * HD)
    )
    key_pre_grad = (
        rotary(key_grad, positions, -1.0).astype(jnp.bfloat16).reshape(tok_rows, head_count * HD)
    )
    value_pre_grad = value_grad.astype(jnp.bfloat16).reshape(tok_rows, head_count * HD)
    wq_grad = jnp.einsum("td,tf->df", normed_in, query_pre_grad, preferred_element_type=jnp.float32)
    wk_grad = jnp.einsum("td,tf->df", normed_in, key_pre_grad, preferred_element_type=jnp.float32)
    wv_grad = jnp.einsum("td,tf->df", normed_in, value_pre_grad, preferred_element_type=jnp.float32)
    in_back = jnp.einsum("tf,df->td", query_pre_grad, wq_all, preferred_element_type=jnp.float32)
    in_back = in_back + jnp.einsum(
        "tf,df->td", key_pre_grad, wk_all, preferred_element_type=jnp.float32
    )
    in_back = in_back + jnp.einsum(
        "tf,df->td", value_pre_grad, wv_all, preferred_element_type=jnp.float32
    )
    first_back, gain_one_grad = norm_back(
        resid_in, scale_one, gain_q1, partial_sums(in_back), model_width, tp_rank
    )
    input_grad = mid_grad + first_back
    dense = (
        lax.psum_scatter(
            gain_one_grad.astype(jnp.bfloat16), ("fsdp", "ctx"), scatter_dimension=0, tiled=True
        ).astype(jnp.float32),
        lax.psum_scatter(
            wq_grad.astype(jnp.bfloat16), ("fsdp", "ctx"), scatter_dimension=0, tiled=True
        ).astype(jnp.float32),
        lax.psum_scatter(
            wk_grad.astype(jnp.bfloat16), ("fsdp", "ctx"), scatter_dimension=0, tiled=True
        ).astype(jnp.float32),
        lax.psum_scatter(
            wv_grad.astype(jnp.bfloat16), ("fsdp", "ctx"), scatter_dimension=0, tiled=True
        ).astype(jnp.float32),
        lax.psum_scatter(
            gain_two_grad.astype(jnp.bfloat16), ("fsdp", "ctx"), scatter_dimension=0, tiled=True
        ).astype(jnp.float32),
        lax.psum_scatter(
            router_grad.astype(jnp.bfloat16), ("fsdp", "ctx"), scatter_dimension=0, tiled=True
        ).astype(jnp.float32),
        lax.psum_scatter(
            shared_gate_grad.astype(jnp.bfloat16), ("fsdp", "ctx"), scatter_dimension=0, tiled=True
        ).astype(jnp.float32),
        lax.psum_scatter(
            shared_up_grad.astype(jnp.bfloat16), ("fsdp", "ctx"), scatter_dimension=0, tiled=True
        ).astype(jnp.float32),
        lax.psum_scatter(
            wo_grad.astype(jnp.bfloat16), ("fsdp", "ctx"), scatter_dimension=1, tiled=True
        ).astype(jnp.float32),
        lax.psum_scatter(
            shared_down_grad.astype(jnp.bfloat16), ("fsdp", "ctx"), scatter_dimension=1, tiled=True
        ).astype(jnp.float32),
    )
    experts_done = (
        lax.psum_scatter(
            egate_grad.astype(jnp.bfloat16), "fsdp", scatter_dimension=1, tiled=True
        ).astype(jnp.float32),
        lax.psum_scatter(
            expert_up_weight_grad.astype(jnp.bfloat16), "fsdp", scatter_dimension=1, tiled=True
        ).astype(jnp.float32),
        lax.psum_scatter(
            edown_grad.astype(jnp.bfloat16), "fsdp", scatter_dimension=2, tiled=True
        ).astype(jnp.float32),
    )
    return (
        layer_out,
        input_grad,
        dense[0],
        dense[1],
        dense[2],
        dense[3],
        dense[8],
        dense[4],
        dense[5],
        dense[6],
        dense[7],
        dense[9],
        experts_done[0],
        experts_done[1],
        experts_done[2],
    )


def per_device_seq(
    hidden_in,
    positions,
    chosen,
    out_grad,
    attn_gain,
    w_query,
    w_key,
    w_value,
    w_out,
    moe_gain,
    router,
    shared_gate,
    shared_up,
    shared_down,
    expert_gate,
    expert_up,
    expert_down,
):
    bf, f32 = jnp.bfloat16, jnp.float32
    f_rank, c_rank, t_rank = (lax.axis_index(name) for name in ("fsdp", "ctx", "tp"))
    n_f, n_c, n_t = (lax.axis_size(name) for name in ("fsdp", "ctx", "tp"))
    rows, quarter = hidden_in.shape
    width = quarter * n_t
    part = w_query.shape[0]
    seq = rows * n_c
    total = seq * n_f
    n_exp = router.shape[1]
    exp_dev = n_exp // n_c
    mine = exp_dev // n_f
    ffe = expert_gate.shape[2]
    shared_rows = shared_gate.shape[1] // (n_f * n_c)
    group = ("fsdp", "ctx")
    every = ("fsdp", "ctx", "tp")

    def nt(left, right):
        return lax.dot_general(left, right, (((1,), (1,)), ((), ())), preferred_element_type=f32)

    def tn(left, right):
        return lax.dot_general(left, right, (((0,), (0,)), ((), ())), preferred_element_type=f32)

    def nn(left, right):
        return jnp.dot(left, right, preferred_element_type=f32)

    def gather_seq(block):
        got = lax.all_gather(block, ("ctx", "tp"), axis=0, tiled=False)
        return got.reshape(n_c, n_t, rows, quarter).swapaxes(1, 2).reshape(seq, width)

    def gather_all(block):
        got = lax.all_gather(block, every, axis=0, tiled=False)
        return got.reshape(n_f * n_c, n_t, rows, quarter).swapaxes(1, 2).reshape(total, width)

    def scatter_seq(partial):
        blocks = partial.astype(bf).reshape(n_c, rows, n_t, quarter).swapaxes(1, 2)
        return lax.psum_scatter(
            blocks.reshape(n_c * n_t, rows, quarter), ("ctx", "tp"), scatter_dimension=0, tiled=True
        )[0].astype(f32)

    def scatter_all(partial):
        blocks = partial.astype(bf).reshape(n_f * n_c, rows, n_t, quarter).swapaxes(1, 2)
        return lax.psum_scatter(
            blocks.reshape(n_f * n_c * n_t, rows, quarter), every, scatter_dimension=0, tiled=True
        )[0].astype(f32)

    def by_head(weight):
        per_head = weight.T.reshape(n_c, HD, part)
        return jnp.broadcast_to(per_head[None], (n_f, n_c, HD, part)).reshape(n_f * n_c, HD, part)

    wo_heads = jnp.broadcast_to(w_out.reshape(1, n_c, HD, part), (n_f, n_c, HD, part))
    small = jnp.concatenate([attn_gain[None], moe_gain[None], router.T], axis=0)
    packed = jnp.concatenate(
        [
            by_head(w_query),
            by_head(w_key),
            by_head(w_value),
            wo_heads.reshape(n_f * n_c, HD, part),
            shared_gate.T.reshape(n_f * n_c, shared_rows, part),
            shared_up.T.reshape(n_f * n_c, shared_rows, part),
            shared_down.reshape(n_f * n_c, shared_rows, part),
            jnp.broadcast_to(small[None], (n_f * n_c,) + small.shape),
        ],
        axis=1,
    )
    arrived = lax.all_to_all(packed, group, split_axis=0, concat_axis=0, tiled=True)
    dense = arrived.swapaxes(0, 1).reshape(packed.shape[1], width)
    w_qkv = dense[: 3 * HD]
    wo = dense[3 * HD : 4 * HD]
    at = 4 * HD
    sg, su, sd = (dense[at + i * shared_rows : at + (i + 1) * shared_rows] for i in range(3))
    at = at + 3 * shared_rows
    gain_one = dense[at].astype(f32)
    gain_two = dense[at + 1].astype(f32)
    router_t = dense[at + 2 : at + 2 + n_exp]
    swap = [(i, n_f - 1 - i) for i in range(n_f)]

    def whole_experts(weight):
        kept = lax.dynamic_slice_in_dim(weight, f_rank * mine, mine, 0)
        given = lax.dynamic_slice_in_dim(weight, (n_f - 1 - f_rank) * mine, mine, 0)
        got = lax.ppermute(given, "fsdp", swap)
        low = jnp.where(f_rank == 0, kept, got)
        high = jnp.where(f_rank == 0, got, kept)
        return jnp.concatenate([low, high], axis=2).reshape(mine * ffe, width)

    eg = whole_experts(expert_gate.swapaxes(1, 2))
    eu = whole_experts(expert_up.swapaxes(1, 2))
    ed = whole_experts(expert_down)

    hidden_seq = gather_seq(hidden_in)
    grad_all = gather_all(out_grad)
    pos_seq = lax.all_gather(positions, "ctx", axis=0, tiled=True)
    chosen_all = lax.all_gather(chosen, group, axis=0, tiled=True)
    resid_in = hidden_in.astype(f32)
    hidden_f = hidden_seq.astype(f32)
    scale_seq = lax.rsqrt(jnp.mean(hidden_f * hidden_f, axis=1, keepdims=True) + EPS)
    normed_in = (hidden_f * scale_seq * gain_one[None, :]).astype(bf)
    qkv = nt(normed_in, w_qkv)
    half = HD // 2
    inverse = 10000.0 ** (-jnp.arange(half, dtype=f32) * 2.0 / HD)
    angles = pos_seq.astype(f32)[:, None] * inverse[None, :]
    cosine, sine = jnp.cos(angles), jnp.sin(angles)

    def rotate(values, sign):
        low, high = values[:, :half], values[:, half:]
        return jnp.concatenate(
            [low * cosine - sign * high * sine, high * cosine + sign * low * sine], axis=1
        )

    query_b = rotate(qkv[:, :HD], 1.0).astype(bf)
    key_b = rotate(qkv[:, HD : 2 * HD], 1.0).astype(bf)
    value_b = qkv[:, 2 * HD :].astype(bf)
    scale_att = HD ** (-0.5)
    visible = jnp.arange(seq)[None, :] <= jnp.arange(seq)[:, None]
    scores = jnp.where(visible, nt(query_b, key_b) * scale_att, NEG_BIG)
    top = jnp.max(scores, axis=1, keepdims=True)
    weights = jnp.exp(scores - top)
    norm = jnp.sum(weights, axis=1, keepdims=True)
    probs = weights / norm
    probs_b = probs.astype(bf)
    heads_f = nn(probs_b, value_b)
    heads_b = heads_f.astype(bf)
    resid_mid = resid_in + scatter_seq(nn(heads_b, wo))

    resid_all = gather_all(resid_mid.astype(bf)).astype(f32)
    scale_all = lax.rsqrt(jnp.mean(resid_all * resid_all, axis=1, keepdims=True) + EPS)
    moe_in = (resid_all * scale_all * gain_two[None, :]).astype(bf)
    probs_all = jax.nn.softmax(nt(moe_in, router_t), axis=1)
    picked = jnp.sum(
        (chosen_all[:, :, None] == jnp.arange(n_exp)[None, None, :]).astype(f32), axis=1
    )
    first = c_rank * exp_dev + f_rank * mine
    mine_hot = (
        jnp.arange(n_exp)[:, None] == first + jnp.arange(mine)[None, :]
    ).astype(f32)
    gate_mine = jnp.sum((probs_all * picked)[:, :, None] * mine_hot[None], axis=1)
    gate_cols = jnp.concatenate(
        [
            jnp.broadcast_to(gate_mine[:, :, None], (total, mine, ffe)).reshape(total, mine * ffe),
            jnp.ones((total, shared_rows), f32),
        ],
        axis=1,
    )
    wg = jnp.concatenate([eg, sg], axis=0)
    wu = jnp.concatenate([eu, su], axis=0)
    wd = jnp.concatenate([ed, sd], axis=0)
    pre_a = nt(moe_in, wg)
    pre_b = nt(moe_in, wu)
    sig = jax.nn.sigmoid(pre_a)
    silu_a = pre_a * sig
    act = (silu_a * pre_b).astype(bf).astype(f32)
    act_g = (act * gate_cols).astype(bf)
    moe_part = nn(act_g, wd)
    dact = nt(grad_all, wd)
    gate_part = jnp.sum(
        (act * dact)[:, : mine * ffe].reshape(total, mine, ffe), axis=2
    )
    p_part = jnp.sum(gate_part[:, None, :] * mine_hot[None], axis=2) * picked
    dact_g = dact * gate_cols
    da = (dact_g * pre_b * (sig * (1.0 + pre_a * (1.0 - sig)))).astype(bf)
    db = (dact_g * silu_a).astype(bf)
    back_part = nn(da, wg) + nn(db, wu)
    p_grad = lax.psum(p_part, every)
    back_q = scatter_all(back_part)
    layer_out = (resid_mid + scatter_all(moe_part)).astype(bf)
    logit_grad = (
        probs_all * (p_grad - jnp.sum(probs_all * p_grad, axis=1, keepdims=True))
    ).astype(bf)
    block = f_rank * n_c + c_rank
    own_logit = lax.dynamic_slice_in_dim(logit_grad, block * rows, rows, 0)
    router_q = lax.dynamic_slice_in_dim(router_t, t_rank * quarter, quarter, 1)
    moe_in_grad = back_q + nn(own_logit, router_q)
    moe_cols = lax.dynamic_slice_in_dim(moe_in, block * part, part, 1)
    router_grad = tn(moe_cols, logit_grad)
    gwd = tn(act_g, grad_all)
    gwg = tn(da, moe_in)
    gwu = tn(db, moe_in)

    def norm_back_rows(values, row_scale, gain_q, grad_normed):
        local = jnp.sum(grad_normed * gain_q[None, :] * values, axis=1)
        row_total = lax.psum(local, "tp")
        gain_local = jnp.sum(grad_normed * values * row_scale, axis=0)
        back = row_scale * gain_q[None, :] * grad_normed - values * (
            row_scale**3 * row_total[:, None] / width
        )
        return back, gain_local

    def own_rows(values):
        return lax.dynamic_slice_in_dim(values, c_rank * rows, rows, 0)

    gain_q1 = lax.dynamic_slice_in_dim(gain_one, t_rank * quarter, quarter)
    gain_q2 = lax.dynamic_slice_in_dim(gain_two, t_rank * quarter, quarter)
    scale_two = lax.dynamic_slice_in_dim(scale_all, block * rows, rows, 0)
    mid_back, gain_two_local = norm_back_rows(resid_mid, scale_two, gain_q2, moe_in_grad)
    mid_grad = out_grad.astype(f32) + mid_back
    mid_seq = gather_seq(mid_grad.astype(bf))

    heads_grad = nt(mid_seq, wo).astype(bf)
    gwo = tn(heads_b, mid_seq)
    delta = jnp.sum(heads_grad.astype(f32) * heads_f, axis=1, keepdims=True)
    value_grad = tn(probs_b, heads_grad)
    score_grad = (probs * (nt(heads_grad, value_b) - delta)).astype(bf)
    query_grad = nn(score_grad, key_b) * scale_att
    key_grad = tn(score_grad, query_b) * scale_att
    dqkv = jnp.concatenate(
        [rotate(query_grad, -1.0).astype(bf), rotate(key_grad, -1.0).astype(bf), value_grad.astype(bf)],
        axis=1,
    )
    in_back = scatter_seq(nn(dqkv, w_qkv))
    gqkv = tn(dqkv, normed_in)
    scale_one = own_rows(scale_seq)
    first_back, gain_one_local = norm_back_rows(resid_in, scale_one, gain_q1, in_back)
    input_grad = mid_grad + first_back

    def placed(gain_local):
        return lax.dynamic_update_slice_in_dim(
            jnp.zeros((width,), f32), gain_local, t_rank * quarter, 0
        )

    gains = lax.psum(jnp.stack([placed(gain_one_local), placed(gain_two_local)]), every)
    gains = lax.dynamic_slice_in_dim(gains, block * part, part, 1)

    def to_owner(grad_rows):
        sent = grad_rows.astype(bf).reshape(-1, n_f * n_c, part).swapaxes(0, 1)
        return lax.all_to_all(sent, group, split_axis=0, concat_axis=0, tiled=True).astype(f32)

    attn_sent = jnp.concatenate([gqkv, gwo], axis=0)
    attn_back = to_owner(attn_sent).reshape(n_f, n_c, 4, HD, part).sum(axis=0)
    shared_sent = jnp.concatenate([g[mine * ffe :] for g in (gwg, gwu, gwd)], axis=0)
    shared_back = to_owner(shared_sent).reshape(n_f * n_c, 3, shared_rows, part)

    def head_cols(i):
        return attn_back[:, i].reshape(n_c * HD, part)

    def shared_cols(i):
        return shared_back[:, i].reshape(n_f * n_c * shared_rows, part)

    def expert_owner(grad_rows):
        grad_rows = grad_rows[: mine * ffe].reshape(mine, ffe, width)
        piece = width // n_f
        kept = lax.dynamic_slice_in_dim(grad_rows, f_rank * piece, piece, 2)
        given = lax.dynamic_slice_in_dim(grad_rows, (n_f - 1 - f_rank) * piece, piece, 2)
        got = lax.ppermute(given.astype(bf), "fsdp", swap).astype(f32)
        return jnp.concatenate(
            [jnp.where(f_rank == 0, kept, got), jnp.where(f_rank == 0, got, kept)], axis=0
        )

    return (
        layer_out,
        input_grad,
        gains[0],
        head_cols(0).T,
        head_cols(1).T,
        head_cols(2).T,
        head_cols(3),
        gains[1],
        router_grad,
        shared_cols(0).T,
        shared_cols(1).T,
        shared_cols(2),
        expert_owner(gwg).swapaxes(1, 2),
        expert_owner(gwu).swapaxes(1, 2),
        expert_owner(gwd),
    )


def one_head_each(mesh, args):
    n_f, n_c, n_t = (mesh.shape[name] for name in ("fsdp", "ctx", "tp"))
    heads = args[5].shape[1] // HD
    experts = args[10].shape[1]
    return (
        n_f == 2
        and n_t == 4
        and heads == n_c * n_t
        and experts % (n_f * n_c) == 0
        and args[11].shape[1] % (8 * n_f * n_c * n_t) == 0
    )


def solution(mesh):
    placed = (
        P(("fsdp", "ctx"), "tp"),
        P(("fsdp", "ctx")),
        P(("fsdp", "ctx"), None),
        P(("fsdp", "ctx"), "tp"),
        P(("fsdp", "ctx")),
        P(("fsdp", "ctx"), "tp"),
        P(("fsdp", "ctx"), "tp"),
        P(("fsdp", "ctx"), "tp"),
        P("tp", ("fsdp", "ctx")),
        P(("fsdp", "ctx")),
        P(("fsdp", "ctx"), None),
        P(("fsdp", "ctx"), "tp"),
        P(("fsdp", "ctx"), "tp"),
        P("tp", ("fsdp", "ctx")),
        P("ctx", "fsdp", "tp"),
        P("ctx", "fsdp", "tp"),
        P("ctx", "tp", "fsdp"),
    )
    def run(*args):
        body = per_device_seq if one_head_each(mesh, args) else per_device
        return jax.shard_map(
        body,
        mesh=mesh,
        in_specs=placed,
        out_specs=(
            P(("fsdp", "ctx"), "tp"),
            P(("fsdp", "ctx"), "tp"),
            P(("fsdp", "ctx")),
            P(("fsdp", "ctx"), "tp"),
            P(("fsdp", "ctx"), "tp"),
            P(("fsdp", "ctx"), "tp"),
            P("tp", ("fsdp", "ctx")),
            P(("fsdp", "ctx")),
            P(("fsdp", "ctx"), None),
            P(("fsdp", "ctx"), "tp"),
            P(("fsdp", "ctx"), "tp"),
            P("tp", ("fsdp", "ctx")),
            P("ctx", "fsdp", "tp"),
            P("ctx", "fsdp", "tp"),
            P("ctx", "tp", "fsdp"),
        ),
        check_vma=False,
    )(*args)

    return run
```

```python
import functools

import jax
import jax.numpy as jnp
from jax import lax
from jax.experimental import pallas as pl
from jax.experimental.pallas import tpu as pltpu
from jax.sharding import PartitionSpec as P

HD = 128
TOPK = 6


EPS = 1e-06
NEG_BIG = -1e30


def as_sent(value):
    return jax.tree.map(lambda a: a.astype(jnp.bfloat16) if a.dtype == jnp.float32 else a, value)


def features(local_part):
    return lax.all_gather(local_part, "tp", axis=1, tiled=True)


def row_stats(partial_terms):
    return lax.psum(partial_terms, "tp")


def partial_sums(partial_terms):
    return jax.tree.map(
        lambda part: part.astype(jnp.float32),
        lax.psum_scatter(as_sent(partial_terms), "tp", scatter_dimension=1, tiled=True),
    )


def to_owners(slot_rows):
    return lax.all_to_all(slot_rows, "ctx", split_axis=0, concat_axis=2, tiled=True)


def to_sources(slot_rows):
    return lax.all_to_all(
        slot_rows.astype(jnp.bfloat16), "ctx", split_axis=2, concat_axis=0, tiled=True
    ).astype(slot_rows.dtype)


def rotary(values, positions, rotate_sign):
    half_dim = values.shape[-1] // 2
    inverse = 10000.0 ** (-jnp.arange(half_dim, dtype=jnp.float32) * 2.0 / values.shape[-1])
    angles = positions.astype(jnp.float32)[:, None] * inverse[None, :]
    cosine = jnp.cos(angles)[:, None, :]
    sine_val = rotate_sign * jnp.sin(angles)[:, None, :]
    lower_half = values[..., :half_dim]
    upper_half = values[..., half_dim:]
    return jnp.concatenate(
        [lower_half * cosine - upper_half * sine_val, upper_half * cosine + lower_half * sine_val],
        axis=-1,
    )


def norm_rows(values, gain_part, model_width):
    square_sum = row_stats(jnp.sum(values * values, axis=1))
    row_scale = lax.rsqrt(square_sum / model_width + EPS)
    return (values * row_scale[:, None] * gain_part[None, :], row_scale)


def norm_back(values, row_scale, gain_part, grad_normed, model_width, tp_rank):
    quarter = values.shape[1]
    local_sum = jnp.sum(grad_normed * gain_part[None, :] * values, axis=1)
    gain_local = jnp.sum(grad_normed * values * row_scale[:, None], axis=0)
    gain_whole = lax.dynamic_update_slice_in_dim(
        jnp.zeros((model_width,), jnp.float32), gain_local, tp_rank * quarter, 0
    )
    row_total, gain_grad = row_stats((local_sum, gain_whole))
    back = (
        row_scale[:, None] * gain_part[None, :] * grad_normed
        - values * (row_scale**3 * row_total / model_width)[:, None]
    )
    return (back, gain_grad)


def scatter_slots(assign_rows, flat_exp, slot_of, n_exp, capacity):
    buffer = jnp.zeros((n_exp, capacity, assign_rows.shape[1]), assign_rows.dtype)
    return buffer.at[flat_exp, slot_of].set(assign_rows)


def silu_grad(pre_act):
    sigmoid_val = jax.nn.sigmoid(pre_act)
    return sigmoid_val * (1.0 + pre_act * (1.0 - sigmoid_val))


def keep_state(carried):
    return carried


def per_device(
    hidden_in,
    positions,
    chosen,
    out_grad,
    attn_gain,
    w_query,
    w_key,
    w_value,
    w_out,
    moe_gain,
    router,
    shared_gate,
    shared_up,
    shared_down,
    expert_gate,
    expert_up,
    expert_down,
):
    tp_rank = lax.axis_index("tp")
    ctx_rank = lax.axis_index("ctx")
    n_ctx = lax.axis_size("ctx")
    tok_rows, quarter = hidden_in.shape
    model_width = quarter * lax.axis_size("tp")
    gain_one, wq_all, wk_all, wv_all, gain_two, router_all, gate_all, up_all, wo_all, down_all = (
        lax.all_gather(attn_gain, ("fsdp", "ctx"), axis=0, tiled=True),
        lax.all_gather(w_query, ("fsdp", "ctx"), axis=0, tiled=True),
        lax.all_gather(w_key, ("fsdp", "ctx"), axis=0, tiled=True),
        lax.all_gather(w_value, ("fsdp", "ctx"), axis=0, tiled=True),
        lax.all_gather(moe_gain, ("fsdp", "ctx"), axis=0, tiled=True),
        lax.all_gather(router, ("fsdp", "ctx"), axis=0, tiled=True),
        lax.all_gather(shared_gate, ("fsdp", "ctx"), axis=0, tiled=True),
        lax.all_gather(shared_up, ("fsdp", "ctx"), axis=0, tiled=True),
        lax.all_gather(w_out, ("fsdp", "ctx"), axis=1, tiled=True),
        lax.all_gather(shared_down, ("fsdp", "ctx"), axis=1, tiled=True),
    )
    expert_gate_weights, expert_up_weights, expert_down_weights = (
        lax.all_gather(expert_gate, "fsdp", axis=1, tiled=True),
        lax.all_gather(expert_up, "fsdp", axis=1, tiled=True),
        lax.all_gather(expert_down, "fsdp", axis=2, tiled=True),
    )
    gain_q1 = lax.dynamic_slice_in_dim(gain_one, tp_rank * quarter, quarter).astype(jnp.float32)
    gain_q2 = lax.dynamic_slice_in_dim(gain_two, tp_rank * quarter, quarter).astype(jnp.float32)
    router_rows = lax.dynamic_slice_in_dim(router_all, tp_rank * quarter, quarter, 0)
    head_count = wq_all.shape[1] // HD
    scale_att = HD ** (-0.5)
    resid_in = hidden_in.astype(jnp.float32)
    normed_one, scale_one = norm_rows(resid_in, gain_q1, model_width)
    normed_in = features(normed_one.astype(jnp.bfloat16))
    query_pre = jnp.dot(normed_in, wq_all, preferred_element_type=jnp.float32).reshape(
        tok_rows, head_count, HD
    )
    key_pre = jnp.dot(normed_in, wk_all, preferred_element_type=jnp.float32).reshape(
        tok_rows, head_count, HD
    )
    value_b = (
        jnp.dot(normed_in, wv_all, preferred_element_type=jnp.float32)
        .astype(jnp.bfloat16)
        .reshape(tok_rows, head_count, HD)
    )
    query_b = rotary(query_pre, positions, 1.0).astype(jnp.bfloat16)
    key_b = rotary(key_pre, positions, 1.0).astype(jnp.bfloat16)
    q_start = ctx_rank * tok_rows
    row_pos = q_start + jnp.arange(tok_rows)
    start_state = (
        jnp.full((tok_rows, head_count), NEG_BIG, jnp.float32),
        jnp.zeros((tok_rows, head_count), jnp.float32),
        jnp.zeros((tok_rows, head_count, HD), jnp.float32),
    )
    keys_blk = lax.all_gather(key_b, "ctx", axis=0, tiled=True)
    vals_blk = lax.all_gather(value_b, "ctx", axis=0, tiled=True)
    key_count = keys_blk.shape[0]

    def compute(state_in):
        run_max, run_sum, run_acc = state_in
        scores = (
            jnp.einsum("qhd,khd->qhk", query_b, keys_blk, preferred_element_type=jnp.float32)
            * scale_att
        )
        visible = jnp.arange(key_count)[None, :] <= row_pos[:, None]
        scores = jnp.where(visible[:, None, :], scores, NEG_BIG)
        new_max = jnp.maximum(run_max, jnp.max(scores, axis=2))
        weights = jnp.exp(scores - new_max[:, :, None])
        new_sum = jnp.sum(weights, axis=2)
        new_acc = jnp.einsum(
            "qhk,khd->qhd",
            weights.astype(jnp.bfloat16),
            vals_blk,
            preferred_element_type=jnp.float32,
        )
        return (new_max, new_sum, new_acc)

    run_max, run_sum, run_acc = lax.cond(
        jnp.int32(0) <= q_start + tok_rows - 1, compute, keep_state, start_state
    )
    heads_f = run_acc / run_sum[:, :, None]
    log_sum = run_max + jnp.log(run_sum)
    heads_b = heads_f.astype(jnp.bfloat16).reshape(tok_rows, head_count * HD)
    resid_mid = resid_in + partial_sums(
        jnp.dot(heads_b, wo_all, preferred_element_type=jnp.float32)
    )
    normed_two, scale_two = norm_rows(resid_mid, gain_q2, model_width)
    moe_part = normed_two.astype(jnp.bfloat16)
    moe_in = features(moe_part)
    n_exp = router_all.shape[1]
    exp_dev = n_exp // n_ctx
    capacity = min(tok_rows, 5 * TOPK * tok_rows // (3 * n_exp))
    logits = jnp.dot(moe_in, router_all, preferred_element_type=jnp.float32)
    probs_all = jax.nn.softmax(logits, axis=1)
    picked = (chosen[:, :, None] == jnp.arange(n_exp)[None, None, :]).astype(jnp.float32)
    gate_vals = jnp.sum(picked * probs_all[:, None, :], axis=2)
    shared_a = jnp.dot(moe_in, gate_all, preferred_element_type=jnp.float32)
    shared_b = jnp.dot(moe_in, up_all, preferred_element_type=jnp.float32)
    shared_act = (jax.nn.silu(shared_a) * shared_b).astype(jnp.bfloat16)
    shared_out = jnp.dot(shared_act, down_all, preferred_element_type=jnp.float32)
    flat_exp = chosen.reshape(-1)
    flat_hot = (flat_exp[:, None] == jnp.arange(n_exp)[None, :]).astype(jnp.int32)
    slot_of = jnp.sum((jnp.cumsum(flat_hot, axis=0) - flat_hot) * flat_hot, axis=1)
    token_of = jnp.arange(tok_rows * TOPK) // TOPK
    slot_count = n_ctx * capacity
    outgoing = scatter_slots(moe_in[token_of], flat_exp, slot_of, n_exp, capacity)
    received_rows = to_owners(outgoing.reshape(n_ctx, exp_dev, capacity, model_width)).reshape(
        exp_dev, slot_count, model_width
    )
    expert_a = jnp.einsum(
        "bmw,bwv->bmv", received_rows, expert_gate_weights, preferred_element_type=jnp.float32
    )
    expert_up_proj = jnp.einsum(
        "bmw,bwv->bmv", received_rows, expert_up_weights, preferred_element_type=jnp.float32
    )
    expert_act = (jax.nn.silu(expert_a) * expert_up_proj).astype(jnp.bfloat16)
    expert_out = jnp.einsum(
        "erf,efd->erd", expert_act, expert_down_weights, preferred_element_type=jnp.float32
    )
    returned = to_sources(expert_out.reshape(1, exp_dev, slot_count, model_width))
    shared_q, slot_q = partial_sums((shared_out, returned.reshape(n_exp * capacity, model_width)))
    slot_rows = slot_q.reshape(n_exp, capacity, quarter)[flat_exp, slot_of].reshape(
        tok_rows, TOPK, quarter
    )
    result = resid_mid + shared_q + jnp.sum(gate_vals[:, :, None] * slot_rows, axis=1)
    layer_out = result.astype(jnp.bfloat16)
    grad_out = out_grad.astype(jnp.float32)
    gate_grad = row_stats(jnp.sum(grad_out[:, None, :] * slot_rows, axis=2))
    prob_grad = jnp.sum(gate_grad[:, :, None] * picked, axis=1)
    logit_grad = (
        probs_all * (prob_grad - jnp.sum(probs_all * prob_grad, axis=1, keepdims=True))
    ).astype(jnp.bfloat16)
    router_grad = jnp.einsum("td,te->de", moe_in, logit_grad, preferred_element_type=jnp.float32)
    router_back_q = jnp.einsum(
        "te,de->td", logit_grad, router_rows, preferred_element_type=jnp.float32
    )
    grad_full = features(out_grad)
    shared_dact = jnp.einsum("td,fd->tf", grad_full, down_all, preferred_element_type=jnp.float32)
    shared_da = (shared_dact * shared_b * silu_grad(shared_a)).astype(jnp.bfloat16)
    shared_db = (shared_dact * jax.nn.silu(shared_a)).astype(jnp.bfloat16)
    shared_down_grad = jnp.einsum(
        "tf,td->fd", shared_act, grad_full, preferred_element_type=jnp.float32
    )
    shared_gate_grad = jnp.einsum(
        "td,tf->df", moe_in, shared_da, preferred_element_type=jnp.float32
    )
    shared_up_grad = jnp.einsum("td,tf->df", moe_in, shared_db, preferred_element_type=jnp.float32)
    shared_back = jnp.einsum(
        "tf,df->td", shared_da, gate_all, preferred_element_type=jnp.float32
    ) + jnp.einsum("tf,df->td", shared_db, up_all, preferred_element_type=jnp.float32)
    assign_grad = (
        (gate_vals[:, :, None] * grad_full[:, None, :])
        .astype(jnp.bfloat16)
        .reshape(tok_rows * TOPK, model_width)
    )
    grad_slots = scatter_slots(assign_grad, flat_exp, slot_of, n_exp, capacity)
    grad_arrived = to_owners(grad_slots.reshape(n_ctx, exp_dev, capacity, model_width)).reshape(
        exp_dev, slot_count, model_width
    )
    expert_dact = jnp.einsum(
        "erd,efd->erf", grad_arrived, expert_down_weights, preferred_element_type=jnp.float32
    )
    expert_da = (expert_dact * expert_up_proj * silu_grad(expert_a)).astype(jnp.bfloat16)
    expert_up_proj_grad = (expert_dact * jax.nn.silu(expert_a)).astype(jnp.bfloat16)
    edown_grad = jnp.einsum(
        "erf,erd->efd", expert_act, grad_arrived, preferred_element_type=jnp.float32
    )
    egate_grad = jnp.einsum(
        "qgo,qgz->qoz", received_rows, expert_da, preferred_element_type=jnp.float32
    )
    expert_up_weight_grad = jnp.einsum(
        "qgo,qgz->qoz", received_rows, expert_up_proj_grad, preferred_element_type=jnp.float32
    )
    expert_back = jnp.einsum(
        "iac,igc->iag", expert_da, expert_gate_weights, preferred_element_type=jnp.float32
    ) + jnp.einsum(
        "iac,igc->iag", expert_up_proj_grad, expert_up_weights, preferred_element_type=jnp.float32
    )
    back_slots = to_sources(expert_back.reshape(1, exp_dev, slot_count, model_width)).reshape(
        n_exp, capacity, model_width
    )
    token_back = jnp.sum(back_slots[flat_exp, slot_of].reshape(tok_rows, TOPK, model_width), axis=1)
    moe_back_q = partial_sums(shared_back + token_back)
    mid_back, gain_two_grad = norm_back(
        resid_mid, scale_two, gain_q2, moe_back_q + router_back_q, model_width, tp_rank
    )
    mid_grad = grad_out + mid_back
    branch_full = features(mid_grad.astype(jnp.bfloat16))
    wo_grad = jnp.einsum("tf,td->fd", heads_b, branch_full, preferred_element_type=jnp.float32)
    heads_grad = (
        jnp.einsum("td,fd->tf", branch_full, wo_all, preferred_element_type=jnp.float32)
        .astype(jnp.bfloat16)
        .reshape(tok_rows, head_count, HD)
    )
    row_delta = jnp.sum(heads_grad.astype(jnp.float32) * heads_f, axis=2)
    seq_len = tok_rows * n_ctx
    back_state = (
        jnp.zeros((tok_rows, head_count, HD), jnp.float32),
        jnp.zeros((seq_len, head_count, HD), jnp.float32),
        jnp.zeros((seq_len, head_count, HD), jnp.float32),
    )
    attend_keys_blk = lax.all_gather(key_b, "ctx", axis=0, tiled=True)
    attend_vals_blk = lax.all_gather(value_b, "ctx", axis=0, tiled=True)
    attend_key_count = attend_keys_blk.shape[0]

    def compute(state_in):
        scores = (
            jnp.einsum("qhd,khd->qhk", query_b, attend_keys_blk, preferred_element_type=jnp.float32)
            * scale_att
        )
        visible = jnp.arange(attend_key_count)[None, :] <= row_pos[:, None]
        probs_blk = jnp.where(visible[:, None, :], jnp.exp(scores - log_sum[:, :, None]), 0.0)
        value_part = jnp.einsum(
            "qhk,qhd->khd",
            probs_blk.astype(jnp.bfloat16),
            heads_grad,
            preferred_element_type=jnp.float32,
        )
        dot_grad = jnp.einsum(
            "qhd,khd->qhk", heads_grad, attend_vals_blk, preferred_element_type=jnp.float32
        )
        score_grad = (probs_blk * (dot_grad - row_delta[:, :, None])).astype(jnp.bfloat16)
        query_acc = (
            jnp.einsum(
                "qhk,khd->qhd", score_grad, attend_keys_blk, preferred_element_type=jnp.float32
            )
            * scale_att
        )
        key_part = (
            jnp.einsum("qhk,qhd->khd", score_grad, query_b, preferred_element_type=jnp.float32)
            * scale_att
        )
        return (query_acc, key_part, value_part)

    query_grad, key_grad_all, value_grad_all = lax.cond(
        jnp.int32(0) <= q_start + tok_rows - 1, compute, keep_state, back_state
    )
    key_grad, value_grad = (
        lax.psum_scatter(
            key_grad_all.astype(jnp.bfloat16), "ctx", scatter_dimension=0, tiled=True
        ).astype(jnp.float32),
        lax.psum_scatter(
            value_grad_all.astype(jnp.bfloat16), "ctx", scatter_dimension=0, tiled=True
        ).astype(jnp.float32),
    )
    query_pre_grad = (
        rotary(query_grad, positions, -1.0).astype(jnp.bfloat16).reshape(tok_rows, head_count * HD)
    )
    key_pre_grad = (
        rotary(key_grad, positions, -1.0).astype(jnp.bfloat16).reshape(tok_rows, head_count * HD)
    )
    value_pre_grad = value_grad.astype(jnp.bfloat16).reshape(tok_rows, head_count * HD)
    wq_grad = jnp.einsum("td,tf->df", normed_in, query_pre_grad, preferred_element_type=jnp.float32)
    wk_grad = jnp.einsum("td,tf->df", normed_in, key_pre_grad, preferred_element_type=jnp.float32)
    wv_grad = jnp.einsum("td,tf->df", normed_in, value_pre_grad, preferred_element_type=jnp.float32)
    in_back = jnp.einsum("tf,df->td", query_pre_grad, wq_all, preferred_element_type=jnp.float32)
    in_back = in_back + jnp.einsum(
        "tf,df->td", key_pre_grad, wk_all, preferred_element_type=jnp.float32
    )
    in_back = in_back + jnp.einsum(
        "tf,df->td", value_pre_grad, wv_all, preferred_element_type=jnp.float32
    )
    first_back, gain_one_grad = norm_back(
        resid_in, scale_one, gain_q1, partial_sums(in_back), model_width, tp_rank
    )
    input_grad = mid_grad + first_back
    dense = (
        lax.psum_scatter(
            gain_one_grad.astype(jnp.bfloat16), ("fsdp", "ctx"), scatter_dimension=0, tiled=True
        ).astype(jnp.float32),
        lax.psum_scatter(
            wq_grad.astype(jnp.bfloat16), ("fsdp", "ctx"), scatter_dimension=0, tiled=True
        ).astype(jnp.float32),
        lax.psum_scatter(
            wk_grad.astype(jnp.bfloat16), ("fsdp", "ctx"), scatter_dimension=0, tiled=True
        ).astype(jnp.float32),
        lax.psum_scatter(
            wv_grad.astype(jnp.bfloat16), ("fsdp", "ctx"), scatter_dimension=0, tiled=True
        ).astype(jnp.float32),
        lax.psum_scatter(
            gain_two_grad.astype(jnp.bfloat16), ("fsdp", "ctx"), scatter_dimension=0, tiled=True
        ).astype(jnp.float32),
        lax.psum_scatter(
            router_grad.astype(jnp.bfloat16), ("fsdp", "ctx"), scatter_dimension=0, tiled=True
        ).astype(jnp.float32),
        lax.psum_scatter(
            shared_gate_grad.astype(jnp.bfloat16), ("fsdp", "ctx"), scatter_dimension=0, tiled=True
        ).astype(jnp.float32),
        lax.psum_scatter(
            shared_up_grad.astype(jnp.bfloat16), ("fsdp", "ctx"), scatter_dimension=0, tiled=True
        ).astype(jnp.float32),
        lax.psum_scatter(
            wo_grad.astype(jnp.bfloat16), ("fsdp", "ctx"), scatter_dimension=1, tiled=True
        ).astype(jnp.float32),
        lax.psum_scatter(
            shared_down_grad.astype(jnp.bfloat16), ("fsdp", "ctx"), scatter_dimension=1, tiled=True
        ).astype(jnp.float32),
    )
    experts_done = (
        lax.psum_scatter(
            egate_grad.astype(jnp.bfloat16), "fsdp", scatter_dimension=1, tiled=True
        ).astype(jnp.float32),
        lax.psum_scatter(
            expert_up_weight_grad.astype(jnp.bfloat16), "fsdp", scatter_dimension=1, tiled=True
        ).astype(jnp.float32),
        lax.psum_scatter(
            edown_grad.astype(jnp.bfloat16), "fsdp", scatter_dimension=2, tiled=True
        ).astype(jnp.float32),
    )
    return (
        layer_out,
        input_grad,
        dense[0],
        dense[1],
        dense[2],
        dense[3],
        dense[8],
        dense[4],
        dense[5],
        dense[6],
        dense[7],
        dense[9],
        experts_done[0],
        experts_done[1],
        experts_done[2],
    )


MESH = pl.DeviceIdType.MESH
HBM = pl.BlockSpec(memory_space=pl.ANY)
VMEM = pl.BlockSpec(memory_space=pltpu.VMEM)
DMA = pltpu.SemaphoreType.DMA
BF, F32 = jnp.bfloat16, jnp.float32
BIG = 60 * 1024 * 1024


def dot_nt(left, right):
    return lax.dot_general(left, right, (((1,), (1,)), ((), ())), preferred_element_type=F32)


def dot_tn(left, right):
    return lax.dot_general(left, right, (((0,), (0,)), ((), ())), preferred_element_type=F32)


def dot_nn(left, right):
    return jnp.dot(left, right, preferred_element_type=F32)


def ranks():
    return lax.axis_index("fsdp"), lax.axis_index("ctx"), lax.axis_index("tp")


def sibling(t):
    return t + 1 - 2 * lax.rem(t, 2)


def opposite(t):
    return lax.rem(t + 2, 4)


def remote(src, dst, send, recv, to):
    return pltpu.make_async_remote_copy(
        src_ref=src, dst_ref=dst, send_sem=send, recv_sem=recv, device_id=to, device_id_type=MESH
    )


def greet(peers):
    barrier = pltpu.get_barrier_semaphore()
    for peer in peers:
        pl.semaphore_signal(barrier, inc=1, device_id=peer, device_id_type=MESH)
    pl.semaphore_wait(barrier, len(peers))


def line_peers(c, n_c):
    return [{"ctx": lax.rem(c + step, n_c)} for step in range(1, n_c)]


def piece(index, size):
    return pl.ds(pl.multiple_of(index * size, size), size)


def nearest(c, n_c, act):
    act(c)
    for step in range(1, n_c):
        for side in (-1, 1):
            place = c + side * step

            @pl.when((place >= 0) & (place < n_c))
            def _():
                act(place)


def spread_sems(n_c):
    return [
        DMA((n_c + 2,)),
        DMA((n_c,)),
        DMA((n_c,)),
        DMA((n_c,)),
        DMA((2 * n_c,)),
        DMA((2 * n_c,)),
        DMA((4 * n_c,)),
        DMA((4 * n_c,)),
        DMA(()),
    ]


def spread(own, place, n_c, both, sems):
    zs, zr, xs, xr, ys, yr, ks, kr, ls = sems
    f, c, t = ranks()
    far = opposite(t)
    to_sib, to_far, to_other = {"tp": sibling(t)}, {"tp": far}, {"fsdp": 1 - f}

    def far_copy(src, i, g, cc):
        return remote(src, place(g, cc, t), ys.at[i], yr.at[i], to_far)

    def sib_copy(src, i, which, g, cc, col):
        at = 2 * i + which
        return remote(src, place(g, cc, col), ks.at[at], kr.at[at], to_sib)

    def other_copy(src, cc):
        return remote(src, place(f, cc, t), xs.at[cc], xr.at[cc], to_other)

    def line_copy(src, cc, sem, to):
        return remote(src, place(f, cc, t), zs.at[sem], zr.at[cc], {"ctx": to})

    def pass_on(src, i, g, cc):
        far_copy(src, i, g, cc).start()
        sib_copy(src, i, 0, g, cc, t).start()

    local = pltpu.make_async_copy(own, place(f, c, t), ls)
    local.start()

    @pl.when(c < n_c - 1)
    def _():
        line_copy(own, c, n_c, c + 1).start()

    @pl.when(c > 0)
    def _():
        line_copy(own, c, n_c + 1, c - 1).start()

    if both:
        other_copy(own, c).start()
    pass_on(own, c, f, c)
    for step in range(1, n_c):
        for side in (-1, 1):
            cc = c + side * step
            onward = c - side

            @pl.when((cc >= 0) & (cc < n_c))
            def _():
                block = place(f, cc, t)
                line_copy(block, cc, cc, c).wait_recv()

                @pl.when((onward >= 0) & (onward < n_c))
                def _():
                    line_copy(block, cc, cc, onward).start()

                if both:
                    other_copy(block, cc).start()
                pass_on(block, cc, f, cc)

    if both:

        def from_other(cc):
            block = place(1 - f, cc, t)
            remote(block, block, xs.at[cc], xr.at[cc], to_other).wait_recv()
            pass_on(block, n_c + cc, 1 - f, cc)

        nearest(c, n_c, from_other)
    for g, base in ((f, 0), (1 - f, n_c))[: 2 if both else 1]:

        def from_far(cc):
            i = base + cc
            block = place(g, cc, far)
            remote(block, block, ys.at[i], yr.at[i], to_far).wait_recv()
            sib_copy(block, i, 1, g, cc, far).start()

        nearest(c, n_c, from_far)
    for g, base in ((f, 0), (1 - f, n_c))[: 2 if both else 1]:
        for cc in range(n_c):
            i = base + cc
            block = place(g, cc, t)
            for which in range(2):
                copy = sib_copy(block, i, which, g, cc, t)
                copy.wait_recv()
                copy.wait_send()
            far_copy(block, i, g, cc).wait_send()
    if both:
        for cc in range(n_c):
            other_copy(place(f, cc, t), cc).wait_send()
    block = place(f, c, t)

    @pl.when(c < n_c - 1)
    def _():
        line_copy(own, c, n_c, c).wait_send()

    @pl.when(c > 0)
    def _():
        line_copy(own, c, n_c + 1, c).wait_send()

    for step in range(1, n_c):
        for side in (-1, 1):
            cc = c + side * step
            onward = c - side

            @pl.when((cc >= 0) & (cc < n_c) & (onward >= 0) & (onward < n_c))
            def _():
                line_copy(block, cc, cc, c).wait_send()

    local.wait()


def front_kernel(n_c, part, hidden, wq, wk, wv, wo, small, seq_out, wqkv_out, wo_out, small_out, *sems):
    ws, wr, ls, xs, xr = sems[:5]
    f, c, t = ranks()
    rows, quarter = hidden.shape
    greet([{"tp": sibling(t)}, {"tp": opposite(t)}, {"fsdp": 1 - f}] + line_peers(c, n_c))

    def targets(g, cc):
        block = piece(g * n_c + cc, part)
        return [wqkv_out.at[block, pl.ds(i * HD, HD)] for i in range(3)] + [
            wo_out.at[:, block],
            small_out.at[:, block],
        ]

    def sources(head):
        cols = piece(head, HD)
        return [wq.at[:, cols], wk.at[:, cols], wv.at[:, cols], wo.at[cols, :], small]

    for step in range(1, n_c):
        to = lax.rem(c + step, n_c)
        for i, (src, dst) in enumerate(zip(sources(to), targets(f, c))):
            remote(src, dst, ws.at[step, i], wr.at[step, i], {"ctx": to}).start()
    own = [
        pltpu.make_async_copy(src, dst, ls.at[i])
        for i, (src, dst) in enumerate(zip(sources(c), targets(f, c)))
    ]
    for copy in own:
        copy.start()
    for copy in own:
        copy.wait()

    def slabs(g, cc):
        block = piece(g * n_c + cc, part)
        return [wqkv_out.at[block, :], wo_out.at[:, block], small_out.at[:, block]]

    def across(step, g, cc):
        return [
            remote(slab, slab, xs.at[step, i], xr.at[step, i], {"fsdp": 1 - f})
            for i, slab in enumerate(slabs(g, cc))
        ]

    for copy in across(0, f, c):
        copy.start()

    def place(g, cc, tt):
        return seq_out.at[piece(cc, rows), piece(tt, quarter)]

    spread(hidden, place, n_c, False, sems[5:])
    for step in range(1, n_c):
        cc = lax.rem(c - step + n_c, n_c)
        for i, dst in enumerate(targets(f, cc)):
            remote(dst, dst, ws.at[step, i], wr.at[step, i], {"ctx": cc}).wait_recv()
        for copy in across(step, f, cc):
            copy.start()
    for step in range(n_c):
        cc = lax.rem(c - step + n_c, n_c)
        for copy in across(step, 1 - f, cc):
            copy.wait_recv()
        for copy in across(step, f, cc):
            copy.wait_send()
    for step in range(1, n_c):
        for i, (src, dst) in enumerate(zip(sources(c), targets(f, c))):
            remote(src, dst, ws.at[step, i], wr.at[step, i], {"ctx": c}).wait_send()


def front(n_c, n_f, n_t, hidden, wq, wk, wv, wo, small):
    rows, quarter = hidden.shape
    part = wq.shape[0]
    width = quarter * n_t
    return pl.pallas_call(
        functools.partial(front_kernel, n_c, part),
        out_shape=(
            jax.ShapeDtypeStruct((rows * n_c, width), BF),
            jax.ShapeDtypeStruct((width, 3 * HD), BF),
            jax.ShapeDtypeStruct((HD, width), BF),
            jax.ShapeDtypeStruct((small.shape[0], width), F32),
        ),
        in_specs=[HBM] * 6,
        out_specs=[HBM] * 4,
        scratch_shapes=[
            DMA((n_c, 5)),
            DMA((n_c, 5)),
            DMA((5,)),
            DMA((n_c, 3)),
            DMA((n_c, 3)),
        ]
        + spread_sems(n_c),
        compiler_params=pltpu.CompilerParams(collective_id=1, has_side_effects=True),
        cost_estimate=pl.CostEstimate(flops=0, bytes_accessed=100 << 20, transcendentals=0),
        name="front",
    )(hidden, wq, wk, wv, wo, small)


def attend_kernel(block, hidden, gain, wqkv, cosine, sine, normed, q_out, k_out, v_out, hf_out, hb_out, lse_out, r_out):
    seq, width = hidden.shape
    scale_att = HD ** (-0.5)
    for start in range(0, seq, block):
        at = pl.ds(start, block)
        h = hidden[at, :].astype(F32)
        r = lax.rsqrt(jnp.sum(h * h, axis=1, keepdims=True) / width + EPS)
        n = (h * r * gain[...]).astype(BF)
        normed[at, :] = n
        r_out[at, :] = jnp.broadcast_to(r, (block, HD))
        qkv = dot_nn(n, wqkv[...])
        cos, sin = cosine[at, :], sine[at, :]

        def rotate(values):
            return (values * cos + pltpu.roll(values, HD // 2, 1) * sin).astype(BF)

        q_out[at, :] = rotate(qkv[:, :HD])
        k_out[at, :] = rotate(qkv[:, HD : 2 * HD])
        v_out[at, :] = qkv[:, 2 * HD :].astype(BF)
    for start in range(0, seq, block):
        at = pl.ds(start, block)
        seen = start + block
        s = dot_nt(q_out[at, :], k_out[:seen, :]) * scale_att
        row = lax.broadcasted_iota(jnp.int32, (block, seen), 0) + start
        col = lax.broadcasted_iota(jnp.int32, (block, seen), 1)
        s = jnp.where(col <= row, s, NEG_BIG)
        top = jnp.max(s, axis=1, keepdims=True)
        e = jnp.exp(s - top)
        total = jnp.sum(e, axis=1, keepdims=True)
        p = (e / total).astype(BF)
        out = dot_nn(p, v_out[:seen, :])
        hf_out[at, :] = out
        hb_out[at, :] = out.astype(BF)
        lse_out[at, :] = jnp.broadcast_to(top + jnp.log(total), (block, HD))


def attend(hidden, gain, wqkv, cosine, sine):
    seq, width = hidden.shape
    head = jax.ShapeDtypeStruct((seq, HD), BF)
    head_f = jax.ShapeDtypeStruct((seq, HD), F32)
    return pl.pallas_call(
        functools.partial(attend_kernel, min(256, seq)),
        out_shape=(jax.ShapeDtypeStruct((seq, width), BF), head, head, head, head_f, head, head_f, head_f),
        in_specs=[VMEM] * 5,
        out_specs=[VMEM] * 8,
        compiler_params=pltpu.CompilerParams(vmem_limit_bytes=BIG),
        cost_estimate=pl.CostEstimate(flops=2 << 30, bytes_accessed=12 << 20, transcendentals=1 << 20),
        name="attend",
    )(hidden, gain, wqkv, cosine, sine)


def reduce_seq_scratch(n_c, rows, quarter):
    return [
        pltpu.VMEM((n_c, 2, rows, quarter), BF),
        pltpu.VMEM((n_c, 2, rows, quarter), BF),
        pltpu.VMEM((n_c, 2, rows, quarter), F32),
        pltpu.VMEM((n_c, rows, quarter), BF),
        pltpu.VMEM((n_c, rows, quarter), BF),
        pltpu.VMEM((n_c, rows, quarter), BF),
        pltpu.VMEM((n_c, rows, quarter), BF),
        DMA((n_c,)),
        DMA((n_c,)),
        DMA((n_c,)),
        DMA((n_c,)),
        DMA((n_c,)),
        DMA((n_c,)),
    ]


def reduce_seq(part_of, n_c, scratch):
    out1, in1, own, out2, in2, out3, in3, s1, r1, s2, r2, s3, r3 = scratch
    f, c, t = ranks()
    far, sib = opposite(t), sibling(t)
    to_sib, to_far = {"tp": sib}, {"tp": far}
    order = [2, 1, 3, 0] if n_c == 4 else list(range(1, n_c)) + [0]
    for d in order:
        cc = lax.rem(c + d, n_c)
        out1[d, 0] = part_of(cc, sib).astype(BF)
        out1[d, 1] = part_of(cc, opposite(sib)).astype(BF)
        remote(out1.at[d], in1.at[d], s1.at[d], r1.at[d], to_sib).start()
        own[d, 0] = part_of(cc, t)
        own[d, 1] = part_of(cc, far)
    for d in order:
        remote(out1.at[d], in1.at[d], s1.at[d], r1.at[d], to_sib).wait()
        out2[d] = (own[d, 1] + in1[d, 1].astype(F32)).astype(BF)
        remote(out2.at[d], in2.at[d], s2.at[d], r2.at[d], to_far).start()
    for d in order:
        remote(out2.at[d], in2.at[d], s2.at[d], r2.at[d], to_far).wait()
        total = own[d, 0] + in1[d, 0].astype(F32) + in2[d].astype(F32)
        if d:
            out3[d] = total.astype(BF)
            cc = lax.rem(c + d, n_c)
            remote(out3.at[d], in3.at[d], s3.at[d], r3.at[d], {"ctx": cc}).start()
    for d in order[:-1]:
        remote(out3.at[d], in3.at[d], s3.at[d], r3.at[d], {"ctx": c}).wait()
        total = total + in3[d].astype(F32)
    return total


def mid_kernel(n_c, heads, wo, hidden, resid_out, all_out, blk, *scratch):
    f, c, t = ranks()
    rows, quarter = hidden.shape
    greet([{"tp": sibling(t)}, {"tp": opposite(t)}, {"fsdp": 1 - f}] + line_peers(c, n_c))

    def part_of(cc, q):
        return dot_nn(heads[piece(cc, rows), :], wo[:, piece(q, quarter)])

    total = reduce_seq(part_of, n_c, scratch[:13])
    resid = hidden[...].astype(F32) + total
    resid_out[...] = resid
    blk[...] = resid.astype(BF)

    def place(g, cc, tt):
        return all_out.at[piece(g * n_c + cc, rows), piece(tt, quarter)]

    spread(blk, place, n_c, True, scratch[13:])


def mid(n_c, n_f, n_t, heads, wo, hidden):
    rows, quarter = hidden.shape
    return pl.pallas_call(
        functools.partial(mid_kernel, n_c),
        out_shape=(
            jax.ShapeDtypeStruct((rows, quarter), F32),
            jax.ShapeDtypeStruct((rows * n_c * n_f, quarter * n_t), BF),
        ),
        in_specs=[VMEM] * 3,
        out_specs=[VMEM, HBM],
        scratch_shapes=[pltpu.VMEM((rows, quarter), BF)]
        + reduce_seq_scratch(n_c, rows, quarter)
        + spread_sems(n_c),
        compiler_params=pltpu.CompilerParams(
            collective_id=2, has_side_effects=True, vmem_limit_bytes=BIG
        ),
        cost_estimate=pl.CostEstimate(flops=1 << 29, bytes_accessed=200 << 20, transcendentals=0),
        name="mid",
    )(heads, wo, hidden)


def expert_kernel(
    n_c, n_f, mine, ffe, srows, hp, x, og, picked, gain, router, wg0, wu0, wd0, wg1, wu1, wd1, shared,
    moe_out, back_out, in_out, gt_out, r_out, prob_out, pgrad_out, wgu, wd, sems,
):
    f, c, t = ranks()
    block, width = x.shape
    used = mine * ffe
    rows_used = used + srows
    part = width // (n_f * n_c)
    half = width // n_f

    @pl.when(pl.program_id(0) == 0)
    def _():
        copies = []

        def fetch(src, dst):
            copy = pltpu.make_async_copy(src, dst, sems.at[len(copies)])
            copy.start()
            copies.append(copy)

        for i, (kept, got) in enumerate(((wg0, wg1), (wu0, wu1), (wd0, wd1))):
            dst, base = ((wgu, 0), (wgu, hp), (wd, 0))[i]
            for e in range(mine):
                at = pl.ds(base + e * ffe, ffe)
                fetch(kept.at[f * mine + e], dst.at[at, piece(f, half)])
                fetch(got.at[e], dst.at[at, piece(1 - f, half)])
            for b in range(n_f * n_c):
                fetch(
                    shared.at[b, pl.ds(i * srows, srows), :],
                    dst.at[pl.ds(base + used, srows), pl.ds(b * part, part)],
                )
        blank = jnp.zeros((hp - rows_used, width), BF)
        wgu[rows_used:hp, :] = blank
        wgu[hp + rows_used :, :] = blank
        wd[rows_used:, :] = blank
        for copy in copies:
            copy.wait()

    h = x[...].astype(F32)
    r = lax.rsqrt(jnp.sum(h * h, axis=1, keepdims=True) / width + EPS)
    r_out[...] = jnp.broadcast_to(r, r_out.shape)
    n = (h * r * gain[...]).astype(BF)
    in_out[...] = n
    logits = dot_nt(n, router[...])
    e = jnp.exp(logits - jnp.max(logits, axis=1, keepdims=True))
    prob = e / jnp.sum(e, axis=1, keepdims=True)
    prob_out[...] = prob
    n_exp = prob.shape[1]
    lane = lax.broadcasted_iota(jnp.int32, (block, n_exp), 1)
    first = (c * n_f + f) * mine
    gated = prob * picked[...]
    col = lax.broadcasted_iota(jnp.int32, (block, hp), 1)
    gate = jnp.ones((block, hp), F32)
    for k in range(mine):
        g = jnp.sum(jnp.where(lane == first + k, gated, 0.0), axis=1, keepdims=True)
        gate = jnp.where((col >= k * ffe) & (col < (k + 1) * ffe), g, gate)
    ab = dot_nt(n, wgu[...])
    a, b = ab[:, :hp], ab[:, hp:]
    og_b = og[...]
    og_rows = jnp.concatenate(
        [jnp.concatenate([og_b[i, q] for q in range(og_b.shape[1])], axis=1) for i in range(og_b.shape[0])],
        axis=0,
    )
    dh = dot_nt(og_rows, wd[...])
    sig = 1.0 / (1.0 + jnp.exp(-a))
    silu = a * sig
    act = (silu * b).astype(BF).astype(F32)
    actg = (act * gate).astype(BF)
    ad = act * dh
    p_grad = jnp.zeros((block, n_exp), F32)
    for k in range(mine):
        s = jnp.sum(
            jnp.where((col >= k * ffe) & (col < (k + 1) * ffe), ad, 0.0), axis=1, keepdims=True
        )
        p_grad = jnp.where(lane == first + k, s, p_grad)
    p_grad = p_grad * picked[...]
    pgrad_out[...] = p_grad
    logit_grad = (prob * (p_grad - jnp.sum(prob * p_grad, axis=1, keepdims=True))).astype(BF)
    dg = dh * gate
    da = (dg * b * (sig * (1.0 + a * (1.0 - sig)))).astype(BF)
    db = (dg * silu).astype(BF)
    gt_out[:rows_used, :] = da.T[:rows_used, :]
    gt_out[rows_used : 2 * rows_used, :] = db.T[:rows_used, :]
    gt_out[2 * rows_used :, :] = actg.T[:rows_used, :]
    out = dot_nn(actg, wd[...]).astype(BF)
    rows, quarter = og_b.shape[2], og_b.shape[3]
    for i in range(og_b.shape[0]):
        for q in range(og_b.shape[1]):
            moe_out[i, q] = out[i * rows : (i + 1) * rows, q * quarter : (q + 1) * quarter]
    back = dot_nn(jnp.concatenate([da, db], axis=1), wgu[...])
    back = back + dot_nn(logit_grad, router[...])
    back_out[...] = back.astype(BF)


def experts(n_c, n_f, n_t, block, mine, ffe, srows, x, og, picked, gain, router, kept, got, shared):
    total, width = x.shape
    n_exp = router.shape[0]
    rows, quarter = og.shape[2], og.shape[3]
    per = block // rows
    used = mine * ffe + srows
    hp = -(-used // HD) * HD
    row_spec = pl.BlockSpec((block, width), lambda i: (i, 0))
    blk_spec = pl.BlockSpec((per, n_t, rows, quarter), lambda i: (i, 0, 0, 0))
    exp_spec = pl.BlockSpec((block, n_exp), lambda i: (i, 0))
    sds = jax.ShapeDtypeStruct
    return pl.pallas_call(
        functools.partial(expert_kernel, n_c, n_f, mine, ffe, srows, hp),
        grid=(total // block,),
        out_shape=(
            sds(og.shape, BF),
            sds((total, width), BF),
            sds((total, width), BF),
            sds((3 * used, total), BF),
            sds((total, HD), F32),
            sds((total, n_exp), F32),
            sds((total, n_exp), F32),
        ),
        in_specs=[
            row_spec,
            blk_spec,
            exp_spec,
            pl.BlockSpec((1, width), lambda i: (0, 0)),
            pl.BlockSpec((n_exp, width), lambda i: (0, 0)),
        ]
        + [HBM] * 7,
        out_specs=[
            blk_spec,
            row_spec,
            row_spec,
            pl.BlockSpec((3 * used, block), lambda i: (0, i)),
            pl.BlockSpec((block, HD), lambda i: (i, 0)),
            exp_spec,
            exp_spec,
        ],
        scratch_shapes=[
            pltpu.VMEM((2 * hp, width), BF),
            pltpu.VMEM((hp, width), BF),
            DMA((3 * (2 * mine + n_f * n_c),)),
        ],
        compiler_params=pltpu.CompilerParams(vmem_limit_bytes=BIG),
        cost_estimate=pl.CostEstimate(
            flops=12 * total * width * used, bytes_accessed=70 << 20, transcendentals=total * used
        ),
        name="experts",
    )(x, og, picked, gain, router, *kept, *got, shared)


def expert_grad_kernel(used, mine, ffe, f_ref, gt, x, og, kg, ku, kd, sg, su, sd, shared):
    del f_ref
    step = pl.program_id(0)
    cols = x.shape[1]
    routed = mine * ffe
    og_rows = og[...].reshape(-1, cols)
    for i, (keep, send) in enumerate(((kg, sg), (ku, su), (kd, sd))):
        rhs = og_rows if i == 2 else x[...]
        g = dot_nn(gt[i * used : (i + 1) * used, :], rhs)
        shared[i * (used - routed) : (i + 1) * (used - routed), :] = g[routed:].astype(BF)

        @pl.when(step < 2)
        def _():
            send[...] = g[:routed].astype(BF).reshape(mine, ffe, cols)

        @pl.when(step >= 2)
        def _():
            keep[...] = g[:routed].reshape(mine, ffe, cols)


def expert_grads(f_rank, n_f, used, mine, ffe, gt, x, og):
    total, width = x.shape
    n_blocks, n_t, rows, quarter = og.shape
    half = width // n_f
    srows = used - mine * ffe
    sds = jax.ShapeDtypeStruct

    def tile(i, f):
        other = 1 - f[0]
        return jnp.where(i < 2, other * 2 + i, f[0] * 2 + i - 2)

    keep_spec = pl.BlockSpec((mine, ffe, quarter), lambda i, f: (f[0], 0, jnp.where(i < 2, 0, i - 2)))
    send_spec = pl.BlockSpec((mine, ffe, quarter), lambda i, f: (0, 0, jnp.where(i < 2, i, 1)))
    return pl.pallas_call(
        functools.partial(expert_grad_kernel, used, mine, ffe),
        grid_spec=pltpu.PrefetchScalarGridSpec(
            num_scalar_prefetch=1,
            grid=(width // quarter,),
            in_specs=[
                pl.BlockSpec(gt.shape, lambda i, f: (0, 0)),
                pl.BlockSpec((total, quarter), lambda i, f: (0, tile(i, f))),
                pl.BlockSpec((n_blocks, 1, rows, quarter), lambda i, f: (0, tile(i, f), 0, 0)),
            ],
            out_specs=[keep_spec] * 3
            + [send_spec] * 3
            + [pl.BlockSpec((3 * srows, quarter), lambda i, f: (0, tile(i, f)))],
        ),
        out_shape=tuple([sds((n_f * mine, ffe, half), F32)] * 3)
        + tuple([sds((mine, ffe, half), BF)] * 3)
        + (sds((3 * srows, width), BF),),
        compiler_params=pltpu.CompilerParams(vmem_limit_bytes=BIG),
        cost_estimate=pl.CostEstimate(
            flops=6 * total * width * used, bytes_accessed=50 << 20, transcendentals=0
        ),
        name="expert_grads",
    )(f_rank, gt, x, og)


def fill_kernel(f_ref, a, b, c, _a, _b, _c, oa, ob, oc):
    del f_ref, _a, _b, _c
    oa[...] = a[...].astype(F32)
    ob[...] = b[...].astype(F32)
    oc[...] = c[...].astype(F32)


def fill_experts(f_rank, arrived, kept):
    mine, ffe, half = arrived[0].shape
    tile = half // 4
    src = pl.BlockSpec((mine, ffe, tile), lambda i, f: (0, 0, i))
    dst = pl.BlockSpec((mine, ffe, tile), lambda i, f: (1 - f[0], 0, i))
    return pl.pallas_call(
        fill_kernel,
        grid_spec=pltpu.PrefetchScalarGridSpec(
            num_scalar_prefetch=1, grid=(4,), in_specs=[src] * 3 + [HBM] * 3, out_specs=[dst] * 3
        ),
        out_shape=tuple(jax.ShapeDtypeStruct(k.shape, k.dtype) for k in kept),
        input_output_aliases={4: 0, 5: 1, 6: 2},
        compiler_params=pltpu.CompilerParams(vmem_limit_bytes=BIG),
        name="fill_experts",
    )(f_rank, *arrived, *kept)


def norm_grad(values, r, gain, grad, width, out, into, send, recv):
    f, c, t = ranks()
    local = jnp.sum(grad * gain * values, axis=1, keepdims=True)
    out[...] = jnp.broadcast_to(local, out.shape)
    peers = [sibling(t), opposite(t), opposite(sibling(t))]
    copies = [
        remote(out, into.at[i], send.at[i], recv.at[i], {"tp": peer}) for i, peer in enumerate(peers)
    ]
    for copy in copies:
        copy.start()
    gain_part = jnp.sum(grad * values * r, axis=0, keepdims=True)
    total = local
    for i, copy in enumerate(copies):
        copy.wait()
        total = total + into[i][:, :1]
    return r * gain * grad - values * (r * r * r * (total / width)), gain_part


def norm_grad_scratch(rows):
    return [
        pltpu.VMEM((rows, HD), F32),
        pltpu.VMEM((3, rows, HD), F32),
        DMA((3,)),
        DMA((3,)),
    ]


def back_kernel(
    n_c, width, part, resid, r_all, gain, og, mid_out, gain_out, seq_out,
    blk, r_own, own, in1, out2, in2, out3, in3, acc, out4, in4,
    ls, rs, s1, r1, s2, r2, s3, r3, s4, r4, *rest,
):
    f, c, t = ranks()
    rows, quarter = og.shape
    far, sib = opposite(t), sibling(t)
    to_sib, to_far, to_other = {"tp": sib}, {"tp": far}, {"fsdp": 1 - f}
    greet([to_sib, to_far, {"tp": opposite(sib)}, to_other] + line_peers(c, n_c))
    order = [2, 1, 3, 0] if n_c == 4 else list(range(1, n_c)) + [0]
    blocks = [(g, d) for g in (1, 0) for d in order]

    def part_at(g, d, q):
        group = 1 - f if g else f
        return part.at[piece(group * n_c + lax.rem(c + d, n_c), rows), piece(q, quarter)]

    def core(g, d):
        i = g * n_c + d
        return [
            remote(part_at(g, d, q), in1.at[i, k], s1.at[i, k], r1.at[i, k], to_sib)
            for k, q in enumerate((opposite(sib), sib))
        ]

    def mine_of(g, d):
        i = g * n_c + d
        return [
            pltpu.make_async_copy(part_at(g, d, q), own.at[i, k], ls.at[i, k])
            for k, q in enumerate((far, t))
        ]

    fetch = pltpu.make_async_copy(r_all.at[piece(f * n_c + c, rows), :], r_own, rs)
    fetch.start()
    for g, d in blocks:
        for copy in core(g, d) + mine_of(g, d):
            copy.start()

    def over(g, d):
        i = g * n_c + d
        return remote(out2.at[i], in2.at[i], s2.at[i], r2.at[i], to_far)

    for g, d in blocks:
        i = g * n_c + d
        for copy in core(g, d) + mine_of(g, d):
            copy.wait()
        out2[i] = (own[i, 0].astype(F32) + in1[i, 0].astype(F32)).astype(BF)
        over(g, d).start()

    def other(d):
        return remote(out3.at[d], in3.at[d], s3.at[d], r3.at[d], to_other)

    for g, d in blocks:
        i = g * n_c + d
        over(g, d).wait()
        total = own[i, 1].astype(F32) + in1[i, 1].astype(F32) + in2[i].astype(F32)
        if g:
            out3[d] = total.astype(BF)
            other(d).start()
        else:
            acc[d] = total

    def line(d, to):
        return remote(out4.at[d], in4.at[d], s4.at[d], r4.at[d], {"ctx": to})

    for d in order:
        other(d).wait()
        total = acc[d] + in3[d].astype(F32)
        if d:
            out4[d] = total.astype(BF)
            line(d, lax.rem(c + d, n_c)).start()
    for d in order[:-1]:
        line(d, c).wait()
        total = total + in4[d].astype(F32)
    fetch.wait()
    back, gain_part = norm_grad(resid[...], r_own[:, :1], gain[...], total, width, *rest[:4])
    gain_out[...] = jnp.broadcast_to(gain_part, gain_out.shape)
    grad = og[...].astype(F32) + back
    mid_out[...] = grad
    blk[...] = grad.astype(BF)

    def place(g, cc, tt):
        return seq_out.at[piece(cc, rows), piece(tt, quarter)]

    spread(blk, place, n_c, False, rest[4:])


def back(n_c, n_f, n_t, part, resid, r_all, gain, og):
    rows, quarter = og.shape
    n_b = n_c * n_f
    sds = jax.ShapeDtypeStruct
    blocks = lambda *lead: pltpu.VMEM(lead + (rows, quarter), BF)
    return pl.pallas_call(
        functools.partial(back_kernel, n_c, quarter * n_t),
        out_shape=(
            sds((rows, quarter), F32),
            sds((8, quarter), F32),
            sds((rows * n_c, quarter * n_t), BF),
        ),
        in_specs=[HBM, VMEM, HBM, VMEM, VMEM],
        out_specs=[VMEM, VMEM, HBM],
        scratch_shapes=[
            blocks(),
            pltpu.VMEM((rows, HD), F32),
            blocks(n_b, 2),
            blocks(n_b, 2),
            blocks(n_b),
            blocks(n_b),
            blocks(n_c),
            blocks(n_c),
            pltpu.VMEM((n_c, rows, quarter), F32),
            blocks(n_c),
            blocks(n_c),
            DMA((n_b, 2)),
            DMA(()),
            DMA((n_b, 2)),
            DMA((n_b, 2)),
            DMA((n_b,)),
            DMA((n_b,)),
            DMA((n_c,)),
            DMA((n_c,)),
            DMA((n_c,)),
            DMA((n_c,)),
        ]
        + norm_grad_scratch(rows)
        + spread_sems(n_c),
        compiler_params=pltpu.CompilerParams(
            collective_id=3, has_side_effects=True, vmem_limit_bytes=BIG
        ),
        cost_estimate=pl.CostEstimate(flops=1 << 20, bytes_accessed=200 << 20, transcendentals=0),
        name="back",
    )(part, resid, r_all, gain, og)


def attend_back_kernel(
    block, mid, wo, q, k, v, hf, lse, cosine, sine, normed, dqkv, gattn, hg, dq, dk, dv
):
    seq = mid.shape[0]
    scale_att = HD ** (-0.5)
    for start in range(0, seq, block):
        at = pl.ds(start, block)
        hg[at, :] = dot_nt(mid[at, :], wo[...]).astype(BF)
    dk[...] = jnp.zeros_like(dk)
    dv[...] = jnp.zeros_like(dv)
    for start in range(0, seq, block):
        at = pl.ds(start, block)
        seen = start + block
        qb, hb = q[at, :], hg[at, :]
        delta = jnp.sum(hb.astype(F32) * hf[at, :], axis=1, keepdims=True)
        s = dot_nt(qb, k[:seen, :]) * scale_att
        row = lax.broadcasted_iota(jnp.int32, (block, seen), 0) + start
        col = lax.broadcasted_iota(jnp.int32, (block, seen), 1)
        p = jnp.where(col <= row, jnp.exp(s - lse[at, :1]), 0.0)
        ds = (p * (dot_nt(hb, v[:seen, :]) - delta)).astype(BF)
        dq[at, :] = dot_nn(ds, k[:seen, :]) * scale_att
        dk[:seen, :] += dot_tn(ds, qb) * scale_att
        dv[:seen, :] += dot_tn(p.astype(BF), hb)

    def rotate(values, at):
        return (values * cosine[at, :] - pltpu.roll(values, HD // 2, 1) * sine[at, :]).astype(BF)

    for start in range(0, seq, block):
        at = pl.ds(start, block)
        dqkv[at, :HD] = rotate(dq[at, :], at)
        dqkv[at, HD : 2 * HD] = rotate(dk[at, :], at)
        dqkv[at, 2 * HD :] = dv[at, :].astype(BF)
    gattn[: 3 * HD, :] = dot_tn(dqkv[...], normed[...]).astype(BF)
    gattn[3 * HD :, :] = dot_tn(hf[...].astype(BF), mid[...]).astype(BF)


def attend_back(mid_seq, wo, q, k, v, hf, lse, cosine, sine, normed):
    seq, width = mid_seq.shape
    sds = jax.ShapeDtypeStruct
    return pl.pallas_call(
        functools.partial(attend_back_kernel, min(256, seq)),
        out_shape=(sds((seq, 3 * HD), BF), sds((4 * HD, width), BF)),
        in_specs=[VMEM] * 10,
        out_specs=[VMEM] * 2,
        scratch_shapes=[pltpu.VMEM((seq, HD), BF)] + [pltpu.VMEM((seq, HD), F32)] * 3,
        compiler_params=pltpu.CompilerParams(vmem_limit_bytes=BIG),
        cost_estimate=pl.CostEstimate(flops=6 << 30, bytes_accessed=16 << 20, transcendentals=1 << 20),
        name="attend_back",
    )(mid_seq, wo, q, k, v, hf, lse, cosine, sine, normed)


def last_kernel(
    n_c, n_f, n_t, width, dqkv, wqkv, hidden, r_all, gain, mid_grad, gain2, gattn,
    in_out, gq, gk, gv, go, gains_out,
    r_own, outx, inx, own, outz, inz, gsend, gin, rs, sx, rx, lx, sz, rz, gs, gr, *rest,
):
    f, c, t = ranks()
    rows, quarter = hidden.shape
    part = width // (n_f * n_c)
    here = f * n_c + c
    others = []
    for df in range(n_f):
        for dc in range(n_c):
            for dt in range(n_t):
                if df or dc or dt:
                    others.append(
                        {
                            "fsdp": lax.rem(f + df, n_f),
                            "ctx": lax.rem(c + dc, n_c),
                            "tp": lax.rem(t + dt, n_t),
                        }
                    )
    gin[...] = jnp.zeros_like(gin)
    greet(others)
    order = [2, 1, 3, 0] if n_c == 4 else list(range(1, n_c)) + [0]

    def cross(d):
        cc = lax.rem(c + d, n_c)
        return remote(
            gattn.at[:, piece((1 - f) * n_c + cc, part)], inx.at[d], sx.at[d], rx.at[d], {"fsdp": 1 - f}
        )

    def keep(d):
        cc = lax.rem(c + d, n_c)
        return pltpu.make_async_copy(gattn.at[:, piece(f * n_c + cc, part)], own.at[d], lx.at[d])

    def line(d, to):
        return remote(outz.at[d], inz.at[d], sz.at[d], rz.at[d], {"ctx": to})

    fetch = pltpu.make_async_copy(r_all.at[piece(c, rows), :], r_own, rs)
    fetch.start()
    for d in order:
        cross(d).start()
        keep(d).start()

    def part_of(cc, q):
        return dot_nt(dqkv[piece(cc, rows), :], wqkv[piece(q, quarter), :])

    total = reduce_seq(part_of, n_c, rest[:13])
    for d in order:
        cross(d).wait()
        keep(d).wait()
        both = own[d].astype(F32) + inx[d].astype(F32)
        if d:
            outz[d] = both.astype(BF)
            line(d, lax.rem(c + d, n_c)).start()
        else:
            mine = both
    fetch.wait()
    back, gain_part = norm_grad(
        hidden[...].astype(F32), r_own[:, :1], gain[...], total, width, *rest[13:17]
    )
    in_out[...] = mid_grad[...] + back

    gsend[0:1, :] = gain_part
    gsend[1:2, :] = gain2[0:1, :]
    gsend[2:, :] = jnp.zeros((6, quarter), F32)
    per = quarter // part
    holder = here // per
    def gain_copy(h, tt):
        b = t * per + h
        return remote(
            gsend.at[:, pl.ds(h * part, part)],
            gin.at[here],
            gs.at[h * n_t + tt],
            gr.at[here],
            {"fsdp": b // n_c, "ctx": lax.rem(b, n_c), "tp": jnp.int32(tt)},
        )

    def is_me(h, tt):
        return (t * per + h == here) & (t == tt)

    for h in range(per):
        for tt in range(n_t):

            @pl.when(jnp.logical_not(is_me(h, tt)))
            def _():
                gain_copy(h, tt).start()

    def put(src, block):
        at = piece(src, HD)
        for i, ref in enumerate((gq, gk, gv)):
            ref[:, at] = block[i * HD : (i + 1) * HD, :].T
        go[at, :] = block[3 * HD :, :]

    put(c, mine)
    for d in order[:-1]:
        line(d, c).wait()
        put(lax.rem(c - d + n_c, n_c), inz[d].astype(F32))
    for h in range(per):
        for tt in range(n_t):

            @pl.when(jnp.logical_not(is_me(h, tt)))
            def _():
                gain_copy(h, tt).wait_send()

    for b in range(n_f * n_c):

        @pl.when((b != here) | (holder != t))
        def _():
            remote(gin.at[b], gin.at[b], gs.at[0], gr.at[b], {"tp": sibling(t)}).wait_recv()

    own_part = jnp.where(
        holder == t,
        gsend[:, piece(lax.rem(here, per), part)],
        jnp.zeros((8, part), F32),
    )
    gains_out[...] = own_part + jnp.sum(gin[...], axis=0)


def last(n_c, n_f, n_t, dqkv, wqkv, hidden, r_all, gain, mid_grad, gain2, gattn):
    rows, quarter = hidden.shape
    width = quarter * n_t
    part = width // (n_f * n_c)
    sds = jax.ShapeDtypeStruct
    slab = pltpu.VMEM((n_c, 4 * HD, part), BF)
    return pl.pallas_call(
        functools.partial(last_kernel, n_c, n_f, n_t, width),
        out_shape=(
            sds((rows, quarter), F32),
            sds((part, n_c * HD), F32),
            sds((part, n_c * HD), F32),
            sds((part, n_c * HD), F32),
            sds((n_c * HD, part), F32),
            sds((8, part), F32),
        ),
        in_specs=[VMEM, VMEM, VMEM, HBM, VMEM, VMEM, VMEM, HBM],
        out_specs=[VMEM] * 6,
        scratch_shapes=[
            pltpu.VMEM((rows, HD), F32),
            slab,
            slab,
            slab,
            slab,
            slab,
            pltpu.VMEM((8, quarter), F32),
            pltpu.VMEM((n_f * n_c, 8, part), F32),
            DMA(()),
            DMA((n_c,)),
            DMA((n_c,)),
            DMA((n_c,)),
            DMA((n_c,)),
            DMA((n_c,)),
            DMA((quarter // part * n_t,)),
            DMA((n_f * n_c,)),
        ]
        + reduce_seq_scratch(n_c, rows, quarter)
        + norm_grad_scratch(rows),
        compiler_params=pltpu.CompilerParams(
            collective_id=4, has_side_effects=True, vmem_limit_bytes=BIG
        ),
        cost_estimate=pl.CostEstimate(flops=2 << 30, bytes_accessed=150 << 20, transcendentals=0),
        name="last",
    )(dqkv, wqkv, hidden, r_all, gain, mid_grad, gain2, gattn)


def per_device_seq(
    hidden_in,
    positions,
    chosen,
    out_grad,
    attn_gain,
    w_query,
    w_key,
    w_value,
    w_out,
    moe_gain,
    router,
    shared_gate,
    shared_up,
    shared_down,
    expert_gate,
    expert_up,
    expert_down,
):
    f_rank, c_rank, t_rank = ranks()
    n_f, n_c, n_t = (lax.axis_size(name) for name in ("fsdp", "ctx", "tp"))
    rows, quarter = hidden_in.shape
    width = quarter * n_t
    part = w_query.shape[0]
    seq = rows * n_c
    n_exp = router.shape[1]
    mine = n_exp // n_c // n_f
    ffe = expert_gate.shape[2]
    group = ("fsdp", "ctx")
    every = ("fsdp", "ctx", "tp")
    n_b = n_f * n_c
    own_shared = shared_gate.shape[1] // n_b
    srows = -(-own_shared // 16) * 16
    block = f_rank * n_c + c_rank
    f_arr = f_rank.astype(jnp.int32).reshape(1)
    swap = [(i, n_f - 1 - i) for i in range(n_f)]

    gate_t, up_t = expert_gate.swapaxes(1, 2), expert_up.swapaxes(1, 2)
    weights = (gate_t, up_t, expert_down)
    got = tuple(
        lax.ppermute(
            lax.dynamic_slice_in_dim(w, (n_f - 1 - f_rank) * mine, mine, 0), "fsdp", swap
        )
        for w in weights
    )

    picked_own = jnp.sum(
        (chosen[:, :, None] == jnp.arange(n_exp)[None, None, :]).astype(F32), axis=1
    )
    small = [
        attn_gain.astype(F32)[None],
        moe_gain.astype(F32)[None],
        router.T.astype(F32),
        picked_own.T,
        positions.astype(F32)[None],
    ]
    small = jnp.concatenate(small, axis=0)
    small = jnp.pad(small, ((0, -small.shape[0] % 8), (0, 0)))
    hidden_seq, wqkv, wo, small_all = front(
        n_c, n_f, n_t, hidden_in, w_query, w_key, w_value, w_out, small
    )
    gain_one, gain_two = small_all[0:1], small_all[1:2]
    router_t = small_all[2 : 2 + n_exp].astype(BF)
    picked = small_all[2 + n_exp : 2 + 2 * n_exp].T
    pos_seq = lax.dynamic_slice(small_all, (2 + 2 * n_exp, f_rank * seq), (1, seq))[0]
    after = lambda x: lax.optimization_barrier((x, hidden_seq))[0]
    grad_all = lax.all_gather(after(out_grad), every, axis=0, tiled=False)
    grad_all = grad_all.reshape(n_b, n_t, rows, quarter)

    def shared_part(weight):
        return jnp.pad(
            weight.reshape(n_b, own_shared, part), ((0, 0), (0, srows - own_shared), (0, 0))
        )

    shared = jnp.concatenate(
        [shared_part(shared_gate.T), shared_part(shared_up.T), shared_part(shared_down)], axis=1
    )
    shared = lax.all_to_all(after(shared), group, split_axis=0, concat_axis=0, tiled=True)

    half = HD // 2
    inverse = 10000.0 ** (-jnp.arange(half, dtype=F32) * 2.0 / HD)
    angles = pos_seq[:, None] * inverse[None, :]
    cosine, sine = jnp.cos(angles), jnp.sin(angles)
    cosine = jnp.concatenate([cosine, cosine], axis=1)
    sine = jnp.concatenate([-sine, sine], axis=1)
    normed, q, k, v, heads_f, heads_b, lse, r_one = attend(hidden_seq, gain_one, wqkv, cosine, sine)
    resid_mid, resid_all = mid(n_c, n_f, n_t, heads_b, wo, hidden_in)

    moe_part, back_part, moe_in, g_t, r_two, prob, p_part = experts(
        n_c, n_f, n_t, rows, mine, ffe, srows, resid_all, grad_all, picked, gain_two, router_t,
        weights, got, shared,
    )
    used = mine * ffe + srows
    kg, ku, kd, sg, su, sd, shared_g = expert_grads(f_arr, n_f, used, mine, ffe, g_t, moe_in, grad_all)
    arrived = tuple(lax.ppermute(s, "fsdp", swap) for s in (sg, su, sd))
    own_cols = lambda x: lax.dynamic_slice_in_dim(x, t_rank * quarter, quarter, 1)
    mid_grad, gain_two_part, mid_seq = back(
        n_c, n_f, n_t, back_part, resid_mid, r_two, own_cols(gain_two), out_grad
    )
    later = lambda x: lax.optimization_barrier((x, mid_seq))[0]
    moe_q = lax.psum_scatter(
        later(moe_part).reshape(n_b * n_t, rows, quarter), every, scatter_dimension=0, tiled=True
    )[0].astype(F32)
    layer_out = (resid_mid + moe_q).astype(BF)
    p_grad = lax.psum(later(p_part), every)
    logit_grad = (prob * (p_grad - jnp.sum(prob * p_grad, axis=1, keepdims=True))).astype(BF)
    router_grad = dot_tn(lax.dynamic_slice_in_dim(moe_in, block * part, part, 1), logit_grad)
    shared_sent = later(shared_g).reshape(3 * srows, n_b, part).swapaxes(0, 1)
    shared_back = lax.all_to_all(shared_sent, group, split_axis=0, concat_axis=0, tiled=True)
    shared_back = shared_back.reshape(n_b, 3, srows, part)[:, :, :own_shared].astype(F32)

    dqkv, gattn = attend_back(mid_seq, wo, q, k, v, heads_f, lse, cosine, sine, normed)
    input_grad, gq, gk, gv, go, gains = last(
        n_c, n_f, n_t, dqkv, wqkv, hidden_in, r_one, own_cols(gain_one), mid_grad, gain_two_part, gattn
    )
    eg, eu, ed = fill_experts(f_arr, arrived, (kg, ku, kd))

    def shared_cols(i):
        return shared_back[:, i].reshape(n_b * own_shared, part)

    return (
        layer_out,
        input_grad,
        gains[0],
        gq,
        gk,
        gv,
        go,
        gains[1],
        router_grad,
        shared_cols(0).T,
        shared_cols(1).T,
        shared_cols(2),
        eg.swapaxes(1, 2),
        eu.swapaxes(1, 2),
        ed,
    )


def one_head_each(mesh, args):
    n_f, n_c, n_t = (mesh.shape[name] for name in ("fsdp", "ctx", "tp"))
    heads = args[5].shape[1] // HD
    experts = args[10].shape[1]
    return (
        n_f == 2
        and n_t == 4
        and heads == n_c * n_t
        and experts % (n_f * n_c) == 0
        and args[11].shape[1] % (8 * n_f * n_c * n_t) == 0
    )


def solution(mesh):
    placed = (
        P(("fsdp", "ctx"), "tp"),
        P(("fsdp", "ctx")),
        P(("fsdp", "ctx"), None),
        P(("fsdp", "ctx"), "tp"),
        P(("fsdp", "ctx")),
        P(("fsdp", "ctx"), "tp"),
        P(("fsdp", "ctx"), "tp"),
        P(("fsdp", "ctx"), "tp"),
        P("tp", ("fsdp", "ctx")),
        P(("fsdp", "ctx")),
        P(("fsdp", "ctx"), None),
        P(("fsdp", "ctx"), "tp"),
        P(("fsdp", "ctx"), "tp"),
        P("tp", ("fsdp", "ctx")),
        P("ctx", "fsdp", "tp"),
        P("ctx", "fsdp", "tp"),
        P("ctx", "tp", "fsdp"),
    )
    def run(*args):
        body = per_device_seq if one_head_each(mesh, args) else per_device
        return jax.shard_map(
        body,
        mesh=mesh,
        in_specs=placed,
        out_specs=(
            P(("fsdp", "ctx"), "tp"),
            P(("fsdp", "ctx"), "tp"),
            P(("fsdp", "ctx")),
            P(("fsdp", "ctx"), "tp"),
            P(("fsdp", "ctx"), "tp"),
            P(("fsdp", "ctx"), "tp"),
            P("tp", ("fsdp", "ctx")),
            P(("fsdp", "ctx")),
            P(("fsdp", "ctx"), None),
            P(("fsdp", "ctx"), "tp"),
            P(("fsdp", "ctx"), "tp"),
            P("tp", ("fsdp", "ctx")),
            P("ctx", "fsdp", "tp"),
            P("ctx", "fsdp", "tp"),
            P("ctx", "tp", "fsdp"),
        ),
        check_vma=False,
    )(*args)

    return run
```

```python
import functools

import jax
import jax.numpy as jnp
from jax import lax
from jax.experimental import pallas as pl
from jax.experimental.pallas import tpu as pltpu
from jax.sharding import PartitionSpec as P

HD = 128
TOPK = 6


EPS = 1e-06
NEG_BIG = -1e30


def as_sent(value):
    return jax.tree.map(lambda a: a.astype(jnp.bfloat16) if a.dtype == jnp.float32 else a, value)


def features(local_part):
    return lax.all_gather(local_part, "tp", axis=1, tiled=True)


def row_stats(partial_terms):
    return lax.psum(partial_terms, "tp")


def partial_sums(partial_terms):
    return jax.tree.map(
        lambda part: part.astype(jnp.float32),
        lax.psum_scatter(as_sent(partial_terms), "tp", scatter_dimension=1, tiled=True),
    )


def to_owners(slot_rows):
    return lax.all_to_all(slot_rows, "ctx", split_axis=0, concat_axis=2, tiled=True)


def to_sources(slot_rows):
    return lax.all_to_all(
        slot_rows.astype(jnp.bfloat16), "ctx", split_axis=2, concat_axis=0, tiled=True
    ).astype(slot_rows.dtype)


def rotary(values, positions, rotate_sign):
    half_dim = values.shape[-1] // 2
    inverse = 10000.0 ** (-jnp.arange(half_dim, dtype=jnp.float32) * 2.0 / values.shape[-1])
    angles = positions.astype(jnp.float32)[:, None] * inverse[None, :]
    cosine = jnp.cos(angles)[:, None, :]
    sine_val = rotate_sign * jnp.sin(angles)[:, None, :]
    lower_half = values[..., :half_dim]
    upper_half = values[..., half_dim:]
    return jnp.concatenate(
        [lower_half * cosine - upper_half * sine_val, upper_half * cosine + lower_half * sine_val],
        axis=-1,
    )


def norm_rows(values, gain_part, model_width):
    square_sum = row_stats(jnp.sum(values * values, axis=1))
    row_scale = lax.rsqrt(square_sum / model_width + EPS)
    return (values * row_scale[:, None] * gain_part[None, :], row_scale)


def norm_back(values, row_scale, gain_part, grad_normed, model_width, tp_rank):
    quarter = values.shape[1]
    local_sum = jnp.sum(grad_normed * gain_part[None, :] * values, axis=1)
    gain_local = jnp.sum(grad_normed * values * row_scale[:, None], axis=0)
    gain_whole = lax.dynamic_update_slice_in_dim(
        jnp.zeros((model_width,), jnp.float32), gain_local, tp_rank * quarter, 0
    )
    row_total, gain_grad = row_stats((local_sum, gain_whole))
    back = (
        row_scale[:, None] * gain_part[None, :] * grad_normed
        - values * (row_scale**3 * row_total / model_width)[:, None]
    )
    return (back, gain_grad)


def scatter_slots(assign_rows, flat_exp, slot_of, n_exp, capacity):
    buffer = jnp.zeros((n_exp, capacity, assign_rows.shape[1]), assign_rows.dtype)
    return buffer.at[flat_exp, slot_of].set(assign_rows)


def silu_grad(pre_act):
    sigmoid_val = jax.nn.sigmoid(pre_act)
    return sigmoid_val * (1.0 + pre_act * (1.0 - sigmoid_val))


def keep_state(carried):
    return carried


def per_device(
    hidden_in,
    positions,
    chosen,
    out_grad,
    attn_gain,
    w_query,
    w_key,
    w_value,
    w_out,
    moe_gain,
    router,
    shared_gate,
    shared_up,
    shared_down,
    expert_gate,
    expert_up,
    expert_down,
):
    tp_rank = lax.axis_index("tp")
    ctx_rank = lax.axis_index("ctx")
    n_ctx = lax.axis_size("ctx")
    tok_rows, quarter = hidden_in.shape
    model_width = quarter * lax.axis_size("tp")
    gain_one, wq_all, wk_all, wv_all, gain_two, router_all, gate_all, up_all, wo_all, down_all = (
        lax.all_gather(attn_gain, ("fsdp", "ctx"), axis=0, tiled=True),
        lax.all_gather(w_query, ("fsdp", "ctx"), axis=0, tiled=True),
        lax.all_gather(w_key, ("fsdp", "ctx"), axis=0, tiled=True),
        lax.all_gather(w_value, ("fsdp", "ctx"), axis=0, tiled=True),
        lax.all_gather(moe_gain, ("fsdp", "ctx"), axis=0, tiled=True),
        lax.all_gather(router, ("fsdp", "ctx"), axis=0, tiled=True),
        lax.all_gather(shared_gate, ("fsdp", "ctx"), axis=0, tiled=True),
        lax.all_gather(shared_up, ("fsdp", "ctx"), axis=0, tiled=True),
        lax.all_gather(w_out, ("fsdp", "ctx"), axis=1, tiled=True),
        lax.all_gather(shared_down, ("fsdp", "ctx"), axis=1, tiled=True),
    )
    expert_gate_weights, expert_up_weights, expert_down_weights = (
        lax.all_gather(expert_gate, "fsdp", axis=1, tiled=True),
        lax.all_gather(expert_up, "fsdp", axis=1, tiled=True),
        lax.all_gather(expert_down, "fsdp", axis=2, tiled=True),
    )
    gain_q1 = lax.dynamic_slice_in_dim(gain_one, tp_rank * quarter, quarter).astype(jnp.float32)
    gain_q2 = lax.dynamic_slice_in_dim(gain_two, tp_rank * quarter, quarter).astype(jnp.float32)
    router_rows = lax.dynamic_slice_in_dim(router_all, tp_rank * quarter, quarter, 0)
    head_count = wq_all.shape[1] // HD
    scale_att = HD ** (-0.5)
    resid_in = hidden_in.astype(jnp.float32)
    normed_one, scale_one = norm_rows(resid_in, gain_q1, model_width)
    normed_in = features(normed_one.astype(jnp.bfloat16))
    query_pre = jnp.dot(normed_in, wq_all, preferred_element_type=jnp.float32).reshape(
        tok_rows, head_count, HD
    )
    key_pre = jnp.dot(normed_in, wk_all, preferred_element_type=jnp.float32).reshape(
        tok_rows, head_count, HD
    )
    value_b = (
        jnp.dot(normed_in, wv_all, preferred_element_type=jnp.float32)
        .astype(jnp.bfloat16)
        .reshape(tok_rows, head_count, HD)
    )
    query_b = rotary(query_pre, positions, 1.0).astype(jnp.bfloat16)
    key_b = rotary(key_pre, positions, 1.0).astype(jnp.bfloat16)
    q_start = ctx_rank * tok_rows
    row_pos = q_start + jnp.arange(tok_rows)
    start_state = (
        jnp.full((tok_rows, head_count), NEG_BIG, jnp.float32),
        jnp.zeros((tok_rows, head_count), jnp.float32),
        jnp.zeros((tok_rows, head_count, HD), jnp.float32),
    )
    keys_blk = lax.all_gather(key_b, "ctx", axis=0, tiled=True)
    vals_blk = lax.all_gather(value_b, "ctx", axis=0, tiled=True)
    key_count = keys_blk.shape[0]

    def compute(state_in):
        run_max, run_sum, run_acc = state_in
        scores = (
            jnp.einsum("qhd,khd->qhk", query_b, keys_blk, preferred_element_type=jnp.float32)
            * scale_att
        )
        visible = jnp.arange(key_count)[None, :] <= row_pos[:, None]
        scores = jnp.where(visible[:, None, :], scores, NEG_BIG)
        new_max = jnp.maximum(run_max, jnp.max(scores, axis=2))
        weights = jnp.exp(scores - new_max[:, :, None])
        new_sum = jnp.sum(weights, axis=2)
        new_acc = jnp.einsum(
            "qhk,khd->qhd",
            weights.astype(jnp.bfloat16),
            vals_blk,
            preferred_element_type=jnp.float32,
        )
        return (new_max, new_sum, new_acc)

    run_max, run_sum, run_acc = lax.cond(
        jnp.int32(0) <= q_start + tok_rows - 1, compute, keep_state, start_state
    )
    heads_f = run_acc / run_sum[:, :, None]
    log_sum = run_max + jnp.log(run_sum)
    heads_b = heads_f.astype(jnp.bfloat16).reshape(tok_rows, head_count * HD)
    resid_mid = resid_in + partial_sums(
        jnp.dot(heads_b, wo_all, preferred_element_type=jnp.float32)
    )
    normed_two, scale_two = norm_rows(resid_mid, gain_q2, model_width)
    moe_part = normed_two.astype(jnp.bfloat16)
    moe_in = features(moe_part)
    n_exp = router_all.shape[1]
    exp_dev = n_exp // n_ctx
    capacity = min(tok_rows, 5 * TOPK * tok_rows // (3 * n_exp))
    logits = jnp.dot(moe_in, router_all, preferred_element_type=jnp.float32)
    probs_all = jax.nn.softmax(logits, axis=1)
    picked = (chosen[:, :, None] == jnp.arange(n_exp)[None, None, :]).astype(jnp.float32)
    gate_vals = jnp.sum(picked * probs_all[:, None, :], axis=2)
    shared_a = jnp.dot(moe_in, gate_all, preferred_element_type=jnp.float32)
    shared_b = jnp.dot(moe_in, up_all, preferred_element_type=jnp.float32)
    shared_act = (jax.nn.silu(shared_a) * shared_b).astype(jnp.bfloat16)
    shared_out = jnp.dot(shared_act, down_all, preferred_element_type=jnp.float32)
    flat_exp = chosen.reshape(-1)
    flat_hot = (flat_exp[:, None] == jnp.arange(n_exp)[None, :]).astype(jnp.int32)
    slot_of = jnp.sum((jnp.cumsum(flat_hot, axis=0) - flat_hot) * flat_hot, axis=1)
    token_of = jnp.arange(tok_rows * TOPK) // TOPK
    slot_count = n_ctx * capacity
    outgoing = scatter_slots(moe_in[token_of], flat_exp, slot_of, n_exp, capacity)
    received_rows = to_owners(outgoing.reshape(n_ctx, exp_dev, capacity, model_width)).reshape(
        exp_dev, slot_count, model_width
    )
    expert_a = jnp.einsum(
        "bmw,bwv->bmv", received_rows, expert_gate_weights, preferred_element_type=jnp.float32
    )
    expert_up_proj = jnp.einsum(
        "bmw,bwv->bmv", received_rows, expert_up_weights, preferred_element_type=jnp.float32
    )
    expert_act = (jax.nn.silu(expert_a) * expert_up_proj).astype(jnp.bfloat16)
    expert_out = jnp.einsum(
        "erf,efd->erd", expert_act, expert_down_weights, preferred_element_type=jnp.float32
    )
    returned = to_sources(expert_out.reshape(1, exp_dev, slot_count, model_width))
    shared_q, slot_q = partial_sums((shared_out, returned.reshape(n_exp * capacity, model_width)))
    slot_rows = slot_q.reshape(n_exp, capacity, quarter)[flat_exp, slot_of].reshape(
        tok_rows, TOPK, quarter
    )
    result = resid_mid + shared_q + jnp.sum(gate_vals[:, :, None] * slot_rows, axis=1)
    layer_out = result.astype(jnp.bfloat16)
    grad_out = out_grad.astype(jnp.float32)
    gate_grad = row_stats(jnp.sum(grad_out[:, None, :] * slot_rows, axis=2))
    prob_grad = jnp.sum(gate_grad[:, :, None] * picked, axis=1)
    logit_grad = (
        probs_all * (prob_grad - jnp.sum(probs_all * prob_grad, axis=1, keepdims=True))
    ).astype(jnp.bfloat16)
    router_grad = jnp.einsum("td,te->de", moe_in, logit_grad, preferred_element_type=jnp.float32)
    router_back_q = jnp.einsum(
        "te,de->td", logit_grad, router_rows, preferred_element_type=jnp.float32
    )
    grad_full = features(out_grad)
    shared_dact = jnp.einsum("td,fd->tf", grad_full, down_all, preferred_element_type=jnp.float32)
    shared_da = (shared_dact * shared_b * silu_grad(shared_a)).astype(jnp.bfloat16)
    shared_db = (shared_dact * jax.nn.silu(shared_a)).astype(jnp.bfloat16)
    shared_down_grad = jnp.einsum(
        "tf,td->fd", shared_act, grad_full, preferred_element_type=jnp.float32
    )
    shared_gate_grad = jnp.einsum(
        "td,tf->df", moe_in, shared_da, preferred_element_type=jnp.float32
    )
    shared_up_grad = jnp.einsum("td,tf->df", moe_in, shared_db, preferred_element_type=jnp.float32)
    shared_back = jnp.einsum(
        "tf,df->td", shared_da, gate_all, preferred_element_type=jnp.float32
    ) + jnp.einsum("tf,df->td", shared_db, up_all, preferred_element_type=jnp.float32)
    assign_grad = (
        (gate_vals[:, :, None] * grad_full[:, None, :])
        .astype(jnp.bfloat16)
        .reshape(tok_rows * TOPK, model_width)
    )
    grad_slots = scatter_slots(assign_grad, flat_exp, slot_of, n_exp, capacity)
    grad_arrived = to_owners(grad_slots.reshape(n_ctx, exp_dev, capacity, model_width)).reshape(
        exp_dev, slot_count, model_width
    )
    expert_dact = jnp.einsum(
        "erd,efd->erf", grad_arrived, expert_down_weights, preferred_element_type=jnp.float32
    )
    expert_da = (expert_dact * expert_up_proj * silu_grad(expert_a)).astype(jnp.bfloat16)
    expert_up_proj_grad = (expert_dact * jax.nn.silu(expert_a)).astype(jnp.bfloat16)
    edown_grad = jnp.einsum(
        "erf,erd->efd", expert_act, grad_arrived, preferred_element_type=jnp.float32
    )
    egate_grad = jnp.einsum(
        "qgo,qgz->qoz", received_rows, expert_da, preferred_element_type=jnp.float32
    )
    expert_up_weight_grad = jnp.einsum(
        "qgo,qgz->qoz", received_rows, expert_up_proj_grad, preferred_element_type=jnp.float32
    )
    expert_back = jnp.einsum(
        "iac,igc->iag", expert_da, expert_gate_weights, preferred_element_type=jnp.float32
    ) + jnp.einsum(
        "iac,igc->iag", expert_up_proj_grad, expert_up_weights, preferred_element_type=jnp.float32
    )
    back_slots = to_sources(expert_back.reshape(1, exp_dev, slot_count, model_width)).reshape(
        n_exp, capacity, model_width
    )
    token_back = jnp.sum(back_slots[flat_exp, slot_of].reshape(tok_rows, TOPK, model_width), axis=1)
    moe_back_q = partial_sums(shared_back + token_back)
    mid_back, gain_two_grad = norm_back(
        resid_mid, scale_two, gain_q2, moe_back_q + router_back_q, model_width, tp_rank
    )
    mid_grad = grad_out + mid_back
    branch_full = features(mid_grad.astype(jnp.bfloat16))
    wo_grad = jnp.einsum("tf,td->fd", heads_b, branch_full, preferred_element_type=jnp.float32)
    heads_grad = (
        jnp.einsum("td,fd->tf", branch_full, wo_all, preferred_element_type=jnp.float32)
        .astype(jnp.bfloat16)
        .reshape(tok_rows, head_count, HD)
    )
    row_delta = jnp.sum(heads_grad.astype(jnp.float32) * heads_f, axis=2)
    seq_len = tok_rows * n_ctx
    back_state = (
        jnp.zeros((tok_rows, head_count, HD), jnp.float32),
        jnp.zeros((seq_len, head_count, HD), jnp.float32),
        jnp.zeros((seq_len, head_count, HD), jnp.float32),
    )
    attend_keys_blk = lax.all_gather(key_b, "ctx", axis=0, tiled=True)
    attend_vals_blk = lax.all_gather(value_b, "ctx", axis=0, tiled=True)
    attend_key_count = attend_keys_blk.shape[0]

    def compute(state_in):
        scores = (
            jnp.einsum("qhd,khd->qhk", query_b, attend_keys_blk, preferred_element_type=jnp.float32)
            * scale_att
        )
        visible = jnp.arange(attend_key_count)[None, :] <= row_pos[:, None]
        probs_blk = jnp.where(visible[:, None, :], jnp.exp(scores - log_sum[:, :, None]), 0.0)
        value_part = jnp.einsum(
            "qhk,qhd->khd",
            probs_blk.astype(jnp.bfloat16),
            heads_grad,
            preferred_element_type=jnp.float32,
        )
        dot_grad = jnp.einsum(
            "qhd,khd->qhk", heads_grad, attend_vals_blk, preferred_element_type=jnp.float32
        )
        score_grad = (probs_blk * (dot_grad - row_delta[:, :, None])).astype(jnp.bfloat16)
        query_acc = (
            jnp.einsum(
                "qhk,khd->qhd", score_grad, attend_keys_blk, preferred_element_type=jnp.float32
            )
            * scale_att
        )
        key_part = (
            jnp.einsum("qhk,qhd->khd", score_grad, query_b, preferred_element_type=jnp.float32)
            * scale_att
        )
        return (query_acc, key_part, value_part)

    query_grad, key_grad_all, value_grad_all = lax.cond(
        jnp.int32(0) <= q_start + tok_rows - 1, compute, keep_state, back_state
    )
    key_grad, value_grad = (
        lax.psum_scatter(
            key_grad_all.astype(jnp.bfloat16), "ctx", scatter_dimension=0, tiled=True
        ).astype(jnp.float32),
        lax.psum_scatter(
            value_grad_all.astype(jnp.bfloat16), "ctx", scatter_dimension=0, tiled=True
        ).astype(jnp.float32),
    )
    query_pre_grad = (
        rotary(query_grad, positions, -1.0).astype(jnp.bfloat16).reshape(tok_rows, head_count * HD)
    )
    key_pre_grad = (
        rotary(key_grad, positions, -1.0).astype(jnp.bfloat16).reshape(tok_rows, head_count * HD)
    )
    value_pre_grad = value_grad.astype(jnp.bfloat16).reshape(tok_rows, head_count * HD)
    wq_grad = jnp.einsum("td,tf->df", normed_in, query_pre_grad, preferred_element_type=jnp.float32)
    wk_grad = jnp.einsum("td,tf->df", normed_in, key_pre_grad, preferred_element_type=jnp.float32)
    wv_grad = jnp.einsum("td,tf->df", normed_in, value_pre_grad, preferred_element_type=jnp.float32)
    in_back = jnp.einsum("tf,df->td", query_pre_grad, wq_all, preferred_element_type=jnp.float32)
    in_back = in_back + jnp.einsum(
        "tf,df->td", key_pre_grad, wk_all, preferred_element_type=jnp.float32
    )
    in_back = in_back + jnp.einsum(
        "tf,df->td", value_pre_grad, wv_all, preferred_element_type=jnp.float32
    )
    first_back, gain_one_grad = norm_back(
        resid_in, scale_one, gain_q1, partial_sums(in_back), model_width, tp_rank
    )
    input_grad = mid_grad + first_back
    dense = (
        lax.psum_scatter(
            gain_one_grad.astype(jnp.bfloat16), ("fsdp", "ctx"), scatter_dimension=0, tiled=True
        ).astype(jnp.float32),
        lax.psum_scatter(
            wq_grad.astype(jnp.bfloat16), ("fsdp", "ctx"), scatter_dimension=0, tiled=True
        ).astype(jnp.float32),
        lax.psum_scatter(
            wk_grad.astype(jnp.bfloat16), ("fsdp", "ctx"), scatter_dimension=0, tiled=True
        ).astype(jnp.float32),
        lax.psum_scatter(
            wv_grad.astype(jnp.bfloat16), ("fsdp", "ctx"), scatter_dimension=0, tiled=True
        ).astype(jnp.float32),
        lax.psum_scatter(
            gain_two_grad.astype(jnp.bfloat16), ("fsdp", "ctx"), scatter_dimension=0, tiled=True
        ).astype(jnp.float32),
        lax.psum_scatter(
            router_grad.astype(jnp.bfloat16), ("fsdp", "ctx"), scatter_dimension=0, tiled=True
        ).astype(jnp.float32),
        lax.psum_scatter(
            shared_gate_grad.astype(jnp.bfloat16), ("fsdp", "ctx"), scatter_dimension=0, tiled=True
        ).astype(jnp.float32),
        lax.psum_scatter(
            shared_up_grad.astype(jnp.bfloat16), ("fsdp", "ctx"), scatter_dimension=0, tiled=True
        ).astype(jnp.float32),
        lax.psum_scatter(
            wo_grad.astype(jnp.bfloat16), ("fsdp", "ctx"), scatter_dimension=1, tiled=True
        ).astype(jnp.float32),
        lax.psum_scatter(
            shared_down_grad.astype(jnp.bfloat16), ("fsdp", "ctx"), scatter_dimension=1, tiled=True
        ).astype(jnp.float32),
    )
    experts_done = (
        lax.psum_scatter(
            egate_grad.astype(jnp.bfloat16), "fsdp", scatter_dimension=1, tiled=True
        ).astype(jnp.float32),
        lax.psum_scatter(
            expert_up_weight_grad.astype(jnp.bfloat16), "fsdp", scatter_dimension=1, tiled=True
        ).astype(jnp.float32),
        lax.psum_scatter(
            edown_grad.astype(jnp.bfloat16), "fsdp", scatter_dimension=2, tiled=True
        ).astype(jnp.float32),
    )
    return (
        layer_out,
        input_grad,
        dense[0],
        dense[1],
        dense[2],
        dense[3],
        dense[8],
        dense[4],
        dense[5],
        dense[6],
        dense[7],
        dense[9],
        experts_done[0],
        experts_done[1],
        experts_done[2],
    )


MESH = pl.DeviceIdType.MESH
HBM = pl.BlockSpec(memory_space=pl.ANY)
VMEM = pl.BlockSpec(memory_space=pltpu.VMEM)
DMA = pltpu.SemaphoreType.DMA
BF, F32 = jnp.bfloat16, jnp.float32
BIG = 60 * 1024 * 1024


def dot_nt(left, right):
    return lax.dot_general(left, right, (((1,), (1,)), ((), ())), preferred_element_type=F32)


def dot_tn(left, right):
    return lax.dot_general(left, right, (((0,), (0,)), ((), ())), preferred_element_type=F32)


def dot_nn(left, right):
    return jnp.dot(left, right, preferred_element_type=F32)


def ranks():
    return lax.axis_index("fsdp"), lax.axis_index("ctx"), lax.axis_index("tp")


def sibling(t):
    return t + 1 - 2 * lax.rem(t, 2)


def opposite(t):
    return lax.rem(t + 2, 4)


def remote(src, dst, send, recv, to):
    return pltpu.make_async_remote_copy(
        src_ref=src, dst_ref=dst, send_sem=send, recv_sem=recv, device_id=to, device_id_type=MESH
    )


def greet(peers):
    barrier = pltpu.get_barrier_semaphore()
    for peer in peers:
        pl.semaphore_signal(barrier, inc=1, device_id=peer, device_id_type=MESH)
    pl.semaphore_wait(barrier, len(peers))


def line_peers(c, n_c):
    return [{"ctx": lax.rem(c + step, n_c)} for step in range(1, n_c)]


def piece(index, size):
    return pl.ds(pl.multiple_of(index * size, size), size)


def nearest(c, n_c, act):
    act(c)
    for step in range(1, n_c):
        for side in (-1, 1):
            place = c + side * step

            @pl.when((place >= 0) & (place < n_c))
            def _():
                act(place)


def spread_sems(n_c):
    return [
        DMA((n_c + 2,)),
        DMA((n_c,)),
        DMA((n_c,)),
        DMA((n_c,)),
        DMA((2 * n_c,)),
        DMA((2 * n_c,)),
        DMA((4 * n_c,)),
        DMA((4 * n_c,)),
        DMA(()),
    ]


def spread(own, place, n_c, both, sems, after_line=None):
    zs, zr, xs, xr, ys, yr, ks, kr, ls = sems
    f, c, t = ranks()
    far = opposite(t)
    to_sib, to_far, to_other = {"tp": sibling(t)}, {"tp": far}, {"fsdp": 1 - f}

    def far_copy(src, i, g, cc):
        return remote(src, place(g, cc, t), ys.at[i], yr.at[i], to_far)

    def sib_copy(src, i, which, g, cc, col):
        at = 2 * i + which
        return remote(src, place(g, cc, col), ks.at[at], kr.at[at], to_sib)

    def other_copy(src, cc):
        return remote(src, place(f, cc, t), xs.at[cc], xr.at[cc], to_other)

    def line_copy(src, cc, sem, to):
        return remote(src, place(f, cc, t), zs.at[sem], zr.at[cc], {"ctx": to})

    def pass_on(src, i, g, cc):
        far_copy(src, i, g, cc).start()
        sib_copy(src, i, 0, g, cc, t).start()

    local = pltpu.make_async_copy(own, place(f, c, t), ls)
    local.start()

    @pl.when(c < n_c - 1)
    def _():
        line_copy(own, c, n_c, c + 1).start()

    @pl.when(c > 0)
    def _():
        line_copy(own, c, n_c + 1, c - 1).start()

    if both:
        other_copy(own, c).start()
    pass_on(own, c, f, c)
    for step in range(1, n_c):
        for side in (-1, 1):
            cc = c + side * step
            onward = c - side

            @pl.when((cc >= 0) & (cc < n_c))
            def _():
                block = place(f, cc, t)
                line_copy(block, cc, cc, c).wait_recv()

                @pl.when((onward >= 0) & (onward < n_c))
                def _():
                    line_copy(block, cc, cc, onward).start()

                if both:
                    other_copy(block, cc).start()
                pass_on(block, cc, f, cc)

    if after_line is not None:
        after_line()
    if both:

        def from_other(cc):
            block = place(1 - f, cc, t)
            remote(block, block, xs.at[cc], xr.at[cc], to_other).wait_recv()
            pass_on(block, n_c + cc, 1 - f, cc)

        nearest(c, n_c, from_other)
    for g, base in ((f, 0), (1 - f, n_c))[: 2 if both else 1]:

        def from_far(cc):
            i = base + cc
            block = place(g, cc, far)
            remote(block, block, ys.at[i], yr.at[i], to_far).wait_recv()
            sib_copy(block, i, 1, g, cc, far).start()

        nearest(c, n_c, from_far)
    for g, base in ((f, 0), (1 - f, n_c))[: 2 if both else 1]:
        for cc in range(n_c):
            i = base + cc
            block = place(g, cc, t)
            for which in range(2):
                copy = sib_copy(block, i, which, g, cc, t)
                copy.wait_recv()
                copy.wait_send()
            far_copy(block, i, g, cc).wait_send()
    if both:
        for cc in range(n_c):
            other_copy(place(f, cc, t), cc).wait_send()
    block = place(f, c, t)

    @pl.when(c < n_c - 1)
    def _():
        line_copy(own, c, n_c, c).wait_send()

    @pl.when(c > 0)
    def _():
        line_copy(own, c, n_c + 1, c).wait_send()

    for step in range(1, n_c):
        for side in (-1, 1):
            cc = c + side * step
            onward = c - side

            @pl.when((cc >= 0) & (cc < n_c) & (onward >= 0) & (onward < n_c))
            def _():
                line_copy(block, cc, cc, c).wait_send()

    local.wait()


def to_each(src_of, dst, n_f, n_c, sems, act):
    send, recv, own = sems
    f, c, _ = ranks()
    here = f * n_c + c
    for df in range(n_f):
        for dc in range(n_c):
            i = df * n_c + dc
            if i == 0:
                copy = pltpu.make_async_copy(src_of(here), dst.at[here], own)
                copy.start() if act == "start" else copy.wait()
                continue
            to_f, to_c = lax.rem(f + df, n_f), lax.rem(c + dc, n_c)
            copy = remote(
                src_of(to_f * n_c + to_c), dst.at[here], send.at[i], recv.at[i], {"fsdp": to_f, "ctx": to_c}
            )
            copy.start() if act == "start" else copy.wait()


def each_peers(f, c, n_f, n_c):
    return [
        {"fsdp": lax.rem(f + df, n_f), "ctx": lax.rem(c + dc, n_c)}
        for df in range(n_f)
        for dc in range(n_c)
        if df or dc
    ]


def front_kernel(n_c, part, hidden, wq, wk, wv, wo, small, seq_out, wqkv_out, wo_out, small_out, *sems):
    ws, wr, ls, xs, xr = sems[:5]
    f, c, t = ranks()
    rows, quarter = hidden.shape
    greet([{"tp": sibling(t)}, {"tp": opposite(t)}, {"fsdp": 1 - f}] + line_peers(c, n_c))

    def targets(g, cc):
        block = piece(g * n_c + cc, part)
        return [wqkv_out.at[block, pl.ds(i * HD, HD)] for i in range(3)] + [
            wo_out.at[:, block],
            small_out.at[:, block],
        ]

    def sources(head):
        cols = piece(head, HD)
        return [wq.at[:, cols], wk.at[:, cols], wv.at[:, cols], wo.at[cols, :], small]

    for step in range(1, n_c):
        to = lax.rem(c + step, n_c)
        for i, (src, dst) in enumerate(zip(sources(to), targets(f, c))):
            remote(src, dst, ws.at[step, i], wr.at[step, i], {"ctx": to}).start()
    own = [
        pltpu.make_async_copy(src, dst, ls.at[i])
        for i, (src, dst) in enumerate(zip(sources(c), targets(f, c)))
    ]
    for copy in own:
        copy.start()
    for copy in own:
        copy.wait()

    def slabs(g, cc):
        block = piece(g * n_c + cc, part)
        return [wqkv_out.at[block, :], wo_out.at[:, block], small_out.at[:, block]]

    def across(step, g, cc):
        return [
            remote(slab, slab, xs.at[step, i], xr.at[step, i], {"fsdp": 1 - f})
            for i, slab in enumerate(slabs(g, cc))
        ]

    for copy in across(0, f, c):
        copy.start()

    def place(g, cc, tt):
        return seq_out.at[piece(cc, rows), piece(tt, quarter)]

    def weights_across():
        for step in range(1, n_c):
            cc = lax.rem(c - step + n_c, n_c)
            for i, dst in enumerate(targets(f, cc)):
                remote(dst, dst, ws.at[step, i], wr.at[step, i], {"ctx": cc}).wait_recv()
            for copy in across(step, f, cc):
                copy.start()

    spread(hidden, place, n_c, False, sems[5:], weights_across)
    for step in range(n_c):
        cc = lax.rem(c - step + n_c, n_c)
        for copy in across(step, 1 - f, cc):
            copy.wait_recv()
        for copy in across(step, f, cc):
            copy.wait_send()
    for step in range(1, n_c):
        for i, (src, dst) in enumerate(zip(sources(c), targets(f, c))):
            remote(src, dst, ws.at[step, i], wr.at[step, i], {"ctx": c}).wait_send()


def front(n_c, n_f, n_t, hidden, wq, wk, wv, wo, small):
    rows, quarter = hidden.shape
    part = wq.shape[0]
    width = quarter * n_t
    return pl.pallas_call(
        functools.partial(front_kernel, n_c, part),
        out_shape=(
            jax.ShapeDtypeStruct((rows * n_c, width), BF),
            jax.ShapeDtypeStruct((width, 3 * HD), BF),
            jax.ShapeDtypeStruct((HD, width), BF),
            jax.ShapeDtypeStruct((small.shape[0], width), F32),
        ),
        in_specs=[HBM] * 6,
        out_specs=[HBM] * 4,
        scratch_shapes=[
            DMA((n_c, 5)),
            DMA((n_c, 5)),
            DMA((5,)),
            DMA((n_c, 3)),
            DMA((n_c, 3)),
        ]
        + spread_sems(n_c),
        compiler_params=pltpu.CompilerParams(collective_id=1, has_side_effects=True),
        cost_estimate=pl.CostEstimate(flops=0, bytes_accessed=100 << 20, transcendentals=0),
        name="front",
    )(hidden, wq, wk, wv, wo, small)


def attend_kernel(block, hidden, gain, wqkv, cosine, sine, normed, q_out, k_out, v_out, hf_out, hb_out, lse_out, r_out):
    seq, width = hidden.shape
    scale_att = HD ** (-0.5)
    for start in range(0, seq, block):
        at = pl.ds(start, block)
        h = hidden[at, :].astype(F32)
        r = lax.rsqrt(jnp.sum(h * h, axis=1, keepdims=True) / width + EPS)
        n = (h * r * gain[...]).astype(BF)
        normed[at, :] = n
        r_out[at, :] = jnp.broadcast_to(r, (block, HD))
        qkv = dot_nn(n, wqkv[...])
        cos, sin = cosine[at, :], sine[at, :]

        def rotate(values):
            return (values * cos + pltpu.roll(values, HD // 2, 1) * sin).astype(BF)

        q_out[at, :] = rotate(qkv[:, :HD])
        k_out[at, :] = rotate(qkv[:, HD : 2 * HD])
        v_out[at, :] = qkv[:, 2 * HD :].astype(BF)
    for start in range(0, seq, block):
        at = pl.ds(start, block)
        seen = start + block
        s = dot_nt(q_out[at, :], k_out[:seen, :]) * scale_att
        row = lax.broadcasted_iota(jnp.int32, (block, seen), 0) + start
        col = lax.broadcasted_iota(jnp.int32, (block, seen), 1)
        s = jnp.where(col <= row, s, NEG_BIG)
        top = jnp.max(s, axis=1, keepdims=True)
        e = jnp.exp(s - top)
        total = jnp.sum(e, axis=1, keepdims=True)
        p = (e / total).astype(BF)
        out = dot_nn(p, v_out[:seen, :])
        hf_out[at, :] = out
        hb_out[at, :] = out.astype(BF)
        lse_out[at, :] = jnp.broadcast_to(top + jnp.log(total), (block, HD))


def attend(hidden, gain, wqkv, cosine, sine):
    seq, width = hidden.shape
    head = jax.ShapeDtypeStruct((seq, HD), BF)
    head_f = jax.ShapeDtypeStruct((seq, HD), F32)
    return pl.pallas_call(
        functools.partial(attend_kernel, min(256, seq)),
        out_shape=(jax.ShapeDtypeStruct((seq, width), BF), head, head, head, head_f, head, head_f, head_f),
        in_specs=[VMEM] * 5,
        out_specs=[VMEM] * 8,
        compiler_params=pltpu.CompilerParams(vmem_limit_bytes=BIG),
        cost_estimate=pl.CostEstimate(flops=2 << 30, bytes_accessed=12 << 20, transcendentals=1 << 20),
        name="attend",
    )(hidden, gain, wqkv, cosine, sine)


def reduce_seq_scratch(n_c, rows, quarter):
    return [
        pltpu.VMEM((n_c, 2, rows, quarter), BF),
        pltpu.VMEM((n_c, 2, rows, quarter), BF),
        pltpu.VMEM((n_c, 2, rows, quarter), F32),
        pltpu.VMEM((n_c, rows, quarter), BF),
        pltpu.VMEM((n_c, rows, quarter), BF),
        pltpu.VMEM((n_c, rows, quarter), BF),
        pltpu.VMEM((n_c, rows, quarter), BF),
        DMA((n_c,)),
        DMA((n_c,)),
        DMA((n_c,)),
        DMA((n_c,)),
        DMA((n_c,)),
        DMA((n_c,)),
    ]


def reduce_seq(part_of, n_c, scratch, between=None):
    out1, in1, own, out2, in2, out3, in3, s1, r1, s2, r2, s3, r3 = scratch
    f, c, t = ranks()
    far, sib = opposite(t), sibling(t)
    to_sib, to_far = {"tp": sib}, {"tp": far}
    order = [2, 1, 3, 0] if n_c == 4 else list(range(1, n_c)) + [0]
    for d in order:
        cc = lax.rem(c + d, n_c)
        out1[d, 0] = part_of(cc, sib).astype(BF)
        out1[d, 1] = part_of(cc, opposite(sib)).astype(BF)
        remote(out1.at[d], in1.at[d], s1.at[d], r1.at[d], to_sib).start()
        own[d, 0] = part_of(cc, t)
        own[d, 1] = part_of(cc, far)
    if between is not None:
        between()
    for d in order:
        remote(out1.at[d], in1.at[d], s1.at[d], r1.at[d], to_sib).wait()
        out2[d] = (own[d, 1] + in1[d, 1].astype(F32)).astype(BF)
        remote(out2.at[d], in2.at[d], s2.at[d], r2.at[d], to_far).start()
    for d in order:
        remote(out2.at[d], in2.at[d], s2.at[d], r2.at[d], to_far).wait()
        total = own[d, 0] + in1[d, 0].astype(F32) + in2[d].astype(F32)
        if d:
            out3[d] = total.astype(BF)
            cc = lax.rem(c + d, n_c)
            remote(out3.at[d], in3.at[d], s3.at[d], r3.at[d], {"ctx": cc}).start()
    for d in order[:-1]:
        remote(out3.at[d], in3.at[d], s3.at[d], r3.at[d], {"ctx": c}).wait()
        total = total + in3[d].astype(F32)
    return total


def mid_kernel(n_c, n_f, heads, wo, hidden, shared, resid_out, all_out, shared_out, blk, ss, sr, sl, *scratch):
    f, c, t = ranks()
    rows, quarter = hidden.shape
    greet([{"tp": sibling(t)}, {"tp": opposite(t)}] + each_peers(f, c, n_f, n_c))
    exchange = lambda act: to_each(lambda b: shared.at[b], shared_out, n_f, n_c, (ss, sr, sl), act)

    def part_of(cc, q):
        return dot_nn(heads[piece(cc, rows), :], wo[:, piece(q, quarter)])

    total = reduce_seq(part_of, n_c, scratch[:13], lambda: exchange("start"))
    resid = hidden[...].astype(F32) + total
    resid_out[...] = resid
    blk[...] = resid.astype(BF)

    def place(g, cc, tt):
        return all_out.at[piece(g * n_c + cc, rows), piece(tt, quarter)]

    spread(blk, place, n_c, True, scratch[13:])
    exchange("wait")


def mid(n_c, n_f, n_t, heads, wo, hidden, shared):
    rows, quarter = hidden.shape
    return pl.pallas_call(
        functools.partial(mid_kernel, n_c, n_f),
        out_shape=(
            jax.ShapeDtypeStruct((rows, quarter), F32),
            jax.ShapeDtypeStruct((rows * n_c * n_f, quarter * n_t), BF),
            jax.ShapeDtypeStruct(shared.shape, BF),
        ),
        in_specs=[VMEM] * 3 + [HBM],
        out_specs=[VMEM, HBM, HBM],
        scratch_shapes=[
            pltpu.VMEM((rows, quarter), BF),
            DMA((n_f * n_c,)),
            DMA((n_f * n_c,)),
            DMA(()),
        ]
        + reduce_seq_scratch(n_c, rows, quarter)
        + spread_sems(n_c),
        compiler_params=pltpu.CompilerParams(
            collective_id=2, has_side_effects=True, vmem_limit_bytes=BIG
        ),
        cost_estimate=pl.CostEstimate(flops=1 << 29, bytes_accessed=200 << 20, transcendentals=0),
        name="mid",
    )(heads, wo, hidden, shared)


def fetch_experts(n_c, n_f, mine, ffe, srows, hp, weights, shared, wgu, wd, sems):
    f = lax.axis_index("fsdp")
    wg0, wu0, wd0, wg1, wu1, wd1 = weights
    width = wd.shape[1]
    used = mine * ffe
    part = width // (n_f * n_c)
    half = width // n_f
    copies = []

    def add(src, dst):
        copies.append(pltpu.make_async_copy(src, dst, sems.at[len(copies)]))

    for i, (kept, got) in enumerate(((wg0, wg1), (wu0, wu1), (wd0, wd1))):
        dst, base = ((wgu, 0), (wgu, hp), (wd, 0))[i]
        for e in range(mine):
            at = pl.ds(base + e * ffe, ffe)
            add(kept.at[f * mine + e], dst.at[at, piece(f, half)])
            add(got.at[e], dst.at[at, piece(1 - f, half)])
        for b in range(n_f * n_c):
            add(
                shared.at[b, pl.ds(i * srows, srows), :],
                dst.at[pl.ds(base + used, srows), pl.ds(b * part, part)],
            )
    return copies


def blank_rows(rows_used, hp, wgu, wd):
    blank = jnp.zeros((hp - rows_used, wd.shape[1]), BF)
    wgu[rows_used:hp, :] = blank
    wgu[hp + rows_used :, :] = blank
    wd[rows_used:, :] = blank


def gates(prob, picked, first, mine, ffe, hp):
    block, n_exp = prob.shape
    lane = lax.broadcasted_iota(jnp.int32, (block, n_exp), 1)
    gated = prob * picked
    col = lax.broadcasted_iota(jnp.int32, (block, hp), 1)
    gate = jnp.ones((block, hp), F32)
    for k in range(mine):
        g = jnp.sum(jnp.where(lane == first + k, gated, 0.0), axis=1, keepdims=True)
        gate = jnp.where((col >= k * ffe) & (col < (k + 1) * ffe), g, gate)
    return gate, lane, col


def reducer_scratch(n_f, n_c, rows, quarter):
    n_b = n_f * n_c
    blocks = lambda *lead: pltpu.VMEM(lead + (rows, quarter), BF)
    return [
        blocks(n_b, 2),
        blocks(n_b, 2),
        blocks(n_b, 2),
        blocks(n_b),
        blocks(n_b),
        blocks(n_c),
        blocks(n_c),
        pltpu.VMEM((n_c, rows, quarter), F32),
        blocks(n_c),
        blocks(n_c),
    ] + [DMA((n_b,))] * 4 + [DMA((n_c,))] * 4


class Reducer:
    def __init__(self, n_c, scratch):
        self.n_c = n_c
        (self.out1, self.in1, self.own, self.out2, self.in2, self.out3, self.in3, self.acc,
         self.out4, self.in4, self.s1, self.r1, self.s2, self.r2, self.s3, self.r3, self.s4, self.r4) = scratch
        self.f, self.c, self.t = ranks()
        self.far, self.sib = opposite(self.t), sibling(self.t)

    def row_block(self, i):
        n_c = self.n_c
        group = jnp.where(i < n_c, 1 - self.f, self.f)
        return group * n_c + lax.rem(self.c + lax.rem(i, n_c) + 1, n_c)

    def core_copy(self, i):
        return remote(self.out1.at[i], self.in1.at[i], self.s1.at[i], self.r1.at[i], {"tp": self.sib})

    def far_copy(self, i):
        return remote(self.out2.at[i], self.in2.at[i], self.s2.at[i], self.r2.at[i], {"tp": self.far})

    def other_copy(self, j):
        return remote(self.out3.at[j], self.in3.at[j], self.s3.at[j], self.r3.at[j], {"fsdp": 1 - self.f})

    def line_copy(self, j, to):
        return remote(self.out4.at[j], self.in4.at[j], self.s4.at[j], self.r4.at[j], {"ctx": to})

    def put(self, i, part_of):
        self.out1[i, 0] = part_of(opposite(self.sib)).astype(BF)
        self.out1[i, 1] = part_of(self.sib).astype(BF)
        self.core_copy(i).start()
        self.own[i, 0] = part_of(self.far).astype(BF)
        self.own[i, 1] = part_of(self.t).astype(BF)

    def over(self, i):
        self.core_copy(i).wait()
        self.out2[i] = (self.own[i, 0].astype(F32) + self.in1[i, 0].astype(F32)).astype(BF)
        self.far_copy(i).start()

    def _sum(self, i):
        self.far_copy(i).wait()
        return self.own[i, 1].astype(F32) + self.in1[i, 1].astype(F32) + self.in2[i].astype(F32)

    def after_other(self, i):
        self.out3[i] = self._sum(i).astype(BF)
        self.other_copy(i).start()

    def after_own(self, i):
        self.acc[i - self.n_c] = self._sum(i)

    def along(self, j):
        self.other_copy(j).wait()
        total = self.acc[j] + self.in3[j].astype(F32)
        if j < self.n_c - 1:
            self.out4[j] = total.astype(BF)
            self.line_copy(j, lax.rem(self.c + j + 1, self.n_c)).start()
        return total

    def total(self, total):
        for j in range(self.n_c - 1):
            self.line_copy(j, self.c).wait()
            total = total + self.in4[j].astype(F32)
        return total

    def loop(self, n_b, compute):
        n_c = self.n_c

        def step(i, carry):
            def between():
                @pl.when(i >= 1)
                def _():
                    self.over(i - 1)

                @pl.when((i >= 3) & (i < 3 + n_c))
                def _():
                    self.after_other(i - 3)

                @pl.when(i >= 3 + n_c)
                def _():
                    self.after_own(i - 3)

            compute(i, between)
            return carry

        lax.fori_loop(0, n_b, step, 0)

    def drain(self, n_b, works):
        works = list(works)
        self.over(n_b - 1)
        for i in range(n_b - 3, n_b):
            if works:
                works.pop(0)()
            self.after_own(i) if i >= self.n_c else self.after_other(i)
        for j in range(self.n_c):
            total = self.along(j)
        for work in works:
            work()
        return self.total(total)


def forward_kernel(
    n_c, n_f, mine, ffe, srows, hp, rows_all, og_all, resid, picked, gain, router,
    wg0, wu0, wd0, wg1, wu1, wd1, shared,
    layer_out, in_out, act_out, silu_out, slope_out, r_out, prob_out, keep_out, send_out, shared_out,
    gt, wsem, xsem, nsem, asem, tsem, osem, *scratch,
):
    f, c, t = ranks()
    n_b = n_f * n_c
    rows, quarter = resid.shape
    width = rows_all.shape[1]
    routed = mine * ffe
    rows_used = routed + srows
    red = Reducer(n_c, scratch)

    def blocks_phase(wgu, wd, xs, ns, acts):
        fetches = fetch_experts(
            n_c, n_f, mine, ffe, srows, hp, (wg0, wu0, wd0, wg1, wu1, wd1), shared, wgu, wd, wsem
        )
        for copy in fetches:
            copy.start()

        def load(i, slot):
            return pltpu.make_async_copy(
                rows_all.at[piece(red.row_block(i), rows), :], xs.at[slot], xsem.at[slot]
            )

        def stores(i, slot):
            at = piece(red.row_block(i), rows)
            return [pltpu.make_async_copy(ns.at[slot], in_out.at[at, :], nsem.at[slot])] + [
                pltpu.make_async_copy(acts.at[slot, k], out.at[at, :], asem.at[slot, k])
                for k, out in enumerate((act_out, silu_out, slope_out))
            ]

        load(0, 0).start()
        blank_rows(rows_used, hp, wgu, wd)
        greet([{"tp": red.sib}, {"tp": red.far}, {"fsdp": 1 - f}] + line_peers(c, n_c))
        for copy in fetches:
            copy.wait()

        def compute(i, between):
            slot = lax.rem(i, 2)
            b = red.row_block(i)
            at = piece(b, rows)
            load(i, slot).wait()

            @pl.when(i + 1 < n_b)
            def _():
                load(i + 1, 1 - slot).start()

            @pl.when(i >= 2)
            def _():
                for copy in stores(i - 2, slot):
                    copy.wait()

            h = xs[slot].astype(F32)
            r = lax.rsqrt(jnp.sum(h * h, axis=1, keepdims=True) / width + EPS)
            r_out[at, :] = jnp.broadcast_to(r, (rows, HD))
            n = (h * r * gain[...]).astype(BF)
            ns[slot] = n
            logits = dot_nt(n, router[...])
            e = jnp.exp(logits - jnp.max(logits, axis=1, keepdims=True))
            prob = e / jnp.sum(e, axis=1, keepdims=True)
            prob_out[at, :] = prob
            gate, _, _ = gates(prob, picked[at, :], (c * n_f + f) * mine, mine, ffe, hp)
            ab = dot_nt(n, wgu[...])
            between()
            a, up = ab[:, :hp], ab[:, hp:]
            sig = 1.0 / (1.0 + jnp.exp(-a))
            silu = a * sig
            act = (silu * up).astype(BF)
            acts[slot, 0] = act
            acts[slot, 1] = silu.astype(BF)
            acts[slot, 2] = (up * (sig * (1.0 + a * (1.0 - sig)))).astype(BF)
            actg = (act.astype(F32) * gate).astype(BF)
            gt[:, at] = actg.T[:rows_used, :]
            for copy in stores(i, slot):
                copy.start()
            red.put(i, lambda q: dot_nn(actg, wd[:, piece(q, quarter)]))

        red.loop(n_b, compute)
        for i in range(n_b - 2, n_b):
            for copy in stores(i, i % 2):
                copy.wait()

    pl.run_scoped(
        blocks_phase,
        pltpu.VMEM((2 * hp, width), BF),
        pltpu.VMEM((hp, width), BF),
        pltpu.VMEM((2, rows, width), BF),
        pltpu.VMEM((2, rows, width), BF),
        pltpu.VMEM((2, 3, rows, hp), BF),
    )

    def grads_phase(tiles, keeps, sends, shs):
        def tile_of(s):
            return (1 - f) * 2 + s if s < 2 else f * 2 + s - 2

        def tile_load(s):
            return pltpu.make_async_copy(og_all.at[:, tile_of(s)], tiles.at[s % 2], tsem.at[s % 2])

        def out_copies(s):
            cols = pl.ds(s % 2 * quarter, quarter)
            if s < 2:
                src, dst = sends.at[s], send_out.at[:, :, cols]
            else:
                src, dst = keeps.at[s - 2], keep_out.at[pl.ds(f * mine, mine), :, cols]
            return [
                pltpu.make_async_copy(src, dst, osem.at[s, 0]),
                pltpu.make_async_copy(
                    shs.at[s], shared_out.at[:, piece(tile_of(s), quarter)], osem.at[s, 1]
                ),
            ]

        def work(s):
            def run():
                tile_load(s).wait()
                if s < 3:
                    tile_load(s + 1).start()
                g = dot_nn(gt[...], tiles[s % 2].reshape(n_b * rows, quarter))
                if s < 2:
                    sends[s] = g[:routed].astype(BF).reshape(mine, ffe, quarter)
                else:
                    keeps[s - 2] = g[:routed].reshape(mine, ffe, quarter)
                shs[s] = g[routed:].astype(BF)
                for copy in out_copies(s):
                    copy.start()

            return run

        tile_load(0).start()
        total = red.drain(n_b, [work(s) for s in range(4)])
        layer_out[...] = (resid[...] + total).astype(BF)
        for s in range(4):
            for copy in out_copies(s):
                copy.wait()

    pl.run_scoped(
        grads_phase,
        pltpu.VMEM((2, n_b, rows, quarter), BF),
        pltpu.VMEM((2, mine, ffe, quarter), F32),
        pltpu.VMEM((2, mine, ffe, quarter), BF),
        pltpu.VMEM((4, srows, quarter), BF),
    )


def expert_sizes(n_c, n_f, n_t, mine, ffe, srows, width):
    used = mine * ffe + srows
    return used, -(-used // HD) * HD, 3 * (2 * mine + n_f * n_c)


def forward(n_c, n_f, n_t, mine, ffe, srows, rows_all, og_all, resid, picked, gain, router, kept, got, shared):
    total, width = rows_all.shape
    rows, quarter = resid.shape
    n_exp = router.shape[0]
    n_b = n_f * n_c
    used, hp, n_fetch = expert_sizes(n_c, n_f, n_t, mine, ffe, srows, width)
    sds = jax.ShapeDtypeStruct
    return pl.pallas_call(
        functools.partial(forward_kernel, n_c, n_f, mine, ffe, srows, hp),
        out_shape=(
            sds((rows, quarter), BF),
            sds((total, width), BF),
            sds((total, hp), BF),
            sds((total, hp), BF),
            sds((total, hp), BF),
            sds((total, HD), F32),
            sds((total, n_exp), F32),
            sds((n_f * mine, ffe, width // n_f), F32),
            sds((mine, ffe, width // n_f), BF),
            sds((srows, width), BF),
        ),
        in_specs=[HBM, HBM, VMEM, VMEM, VMEM, VMEM] + [HBM] * 7,
        out_specs=[VMEM, HBM, HBM, HBM, HBM, VMEM, VMEM, HBM, HBM, HBM],
        scratch_shapes=[
            pltpu.VMEM((used, total), BF),
            DMA((n_fetch,)),
            DMA((2,)),
            DMA((2,)),
            DMA((2, 3)),
            DMA((2,)),
            DMA((4, 2)),
        ]
        + reducer_scratch(n_f, n_c, rows, quarter),
        compiler_params=pltpu.CompilerParams(
            collective_id=5, has_side_effects=True, vmem_limit_bytes=BIG
        ),
        cost_estimate=pl.CostEstimate(
            flops=8 * total * width * used, bytes_accessed=80 << 20, transcendentals=total * used
        ),
        name="forward",
    )(rows_all, og_all, resid, picked, gain, router, *kept, *got, shared)


def backward_kernel(
    n_c, n_f, mine, ffe, srows, hp, og_all, act, silu, slope, moe_in, r_all, shared_d, prob_in, picked, router,
    resid, gain, og, wg0, wu0, wd0, wg1, wu1, wd1, shared,
    mid_out, gain_out, seq_out, shared_out, kg_out, ku_out, gg_out, gu_out,
    gt, blk, r_own, sends, shs, wsem, xsem, tsem, ksem, ss, sr, rs, es, er, el, ds, dr, dl, *rest,
):
    f, c, t = ranks()
    n_b = n_f * n_c
    rows, quarter = resid.shape
    width = shared_d.shape[1]
    n_exp = router.shape[0]
    routed = mine * ffe
    rows_used = routed + srows
    first = (c * n_f + f) * mine
    red = Reducer(n_c, rest[:18])

    def blocks_phase(wgu, wd, ogs, acts):
        fetches = fetch_experts(
            n_c, n_f, mine, ffe, srows, hp, (wg0, wu0, wd0, wg1, wu1, wd1), shared, wgu, wd, wsem
        )
        for copy in fetches:
            copy.start()

        def loads(i, slot):
            b = red.row_block(i)
            return [
                pltpu.make_async_copy(
                    og_all.at[b, q], ogs.at[slot, :, pl.ds(q * quarter, quarter)], xsem.at[slot, q]
                )
                for q in range(4)
            ] + [
                pltpu.make_async_copy(src.at[piece(b, rows), :], acts.at[slot, k], xsem.at[slot, 4 + k])
                for k, src in enumerate((act, silu, slope))
            ]

        for copy in loads(0, 0):
            copy.start()
        blank_rows(rows_used, hp, wgu, wd)
        greet([{"tp": red.sib}, {"tp": red.far}, {"tp": opposite(red.sib)}] + each_peers(f, c, n_f, n_c))
        for copy in fetches:
            copy.wait()

        def compute(i, between):
            slot = lax.rem(i, 2)
            at = piece(red.row_block(i), rows)
            for copy in loads(i, slot):
                copy.wait()

            @pl.when(i + 1 < n_b)
            def _():
                for copy in loads(i + 1, 1 - slot):
                    copy.start()

            prob = prob_in[at, :]
            chosen = picked[at, :]
            gate, lane, col = gates(prob, chosen, first, mine, ffe, hp)
            dh = dot_nt(ogs[slot], wd[...])
            between()
            ad = acts[slot, 0].astype(F32) * dh
            p_grad = jnp.zeros(prob.shape, F32)
            for k in range(mine):
                s = jnp.sum(
                    jnp.where((col >= k * ffe) & (col < (k + 1) * ffe), ad, 0.0), axis=1, keepdims=True
                )
                p_grad = jnp.where(lane == first + k, s, p_grad)
            p_grad = p_grad * chosen
            logit_f = prob * (p_grad - jnp.sum(prob * p_grad, axis=1, keepdims=True))
            logit_grad = logit_f.astype(BF)
            dg = dh * gate
            da = (dg * acts[slot, 2].astype(F32)).astype(BF)
            db = (dg * acts[slot, 1].astype(F32)).astype(BF)
            gt[:rows_used, at] = da.T[:rows_used, :]
            gt[rows_used : 2 * rows_used, at] = db.T[:rows_used, :]
            gt[2 * rows_used :, at] = logit_f.T.astype(BF)
            dab = jnp.concatenate([da, db], axis=1)

            def part_of(q):
                cols = piece(q, quarter)
                return dot_nn(dab, wgu[:, cols]) + dot_nn(logit_grad, router[:, cols])

            red.put(i, part_of)

        red.loop(n_b, compute)

    pl.run_scoped(
        blocks_phase,
        pltpu.VMEM((2 * hp, width), BF),
        pltpu.VMEM((hp, width), BF),
        pltpu.VMEM((2, rows, width), BF),
        pltpu.VMEM((2, 3, rows, hp), BF),
    )

    def send_copy(s, m):
        dst = (gg_out, gu_out)[m].at[:, :, pl.ds(s * quarter, quarter)]
        return remote(sends.at[s, m], dst, ss.at[s, m], sr.at[s, m], {"fsdp": 1 - f})

    def grads_phase(tiles, keeps):
        def tile_of(s):
            return (1 - f) * 2 + s if s < 2 else f * 2 + s - 2

        def tile_load(s):
            return pltpu.make_async_copy(
                moe_in.at[:, piece(tile_of(s), quarter)], tiles.at[s % 2], tsem.at[s % 2]
            )

        def keep_copy(s, m):
            dst = (kg_out, ku_out)[m].at[pl.ds(f * mine, mine), :, pl.ds((s - 2) * quarter, quarter)]
            return pltpu.make_async_copy(keeps.at[s - 2, m], dst, ksem.at[s - 2, m])

        def work(s):
            def run():
                tile_load(s).wait()
                if s < 3:
                    tile_load(s + 1).start()
                g = dot_nn(gt[...], tiles[s % 2])
                cols = piece(tile_of(s), quarter)
                for m in range(2):
                    base = m * rows_used
                    if s < 2:
                        sends[s, m] = g[base : base + routed].astype(BF).reshape(mine, ffe, quarter)
                        send_copy(s, m).start()
                    else:
                        keeps[s - 2, m] = g[base : base + routed].reshape(mine, ffe, quarter)
                        keep_copy(s, m).start()
                    shs[m * srows : (m + 1) * srows, cols] = g[base + routed : base + rows_used].astype(BF)
                shs[2 * srows :, cols] = g[2 * rows_used :].astype(BF)

            return run

        tile_load(0).start()
        blk[...] = red.drain(n_b, [work(s) for s in range(4)])
        for s in (2, 3):
            for m in range(2):
                keep_copy(s, m).wait()

    fetch = pltpu.make_async_copy(r_all.at[piece(f * n_c + c, rows), :], r_own, rs)
    fetch.start()
    pl.run_scoped(
        grads_phase,
        pltpu.VMEM((2, n_b * rows, quarter), BF),
        pltpu.VMEM((2, 2, mine, ffe, quarter), F32),
    )
    cols = width // n_b
    n_gu = shs.shape[0]

    def exchange(act):
        for src, at, sems in (
            (shs, pl.ds(0, n_gu), (es, er, el)),
            (shared_d, pl.ds(n_gu, srows), (ds, dr, dl)),
        ):
            to_each(lambda b: src.at[:, piece(b, cols)], shared_out.at[:, at, :], n_f, n_c, sems, act)

    fetch.wait()
    back, gain_part = norm_grad(resid[...], r_own[:, :1], gain[...], blk[...], width, *rest[18:22])
    gain_out[...] = jnp.broadcast_to(gain_part, gain_out.shape)
    grad = og[...].astype(F32) + back
    mid_out[...] = grad
    own = rest[22]
    own[...] = grad.astype(BF)

    def place(g, cc, tt):
        return seq_out.at[piece(cc, rows), piece(tt, quarter)]

    spread(own, place, n_c, False, rest[23:], lambda: exchange("start"))
    exchange("wait")
    for s in range(2):
        for m in range(2):
            send_copy(s, m).wait()


def backward(
    n_c, n_f, n_t, mine, ffe, srows, og_all, act, silu, slope, moe_in, r_all, shared_d, prob, picked, router,
    resid, gain, og, kept, got, shared,
):
    total, width = moe_in.shape
    rows, quarter = resid.shape
    n_exp = router.shape[0]
    n_b = n_f * n_c
    used, hp, n_fetch = expert_sizes(n_c, n_f, n_t, mine, ffe, srows, width)
    sds = jax.ShapeDtypeStruct
    kept_g = sds((n_f * mine, ffe, width // n_f), F32)
    sent_g = sds((mine, ffe, width // n_f), BF)
    return pl.pallas_call(
        functools.partial(backward_kernel, n_c, n_f, mine, ffe, srows, hp),
        out_shape=(
            sds((rows, quarter), F32),
            sds((8, quarter), F32),
            sds((rows * n_c, width), BF),
            sds((n_b, 3 * srows + n_exp, width // n_b), BF),
            kept_g,
            kept_g,
            sent_g,
            sent_g,
        ),
        in_specs=[HBM] * 7 + [VMEM] * 6 + [HBM] * 7,
        out_specs=[VMEM, VMEM] + [HBM] * 6,
        scratch_shapes=[
            pltpu.VMEM((2 * used + n_exp, total), BF),
            pltpu.VMEM((rows, quarter), F32),
            pltpu.VMEM((rows, HD), F32),
            pltpu.VMEM((2, 2, mine, ffe, quarter), BF),
            pltpu.VMEM((2 * srows + n_exp, width), BF),
            DMA((n_fetch,)),
            DMA((2, 7)),
            DMA((2,)),
            DMA((2, 2)),
            DMA((2, 2)),
            DMA((2, 2)),
            DMA(()),
            DMA((n_b,)),
            DMA((n_b,)),
            DMA(()),
            DMA((n_b,)),
            DMA((n_b,)),
            DMA(()),
        ]
        + reducer_scratch(n_f, n_c, rows, quarter)
        + norm_grad_scratch(rows)
        + [pltpu.VMEM((rows, quarter), BF)]
        + spread_sems(n_c),
        compiler_params=pltpu.CompilerParams(
            collective_id=3, has_side_effects=True, vmem_limit_bytes=BIG
        ),
        cost_estimate=pl.CostEstimate(
            flops=10 * total * width * used, bytes_accessed=200 << 20, transcendentals=0
        ),
        name="backward",
    )(
        og_all, act, silu, slope, moe_in, r_all, shared_d, prob, picked, router, resid, gain, og,
        *kept, *got, shared,
    )


def fill_kernel(f_ref, a, b, c, _a, _b, _c, oa, ob, oc):
    del f_ref, _a, _b, _c
    oa[...] = a[...].astype(F32)
    ob[...] = b[...].astype(F32)
    oc[...] = c[...].astype(F32)


def fill_experts(f_rank, arrived, kept):
    mine, ffe, half = arrived[0].shape
    tile = half // 4
    src = pl.BlockSpec((mine, ffe, tile), lambda i, f: (0, 0, i))
    dst = pl.BlockSpec((mine, ffe, tile), lambda i, f: (1 - f[0], 0, i))
    return pl.pallas_call(
        fill_kernel,
        grid_spec=pltpu.PrefetchScalarGridSpec(
            num_scalar_prefetch=1, grid=(4,), in_specs=[src] * 3 + [HBM] * 3, out_specs=[dst] * 3
        ),
        out_shape=tuple(jax.ShapeDtypeStruct(k.shape, k.dtype) for k in kept),
        input_output_aliases={4: 0, 5: 1, 6: 2},
        compiler_params=pltpu.CompilerParams(vmem_limit_bytes=BIG),
        name="fill_experts",
    )(f_rank, *arrived, *kept)


def norm_grad(values, r, gain, grad, width, out, into, send, recv):
    f, c, t = ranks()
    local = jnp.sum(grad * gain * values, axis=1, keepdims=True)
    out[...] = jnp.broadcast_to(local, out.shape)
    peers = [sibling(t), opposite(t), opposite(sibling(t))]
    copies = [
        remote(out, into.at[i], send.at[i], recv.at[i], {"tp": peer}) for i, peer in enumerate(peers)
    ]
    for copy in copies:
        copy.start()
    gain_part = jnp.sum(grad * values * r, axis=0, keepdims=True)
    total = local
    for i, copy in enumerate(copies):
        copy.wait()
        total = total + into[i][:, :1]
    return r * gain * grad - values * (r * r * r * (total / width)), gain_part


def norm_grad_scratch(rows):
    return [
        pltpu.VMEM((rows, HD), F32),
        pltpu.VMEM((3, rows, HD), F32),
        DMA((3,)),
        DMA((3,)),
    ]


def attend_back_kernel(
    block, mid, wo, q, k, v, hf, lse, cosine, sine, normed, dqkv, gattn, hg, dq, dk, dv
):
    seq = mid.shape[0]
    scale_att = HD ** (-0.5)
    for start in range(0, seq, block):
        at = pl.ds(start, block)
        hg[at, :] = dot_nt(mid[at, :], wo[...]).astype(BF)
    dk[...] = jnp.zeros_like(dk)
    dv[...] = jnp.zeros_like(dv)
    for start in range(0, seq, block):
        at = pl.ds(start, block)
        seen = start + block
        qb, hb = q[at, :], hg[at, :]
        delta = jnp.sum(hb.astype(F32) * hf[at, :], axis=1, keepdims=True)
        s = dot_nt(qb, k[:seen, :]) * scale_att
        row = lax.broadcasted_iota(jnp.int32, (block, seen), 0) + start
        col = lax.broadcasted_iota(jnp.int32, (block, seen), 1)
        p = jnp.where(col <= row, jnp.exp(s - lse[at, :1]), 0.0)
        ds = (p * (dot_nt(hb, v[:seen, :]) - delta)).astype(BF)
        dq[at, :] = dot_nn(ds, k[:seen, :]) * scale_att
        dk[:seen, :] += dot_tn(ds, qb) * scale_att
        dv[:seen, :] += dot_tn(p.astype(BF), hb)

    def rotate(values, at):
        return (values * cosine[at, :] - pltpu.roll(values, HD // 2, 1) * sine[at, :]).astype(BF)

    for start in range(0, seq, block):
        at = pl.ds(start, block)
        dqkv[at, :HD] = rotate(dq[at, :], at)
        dqkv[at, HD : 2 * HD] = rotate(dk[at, :], at)
        dqkv[at, 2 * HD :] = dv[at, :].astype(BF)
    gattn[: 3 * HD, :] = dot_tn(dqkv[...], normed[...]).astype(BF)
    gattn[3 * HD :, :] = dot_tn(hf[...].astype(BF), mid[...]).astype(BF)


def attend_back(mid_seq, wo, q, k, v, hf, lse, cosine, sine, normed):
    seq, width = mid_seq.shape
    sds = jax.ShapeDtypeStruct
    return pl.pallas_call(
        functools.partial(attend_back_kernel, min(256, seq)),
        out_shape=(sds((seq, 3 * HD), BF), sds((4 * HD, width), BF)),
        in_specs=[VMEM] * 10,
        out_specs=[VMEM] * 2,
        scratch_shapes=[pltpu.VMEM((seq, HD), BF)] + [pltpu.VMEM((seq, HD), F32)] * 3,
        compiler_params=pltpu.CompilerParams(vmem_limit_bytes=BIG),
        cost_estimate=pl.CostEstimate(flops=6 << 30, bytes_accessed=16 << 20, transcendentals=1 << 20),
        name="attend_back",
    )(mid_seq, wo, q, k, v, hf, lse, cosine, sine, normed)


def last_kernel(
    n_c, n_f, n_t, width, dqkv, wqkv, hidden, r_all, gain, mid_grad, gain2, rpart, gattn,
    in_out, gq, gk, gv, go, gains_out, router_out,
    rin, rss, rsr, r_own, outx, inx, own, outz, inz, gsend, gin, rs, sx, rx, lx, sz, rz, gs, gr, *rest,
):
    f, c, t = ranks()
    rows, quarter = hidden.shape
    part = width // (n_f * n_c)
    here = f * n_c + c
    others = []
    for df in range(n_f):
        for dc in range(n_c):
            for dt in range(n_t):
                if df or dc or dt:
                    others.append(
                        {
                            "fsdp": lax.rem(f + df, n_f),
                            "ctx": lax.rem(c + dc, n_c),
                            "tp": lax.rem(t + dt, n_t),
                        }
                    )
    gin[...] = jnp.zeros_like(gin)
    greet(others)
    order = [2, 1, 3, 0] if n_c == 4 else list(range(1, n_c)) + [0]

    def cross(d):
        cc = lax.rem(c + d, n_c)
        return remote(
            gattn.at[:, piece((1 - f) * n_c + cc, part)], inx.at[d], sx.at[d], rx.at[d], {"fsdp": 1 - f}
        )

    def keep(d):
        cc = lax.rem(c + d, n_c)
        return pltpu.make_async_copy(gattn.at[:, piece(f * n_c + cc, part)], own.at[d], lx.at[d])

    def line(d, to):
        return remote(outz.at[d], inz.at[d], sz.at[d], rz.at[d], {"ctx": to})

    router_copies = [
        remote(rpart, rin.at[i], rss.at[i], rsr.at[i], {"tp": peer})
        for i, peer in enumerate([sibling(t), opposite(t), opposite(sibling(t))])
    ]
    for copy in router_copies:
        copy.start()
    fetch = pltpu.make_async_copy(r_all.at[piece(c, rows), :], r_own, rs)
    fetch.start()
    for d in order:
        cross(d).start()
        keep(d).start()

    def part_of(cc, q):
        return dot_nt(dqkv[piece(cc, rows), :], wqkv[piece(q, quarter), :])

    total = reduce_seq(part_of, n_c, rest[:13])
    for d in order:
        cross(d).wait()
        keep(d).wait()
        both = own[d].astype(F32) + inx[d].astype(F32)
        if d:
            outz[d] = both.astype(BF)
            line(d, lax.rem(c + d, n_c)).start()
        else:
            mine = both
    fetch.wait()
    back, gain_part = norm_grad(
        hidden[...].astype(F32), r_own[:, :1], gain[...], total, width, *rest[13:17]
    )
    in_out[...] = mid_grad[...] + back

    gsend[0:1, :] = gain_part
    gsend[1:2, :] = gain2[0:1, :]
    gsend[2:, :] = jnp.zeros((6, quarter), F32)
    per = quarter // part
    holder = here // per
    def gain_copy(h, tt):
        b = t * per + h
        return remote(
            gsend.at[:, pl.ds(h * part, part)],
            gin.at[here],
            gs.at[h * n_t + tt],
            gr.at[here],
            {"fsdp": b // n_c, "ctx": lax.rem(b, n_c), "tp": jnp.int32(tt)},
        )

    def is_me(h, tt):
        return (t * per + h == here) & (t == tt)

    for h in range(per):
        for tt in range(n_t):

            @pl.when(jnp.logical_not(is_me(h, tt)))
            def _():
                gain_copy(h, tt).start()

    def put(src, block):
        at = piece(src, HD)
        for i, ref in enumerate((gq, gk, gv)):
            ref[:, at] = block[i * HD : (i + 1) * HD, :].T
        go[at, :] = block[3 * HD :, :]

    put(c, mine)
    for d in order[:-1]:
        line(d, c).wait()
        put(lax.rem(c - d + n_c, n_c), inz[d].astype(F32))
    for h in range(per):
        for tt in range(n_t):

            @pl.when(jnp.logical_not(is_me(h, tt)))
            def _():
                gain_copy(h, tt).wait_send()

    for b in range(n_f * n_c):

        @pl.when((b != here) | (holder != t))
        def _():
            remote(gin.at[b], gin.at[b], gs.at[0], gr.at[b], {"tp": sibling(t)}).wait_recv()

    own_part = jnp.where(
        holder == t,
        gsend[:, piece(lax.rem(here, per), part)],
        jnp.zeros((8, part), F32),
    )
    gains_out[...] = own_part + jnp.sum(gin[...], axis=0)
    for copy in router_copies:
        copy.wait()
    router_out[...] = rpart[...] + jnp.sum(rin[...], axis=0)


def last(n_c, n_f, n_t, dqkv, wqkv, hidden, r_all, gain, mid_grad, gain2, rpart, gattn):
    rows, quarter = hidden.shape
    width = quarter * n_t
    part = width // (n_f * n_c)
    sds = jax.ShapeDtypeStruct
    slab = pltpu.VMEM((n_c, 4 * HD, part), BF)
    return pl.pallas_call(
        functools.partial(last_kernel, n_c, n_f, n_t, width),
        out_shape=(
            sds((rows, quarter), F32),
            sds((part, n_c * HD), F32),
            sds((part, n_c * HD), F32),
            sds((part, n_c * HD), F32),
            sds((n_c * HD, part), F32),
            sds((8, part), F32),
            sds(rpart.shape, F32),
        ),
        in_specs=[VMEM, VMEM, VMEM, HBM, VMEM, VMEM, VMEM, VMEM, HBM],
        out_specs=[VMEM] * 7,
        scratch_shapes=[
            pltpu.VMEM((3,) + rpart.shape, F32),
            DMA((3,)),
            DMA((3,)),
            pltpu.VMEM((rows, HD), F32),
            slab,
            slab,
            slab,
            slab,
            slab,
            pltpu.VMEM((8, quarter), F32),
            pltpu.VMEM((n_f * n_c, 8, part), F32),
            DMA(()),
            DMA((n_c,)),
            DMA((n_c,)),
            DMA((n_c,)),
            DMA((n_c,)),
            DMA((n_c,)),
            DMA((quarter // part * n_t,)),
            DMA((n_f * n_c,)),
        ]
        + reduce_seq_scratch(n_c, rows, quarter)
        + norm_grad_scratch(rows),
        compiler_params=pltpu.CompilerParams(
            collective_id=4, has_side_effects=True, vmem_limit_bytes=BIG
        ),
        cost_estimate=pl.CostEstimate(flops=2 << 30, bytes_accessed=150 << 20, transcendentals=0),
        name="last",
    )(dqkv, wqkv, hidden, r_all, gain, mid_grad, gain2, rpart, gattn)


def per_device_seq(
    hidden_in,
    positions,
    chosen,
    out_grad,
    attn_gain,
    w_query,
    w_key,
    w_value,
    w_out,
    moe_gain,
    router,
    shared_gate,
    shared_up,
    shared_down,
    expert_gate,
    expert_up,
    expert_down,
):
    f_rank, c_rank, t_rank = ranks()
    n_f, n_c, n_t = (lax.axis_size(name) for name in ("fsdp", "ctx", "tp"))
    rows, quarter = hidden_in.shape
    width = quarter * n_t
    part = w_query.shape[0]
    seq = rows * n_c
    n_exp = router.shape[1]
    mine = n_exp // n_c // n_f
    ffe = expert_gate.shape[2]
    group = ("fsdp", "ctx")
    every = ("fsdp", "ctx", "tp")
    n_b = n_f * n_c
    own_shared = shared_gate.shape[1] // n_b
    srows = -(-own_shared // 16) * 16
    block = f_rank * n_c + c_rank
    f_arr = f_rank.astype(jnp.int32).reshape(1)
    swap = [(i, n_f - 1 - i) for i in range(n_f)]

    gate_t, up_t = expert_gate.swapaxes(1, 2), expert_up.swapaxes(1, 2)
    weights = (gate_t, up_t, expert_down)

    def swapped(weight):
        given = lax.dynamic_slice_in_dim(weight, (n_f - 1 - f_rank) * mine, mine, 0)
        return lax.ppermute(given, "fsdp", swap)

    got_down = swapped(expert_down)

    picked_own = jnp.sum(
        (chosen[:, :, None] == jnp.arange(n_exp)[None, None, :]).astype(F32), axis=1
    )
    small = [
        attn_gain.astype(F32)[None],
        moe_gain.astype(F32)[None],
        router.T.astype(F32),
        picked_own.T,
        positions.astype(F32)[None],
    ]
    small = jnp.concatenate(small, axis=0)
    small = jnp.pad(small, ((0, -small.shape[0] % 8), (0, 0)))
    hidden_seq, wqkv, wo, small_all = front(
        n_c, n_f, n_t, hidden_in, w_query, w_key, w_value, w_out, small
    )
    gain_one, gain_two = small_all[0:1], small_all[1:2]
    router_t = small_all[2 : 2 + n_exp].astype(BF)
    picked = small_all[2 + n_exp : 2 + 2 * n_exp].T
    pos_seq = lax.dynamic_slice(small_all, (2 + 2 * n_exp, f_rank * seq), (1, seq))[0]
    after = lambda x, y: lax.optimization_barrier((x, y))[0]
    got = (swapped(after(gate_t, hidden_seq)), swapped(after(up_t, hidden_seq)), got_down)
    grad_all = lax.all_gather(after(out_grad, hidden_seq), every, axis=0, tiled=False)
    grad_all = grad_all.reshape(n_b, n_t, rows, quarter)

    def shared_part(weight):
        return jnp.pad(
            weight.reshape(n_b, own_shared, part), ((0, 0), (0, srows - own_shared), (0, 0))
        )

    shared = jnp.concatenate(
        [shared_part(shared_gate.T), shared_part(shared_up.T), shared_part(shared_down)], axis=1
    )

    half = HD // 2
    inverse = 10000.0 ** (-jnp.arange(half, dtype=F32) * 2.0 / HD)
    angles = pos_seq[:, None] * inverse[None, :]
    cosine, sine = jnp.cos(angles), jnp.sin(angles)
    cosine = jnp.concatenate([cosine, cosine], axis=1)
    sine = jnp.concatenate([-sine, sine], axis=1)
    normed, q, k, v, heads_f, heads_b, lse, r_one = attend(hidden_seq, gain_one, wqkv, cosine, sine)
    resid_mid, resid_all, shared = mid(n_c, n_f, n_t, heads_b, wo, hidden_in, shared)

    sizes = (n_c, n_f, n_t, mine, ffe, srows)
    layer_out, moe_in, act, silu, slope, r_two, prob, kd, sd, shared_d = forward(
        *sizes, resid_all, grad_all, resid_mid, picked, gain_two, router_t, weights, got, shared
    )
    arrived_d = lax.ppermute(sd, "fsdp", swap)
    own_cols = lambda x: lax.dynamic_slice_in_dim(x, t_rank * quarter, quarter, 1)
    mid_grad, gain_two_part, mid_seq, shared_back, kg, ku, gg, gu = backward(
        *sizes, grad_all, act, silu, slope, moe_in, r_two, shared_d, prob, picked, router_t,
        resid_mid, own_cols(gain_two), out_grad, weights, got, shared,
    )
    n_gu = 2 * srows
    router_part = jnp.sum(shared_back[:, n_gu : n_gu + n_exp].astype(F32), axis=0)
    shared_back = jnp.concatenate([shared_back[:, :n_gu], shared_back[:, n_gu + n_exp :]], axis=1)
    shared_back = shared_back.reshape(n_b, 3, srows, part)[:, :, :own_shared].astype(F32)

    dqkv, gattn = attend_back(mid_seq, wo, q, k, v, heads_f, lse, cosine, sine, normed)
    input_grad, gq, gk, gv, go, gains, router_grad = last(
        n_c, n_f, n_t, dqkv, wqkv, hidden_in, r_one, own_cols(gain_one), mid_grad, gain_two_part,
        router_part, gattn,
    )
    eg, eu, ed = fill_experts(f_arr, (gg, gu, arrived_d), (kg, ku, kd))

    def shared_cols(i):
        return shared_back[:, i].reshape(n_b * own_shared, part)

    return (
        layer_out,
        input_grad,
        gains[0],
        gq,
        gk,
        gv,
        go,
        gains[1],
        router_grad.T,
        shared_cols(0).T,
        shared_cols(1).T,
        shared_cols(2),
        eg.swapaxes(1, 2),
        eu.swapaxes(1, 2),
        ed,
    )


def one_head_each(mesh, args):
    n_f, n_c, n_t = (mesh.shape[name] for name in ("fsdp", "ctx", "tp"))
    heads = args[5].shape[1] // HD
    experts = args[10].shape[1]
    return (
        n_f == 2
        and n_t == 4
        and heads == n_c * n_t
        and experts % (n_f * n_c) == 0
        and args[11].shape[1] % (8 * n_f * n_c * n_t) == 0
    )


def solution(mesh):
    placed = (
        P(("fsdp", "ctx"), "tp"),
        P(("fsdp", "ctx")),
        P(("fsdp", "ctx"), None),
        P(("fsdp", "ctx"), "tp"),
        P(("fsdp", "ctx")),
        P(("fsdp", "ctx"), "tp"),
        P(("fsdp", "ctx"), "tp"),
        P(("fsdp", "ctx"), "tp"),
        P("tp", ("fsdp", "ctx")),
        P(("fsdp", "ctx")),
        P(("fsdp", "ctx"), None),
        P(("fsdp", "ctx"), "tp"),
        P(("fsdp", "ctx"), "tp"),
        P("tp", ("fsdp", "ctx")),
        P("ctx", "fsdp", "tp"),
        P("ctx", "fsdp", "tp"),
        P("ctx", "tp", "fsdp"),
    )
    def run(*args):
        body = per_device_seq if one_head_each(mesh, args) else per_device
        return jax.shard_map(
        body,
        mesh=mesh,
        in_specs=placed,
        out_specs=(
            P(("fsdp", "ctx"), "tp"),
            P(("fsdp", "ctx"), "tp"),
            P(("fsdp", "ctx")),
            P(("fsdp", "ctx"), "tp"),
            P(("fsdp", "ctx"), "tp"),
            P(("fsdp", "ctx"), "tp"),
            P("tp", ("fsdp", "ctx")),
            P(("fsdp", "ctx")),
            P(("fsdp", "ctx"), None),
            P(("fsdp", "ctx"), "tp"),
            P(("fsdp", "ctx"), "tp"),
            P("tp", ("fsdp", "ctx")),
            P("ctx", "fsdp", "tp"),
            P("ctx", "fsdp", "tp"),
            P("ctx", "tp", "fsdp"),
        ),
        check_vma=False,
    )(*args)

    return run
```

```python
import functools

import jax
import jax.numpy as jnp
from jax import lax
from jax.experimental import pallas as pl
from jax.experimental.pallas import tpu as pltpu
from jax.sharding import PartitionSpec as P

HD = 128
TOPK = 6


EPS = 1e-06
NEG_BIG = -1e30


def as_sent(value):
    return jax.tree.map(lambda a: a.astype(jnp.bfloat16) if a.dtype == jnp.float32 else a, value)


def features(local_part):
    return lax.all_gather(local_part, "tp", axis=1, tiled=True)


def row_stats(partial_terms):
    return lax.psum(partial_terms, "tp")


def partial_sums(partial_terms):
    return jax.tree.map(
        lambda part: part.astype(jnp.float32),
        lax.psum_scatter(as_sent(partial_terms), "tp", scatter_dimension=1, tiled=True),
    )


def to_owners(slot_rows):
    return lax.all_to_all(slot_rows, "ctx", split_axis=0, concat_axis=2, tiled=True)


def to_sources(slot_rows):
    return lax.all_to_all(
        slot_rows.astype(jnp.bfloat16), "ctx", split_axis=2, concat_axis=0, tiled=True
    ).astype(slot_rows.dtype)


def rotary(values, positions, rotate_sign):
    half_dim = values.shape[-1] // 2
    inverse = 10000.0 ** (-jnp.arange(half_dim, dtype=jnp.float32) * 2.0 / values.shape[-1])
    angles = positions.astype(jnp.float32)[:, None] * inverse[None, :]
    cosine = jnp.cos(angles)[:, None, :]
    sine_val = rotate_sign * jnp.sin(angles)[:, None, :]
    lower_half = values[..., :half_dim]
    upper_half = values[..., half_dim:]
    return jnp.concatenate(
        [lower_half * cosine - upper_half * sine_val, upper_half * cosine + lower_half * sine_val],
        axis=-1,
    )


def norm_rows(values, gain_part, model_width):
    square_sum = row_stats(jnp.sum(values * values, axis=1))
    row_scale = lax.rsqrt(square_sum / model_width + EPS)
    return (values * row_scale[:, None] * gain_part[None, :], row_scale)


def norm_back(values, row_scale, gain_part, grad_normed, model_width, tp_rank):
    quarter = values.shape[1]
    local_sum = jnp.sum(grad_normed * gain_part[None, :] * values, axis=1)
    gain_local = jnp.sum(grad_normed * values * row_scale[:, None], axis=0)
    gain_whole = lax.dynamic_update_slice_in_dim(
        jnp.zeros((model_width,), jnp.float32), gain_local, tp_rank * quarter, 0
    )
    row_total, gain_grad = row_stats((local_sum, gain_whole))
    back = (
        row_scale[:, None] * gain_part[None, :] * grad_normed
        - values * (row_scale**3 * row_total / model_width)[:, None]
    )
    return (back, gain_grad)


def scatter_slots(assign_rows, flat_exp, slot_of, n_exp, capacity):
    buffer = jnp.zeros((n_exp, capacity, assign_rows.shape[1]), assign_rows.dtype)
    return buffer.at[flat_exp, slot_of].set(assign_rows)


def silu_grad(pre_act):
    sigmoid_val = jax.nn.sigmoid(pre_act)
    return sigmoid_val * (1.0 + pre_act * (1.0 - sigmoid_val))


def keep_state(carried):
    return carried


def per_device(
    hidden_in,
    positions,
    chosen,
    out_grad,
    attn_gain,
    w_query,
    w_key,
    w_value,
    w_out,
    moe_gain,
    router,
    shared_gate,
    shared_up,
    shared_down,
    expert_gate,
    expert_up,
    expert_down,
):
    tp_rank = lax.axis_index("tp")
    ctx_rank = lax.axis_index("ctx")
    n_ctx = lax.axis_size("ctx")
    tok_rows, quarter = hidden_in.shape
    model_width = quarter * lax.axis_size("tp")
    gain_one, wq_all, wk_all, wv_all, gain_two, router_all, gate_all, up_all, wo_all, down_all = (
        lax.all_gather(attn_gain, ("fsdp", "ctx"), axis=0, tiled=True),
        lax.all_gather(w_query, ("fsdp", "ctx"), axis=0, tiled=True),
        lax.all_gather(w_key, ("fsdp", "ctx"), axis=0, tiled=True),
        lax.all_gather(w_value, ("fsdp", "ctx"), axis=0, tiled=True),
        lax.all_gather(moe_gain, ("fsdp", "ctx"), axis=0, tiled=True),
        lax.all_gather(router, ("fsdp", "ctx"), axis=0, tiled=True),
        lax.all_gather(shared_gate, ("fsdp", "ctx"), axis=0, tiled=True),
        lax.all_gather(shared_up, ("fsdp", "ctx"), axis=0, tiled=True),
        lax.all_gather(w_out, ("fsdp", "ctx"), axis=1, tiled=True),
        lax.all_gather(shared_down, ("fsdp", "ctx"), axis=1, tiled=True),
    )
    expert_gate_weights, expert_up_weights, expert_down_weights = (
        lax.all_gather(expert_gate, "fsdp", axis=1, tiled=True),
        lax.all_gather(expert_up, "fsdp", axis=1, tiled=True),
        lax.all_gather(expert_down, "fsdp", axis=2, tiled=True),
    )
    gain_q1 = lax.dynamic_slice_in_dim(gain_one, tp_rank * quarter, quarter).astype(jnp.float32)
    gain_q2 = lax.dynamic_slice_in_dim(gain_two, tp_rank * quarter, quarter).astype(jnp.float32)
    router_rows = lax.dynamic_slice_in_dim(router_all, tp_rank * quarter, quarter, 0)
    head_count = wq_all.shape[1] // HD
    scale_att = HD ** (-0.5)
    resid_in = hidden_in.astype(jnp.float32)
    normed_one, scale_one = norm_rows(resid_in, gain_q1, model_width)
    normed_in = features(normed_one.astype(jnp.bfloat16))
    query_pre = jnp.dot(normed_in, wq_all, preferred_element_type=jnp.float32).reshape(
        tok_rows, head_count, HD
    )
    key_pre = jnp.dot(normed_in, wk_all, preferred_element_type=jnp.float32).reshape(
        tok_rows, head_count, HD
    )
    value_b = (
        jnp.dot(normed_in, wv_all, preferred_element_type=jnp.float32)
        .astype(jnp.bfloat16)
        .reshape(tok_rows, head_count, HD)
    )
    query_b = rotary(query_pre, positions, 1.0).astype(jnp.bfloat16)
    key_b = rotary(key_pre, positions, 1.0).astype(jnp.bfloat16)
    q_start = ctx_rank * tok_rows
    row_pos = q_start + jnp.arange(tok_rows)
    start_state = (
        jnp.full((tok_rows, head_count), NEG_BIG, jnp.float32),
        jnp.zeros((tok_rows, head_count), jnp.float32),
        jnp.zeros((tok_rows, head_count, HD), jnp.float32),
    )
    keys_blk = lax.all_gather(key_b, "ctx", axis=0, tiled=True)
    vals_blk = lax.all_gather(value_b, "ctx", axis=0, tiled=True)
    key_count = keys_blk.shape[0]

    def compute(state_in):
        run_max, run_sum, run_acc = state_in
        scores = (
            jnp.einsum("qhd,khd->qhk", query_b, keys_blk, preferred_element_type=jnp.float32)
            * scale_att
        )
        visible = jnp.arange(key_count)[None, :] <= row_pos[:, None]
        scores = jnp.where(visible[:, None, :], scores, NEG_BIG)
        new_max = jnp.maximum(run_max, jnp.max(scores, axis=2))
        weights = jnp.exp(scores - new_max[:, :, None])
        new_sum = jnp.sum(weights, axis=2)
        new_acc = jnp.einsum(
            "qhk,khd->qhd",
            weights.astype(jnp.bfloat16),
            vals_blk,
            preferred_element_type=jnp.float32,
        )
        return (new_max, new_sum, new_acc)

    run_max, run_sum, run_acc = lax.cond(
        jnp.int32(0) <= q_start + tok_rows - 1, compute, keep_state, start_state
    )
    heads_f = run_acc / run_sum[:, :, None]
    log_sum = run_max + jnp.log(run_sum)
    heads_b = heads_f.astype(jnp.bfloat16).reshape(tok_rows, head_count * HD)
    resid_mid = resid_in + partial_sums(
        jnp.dot(heads_b, wo_all, preferred_element_type=jnp.float32)
    )
    normed_two, scale_two = norm_rows(resid_mid, gain_q2, model_width)
    moe_part = normed_two.astype(jnp.bfloat16)
    moe_in = features(moe_part)
    n_exp = router_all.shape[1]
    exp_dev = n_exp // n_ctx
    capacity = min(tok_rows, 5 * TOPK * tok_rows // (3 * n_exp))
    logits = jnp.dot(moe_in, router_all, preferred_element_type=jnp.float32)
    probs_all = jax.nn.softmax(logits, axis=1)
    picked = (chosen[:, :, None] == jnp.arange(n_exp)[None, None, :]).astype(jnp.float32)
    gate_vals = jnp.sum(picked * probs_all[:, None, :], axis=2)
    shared_a = jnp.dot(moe_in, gate_all, preferred_element_type=jnp.float32)
    shared_b = jnp.dot(moe_in, up_all, preferred_element_type=jnp.float32)
    shared_act = (jax.nn.silu(shared_a) * shared_b).astype(jnp.bfloat16)
    shared_out = jnp.dot(shared_act, down_all, preferred_element_type=jnp.float32)
    flat_exp = chosen.reshape(-1)
    flat_hot = (flat_exp[:, None] == jnp.arange(n_exp)[None, :]).astype(jnp.int32)
    slot_of = jnp.sum((jnp.cumsum(flat_hot, axis=0) - flat_hot) * flat_hot, axis=1)
    token_of = jnp.arange(tok_rows * TOPK) // TOPK
    slot_count = n_ctx * capacity
    outgoing = scatter_slots(moe_in[token_of], flat_exp, slot_of, n_exp, capacity)
    received_rows = to_owners(outgoing.reshape(n_ctx, exp_dev, capacity, model_width)).reshape(
        exp_dev, slot_count, model_width
    )
    expert_a = jnp.einsum(
        "bmw,bwv->bmv", received_rows, expert_gate_weights, preferred_element_type=jnp.float32
    )
    expert_up_proj = jnp.einsum(
        "bmw,bwv->bmv", received_rows, expert_up_weights, preferred_element_type=jnp.float32
    )
    expert_act = (jax.nn.silu(expert_a) * expert_up_proj).astype(jnp.bfloat16)
    expert_out = jnp.einsum(
        "erf,efd->erd", expert_act, expert_down_weights, preferred_element_type=jnp.float32
    )
    returned = to_sources(expert_out.reshape(1, exp_dev, slot_count, model_width))
    shared_q, slot_q = partial_sums((shared_out, returned.reshape(n_exp * capacity, model_width)))
    slot_rows = slot_q.reshape(n_exp, capacity, quarter)[flat_exp, slot_of].reshape(
        tok_rows, TOPK, quarter
    )
    result = resid_mid + shared_q + jnp.sum(gate_vals[:, :, None] * slot_rows, axis=1)
    layer_out = result.astype(jnp.bfloat16)
    grad_out = out_grad.astype(jnp.float32)
    gate_grad = row_stats(jnp.sum(grad_out[:, None, :] * slot_rows, axis=2))
    prob_grad = jnp.sum(gate_grad[:, :, None] * picked, axis=1)
    logit_grad = (
        probs_all * (prob_grad - jnp.sum(probs_all * prob_grad, axis=1, keepdims=True))
    ).astype(jnp.bfloat16)
    router_grad = jnp.einsum("td,te->de", moe_in, logit_grad, preferred_element_type=jnp.float32)
    router_back_q = jnp.einsum(
        "te,de->td", logit_grad, router_rows, preferred_element_type=jnp.float32
    )
    grad_full = features(out_grad)
    shared_dact = jnp.einsum("td,fd->tf", grad_full, down_all, preferred_element_type=jnp.float32)
    shared_da = (shared_dact * shared_b * silu_grad(shared_a)).astype(jnp.bfloat16)
    shared_db = (shared_dact * jax.nn.silu(shared_a)).astype(jnp.bfloat16)
    shared_down_grad = jnp.einsum(
        "tf,td->fd", shared_act, grad_full, preferred_element_type=jnp.float32
    )
    shared_gate_grad = jnp.einsum(
        "td,tf->df", moe_in, shared_da, preferred_element_type=jnp.float32
    )
    shared_up_grad = jnp.einsum("td,tf->df", moe_in, shared_db, preferred_element_type=jnp.float32)
    shared_back = jnp.einsum(
        "tf,df->td", shared_da, gate_all, preferred_element_type=jnp.float32
    ) + jnp.einsum("tf,df->td", shared_db, up_all, preferred_element_type=jnp.float32)
    assign_grad = (
        (gate_vals[:, :, None] * grad_full[:, None, :])
        .astype(jnp.bfloat16)
        .reshape(tok_rows * TOPK, model_width)
    )
    grad_slots = scatter_slots(assign_grad, flat_exp, slot_of, n_exp, capacity)
    grad_arrived = to_owners(grad_slots.reshape(n_ctx, exp_dev, capacity, model_width)).reshape(
        exp_dev, slot_count, model_width
    )
    expert_dact = jnp.einsum(
        "erd,efd->erf", grad_arrived, expert_down_weights, preferred_element_type=jnp.float32
    )
    expert_da = (expert_dact * expert_up_proj * silu_grad(expert_a)).astype(jnp.bfloat16)
    expert_up_proj_grad = (expert_dact * jax.nn.silu(expert_a)).astype(jnp.bfloat16)
    edown_grad = jnp.einsum(
        "erf,erd->efd", expert_act, grad_arrived, preferred_element_type=jnp.float32
    )
    egate_grad = jnp.einsum(
        "qgo,qgz->qoz", received_rows, expert_da, preferred_element_type=jnp.float32
    )
    expert_up_weight_grad = jnp.einsum(
        "qgo,qgz->qoz", received_rows, expert_up_proj_grad, preferred_element_type=jnp.float32
    )
    expert_back = jnp.einsum(
        "iac,igc->iag", expert_da, expert_gate_weights, preferred_element_type=jnp.float32
    ) + jnp.einsum(
        "iac,igc->iag", expert_up_proj_grad, expert_up_weights, preferred_element_type=jnp.float32
    )
    back_slots = to_sources(expert_back.reshape(1, exp_dev, slot_count, model_width)).reshape(
        n_exp, capacity, model_width
    )
    token_back = jnp.sum(back_slots[flat_exp, slot_of].reshape(tok_rows, TOPK, model_width), axis=1)
    moe_back_q = partial_sums(shared_back + token_back)
    mid_back, gain_two_grad = norm_back(
        resid_mid, scale_two, gain_q2, moe_back_q + router_back_q, model_width, tp_rank
    )
    mid_grad = grad_out + mid_back
    branch_full = features(mid_grad.astype(jnp.bfloat16))
    wo_grad = jnp.einsum("tf,td->fd", heads_b, branch_full, preferred_element_type=jnp.float32)
    heads_grad = (
        jnp.einsum("td,fd->tf", branch_full, wo_all, preferred_element_type=jnp.float32)
        .astype(jnp.bfloat16)
        .reshape(tok_rows, head_count, HD)
    )
    row_delta = jnp.sum(heads_grad.astype(jnp.float32) * heads_f, axis=2)
    seq_len = tok_rows * n_ctx
    back_state = (
        jnp.zeros((tok_rows, head_count, HD), jnp.float32),
        jnp.zeros((seq_len, head_count, HD), jnp.float32),
        jnp.zeros((seq_len, head_count, HD), jnp.float32),
    )
    attend_keys_blk = lax.all_gather(key_b, "ctx", axis=0, tiled=True)
    attend_vals_blk = lax.all_gather(value_b, "ctx", axis=0, tiled=True)
    attend_key_count = attend_keys_blk.shape[0]

    def compute(state_in):
        scores = (
            jnp.einsum("qhd,khd->qhk", query_b, attend_keys_blk, preferred_element_type=jnp.float32)
            * scale_att
        )
        visible = jnp.arange(attend_key_count)[None, :] <= row_pos[:, None]
        probs_blk = jnp.where(visible[:, None, :], jnp.exp(scores - log_sum[:, :, None]), 0.0)
        value_part = jnp.einsum(
            "qhk,qhd->khd",
            probs_blk.astype(jnp.bfloat16),
            heads_grad,
            preferred_element_type=jnp.float32,
        )
        dot_grad = jnp.einsum(
            "qhd,khd->qhk", heads_grad, attend_vals_blk, preferred_element_type=jnp.float32
        )
        score_grad = (probs_blk * (dot_grad - row_delta[:, :, None])).astype(jnp.bfloat16)
        query_acc = (
            jnp.einsum(
                "qhk,khd->qhd", score_grad, attend_keys_blk, preferred_element_type=jnp.float32
            )
            * scale_att
        )
        key_part = (
            jnp.einsum("qhk,qhd->khd", score_grad, query_b, preferred_element_type=jnp.float32)
            * scale_att
        )
        return (query_acc, key_part, value_part)

    query_grad, key_grad_all, value_grad_all = lax.cond(
        jnp.int32(0) <= q_start + tok_rows - 1, compute, keep_state, back_state
    )
    key_grad, value_grad = (
        lax.psum_scatter(
            key_grad_all.astype(jnp.bfloat16), "ctx", scatter_dimension=0, tiled=True
        ).astype(jnp.float32),
        lax.psum_scatter(
            value_grad_all.astype(jnp.bfloat16), "ctx", scatter_dimension=0, tiled=True
        ).astype(jnp.float32),
    )
    query_pre_grad = (
        rotary(query_grad, positions, -1.0).astype(jnp.bfloat16).reshape(tok_rows, head_count * HD)
    )
    key_pre_grad = (
        rotary(key_grad, positions, -1.0).astype(jnp.bfloat16).reshape(tok_rows, head_count * HD)
    )
    value_pre_grad = value_grad.astype(jnp.bfloat16).reshape(tok_rows, head_count * HD)
    wq_grad = jnp.einsum("td,tf->df", normed_in, query_pre_grad, preferred_element_type=jnp.float32)
    wk_grad = jnp.einsum("td,tf->df", normed_in, key_pre_grad, preferred_element_type=jnp.float32)
    wv_grad = jnp.einsum("td,tf->df", normed_in, value_pre_grad, preferred_element_type=jnp.float32)
    in_back = jnp.einsum("tf,df->td", query_pre_grad, wq_all, preferred_element_type=jnp.float32)
    in_back = in_back + jnp.einsum(
        "tf,df->td", key_pre_grad, wk_all, preferred_element_type=jnp.float32
    )
    in_back = in_back + jnp.einsum(
        "tf,df->td", value_pre_grad, wv_all, preferred_element_type=jnp.float32
    )
    first_back, gain_one_grad = norm_back(
        resid_in, scale_one, gain_q1, partial_sums(in_back), model_width, tp_rank
    )
    input_grad = mid_grad + first_back
    dense = (
        lax.psum_scatter(
            gain_one_grad.astype(jnp.bfloat16), ("fsdp", "ctx"), scatter_dimension=0, tiled=True
        ).astype(jnp.float32),
        lax.psum_scatter(
            wq_grad.astype(jnp.bfloat16), ("fsdp", "ctx"), scatter_dimension=0, tiled=True
        ).astype(jnp.float32),
        lax.psum_scatter(
            wk_grad.astype(jnp.bfloat16), ("fsdp", "ctx"), scatter_dimension=0, tiled=True
        ).astype(jnp.float32),
        lax.psum_scatter(
            wv_grad.astype(jnp.bfloat16), ("fsdp", "ctx"), scatter_dimension=0, tiled=True
        ).astype(jnp.float32),
        lax.psum_scatter(
            gain_two_grad.astype(jnp.bfloat16), ("fsdp", "ctx"), scatter_dimension=0, tiled=True
        ).astype(jnp.float32),
        lax.psum_scatter(
            router_grad.astype(jnp.bfloat16), ("fsdp", "ctx"), scatter_dimension=0, tiled=True
        ).astype(jnp.float32),
        lax.psum_scatter(
            shared_gate_grad.astype(jnp.bfloat16), ("fsdp", "ctx"), scatter_dimension=0, tiled=True
        ).astype(jnp.float32),
        lax.psum_scatter(
            shared_up_grad.astype(jnp.bfloat16), ("fsdp", "ctx"), scatter_dimension=0, tiled=True
        ).astype(jnp.float32),
        lax.psum_scatter(
            wo_grad.astype(jnp.bfloat16), ("fsdp", "ctx"), scatter_dimension=1, tiled=True
        ).astype(jnp.float32),
        lax.psum_scatter(
            shared_down_grad.astype(jnp.bfloat16), ("fsdp", "ctx"), scatter_dimension=1, tiled=True
        ).astype(jnp.float32),
    )
    experts_done = (
        lax.psum_scatter(
            egate_grad.astype(jnp.bfloat16), "fsdp", scatter_dimension=1, tiled=True
        ).astype(jnp.float32),
        lax.psum_scatter(
            expert_up_weight_grad.astype(jnp.bfloat16), "fsdp", scatter_dimension=1, tiled=True
        ).astype(jnp.float32),
        lax.psum_scatter(
            edown_grad.astype(jnp.bfloat16), "fsdp", scatter_dimension=2, tiled=True
        ).astype(jnp.float32),
    )
    return (
        layer_out,
        input_grad,
        dense[0],
        dense[1],
        dense[2],
        dense[3],
        dense[8],
        dense[4],
        dense[5],
        dense[6],
        dense[7],
        dense[9],
        experts_done[0],
        experts_done[1],
        experts_done[2],
    )


MESH = pl.DeviceIdType.MESH
HBM = pl.BlockSpec(memory_space=pl.ANY)
VMEM = pl.BlockSpec(memory_space=pltpu.VMEM)
DMA = pltpu.SemaphoreType.DMA
BF, F32 = jnp.bfloat16, jnp.float32
BIG = 60 * 1024 * 1024


def dot_nt(left, right):
    return lax.dot_general(left, right, (((1,), (1,)), ((), ())), preferred_element_type=F32)


def dot_tn(left, right):
    return lax.dot_general(left, right, (((0,), (0,)), ((), ())), preferred_element_type=F32)


def dot_nn(left, right):
    return jnp.dot(left, right, preferred_element_type=F32)


def ranks():
    return lax.axis_index("fsdp"), lax.axis_index("ctx"), lax.axis_index("tp")


def sibling(t):
    return t + 1 - 2 * lax.rem(t, 2)


def opposite(t):
    return lax.rem(t + 2, 4)


def remote(src, dst, send, recv, to):
    return pltpu.make_async_remote_copy(
        src_ref=src, dst_ref=dst, send_sem=send, recv_sem=recv, device_id=to, device_id_type=MESH
    )


def greet(peers):
    barrier = pltpu.get_barrier_semaphore()
    for peer in peers:
        pl.semaphore_signal(barrier, inc=1, device_id=peer, device_id_type=MESH)
    pl.semaphore_wait(barrier, len(peers))


def line_peers(c, n_c):
    return [{"ctx": lax.rem(c + step, n_c)} for step in range(1, n_c)]


def piece(index, size):
    return pl.ds(pl.multiple_of(index * size, size), size)


def nearest(c, n_c, act):
    act(c)
    for step in range(1, n_c):
        for side in (-1, 1):
            place = c + side * step

            @pl.when((place >= 0) & (place < n_c))
            def _():
                act(place)


def spread_sems(n_c):
    return [
        DMA((n_c + 2,)),
        DMA((n_c,)),
        DMA((n_c,)),
        DMA((n_c,)),
        DMA((2 * n_c,)),
        DMA((2 * n_c,)),
        DMA((4 * n_c,)),
        DMA((4 * n_c,)),
        DMA(()),
    ]


class Spread:
    def __init__(self, own, place, n_c, both, sems):
        self.own, self.place, self.n_c, self.both = own, place, n_c, both
        self.zs, self.zr, self.xs, self.xr, self.ys, self.yr, self.ks, self.kr, self.ls = sems
        self.f, self.c, self.t = ranks()
        self.other_t = opposite(self.t)
        self.groups = ((self.f, 0), (1 - self.f, n_c))[: 2 if both else 1]

    def local(self):
        return pltpu.make_async_copy(self.own, self.place(self.f, self.c, self.t), self.ls)

    def far_copy(self, src, i, g, cc, col):
        return remote(src, self.place(g, cc, col), self.ys.at[i], self.yr.at[i], {"tp": self.other_t})

    def sib_copy(self, src, i, which, g, cc, col):
        at = 2 * i + which
        return remote(src, self.place(g, cc, col), self.ks.at[at], self.kr.at[at], {"tp": sibling(self.t)})

    def other_copy(self, src, g, cc):
        return remote(src, self.place(g, cc, self.t), self.xs.at[cc], self.xr.at[cc], {"fsdp": 1 - self.f})

    def line_copy(self, src, cc, sem, to):
        return remote(src, self.place(self.f, cc, self.t), self.zs.at[sem], self.zr.at[cc], {"ctx": to})

    def pass_on(self, src, i, g, cc):
        self.far_copy(src, i, g, cc, self.t).start()
        self.sib_copy(src, i, 0, g, cc, self.t).start()

    def start(self):
        self.local().start()
        n_c, c, own = self.n_c, self.c, self.own

        @pl.when(c < n_c - 1)
        def _():
            self.line_copy(own, c, n_c, c + 1).start()

        @pl.when(c > 0)
        def _():
            self.line_copy(own, c, n_c + 1, c - 1).start()

        if self.both:
            self.other_copy(own, self.f, c).start()
        self.pass_on(own, c, self.f, c)

    def each_other(self, act):
        for step in range(1, self.n_c):
            for side in (-1, 1):
                cc = self.c + side * step

                @pl.when((cc >= 0) & (cc < self.n_c))
                def _():
                    act(cc, self.c - side)

    def line(self):
        n_c = self.n_c

        def arrive(cc, onward):
            block = self.place(self.f, cc, self.t)
            self.line_copy(block, cc, cc, self.c).wait_recv()

            @pl.when((onward >= 0) & (onward < n_c))
            def _():
                self.line_copy(block, cc, cc, onward).start()

            if self.both:
                self.other_copy(block, self.f, cc).start()
            self.pass_on(block, cc, self.f, cc)

        self.each_other(arrive)

    def other(self):
        def arrive(cc):
            block = self.place(1 - self.f, cc, self.t)
            self.other_copy(block, 1 - self.f, cc).wait_recv()
            self.pass_on(block, self.n_c + cc, 1 - self.f, cc)

        nearest(self.c, self.n_c, arrive)

    def far(self, which):
        g, base = self.groups[which]

        def arrive(cc):
            i = base + cc
            block = self.place(g, cc, self.other_t)
            self.far_copy(block, i, g, cc, self.other_t).wait_recv()
            self.sib_copy(block, i, 1, g, cc, self.other_t).start()

        nearest(self.c, self.n_c, arrive)

    def arrived(self, which):
        g, base = self.groups[which]
        for cc in range(self.n_c):
            block = self.place(g, cc, self.t)
            for half in range(2):
                self.sib_copy(block, base + cc, half, g, cc, self.t).wait_recv()

    def finish(self):
        n_c, c, f, t, own = self.n_c, self.c, self.f, self.t, self.own
        for g, base in self.groups:
            for cc in range(n_c):
                block = self.place(g, cc, t)
                for half in range(2):
                    self.sib_copy(block, base + cc, half, g, cc, t).wait_send()
                self.far_copy(block, base + cc, g, cc, t).wait_send()
        if self.both:
            for cc in range(n_c):
                self.other_copy(self.place(f, cc, t), f, cc).wait_send()
        block = self.place(f, c, t)

        @pl.when(c < n_c - 1)
        def _():
            self.line_copy(block, c, n_c, c).wait_send()

        @pl.when(c > 0)
        def _():
            self.line_copy(block, c, n_c + 1, c).wait_send()

        def sent(cc, onward):
            @pl.when((onward >= 0) & (onward < n_c))
            def _():
                self.line_copy(block, cc, cc, c).wait_send()

        self.each_other(sent)


def to_each(src_of, dst, n_f, n_c, sems, act):
    send, recv, own = sems
    f, c, _ = ranks()
    here = f * n_c + c
    for df in range(n_f):
        for dc in range(n_c):
            i = df * n_c + dc
            if i == 0:
                copy = pltpu.make_async_copy(src_of(here), dst.at[here], own)
                copy.start() if act == "start" else copy.wait()
                continue
            to_f, to_c = lax.rem(f + df, n_f), lax.rem(c + dc, n_c)
            copy = remote(
                src_of(to_f * n_c + to_c), dst.at[here], send.at[i], recv.at[i], {"fsdp": to_f, "ctx": to_c}
            )
            copy.start() if act == "start" else copy.wait()


def each_peers(f, c, n_f, n_c):
    return [
        {"fsdp": lax.rem(f + df, n_f), "ctx": lax.rem(c + dc, n_c)}
        for df in range(n_f)
        for dc in range(n_c)
        if df or dc
    ]


def reduce_seq_scratch(n_c, rows, quarter):
    return [
        pltpu.VMEM((n_c, 2, rows, quarter), BF),
        pltpu.VMEM((n_c, 2, rows, quarter), BF),
        pltpu.VMEM((n_c, 2, rows, quarter), F32),
        pltpu.VMEM((n_c, rows, quarter), BF),
        pltpu.VMEM((n_c, rows, quarter), BF),
        pltpu.VMEM((n_c, rows, quarter), BF),
        pltpu.VMEM((n_c, rows, quarter), BF),
        DMA((n_c,)),
        DMA((n_c,)),
        DMA((n_c,)),
        DMA((n_c,)),
        DMA((n_c,)),
        DMA((n_c,)),
    ]


def reduce_seq(part_of, n_c, scratch, between=None, before_last=None):
    out1, in1, own, out2, in2, out3, in3, s1, r1, s2, r2, s3, r3 = scratch
    f, c, t = ranks()
    far, sib = opposite(t), sibling(t)
    to_sib, to_far = {"tp": sib}, {"tp": far}
    order = [2, 1, 3, 0] if n_c == 4 else list(range(1, n_c)) + [0]
    for d in order:
        cc = lax.rem(c + d, n_c)
        out1[d, 0] = part_of(cc, sib).astype(BF)
        out1[d, 1] = part_of(cc, opposite(sib)).astype(BF)
        remote(out1.at[d], in1.at[d], s1.at[d], r1.at[d], to_sib).start()
        own[d, 0] = part_of(cc, t)
        own[d, 1] = part_of(cc, far)
    if between is not None:
        between()
    for d in order:
        remote(out1.at[d], in1.at[d], s1.at[d], r1.at[d], to_sib).wait()
        out2[d] = (own[d, 1] + in1[d, 1].astype(F32)).astype(BF)
        remote(out2.at[d], in2.at[d], s2.at[d], r2.at[d], to_far).start()
    for d in order:
        remote(out2.at[d], in2.at[d], s2.at[d], r2.at[d], to_far).wait()
        total = own[d, 0] + in1[d, 0].astype(F32) + in2[d].astype(F32)
        if d:
            out3[d] = total.astype(BF)
            cc = lax.rem(c + d, n_c)
            remote(out3.at[d], in3.at[d], s3.at[d], r3.at[d], {"ctx": cc}).start()
    if before_last is not None:
        before_last()
    for d in order[:-1]:
        remote(out3.at[d], in3.at[d], s3.at[d], r3.at[d], {"ctx": c}).wait()
        total = total + in3[d].astype(F32)
    return total


def first_kernel(
    n_c, n_f, n_exp, mine, hidden, wq, wk, wv, wo, small, og, gate_t, up_t, down, shared, angle,
    normed, q_out, k_out, v_out, hf_out, lse_out, r_out, cos_out, sin_out, resid_out,
    wqkv_out, wo_out, small_out, all_out, og_out, shared_out, gg_out, gu_out, gd_out,
    seq, wqkv, wo_all, small_all, hb, blk, own_og,
    ws, wr, ls, xs, xr, ss, sr, sl, es, er, os, *scratch,
):
    f, c, t = ranks()
    rows, quarter = blk.shape
    part = wo.shape[1]
    tokens, width = seq.shape
    n_s = len(spread_sems(n_c))
    greet([{"tp": sibling(t)}, {"tp": opposite(t)}] + each_peers(f, c, n_f, n_c))
    seq_place = lambda g, cc, tt: seq.at[piece(cc, rows), piece(tt, quarter)]
    og_place = lambda g, cc, tt: og_out.at[g * n_c + cc, tt]
    all_place = lambda g, cc, tt: all_out.at[piece(g * n_c + cc, rows), piece(tt, quarter)]
    hid = Spread(hidden, seq_place, n_c, False, scratch[:n_s])
    grad = Spread(og, og_place, n_c, True, scratch[n_s : 2 * n_s])
    res = Spread(blk, all_place, n_c, True, scratch[2 * n_s : 3 * n_s])

    def targets(g, cc):
        block = piece(g * n_c + cc, part)
        return [wqkv.at[block, pl.ds(i * HD, HD)] for i in range(3)] + [
            wo_all.at[:, block],
            small_all.at[:, block],
        ]

    def sources(head):
        cols = piece(head, HD)
        return [wq.at[:, cols], wk.at[:, cols], wv.at[:, cols], wo.at[cols, :], small]

    def slabs(g, cc):
        block = piece(g * n_c + cc, part)
        return [wqkv.at[block, :], wo_all.at[:, block], small_all.at[:, block]]

    def across(step, g, cc):
        return [
            remote(slab, slab, xs.at[step, i], xr.at[step, i], {"fsdp": 1 - f})
            for i, slab in enumerate(slabs(g, cc))
        ]

    def swap(weight, out, k):
        return [
            remote(weight.at[(1 - f) * mine + e], out.at[e], es.at[k, e], er.at[k, e], {"fsdp": 1 - f})
            for e in range(mine)
        ]

    more = swap(down, gd_out, 2)
    for copy in more:
        copy.start()
    hid.start()
    for step in range(1, n_c):
        to = lax.rem(c + step, n_c)
        for i, (src, dst) in enumerate(zip(sources(to), targets(f, c))):
            remote(src, dst, ws.at[step, i], wr.at[step, i], {"ctx": to}).start()
    own = [
        pltpu.make_async_copy(src, dst, ls.at[i])
        for i, (src, dst) in enumerate(zip(sources(c), targets(f, c)))
    ]
    for copy in own:
        copy.start()
    for copy in own:
        copy.wait()
    for copy in across(0, f, c):
        copy.start()
    grad.start()
    hid.line()
    for step in range(1, n_c):
        cc = lax.rem(c - step + n_c, n_c)
        for i, dst in enumerate(targets(f, cc)):
            remote(dst, dst, ws.at[step, i], wr.at[step, i], {"ctx": cc}).wait_recv()
        for copy in across(step, f, cc):
            copy.start()
    grad.line()
    swaps = swap(gate_t, gg_out, 0) + swap(up_t, gu_out, 1)
    for copy in swaps:
        copy.start()
    hid.far(0)
    hid.arrived(0)
    hid.local().wait()
    for step in range(n_c):
        for copy in across(step, 1 - f, lax.rem(c - step + n_c, n_c)):
            copy.wait_recv()
    outs = [
        pltpu.make_async_copy(src, dst, os.at[i])
        for i, (src, dst) in enumerate(((wqkv, wqkv_out), (wo_all, wo_out), (small_all, small_out)))
    ]
    for copy in outs:
        copy.start()
    grad.other()

    scale_att = HD ** (-0.5)
    gain = small_all[0:1, :].astype(F32)
    place_row = 2 + 2 * n_exp
    for start in range(0, tokens, rows):
        at = pl.ds(start, rows)
        h = seq[at, :].astype(F32)
        r = lax.rsqrt(jnp.sum(h * h, axis=1, keepdims=True) / width + EPS)
        n = (h * r * gain).astype(BF)
        normed[at, :] = n
        r_out[at, :] = jnp.broadcast_to(r, (rows, HD))
        cols = pl.ds(pl.multiple_of(f * tokens + start, rows), rows)
        pos = small_all[place_row : place_row + 2, cols].astype(F32)
        pos = pos[0:1] * 64.0 + pos[1:2]
        turn = jnp.broadcast_to(pos, (HD, rows)).T * angle[0:1, :]
        cos, sin = jnp.cos(turn), jnp.sin(turn) * angle[1:2, :]
        cos_out[at, :] = cos
        sin_out[at, :] = sin
        qkv = dot_nn(n, wqkv[...])

        def rotate(values):
            return (values * cos + pltpu.roll(values, HD // 2, 1) * sin).astype(BF)

        q_out[at, :] = rotate(qkv[:, :HD])
        k_out[at, :] = rotate(qkv[:, HD : 2 * HD])
        v_out[at, :] = qkv[:, 2 * HD :].astype(BF)
    for start in range(0, tokens, rows):
        at = pl.ds(start, rows)
        seen = start + rows
        s = dot_nt(q_out[at, :], k_out[:seen, :]) * scale_att
        row = lax.broadcasted_iota(jnp.int32, (rows, seen), 0) + start
        col = lax.broadcasted_iota(jnp.int32, (rows, seen), 1)
        s = jnp.where(col <= row, s, NEG_BIG)
        top = jnp.max(s, axis=1, keepdims=True)
        e = jnp.exp(s - top)
        total = jnp.sum(e, axis=1, keepdims=True)
        out = dot_nn((e / total).astype(BF), v_out[:seen, :])
        hf_out[at, :] = out
        hb[at, :] = out.astype(BF)
        lse_out[at, :] = jnp.broadcast_to(top + jnp.log(total), (rows, HD))

    exchange = lambda act: to_each(lambda b: shared.at[b], shared_out, n_f, n_c, (ss, sr, sl), act)

    def part_of(cc, q):
        return dot_nn(hb[piece(cc, rows), :], wo_all[:, piece(q, quarter)])

    fetch = pltpu.make_async_copy(hidden, own_og, os.at[3])
    fetch.start()
    total = reduce_seq(part_of, n_c, scratch[3 * n_s :])
    fetch.wait()
    resid = own_og[...].astype(F32) + total
    resid_out[...] = resid
    blk[...] = resid.astype(BF)
    res.start()
    res.line()
    exchange("start")
    grad.far(0)
    grad.far(1)
    res.other()
    res.far(0)
    res.far(1)
    for which in range(2):
        grad.arrived(which)
        res.arrived(which)
    exchange("wait")
    for copy in swaps + more:
        copy.wait()
    for step in range(1, n_c):
        for i, (src, dst) in enumerate(zip(sources(c), targets(f, c))):
            remote(src, dst, ws.at[step, i], wr.at[step, i], {"ctx": c}).wait_send()
    for step in range(n_c):
        for copy in across(step, f, lax.rem(c - step + n_c, n_c)):
            copy.wait_send()
    for item in (hid, grad, res):
        item.finish()
    grad.local().wait()
    res.local().wait()
    for copy in outs:
        copy.wait()


def first(n_c, n_f, n_t, mine, hidden, wq, wk, wv, wo, small, og, weights, shared, angle):
    rows, quarter = hidden.shape
    width = quarter * n_t
    seq = rows * n_c
    n_exp = mine * n_f * n_c
    ffe, half = weights[0].shape[1:]
    sds = jax.ShapeDtypeStruct
    head, head_f = sds((seq, HD), BF), sds((seq, HD), F32)
    got = sds((mine, ffe, half), BF)
    return pl.pallas_call(
        functools.partial(first_kernel, n_c, n_f, n_exp, mine),
        out_shape=(
            sds((seq, width), BF),
            head,
            head,
            head,
            head_f,
            head_f,
            head_f,
            head_f,
            head_f,
            sds((rows, quarter), F32),
            sds((width, 3 * HD), BF),
            sds((HD, width), BF),
            sds((small.shape[0], width), BF),
            sds((seq * n_f, width), BF),
            sds((n_f * n_c, n_t, rows, quarter), BF),
            sds(shared.shape, BF),
            got,
            got,
            got,
        ),
        in_specs=[HBM] * 11 + [VMEM],
        out_specs=[VMEM] * 10 + [HBM] * 9,
        scratch_shapes=[
            pltpu.VMEM((seq, width), BF),
            pltpu.VMEM((width, 3 * HD), BF),
            pltpu.VMEM((HD, width), BF),
            pltpu.VMEM((small.shape[0], width), BF),
            pltpu.VMEM((seq, HD), BF),
            pltpu.VMEM((rows, quarter), BF),
            pltpu.VMEM((rows, quarter), BF),
            DMA((n_c, 5)),
            DMA((n_c, 5)),
            DMA((5,)),
            DMA((n_c, 3)),
            DMA((n_c, 3)),
            DMA((n_f * n_c,)),
            DMA((n_f * n_c,)),
            DMA(()),
            DMA((3, mine)),
            DMA((3, mine)),
            DMA((4,)),
        ]
        + spread_sems(n_c) * 3
        + reduce_seq_scratch(n_c, rows, quarter),
        compiler_params=pltpu.CompilerParams(
            collective_id=1, has_side_effects=True, vmem_limit_bytes=BIG
        ),
        cost_estimate=pl.CostEstimate(
            flops=5 << 30, bytes_accessed=300 << 20, transcendentals=1 << 20
        ),
        name="first",
    )(hidden, wq, wk, wv, wo, small, og, *weights, shared, angle)


def fetch_experts(n_c, n_f, mine, ffe, srows, hp, weights, shared, wgu, wd, sems):
    f = lax.axis_index("fsdp")
    wg0, wu0, wd0, wg1, wu1, wd1 = weights
    width = wd.shape[1]
    used = mine * ffe
    part = width // (n_f * n_c)
    half = width // n_f
    copies = []

    def add(src, dst):
        copies.append(pltpu.make_async_copy(src, dst, sems.at[len(copies)]))

    for i, (kept, got) in enumerate(((wg0, wg1), (wu0, wu1), (wd0, wd1))):
        dst, base = ((wgu, 0), (wgu, hp), (wd, 0))[i]
        for e in range(mine):
            at = pl.ds(base + e * ffe, ffe)
            add(kept.at[f * mine + e], dst.at[at, piece(f, half)])
            add(got.at[e], dst.at[at, piece(1 - f, half)])
        for b in range(n_f * n_c):
            add(
                shared.at[b, pl.ds(i * srows, srows), :],
                dst.at[pl.ds(base + used, srows), pl.ds(b * part, part)],
            )
    return copies


def blank_rows(rows_used, hp, wgu, wd):
    blank = jnp.zeros((hp - rows_used, wd.shape[1]), BF)
    wgu[rows_used:hp, :] = blank
    wgu[hp + rows_used :, :] = blank
    wd[rows_used:, :] = blank


def gates(prob, picked, first, mine, ffe, hp):
    block, n_exp = prob.shape
    lane = lax.broadcasted_iota(jnp.int32, (block, n_exp), 1)
    gated = prob * picked
    col = lax.broadcasted_iota(jnp.int32, (block, hp), 1)
    gate = jnp.ones((block, hp), F32)
    for k in range(mine):
        g = jnp.sum(jnp.where(lane == first + k, gated, 0.0), axis=1, keepdims=True)
        gate = jnp.where((col >= k * ffe) & (col < (k + 1) * ffe), g, gate)
    return gate, lane, col


def reducer_scratch(n_f, n_c, rows, quarter):
    n_b = n_f * n_c
    blocks = lambda *lead: pltpu.VMEM(lead + (rows, quarter), BF)
    return [
        blocks(n_b, 2),
        blocks(n_b, 2),
        blocks(n_b, 2),
        blocks(n_b),
        blocks(n_b),
        blocks(n_c),
        blocks(n_c),
        pltpu.VMEM((n_c, rows, quarter), F32),
        blocks(n_c),
        blocks(n_c),
    ] + [DMA((n_b,))] * 4 + [DMA((n_c,))] * 4


class Reducer:
    def __init__(self, n_c, scratch):
        self.n_c = n_c
        (self.out1, self.in1, self.own, self.out2, self.in2, self.out3, self.in3, self.acc,
         self.out4, self.in4, self.s1, self.r1, self.s2, self.r2, self.s3, self.r3, self.s4, self.r4) = scratch
        self.f, self.c, self.t = ranks()
        self.far, self.sib = opposite(self.t), sibling(self.t)

    def row_block(self, i):
        n_c = self.n_c
        group = jnp.where(i < n_c, 1 - self.f, self.f)
        return group * n_c + lax.rem(self.c + lax.rem(i, n_c) + 1, n_c)

    def core_copy(self, i):
        return remote(self.out1.at[i], self.in1.at[i], self.s1.at[i], self.r1.at[i], {"tp": self.sib})

    def far_copy(self, i):
        return remote(self.out2.at[i], self.in2.at[i], self.s2.at[i], self.r2.at[i], {"tp": self.far})

    def other_copy(self, j):
        return remote(self.out3.at[j], self.in3.at[j], self.s3.at[j], self.r3.at[j], {"fsdp": 1 - self.f})

    def line_copy(self, j, to):
        return remote(self.out4.at[j], self.in4.at[j], self.s4.at[j], self.r4.at[j], {"ctx": to})

    def put(self, i, part_of):
        self.out1[i, 0] = part_of(opposite(self.sib)).astype(BF)
        self.out1[i, 1] = part_of(self.sib).astype(BF)
        self.core_copy(i).start()
        self.own[i, 0] = part_of(self.far).astype(BF)
        self.own[i, 1] = part_of(self.t).astype(BF)

    def over(self, i):
        self.core_copy(i).wait()
        self.out2[i] = (self.own[i, 0].astype(F32) + self.in1[i, 0].astype(F32)).astype(BF)
        self.far_copy(i).start()

    def _sum(self, i):
        self.far_copy(i).wait()
        return self.own[i, 1].astype(F32) + self.in1[i, 1].astype(F32) + self.in2[i].astype(F32)

    def after_other(self, i):
        self.out3[i] = self._sum(i).astype(BF)
        self.other_copy(i).start()

    def after_own(self, i):
        self.acc[i - self.n_c] = self._sum(i)

    def along(self, j):
        self.other_copy(j).wait()
        total = self.acc[j] + self.in3[j].astype(F32)
        if j < self.n_c - 1:
            self.out4[j] = total.astype(BF)
            self.line_copy(j, lax.rem(self.c + j + 1, self.n_c)).start()
        return total

    def total(self, total):
        for j in range(self.n_c - 1):
            self.line_copy(j, self.c).wait()
            total = total + self.in4[j].astype(F32)
        return total

    def loop(self, n_b, compute):
        n_c = self.n_c

        def step(i, carry):
            def between():
                @pl.when(i >= 1)
                def _():
                    self.over(i - 1)

                @pl.when((i >= 3) & (i < 3 + n_c))
                def _():
                    self.after_other(i - 3)

                @pl.when(i >= 3 + n_c)
                def _():
                    self.after_own(i - 3)

            compute(i, between)
            return carry

        lax.fori_loop(0, n_b, step, 0)

    def drain(self, n_b, works):
        works = list(works)
        self.over(n_b - 1)
        for i in range(n_b - 4, n_b):
            if i > n_b - 4:
                self.after_own(i) if i >= self.n_c else self.after_other(i)
            if i >= self.n_c:
                total = self.along(i - self.n_c)
            if works:
                works.pop(0)()
        for work in works:
            work()
        return self.total(total)


def forward_kernel(
    n_c, n_f, mine, ffe, srows, hp, rows_all, og_all, resid, picked, gain, router,
    wg0, wu0, wd0, wg1, wu1, wd1, shared,
    layer_out, in_out, act_out, silu_out, slope_out, r_out, prob_out, keep_out, send_out, shared_out,
    gt, wsem, xsem, nsem, asem, tsem, osem, *scratch,
):
    f, c, t = ranks()
    n_b = n_f * n_c
    rows, quarter = resid.shape
    width = rows_all.shape[1]
    routed = mine * ffe
    rows_used = routed + srows
    red = Reducer(n_c, scratch)

    def blocks_phase(wgu, wd, xs, ns, acts):
        fetches = fetch_experts(
            n_c, n_f, mine, ffe, srows, hp, (wg0, wu0, wd0, wg1, wu1, wd1), shared, wgu, wd, wsem
        )
        for copy in fetches:
            copy.start()

        def load(i, slot):
            return pltpu.make_async_copy(
                rows_all.at[piece(red.row_block(i), rows), :], xs.at[slot], xsem.at[slot]
            )

        def stores(i, slot):
            at = piece(red.row_block(i), rows)
            return [pltpu.make_async_copy(ns.at[slot], in_out.at[at, :], nsem.at[slot])] + [
                pltpu.make_async_copy(acts.at[slot, k], out.at[at, :], asem.at[slot, k])
                for k, out in enumerate((act_out, silu_out, slope_out))
            ]

        load(0, 0).start()
        blank_rows(rows_used, hp, wgu, wd)
        greet([{"tp": red.sib}, {"tp": red.far}, {"fsdp": 1 - f}] + line_peers(c, n_c))
        for copy in fetches:
            copy.wait()

        def compute(i, between):
            slot = lax.rem(i, 2)
            b = red.row_block(i)
            at = piece(b, rows)
            load(i, slot).wait()

            @pl.when(i + 1 < n_b)
            def _():
                load(i + 1, 1 - slot).start()

            @pl.when(i >= 2)
            def _():
                for copy in stores(i - 2, slot):
                    copy.wait()

            h = xs[slot].astype(F32)
            r = lax.rsqrt(jnp.sum(h * h, axis=1, keepdims=True) / width + EPS)
            r_out[at, :] = jnp.broadcast_to(r, (rows, HD))
            n = (h * r * gain[...]).astype(BF)
            ns[slot] = n
            logits = dot_nt(n, router[...])
            e = jnp.exp(logits - jnp.max(logits, axis=1, keepdims=True))
            prob = e / jnp.sum(e, axis=1, keepdims=True)
            prob_out[at, :] = prob
            gate, _, _ = gates(prob, picked[at, :], (c * n_f + f) * mine, mine, ffe, hp)
            ab = dot_nt(n, wgu[...])
            between()
            a, up = ab[:, :hp], ab[:, hp:]
            sig = 1.0 / (1.0 + jnp.exp(-a))
            silu = a * sig
            act = (silu * up).astype(BF)
            acts[slot, 0] = act
            acts[slot, 1] = silu.astype(BF)
            acts[slot, 2] = (up * (sig * (1.0 + a * (1.0 - sig)))).astype(BF)
            actg = (act.astype(F32) * gate).astype(BF)
            gt[:, at] = actg.T[:rows_used, :]
            for copy in stores(i, slot):
                copy.start()
            red.put(i, lambda q: dot_nn(actg, wd[:, piece(q, quarter)]))

        red.loop(n_b, compute)
        for i in range(n_b - 2, n_b):
            for copy in stores(i, i % 2):
                copy.wait()

    pl.run_scoped(
        blocks_phase,
        pltpu.VMEM((2 * hp, width), BF),
        pltpu.VMEM((hp, width), BF),
        pltpu.VMEM((2, rows, width), BF),
        pltpu.VMEM((2, rows, width), BF),
        pltpu.VMEM((2, 3, rows, hp), BF),
    )

    def grads_phase(tiles, keeps, sends, shs):
        def tile_of(s):
            return (1 - f) * 2 + s if s < 2 else f * 2 + s - 2

        def tile_load(s):
            return pltpu.make_async_copy(og_all.at[:, tile_of(s)], tiles.at[s % 2], tsem.at[s % 2])

        def out_copies(s):
            cols = pl.ds(s % 2 * quarter, quarter)
            if s < 2:
                src, dst = sends.at[s], send_out.at[:, :, cols]
            else:
                src, dst = keeps.at[s - 2], keep_out.at[:, :, cols]
            return [
                pltpu.make_async_copy(src, dst, osem.at[s, 0]),
                pltpu.make_async_copy(
                    shs.at[s], shared_out.at[:, piece(tile_of(s), quarter)], osem.at[s, 1]
                ),
            ]

        def work(s):
            def run():
                tile_load(s).wait()
                if s < 3:
                    tile_load(s + 1).start()
                g = dot_nn(gt[...], tiles[s % 2].reshape(n_b * rows, quarter))
                if s < 2:
                    sends[s] = g[:routed].astype(BF).reshape(mine, ffe, quarter)
                else:
                    keeps[s - 2] = g[:routed].reshape(mine, ffe, quarter)
                shs[s] = g[routed:].astype(BF)
                for copy in out_copies(s):
                    copy.start()

            return run

        tile_load(0).start()
        total = red.drain(n_b, [work(s) for s in range(4)])
        layer_out[...] = (resid[...] + total).astype(BF)
        for s in range(4):
            for copy in out_copies(s):
                copy.wait()

    pl.run_scoped(
        grads_phase,
        pltpu.VMEM((2, n_b, rows, quarter), BF),
        pltpu.VMEM((2, mine, ffe, quarter), F32),
        pltpu.VMEM((2, mine, ffe, quarter), BF),
        pltpu.VMEM((4, srows, quarter), BF),
    )


def expert_sizes(n_c, n_f, n_t, mine, ffe, srows, width):
    used = mine * ffe + srows
    return used, -(-used // HD) * HD, 3 * (2 * mine + n_f * n_c)


def forward(n_c, n_f, n_t, mine, ffe, srows, rows_all, og_all, resid, picked, gain, router, kept, got, shared):
    total, width = rows_all.shape
    rows, quarter = resid.shape
    n_exp = router.shape[0]
    n_b = n_f * n_c
    used, hp, n_fetch = expert_sizes(n_c, n_f, n_t, mine, ffe, srows, width)
    sds = jax.ShapeDtypeStruct
    return pl.pallas_call(
        functools.partial(forward_kernel, n_c, n_f, mine, ffe, srows, hp),
        out_shape=(
            sds((rows, quarter), BF),
            sds((total, width), BF),
            sds((total, hp), BF),
            sds((total, hp), BF),
            sds((total, hp), BF),
            sds((total, HD), F32),
            sds((total, n_exp), F32),
            sds((mine, ffe, width // n_f), F32),
            sds((mine, ffe, width // n_f), BF),
            sds((srows, width), BF),
        ),
        in_specs=[HBM, HBM, VMEM, VMEM, VMEM, VMEM] + [HBM] * 7,
        out_specs=[VMEM, HBM, HBM, HBM, HBM, VMEM, VMEM, HBM, HBM, HBM],
        scratch_shapes=[
            pltpu.VMEM((used, total), BF),
            DMA((n_fetch,)),
            DMA((2,)),
            DMA((2,)),
            DMA((2, 3)),
            DMA((2,)),
            DMA((4, 2)),
        ]
        + reducer_scratch(n_f, n_c, rows, quarter),
        compiler_params=pltpu.CompilerParams(
            collective_id=5, has_side_effects=True, vmem_limit_bytes=BIG
        ),
        cost_estimate=pl.CostEstimate(
            flops=8 * total * width * used, bytes_accessed=80 << 20, transcendentals=total * used
        ),
        name="forward",
    )(rows_all, og_all, resid, picked, gain, router, *kept, *got, shared)


def backward_kernel(
    n_c, n_f, mine, ffe, srows, hp, og_all, act, silu, slope, moe_in, r_all, shared_d, prob_in, picked, router,
    resid, gain, og, wg0, wu0, wd0, wg1, wu1, wd1, shared,
    mid_out, gain_out, seq_out, shared_out, kg_out, ku_out, gg_out, gu_out, lg_out, lu_out,
    gt, blk, r_own, sends, shs, wsem, xsem, tsem, ksem, ss, sr, rs, es, er, el, ds, dr, dl, *rest,
):
    f, c, t = ranks()
    n_b = n_f * n_c
    rows, quarter = resid.shape
    width = shared_d.shape[1]
    n_exp = router.shape[0]
    routed = mine * ffe
    rows_used = routed + srows
    first = (c * n_f + f) * mine
    red = Reducer(n_c, rest[:18])

    cols = width // n_b
    n_gu = shs.shape[0]

    def exchange(act, which):
        src, at, sems = (
            (shs, pl.ds(0, n_gu), (es, er, el)),
            (shared_d, pl.ds(n_gu, srows), (ds, dr, dl)),
        )[which]
        to_each(lambda b: src.at[:, piece(b, cols)], shared_out.at[:, at, :], n_f, n_c, sems, act)

    def blocks_phase(wgu, wd, ogs, acts):
        fetches = fetch_experts(
            n_c, n_f, mine, ffe, srows, hp, (wg0, wu0, wd0, wg1, wu1, wd1), shared, wgu, wd, wsem
        )
        for copy in fetches:
            copy.start()

        def loads(i, slot):
            b = red.row_block(i)
            return [
                pltpu.make_async_copy(
                    og_all.at[b, q], ogs.at[slot, :, pl.ds(q * quarter, quarter)], xsem.at[slot, q]
                )
                for q in range(4)
            ] + [
                pltpu.make_async_copy(src.at[piece(b, rows), :], acts.at[slot, k], xsem.at[slot, 4 + k])
                for k, src in enumerate((act, silu, slope))
            ]

        for copy in loads(0, 0):
            copy.start()
        blank_rows(rows_used, hp, wgu, wd)
        greet([{"tp": red.sib}, {"tp": red.far}, {"tp": opposite(red.sib)}] + each_peers(f, c, n_f, n_c))
        exchange("start", 1)
        for copy in fetches:
            copy.wait()

        def compute(i, between):
            slot = lax.rem(i, 2)
            at = piece(red.row_block(i), rows)
            for copy in loads(i, slot):
                copy.wait()

            @pl.when(i + 1 < n_b)
            def _():
                for copy in loads(i + 1, 1 - slot):
                    copy.start()

            prob = prob_in[at, :]
            chosen = picked[at, :]
            gate, lane, col = gates(prob, chosen, first, mine, ffe, hp)
            dh = dot_nt(ogs[slot], wd[...])
            between()
            ad = acts[slot, 0].astype(F32) * dh
            p_grad = jnp.zeros(prob.shape, F32)
            for k in range(mine):
                s = jnp.sum(
                    jnp.where((col >= k * ffe) & (col < (k + 1) * ffe), ad, 0.0), axis=1, keepdims=True
                )
                p_grad = jnp.where(lane == first + k, s, p_grad)
            p_grad = p_grad * chosen
            logit_f = prob * (p_grad - jnp.sum(prob * p_grad, axis=1, keepdims=True))
            logit_grad = logit_f.astype(BF)
            dg = dh * gate
            da = (dg * acts[slot, 2].astype(F32)).astype(BF)
            db = (dg * acts[slot, 1].astype(F32)).astype(BF)
            gt[:rows_used, at] = da.T[:rows_used, :]
            gt[rows_used : 2 * rows_used, at] = db.T[:rows_used, :]
            gt[2 * rows_used :, at] = logit_f.T.astype(BF)
            dab = jnp.concatenate([da, db], axis=1)

            def part_of(q):
                cols = piece(q, quarter)
                return dot_nn(dab, wgu[:, cols]) + dot_nn(logit_grad, router[:, cols])

            red.put(i, part_of)

        red.loop(n_b, compute)

    pl.run_scoped(
        blocks_phase,
        pltpu.VMEM((2 * hp, width), BF),
        pltpu.VMEM((hp, width), BF),
        pltpu.VMEM((2, rows, width), BF),
        pltpu.VMEM((2, 3, rows, hp), BF),
    )

    def send_copy(s, m):
        if s:
            return pltpu.make_async_copy(sends.at[s, m], (lg_out, lu_out)[m], ss.at[s, m])
        return remote(sends.at[s, m], (gg_out, gu_out)[m], ss.at[s, m], sr.at[m], {"fsdp": 1 - f})

    def grads_phase(tiles, keeps):
        def tile_of(s):
            return (1 - f) * 2 + s if s < 2 else f * 2 + s - 2

        def tile_load(s):
            return pltpu.make_async_copy(
                moe_in.at[:, piece(tile_of(s), quarter)], tiles.at[s % 2], tsem.at[s % 2]
            )

        def keep_copy(s, m):
            dst = (kg_out, ku_out)[m].at[:, :, pl.ds((s - 2) * quarter, quarter)]
            return pltpu.make_async_copy(keeps.at[s - 2, m], dst, ksem.at[s - 2, m])

        def work(s):
            def run():
                tile_load(s).wait()
                if s < 3:
                    tile_load(s + 1).start()
                g = dot_nn(gt[...], tiles[s % 2])
                cols = piece(tile_of(s), quarter)
                for m in range(2):
                    base = m * rows_used
                    if s < 2:
                        sends[s, m] = g[base : base + routed].astype(BF).reshape(mine, ffe, quarter)
                        send_copy(s, m).start()
                    else:
                        keeps[s - 2, m] = g[base : base + routed].reshape(mine, ffe, quarter)
                        keep_copy(s, m).start()
                    shs[m * srows : (m + 1) * srows, cols] = g[base + routed : base + rows_used].astype(BF)
                shs[2 * srows :, cols] = g[2 * rows_used :].astype(BF)

            return run

        tile_load(0).start()
        blk[...] = red.drain(n_b, [work(s) for s in range(4)])
        for s in (2, 3):
            for m in range(2):
                keep_copy(s, m).wait()

    fetch = pltpu.make_async_copy(r_all.at[piece(f * n_c + c, rows), :], r_own, rs)
    fetch.start()
    pl.run_scoped(
        grads_phase,
        pltpu.VMEM((2, n_b * rows, quarter), BF),
        pltpu.VMEM((2, 2, mine, ffe, quarter), F32),
    )
    fetch.wait()
    back, gain_part = norm_grad(resid[...], r_own[:, :1], gain[...], blk[...], width, *rest[18:22])
    gain_out[...] = jnp.broadcast_to(gain_part, gain_out.shape)
    grad = og[...].astype(F32) + back
    mid_out[...] = grad
    own = rest[22]
    own[...] = grad.astype(BF)

    def place(g, cc, tt):
        return seq_out.at[piece(cc, rows), piece(tt, quarter)]

    sequence = Spread(own, place, n_c, False, rest[23:])
    sequence.start()
    sequence.line()
    exchange("start", 0)
    sequence.far(0)
    sequence.arrived(0)
    sequence.finish()
    sequence.local().wait()
    exchange("wait", 0)
    exchange("wait", 1)
    for s in range(2):
        for m in range(2):
            send_copy(s, m).wait()


def backward(
    n_c, n_f, n_t, mine, ffe, srows, og_all, act, silu, slope, moe_in, r_all, shared_d, prob, picked, router,
    resid, gain, og, kept, got, shared,
):
    total, width = moe_in.shape
    rows, quarter = resid.shape
    n_exp = router.shape[0]
    n_b = n_f * n_c
    used, hp, n_fetch = expert_sizes(n_c, n_f, n_t, mine, ffe, srows, width)
    sds = jax.ShapeDtypeStruct
    kept_g = sds((mine, ffe, width // n_f), F32)
    sent_g = sds((mine, ffe, quarter), BF)
    return pl.pallas_call(
        functools.partial(backward_kernel, n_c, n_f, mine, ffe, srows, hp),
        out_shape=(
            sds((rows, quarter), F32),
            sds((8, quarter), F32),
            sds((rows * n_c, width), BF),
            sds((n_b, 3 * srows + n_exp, width // n_b), BF),
            kept_g,
            kept_g,
            sent_g,
            sent_g,
            sent_g,
            sent_g,
        ),
        in_specs=[HBM] * 7 + [VMEM] * 6 + [HBM] * 7,
        out_specs=[VMEM, VMEM] + [HBM] * 8,
        scratch_shapes=[
            pltpu.VMEM((2 * used + n_exp, total), BF),
            pltpu.VMEM((rows, quarter), F32),
            pltpu.VMEM((rows, HD), F32),
            pltpu.VMEM((2, 2, mine, ffe, quarter), BF),
            pltpu.VMEM((2 * srows + n_exp, width), BF),
            DMA((n_fetch,)),
            DMA((2, 7)),
            DMA((2,)),
            DMA((2, 2)),
            DMA((2, 2)),
            DMA((2,)),
            DMA(()),
            DMA((n_b,)),
            DMA((n_b,)),
            DMA(()),
            DMA((n_b,)),
            DMA((n_b,)),
            DMA(()),
        ]
        + reducer_scratch(n_f, n_c, rows, quarter)
        + norm_grad_scratch(rows)
        + [pltpu.VMEM((rows, quarter), BF)]
        + spread_sems(n_c),
        compiler_params=pltpu.CompilerParams(
            collective_id=3, has_side_effects=True, vmem_limit_bytes=BIG
        ),
        cost_estimate=pl.CostEstimate(
            flops=10 * total * width * used, bytes_accessed=200 << 20, transcendentals=0
        ),
        name="backward",
    )(
        og_all, act, silu, slope, moe_in, r_all, shared_d, prob, picked, router, resid, gain, og,
        *kept, *got, shared,
    )


def fill_kernel(f_ref, ga, gb, ua, ub, d, kg, ku, kd, og, ou, od):
    step = pl.program_id(0)
    f = f_ref[0]
    n_e = kg.shape[0]

    def put(own, at):
        for keep, out in ((kg, og), (ku, ou), (kd, od)):
            out[at : at + n_e] = keep[...]
        for out, halves in ((og, (ga, gb)), (ou, (ua, ub))):
            @pl.when(step < 2)
            def _():
                out[n_e - at : 2 * n_e - at] = halves[0][...].astype(F32)

            @pl.when(step >= 2)
            def _():
                out[n_e - at : 2 * n_e - at] = halves[1][...].astype(F32)

        od[n_e - at : 2 * n_e - at] = d[...].astype(F32)

    @pl.when(f == 0)
    def _():
        put(0, 0)

    @pl.when(f != 0)
    def _():
        put(1, n_e)


def fill_experts(f_rank, arrived, kept):
    mine, ffe, quarter = arrived[0].shape
    half = kept[0].shape[2]
    tile = half // 4
    first = pl.BlockSpec((mine, ffe, tile), lambda i, f: (0, 0, jnp.minimum(i, 1)))
    second = pl.BlockSpec((mine, ffe, tile), lambda i, f: (0, 0, jnp.maximum(i - 2, 0)))
    every = pl.BlockSpec((mine, ffe, tile), lambda i, f: (0, 0, i))
    out = pl.BlockSpec((2 * mine, ffe, tile), lambda i, f: (0, 0, i))
    return pl.pallas_call(
        fill_kernel,
        grid_spec=pltpu.PrefetchScalarGridSpec(
            num_scalar_prefetch=1,
            grid=(4,),
            in_specs=[first, second, first, second, every] + [every] * 3,
            out_specs=[out] * 3,
        ),
        out_shape=tuple(jax.ShapeDtypeStruct((2 * mine, ffe, half), F32) for k in kept),
        compiler_params=pltpu.CompilerParams(vmem_limit_bytes=BIG),
        name="fill_experts",
    )(f_rank, *arrived, *kept)


def norm_grad(values, r, gain, grad, width, out, into, send, recv):
    f, c, t = ranks()
    rows = values.shape[0]
    local = jnp.sum(grad * gain * values, axis=1, keepdims=True)
    out[...] = jnp.broadcast_to(local, (rows, HD)).T[:8, :]
    peers = [sibling(t), opposite(t), opposite(sibling(t))]
    copies = [
        remote(out, into.at[i], send.at[i], recv.at[i], {"tp": peer}) for i, peer in enumerate(peers)
    ]
    for copy in copies:
        copy.start()
    gain_part = jnp.sum(grad * values * r, axis=0, keepdims=True)
    total = out[...]
    for i, copy in enumerate(copies):
        copy.wait()
        total = total + into[i]
    total = jnp.broadcast_to(total[0:1, :], (HD, rows)).T[:, :1]
    return r * gain * grad - values * (r * r * r * (total / width)), gain_part


def norm_grad_scratch(rows):
    return [
        pltpu.VMEM((8, rows), F32),
        pltpu.VMEM((3, 8, rows), F32),
        DMA((3,)),
        DMA((3,)),
    ]


def attend_back_kernel(
    block, mid, wo, q, k, v, hf, lse, cosine, sine, normed, dqkv, gattn, hg, dq, dk, dv
):
    seq = mid.shape[0]
    scale_att = HD ** (-0.5)
    for start in range(0, seq, block):
        at = pl.ds(start, block)
        hg[at, :] = dot_nt(mid[at, :], wo[...]).astype(BF)
    dk[...] = jnp.zeros_like(dk)
    dv[...] = jnp.zeros_like(dv)
    for start in range(0, seq, block):
        at = pl.ds(start, block)
        seen = start + block
        qb, hb = q[at, :], hg[at, :]
        delta = jnp.sum(hb.astype(F32) * hf[at, :], axis=1, keepdims=True)
        s = dot_nt(qb, k[:seen, :]) * scale_att
        row = lax.broadcasted_iota(jnp.int32, (block, seen), 0) + start
        col = lax.broadcasted_iota(jnp.int32, (block, seen), 1)
        p = jnp.where(col <= row, jnp.exp(s - lse[at, :1]), 0.0)
        ds = (p * (dot_nt(hb, v[:seen, :]) - delta)).astype(BF)
        dq[at, :] = dot_nn(ds, k[:seen, :]) * scale_att
        dk[:seen, :] += dot_tn(ds, qb) * scale_att
        dv[:seen, :] += dot_tn(p.astype(BF), hb)

    def rotate(values, at):
        return (values * cosine[at, :] - pltpu.roll(values, HD // 2, 1) * sine[at, :]).astype(BF)

    for start in range(0, seq, block):
        at = pl.ds(start, block)
        dqkv[at, :HD] = rotate(dq[at, :], at)
        dqkv[at, HD : 2 * HD] = rotate(dk[at, :], at)
        dqkv[at, 2 * HD :] = dv[at, :].astype(BF)
    gattn[: 3 * HD, :] = dot_tn(dqkv[...], normed[...]).astype(BF)
    gattn[3 * HD :, :] = dot_tn(hf[...].astype(BF), mid[...]).astype(BF)


def attend_back(mid_seq, wo, q, k, v, hf, lse, cosine, sine, normed):
    seq, width = mid_seq.shape
    sds = jax.ShapeDtypeStruct
    return pl.pallas_call(
        functools.partial(attend_back_kernel, min(256, seq)),
        out_shape=(sds((seq, 3 * HD), BF), sds((4 * HD, width), BF)),
        in_specs=[VMEM] * 10,
        out_specs=[VMEM] * 2,
        scratch_shapes=[pltpu.VMEM((seq, HD), BF)] + [pltpu.VMEM((seq, HD), F32)] * 3,
        compiler_params=pltpu.CompilerParams(vmem_limit_bytes=BIG),
        cost_estimate=pl.CostEstimate(flops=6 << 30, bytes_accessed=16 << 20, transcendentals=1 << 20),
        name="attend_back",
    )(mid_seq, wo, q, k, v, hf, lse, cosine, sine, normed)


def last_kernel(
    n_c, n_f, n_t, width, dqkv, wqkv, hidden, r_all, gain, mid_grad, gain2, rpart, gattn, lg, lu,
    in_out, gq, gk, gv, go, gains_out, router_out, lg_out, lu_out,
    es, er, rin, rss, rsr, r_own, mine, inx, own, outz, inz, gsend, gin, rs, sx, rx, lx, sz, rz, gs, gr, *rest,
):
    f, c, t = ranks()
    rows, quarter = hidden.shape
    part = width // (n_f * n_c)
    here = f * n_c + c
    others = []
    for df in range(n_f):
        for dc in range(n_c):
            for dt in range(n_t):
                if df or dc or dt:
                    others.append(
                        {
                            "fsdp": lax.rem(f + df, n_f),
                            "ctx": lax.rem(c + dc, n_c),
                            "tp": lax.rem(t + dt, n_t),
                        }
                    )
    gin[...] = jnp.zeros_like(gin)
    greet(others)
    order = [2, 1, 3, 0] if n_c == 4 else list(range(1, n_c)) + [0]

    def cross(d):
        cc = lax.rem(c + d, n_c)
        return remote(
            gattn.at[:, piece((1 - f) * n_c + cc, part)], inx.at[d], sx.at[d], rx.at[d], {"fsdp": 1 - f}
        )

    def keep(d):
        cc = lax.rem(c + d, n_c)
        return pltpu.make_async_copy(gattn.at[:, piece(f * n_c + cc, part)], own.at[d], lx.at[d])

    def line(d, to):
        return remote(outz.at[d], inz.at[d], sz.at[d], rz.at[d], {"ctx": to})

    router_copies = [
        remote(rpart, rin.at[i], rss.at[i], rsr.at[i], {"tp": peer})
        for i, peer in enumerate([sibling(t), opposite(t), opposite(sibling(t))])
    ]
    late = [
        remote(src, dst, es.at[i], er.at[i], {"fsdp": 1 - f})
        for i, (src, dst) in enumerate(((lg, lg_out), (lu, lu_out)))
    ]
    for copy in router_copies:
        copy.start()
    fetch = pltpu.make_async_copy(r_all.at[piece(c, rows), :], r_own, rs)
    fetch.start()
    for d in order:
        cross(d).start()
        keep(d).start()
    for copy in late:
        copy.start()

    def part_of(cc, q):
        return dot_nt(dqkv[piece(cc, rows), :], wqkv[piece(q, quarter), :])

    def pass_weights():
        for d in order:
            cross(d).wait()
            keep(d).wait()
            both = own[d].astype(F32) + inx[d].astype(F32)
            if d:
                outz[d] = both.astype(BF)
                line(d, lax.rem(c + d, n_c)).start()
            else:
                mine[...] = both

    total = reduce_seq(part_of, n_c, rest[:13], None, pass_weights)
    fetch.wait()
    back, gain_part = norm_grad(
        hidden[...].astype(F32), r_own[:, :1], gain[...], total, width, *rest[13:17]
    )
    in_out[...] = mid_grad[...] + back

    gsend[0:1, :] = gain_part
    gsend[1:2, :] = gain2[0:1, :]
    gsend[2:, :] = jnp.zeros((6, quarter), F32)
    per = quarter // part
    holder = here // per
    def gain_copy(h, tt):
        b = t * per + h
        return remote(
            gsend.at[:, pl.ds(h * part, part)],
            gin.at[here],
            gs.at[h * n_t + tt],
            gr.at[here],
            {"fsdp": b // n_c, "ctx": lax.rem(b, n_c), "tp": jnp.int32(tt)},
        )

    def is_me(h, tt):
        return (t * per + h == here) & (t == tt)

    for h in range(per):
        for tt in range(n_t):

            @pl.when(jnp.logical_not(is_me(h, tt)))
            def _():
                gain_copy(h, tt).start()

    def put(src, block):
        at = piece(src, HD)
        for i, ref in enumerate((gq, gk, gv)):
            ref[:, at] = block[i * HD : (i + 1) * HD, :].T
        go[at, :] = block[3 * HD :, :]

    put(c, mine[...])
    for d in order[:-1]:
        line(d, c).wait()
        put(lax.rem(c - d + n_c, n_c), inz[d].astype(F32))
    for h in range(per):
        for tt in range(n_t):

            @pl.when(jnp.logical_not(is_me(h, tt)))
            def _():
                gain_copy(h, tt).wait_send()

    for b in range(n_f * n_c):

        @pl.when((b != here) | (holder != t))
        def _():
            remote(gin.at[b], gin.at[b], gs.at[0], gr.at[b], {"tp": sibling(t)}).wait_recv()

    own_part = jnp.where(
        holder == t,
        gsend[:, piece(lax.rem(here, per), part)],
        jnp.zeros((8, part), F32),
    )
    gains_out[...] = own_part + jnp.sum(gin[...], axis=0)
    for copy in router_copies + late:
        copy.wait()
    router_out[...] = rpart[...] + jnp.sum(rin[...], axis=0)


def last(n_c, n_f, n_t, dqkv, wqkv, hidden, r_all, gain, mid_grad, gain2, rpart, gattn, lg, lu):
    rows, quarter = hidden.shape
    width = quarter * n_t
    part = width // (n_f * n_c)
    sds = jax.ShapeDtypeStruct
    slab = pltpu.VMEM((n_c, 4 * HD, part), BF)
    return pl.pallas_call(
        functools.partial(last_kernel, n_c, n_f, n_t, width),
        out_shape=(
            sds((rows, quarter), F32),
            sds((part, n_c * HD), F32),
            sds((part, n_c * HD), F32),
            sds((part, n_c * HD), F32),
            sds((n_c * HD, part), F32),
            sds((8, part), F32),
            sds(rpart.shape, F32),
            sds(lg.shape, BF),
            sds(lu.shape, BF),
        ),
        in_specs=[VMEM, VMEM, VMEM, HBM, VMEM, VMEM, VMEM, VMEM, HBM, HBM, HBM],
        out_specs=[VMEM] * 7 + [HBM] * 2,
        scratch_shapes=[
            DMA((2,)),
            DMA((2,)),
            pltpu.VMEM((3,) + rpart.shape, F32),
            DMA((3,)),
            DMA((3,)),
            pltpu.VMEM((rows, HD), F32),
            pltpu.VMEM((4 * HD, part), F32),
            slab,
            slab,
            slab,
            slab,
            pltpu.VMEM((8, quarter), F32),
            pltpu.VMEM((n_f * n_c, 8, part), F32),
            DMA(()),
            DMA((n_c,)),
            DMA((n_c,)),
            DMA((n_c,)),
            DMA((n_c,)),
            DMA((n_c,)),
            DMA((quarter // part * n_t,)),
            DMA((n_f * n_c,)),
        ]
        + reduce_seq_scratch(n_c, rows, quarter)
        + norm_grad_scratch(rows),
        compiler_params=pltpu.CompilerParams(
            collective_id=4, has_side_effects=True, vmem_limit_bytes=BIG
        ),
        cost_estimate=pl.CostEstimate(flops=2 << 30, bytes_accessed=150 << 20, transcendentals=0),
        name="last",
    )(dqkv, wqkv, hidden, r_all, gain, mid_grad, gain2, rpart, gattn, lg, lu)


def per_device_seq(
    hidden_in,
    positions,
    chosen,
    out_grad,
    attn_gain,
    w_query,
    w_key,
    w_value,
    w_out,
    moe_gain,
    router,
    shared_gate,
    shared_up,
    shared_down,
    expert_gate,
    expert_up,
    expert_down,
):
    f_rank, c_rank, t_rank = ranks()
    n_f, n_c, n_t = (lax.axis_size(name) for name in ("fsdp", "ctx", "tp"))
    rows, quarter = hidden_in.shape
    width = quarter * n_t
    part = w_query.shape[0]
    seq = rows * n_c
    n_exp = router.shape[1]
    mine = n_exp // n_c // n_f
    ffe = expert_gate.shape[2]
    group = ("fsdp", "ctx")
    every = ("fsdp", "ctx", "tp")
    n_b = n_f * n_c
    own_shared = shared_gate.shape[1] // n_b
    srows = -(-own_shared // 16) * 16
    block = f_rank * n_c + c_rank
    f_arr = f_rank.astype(jnp.int32).reshape(1)
    swap = [(i, n_f - 1 - i) for i in range(n_f)]
    weights = (expert_gate.swapaxes(1, 2), expert_up.swapaxes(1, 2), expert_down)

    picked_own = jnp.sum(
        (chosen[:, :, None] == jnp.arange(n_exp)[None, None, :]).astype(F32), axis=1
    )
    small = [
        attn_gain[None],
        moe_gain[None],
        router.T,
        picked_own.T.astype(BF),
        (positions // 64).astype(BF)[None],
        (positions % 64).astype(BF)[None],
    ]
    small = jnp.concatenate(small, axis=0)
    small = jnp.pad(small, ((0, -small.shape[0] % 16), (0, 0)))

    def shared_part(weight):
        return jnp.pad(
            weight.reshape(n_b, own_shared, part), ((0, 0), (0, srows - own_shared), (0, 0))
        )

    shared = jnp.concatenate(
        [shared_part(shared_gate.T), shared_part(shared_up.T), shared_part(shared_down)], axis=1
    )
    half = HD // 2
    inverse = 10000.0 ** (-jnp.arange(half, dtype=F32) * 2.0 / HD)
    angle = jnp.stack([jnp.tile(inverse, 2), jnp.where(jnp.arange(HD) < half, -1.0, 1.0)])
    (
        normed, q, k, v, heads_f, lse, r_one, cosine, sine, resid_mid,
        wqkv, wo, small_all, resid_all, grad_all, shared, *got,
    ) = first(
        n_c, n_f, n_t, mine, hidden_in, w_query, w_key, w_value, w_out, small, out_grad, weights, shared, angle
    )
    gain_one, gain_two = small_all[0:1].astype(F32), small_all[1:2].astype(F32)
    router_t = small_all[2 : 2 + n_exp]
    picked = small_all[2 + n_exp : 2 + 2 * n_exp].astype(F32).T
    sizes = (n_c, n_f, n_t, mine, ffe, srows)
    layer_out, moe_in, act, silu, slope, r_two, prob, kd, sd, shared_d = forward(
        *sizes, resid_all, grad_all, resid_mid, picked, gain_two, router_t, weights, got, shared
    )
    arrived_d = lax.ppermute(sd, "fsdp", swap)
    own_cols = lambda x: lax.dynamic_slice_in_dim(x, t_rank * quarter, quarter, 1)
    mid_grad, gain_two_part, mid_seq, shared_back, kg, ku, gg, gu, lg, lu = backward(
        *sizes, grad_all, act, silu, slope, moe_in, r_two, shared_d, prob, picked, router_t,
        resid_mid, own_cols(gain_two), out_grad, weights, got, shared,
    )
    n_gu = 2 * srows
    router_part = jnp.sum(shared_back[:, n_gu : n_gu + n_exp].astype(F32), axis=0)
    shared_back = jnp.concatenate([shared_back[:, :n_gu], shared_back[:, n_gu + n_exp :]], axis=1)
    shared_back = shared_back.reshape(n_b, 3, srows, part)[:, :, :own_shared].astype(F32)

    dqkv, gattn = attend_back(mid_seq, wo, q, k, v, heads_f, lse, cosine, sine, normed)
    input_grad, gq, gk, gv, go, gains, router_grad, lg, lu = last(
        n_c, n_f, n_t, dqkv, wqkv, hidden_in, r_one, own_cols(gain_one), mid_grad, gain_two_part,
        router_part, gattn, lg, lu,
    )
    eg, eu, ed = fill_experts(f_arr, (gg, lg, gu, lu, arrived_d), (kg, ku, kd))

    def shared_cols(i):
        return shared_back[:, i].reshape(n_b * own_shared, part)

    return (
        layer_out,
        input_grad,
        gains[0],
        gq,
        gk,
        gv,
        go,
        gains[1],
        router_grad.T,
        shared_cols(0).T,
        shared_cols(1).T,
        shared_cols(2),
        eg.swapaxes(1, 2),
        eu.swapaxes(1, 2),
        ed,
    )


def one_head_each(mesh, args):
    n_f, n_c, n_t = (mesh.shape[name] for name in ("fsdp", "ctx", "tp"))
    heads = args[5].shape[1] // HD
    experts = args[10].shape[1]
    return (
        n_f == 2
        and n_t == 4
        and heads == n_c * n_t
        and experts % (n_f * n_c) == 0
        and args[11].shape[1] % (8 * n_f * n_c * n_t) == 0
    )


def solution(mesh):
    placed = (
        P(("fsdp", "ctx"), "tp"),
        P(("fsdp", "ctx")),
        P(("fsdp", "ctx"), None),
        P(("fsdp", "ctx"), "tp"),
        P(("fsdp", "ctx")),
        P(("fsdp", "ctx"), "tp"),
        P(("fsdp", "ctx"), "tp"),
        P(("fsdp", "ctx"), "tp"),
        P("tp", ("fsdp", "ctx")),
        P(("fsdp", "ctx")),
        P(("fsdp", "ctx"), None),
        P(("fsdp", "ctx"), "tp"),
        P(("fsdp", "ctx"), "tp"),
        P("tp", ("fsdp", "ctx")),
        P("ctx", "fsdp", "tp"),
        P("ctx", "fsdp", "tp"),
        P("ctx", "tp", "fsdp"),
    )
    def run(*args):
        body = per_device_seq if one_head_each(mesh, args) else per_device
        return jax.shard_map(
        body,
        mesh=mesh,
        in_specs=placed,
        out_specs=(
            P(("fsdp", "ctx"), "tp"),
            P(("fsdp", "ctx"), "tp"),
            P(("fsdp", "ctx")),
            P(("fsdp", "ctx"), "tp"),
            P(("fsdp", "ctx"), "tp"),
            P(("fsdp", "ctx"), "tp"),
            P("tp", ("fsdp", "ctx")),
            P(("fsdp", "ctx")),
            P(("fsdp", "ctx"), None),
            P(("fsdp", "ctx"), "tp"),
            P(("fsdp", "ctx"), "tp"),
            P("tp", ("fsdp", "ctx")),
            P("ctx", "fsdp", "tp"),
            P("ctx", "fsdp", "tp"),
            P("ctx", "tp", "fsdp"),
        ),
        check_vma=False,
    )(*args)

    return run
```

```python
import functools

import jax
import jax.numpy as jnp
import numpy as np
from jax import lax
from jax.experimental import pallas as pl
from jax.experimental.pallas import tpu as pltpu
from jax.sharding import PartitionSpec as P

HD = 128
TOPK = 6


EPS = 1e-06
NEG_BIG = -1e30


def as_sent(value):
    return jax.tree.map(lambda a: a.astype(jnp.bfloat16) if a.dtype == jnp.float32 else a, value)


def features(local_part):
    return lax.all_gather(local_part, "tp", axis=1, tiled=True)


def row_stats(partial_terms):
    return lax.psum(partial_terms, "tp")


def partial_sums(partial_terms):
    return jax.tree.map(
        lambda part: part.astype(jnp.float32),
        lax.psum_scatter(as_sent(partial_terms), "tp", scatter_dimension=1, tiled=True),
    )


def to_owners(slot_rows):
    return lax.all_to_all(slot_rows, "ctx", split_axis=0, concat_axis=2, tiled=True)


def to_sources(slot_rows):
    return lax.all_to_all(
        slot_rows.astype(jnp.bfloat16), "ctx", split_axis=2, concat_axis=0, tiled=True
    ).astype(slot_rows.dtype)


def rotary(values, positions, rotate_sign):
    half_dim = values.shape[-1] // 2
    inverse = 10000.0 ** (-jnp.arange(half_dim, dtype=jnp.float32) * 2.0 / values.shape[-1])
    angles = positions.astype(jnp.float32)[:, None] * inverse[None, :]
    cosine = jnp.cos(angles)[:, None, :]
    sine_val = rotate_sign * jnp.sin(angles)[:, None, :]
    lower_half = values[..., :half_dim]
    upper_half = values[..., half_dim:]
    return jnp.concatenate(
        [lower_half * cosine - upper_half * sine_val, upper_half * cosine + lower_half * sine_val],
        axis=-1,
    )


def norm_rows(values, gain_part, model_width):
    square_sum = row_stats(jnp.sum(values * values, axis=1))
    row_scale = lax.rsqrt(square_sum / model_width + EPS)
    return (values * row_scale[:, None] * gain_part[None, :], row_scale)


def norm_back(values, row_scale, gain_part, grad_normed, model_width, tp_rank):
    quarter = values.shape[1]
    local_sum = jnp.sum(grad_normed * gain_part[None, :] * values, axis=1)
    gain_local = jnp.sum(grad_normed * values * row_scale[:, None], axis=0)
    gain_whole = lax.dynamic_update_slice_in_dim(
        jnp.zeros((model_width,), jnp.float32), gain_local, tp_rank * quarter, 0
    )
    row_total, gain_grad = row_stats((local_sum, gain_whole))
    back = (
        row_scale[:, None] * gain_part[None, :] * grad_normed
        - values * (row_scale**3 * row_total / model_width)[:, None]
    )
    return (back, gain_grad)


def scatter_slots(assign_rows, flat_exp, slot_of, n_exp, capacity):
    buffer = jnp.zeros((n_exp, capacity, assign_rows.shape[1]), assign_rows.dtype)
    return buffer.at[flat_exp, slot_of].set(assign_rows)


def silu_grad(pre_act):
    sigmoid_val = jax.nn.sigmoid(pre_act)
    return sigmoid_val * (1.0 + pre_act * (1.0 - sigmoid_val))


def keep_state(carried):
    return carried


def per_device(
    hidden_in,
    positions,
    chosen,
    out_grad,
    attn_gain,
    w_query,
    w_key,
    w_value,
    w_out,
    moe_gain,
    router,
    shared_gate,
    shared_up,
    shared_down,
    expert_gate,
    expert_up,
    expert_down,
):
    tp_rank = lax.axis_index("tp")
    ctx_rank = lax.axis_index("ctx")
    n_ctx = lax.axis_size("ctx")
    tok_rows, quarter = hidden_in.shape
    model_width = quarter * lax.axis_size("tp")
    gain_one, wq_all, wk_all, wv_all, gain_two, router_all, gate_all, up_all, wo_all, down_all = (
        lax.all_gather(attn_gain, ("fsdp", "ctx"), axis=0, tiled=True),
        lax.all_gather(w_query, ("fsdp", "ctx"), axis=0, tiled=True),
        lax.all_gather(w_key, ("fsdp", "ctx"), axis=0, tiled=True),
        lax.all_gather(w_value, ("fsdp", "ctx"), axis=0, tiled=True),
        lax.all_gather(moe_gain, ("fsdp", "ctx"), axis=0, tiled=True),
        lax.all_gather(router, ("fsdp", "ctx"), axis=0, tiled=True),
        lax.all_gather(shared_gate, ("fsdp", "ctx"), axis=0, tiled=True),
        lax.all_gather(shared_up, ("fsdp", "ctx"), axis=0, tiled=True),
        lax.all_gather(w_out, ("fsdp", "ctx"), axis=1, tiled=True),
        lax.all_gather(shared_down, ("fsdp", "ctx"), axis=1, tiled=True),
    )
    expert_gate_weights, expert_up_weights, expert_down_weights = (
        lax.all_gather(expert_gate, "fsdp", axis=1, tiled=True),
        lax.all_gather(expert_up, "fsdp", axis=1, tiled=True),
        lax.all_gather(expert_down, "fsdp", axis=2, tiled=True),
    )
    gain_q1 = lax.dynamic_slice_in_dim(gain_one, tp_rank * quarter, quarter).astype(jnp.float32)
    gain_q2 = lax.dynamic_slice_in_dim(gain_two, tp_rank * quarter, quarter).astype(jnp.float32)
    router_rows = lax.dynamic_slice_in_dim(router_all, tp_rank * quarter, quarter, 0)
    head_count = wq_all.shape[1] // HD
    scale_att = HD ** (-0.5)
    resid_in = hidden_in.astype(jnp.float32)
    normed_one, scale_one = norm_rows(resid_in, gain_q1, model_width)
    normed_in = features(normed_one.astype(jnp.bfloat16))
    query_pre = jnp.dot(normed_in, wq_all, preferred_element_type=jnp.float32).reshape(
        tok_rows, head_count, HD
    )
    key_pre = jnp.dot(normed_in, wk_all, preferred_element_type=jnp.float32).reshape(
        tok_rows, head_count, HD
    )
    value_b = (
        jnp.dot(normed_in, wv_all, preferred_element_type=jnp.float32)
        .astype(jnp.bfloat16)
        .reshape(tok_rows, head_count, HD)
    )
    query_b = rotary(query_pre, positions, 1.0).astype(jnp.bfloat16)
    key_b = rotary(key_pre, positions, 1.0).astype(jnp.bfloat16)
    q_start = ctx_rank * tok_rows
    row_pos = q_start + jnp.arange(tok_rows)
    start_state = (
        jnp.full((tok_rows, head_count), NEG_BIG, jnp.float32),
        jnp.zeros((tok_rows, head_count), jnp.float32),
        jnp.zeros((tok_rows, head_count, HD), jnp.float32),
    )
    keys_blk = lax.all_gather(key_b, "ctx", axis=0, tiled=True)
    vals_blk = lax.all_gather(value_b, "ctx", axis=0, tiled=True)
    key_count = keys_blk.shape[0]

    def compute(state_in):
        run_max, run_sum, run_acc = state_in
        scores = (
            jnp.einsum("qhd,khd->qhk", query_b, keys_blk, preferred_element_type=jnp.float32)
            * scale_att
        )
        visible = jnp.arange(key_count)[None, :] <= row_pos[:, None]
        scores = jnp.where(visible[:, None, :], scores, NEG_BIG)
        new_max = jnp.maximum(run_max, jnp.max(scores, axis=2))
        weights = jnp.exp(scores - new_max[:, :, None])
        new_sum = jnp.sum(weights, axis=2)
        new_acc = jnp.einsum(
            "qhk,khd->qhd",
            weights.astype(jnp.bfloat16),
            vals_blk,
            preferred_element_type=jnp.float32,
        )
        return (new_max, new_sum, new_acc)

    run_max, run_sum, run_acc = lax.cond(
        jnp.int32(0) <= q_start + tok_rows - 1, compute, keep_state, start_state
    )
    heads_f = run_acc / run_sum[:, :, None]
    log_sum = run_max + jnp.log(run_sum)
    heads_b = heads_f.astype(jnp.bfloat16).reshape(tok_rows, head_count * HD)
    resid_mid = resid_in + partial_sums(
        jnp.dot(heads_b, wo_all, preferred_element_type=jnp.float32)
    )
    normed_two, scale_two = norm_rows(resid_mid, gain_q2, model_width)
    moe_part = normed_two.astype(jnp.bfloat16)
    moe_in = features(moe_part)
    n_exp = router_all.shape[1]
    exp_dev = n_exp // n_ctx
    capacity = min(tok_rows, 5 * TOPK * tok_rows // (3 * n_exp))
    logits = jnp.dot(moe_in, router_all, preferred_element_type=jnp.float32)
    probs_all = jax.nn.softmax(logits, axis=1)
    picked = (chosen[:, :, None] == jnp.arange(n_exp)[None, None, :]).astype(jnp.float32)
    gate_vals = jnp.sum(picked * probs_all[:, None, :], axis=2)
    shared_a = jnp.dot(moe_in, gate_all, preferred_element_type=jnp.float32)
    shared_b = jnp.dot(moe_in, up_all, preferred_element_type=jnp.float32)
    shared_act = (jax.nn.silu(shared_a) * shared_b).astype(jnp.bfloat16)
    shared_out = jnp.dot(shared_act, down_all, preferred_element_type=jnp.float32)
    flat_exp = chosen.reshape(-1)
    flat_hot = (flat_exp[:, None] == jnp.arange(n_exp)[None, :]).astype(jnp.int32)
    slot_of = jnp.sum((jnp.cumsum(flat_hot, axis=0) - flat_hot) * flat_hot, axis=1)
    token_of = jnp.arange(tok_rows * TOPK) // TOPK
    slot_count = n_ctx * capacity
    outgoing = scatter_slots(moe_in[token_of], flat_exp, slot_of, n_exp, capacity)
    received_rows = to_owners(outgoing.reshape(n_ctx, exp_dev, capacity, model_width)).reshape(
        exp_dev, slot_count, model_width
    )
    expert_a = jnp.einsum(
        "bmw,bwv->bmv", received_rows, expert_gate_weights, preferred_element_type=jnp.float32
    )
    expert_up_proj = jnp.einsum(
        "bmw,bwv->bmv", received_rows, expert_up_weights, preferred_element_type=jnp.float32
    )
    expert_act = (jax.nn.silu(expert_a) * expert_up_proj).astype(jnp.bfloat16)
    expert_out = jnp.einsum(
        "erf,efd->erd", expert_act, expert_down_weights, preferred_element_type=jnp.float32
    )
    returned = to_sources(expert_out.reshape(1, exp_dev, slot_count, model_width))
    shared_q, slot_q = partial_sums((shared_out, returned.reshape(n_exp * capacity, model_width)))
    slot_rows = slot_q.reshape(n_exp, capacity, quarter)[flat_exp, slot_of].reshape(
        tok_rows, TOPK, quarter
    )
    result = resid_mid + shared_q + jnp.sum(gate_vals[:, :, None] * slot_rows, axis=1)
    layer_out = result.astype(jnp.bfloat16)
    grad_out = out_grad.astype(jnp.float32)
    gate_grad = row_stats(jnp.sum(grad_out[:, None, :] * slot_rows, axis=2))
    prob_grad = jnp.sum(gate_grad[:, :, None] * picked, axis=1)
    logit_grad = (
        probs_all * (prob_grad - jnp.sum(probs_all * prob_grad, axis=1, keepdims=True))
    ).astype(jnp.bfloat16)
    router_grad = jnp.einsum("td,te->de", moe_in, logit_grad, preferred_element_type=jnp.float32)
    router_back_q = jnp.einsum(
        "te,de->td", logit_grad, router_rows, preferred_element_type=jnp.float32
    )
    grad_full = features(out_grad)
    shared_dact = jnp.einsum("td,fd->tf", grad_full, down_all, preferred_element_type=jnp.float32)
    shared_da = (shared_dact * shared_b * silu_grad(shared_a)).astype(jnp.bfloat16)
    shared_db = (shared_dact * jax.nn.silu(shared_a)).astype(jnp.bfloat16)
    shared_down_grad = jnp.einsum(
        "tf,td->fd", shared_act, grad_full, preferred_element_type=jnp.float32
    )
    shared_gate_grad = jnp.einsum(
        "td,tf->df", moe_in, shared_da, preferred_element_type=jnp.float32
    )
    shared_up_grad = jnp.einsum("td,tf->df", moe_in, shared_db, preferred_element_type=jnp.float32)
    shared_back = jnp.einsum(
        "tf,df->td", shared_da, gate_all, preferred_element_type=jnp.float32
    ) + jnp.einsum("tf,df->td", shared_db, up_all, preferred_element_type=jnp.float32)
    assign_grad = (
        (gate_vals[:, :, None] * grad_full[:, None, :])
        .astype(jnp.bfloat16)
        .reshape(tok_rows * TOPK, model_width)
    )
    grad_slots = scatter_slots(assign_grad, flat_exp, slot_of, n_exp, capacity)
    grad_arrived = to_owners(grad_slots.reshape(n_ctx, exp_dev, capacity, model_width)).reshape(
        exp_dev, slot_count, model_width
    )
    expert_dact = jnp.einsum(
        "erd,efd->erf", grad_arrived, expert_down_weights, preferred_element_type=jnp.float32
    )
    expert_da = (expert_dact * expert_up_proj * silu_grad(expert_a)).astype(jnp.bfloat16)
    expert_up_proj_grad = (expert_dact * jax.nn.silu(expert_a)).astype(jnp.bfloat16)
    edown_grad = jnp.einsum(
        "erf,erd->efd", expert_act, grad_arrived, preferred_element_type=jnp.float32
    )
    egate_grad = jnp.einsum(
        "qgo,qgz->qoz", received_rows, expert_da, preferred_element_type=jnp.float32
    )
    expert_up_weight_grad = jnp.einsum(
        "qgo,qgz->qoz", received_rows, expert_up_proj_grad, preferred_element_type=jnp.float32
    )
    expert_back = jnp.einsum(
        "iac,igc->iag", expert_da, expert_gate_weights, preferred_element_type=jnp.float32
    ) + jnp.einsum(
        "iac,igc->iag", expert_up_proj_grad, expert_up_weights, preferred_element_type=jnp.float32
    )
    back_slots = to_sources(expert_back.reshape(1, exp_dev, slot_count, model_width)).reshape(
        n_exp, capacity, model_width
    )
    token_back = jnp.sum(back_slots[flat_exp, slot_of].reshape(tok_rows, TOPK, model_width), axis=1)
    moe_back_q = partial_sums(shared_back + token_back)
    mid_back, gain_two_grad = norm_back(
        resid_mid, scale_two, gain_q2, moe_back_q + router_back_q, model_width, tp_rank
    )
    mid_grad = grad_out + mid_back
    branch_full = features(mid_grad.astype(jnp.bfloat16))
    wo_grad = jnp.einsum("tf,td->fd", heads_b, branch_full, preferred_element_type=jnp.float32)
    heads_grad = (
        jnp.einsum("td,fd->tf", branch_full, wo_all, preferred_element_type=jnp.float32)
        .astype(jnp.bfloat16)
        .reshape(tok_rows, head_count, HD)
    )
    row_delta = jnp.sum(heads_grad.astype(jnp.float32) * heads_f, axis=2)
    seq_len = tok_rows * n_ctx
    back_state = (
        jnp.zeros((tok_rows, head_count, HD), jnp.float32),
        jnp.zeros((seq_len, head_count, HD), jnp.float32),
        jnp.zeros((seq_len, head_count, HD), jnp.float32),
    )
    attend_keys_blk = lax.all_gather(key_b, "ctx", axis=0, tiled=True)
    attend_vals_blk = lax.all_gather(value_b, "ctx", axis=0, tiled=True)
    attend_key_count = attend_keys_blk.shape[0]

    def compute(state_in):
        scores = (
            jnp.einsum("qhd,khd->qhk", query_b, attend_keys_blk, preferred_element_type=jnp.float32)
            * scale_att
        )
        visible = jnp.arange(attend_key_count)[None, :] <= row_pos[:, None]
        probs_blk = jnp.where(visible[:, None, :], jnp.exp(scores - log_sum[:, :, None]), 0.0)
        value_part = jnp.einsum(
            "qhk,qhd->khd",
            probs_blk.astype(jnp.bfloat16),
            heads_grad,
            preferred_element_type=jnp.float32,
        )
        dot_grad = jnp.einsum(
            "qhd,khd->qhk", heads_grad, attend_vals_blk, preferred_element_type=jnp.float32
        )
        score_grad = (probs_blk * (dot_grad - row_delta[:, :, None])).astype(jnp.bfloat16)
        query_acc = (
            jnp.einsum(
                "qhk,khd->qhd", score_grad, attend_keys_blk, preferred_element_type=jnp.float32
            )
            * scale_att
        )
        key_part = (
            jnp.einsum("qhk,qhd->khd", score_grad, query_b, preferred_element_type=jnp.float32)
            * scale_att
        )
        return (query_acc, key_part, value_part)

    query_grad, key_grad_all, value_grad_all = lax.cond(
        jnp.int32(0) <= q_start + tok_rows - 1, compute, keep_state, back_state
    )
    key_grad, value_grad = (
        lax.psum_scatter(
            key_grad_all.astype(jnp.bfloat16), "ctx", scatter_dimension=0, tiled=True
        ).astype(jnp.float32),
        lax.psum_scatter(
            value_grad_all.astype(jnp.bfloat16), "ctx", scatter_dimension=0, tiled=True
        ).astype(jnp.float32),
    )
    query_pre_grad = (
        rotary(query_grad, positions, -1.0).astype(jnp.bfloat16).reshape(tok_rows, head_count * HD)
    )
    key_pre_grad = (
        rotary(key_grad, positions, -1.0).astype(jnp.bfloat16).reshape(tok_rows, head_count * HD)
    )
    value_pre_grad = value_grad.astype(jnp.bfloat16).reshape(tok_rows, head_count * HD)
    wq_grad = jnp.einsum("td,tf->df", normed_in, query_pre_grad, preferred_element_type=jnp.float32)
    wk_grad = jnp.einsum("td,tf->df", normed_in, key_pre_grad, preferred_element_type=jnp.float32)
    wv_grad = jnp.einsum("td,tf->df", normed_in, value_pre_grad, preferred_element_type=jnp.float32)
    in_back = jnp.einsum("tf,df->td", query_pre_grad, wq_all, preferred_element_type=jnp.float32)
    in_back = in_back + jnp.einsum(
        "tf,df->td", key_pre_grad, wk_all, preferred_element_type=jnp.float32
    )
    in_back = in_back + jnp.einsum(
        "tf,df->td", value_pre_grad, wv_all, preferred_element_type=jnp.float32
    )
    first_back, gain_one_grad = norm_back(
        resid_in, scale_one, gain_q1, partial_sums(in_back), model_width, tp_rank
    )
    input_grad = mid_grad + first_back
    dense = (
        lax.psum_scatter(
            gain_one_grad.astype(jnp.bfloat16), ("fsdp", "ctx"), scatter_dimension=0, tiled=True
        ).astype(jnp.float32),
        lax.psum_scatter(
            wq_grad.astype(jnp.bfloat16), ("fsdp", "ctx"), scatter_dimension=0, tiled=True
        ).astype(jnp.float32),
        lax.psum_scatter(
            wk_grad.astype(jnp.bfloat16), ("fsdp", "ctx"), scatter_dimension=0, tiled=True
        ).astype(jnp.float32),
        lax.psum_scatter(
            wv_grad.astype(jnp.bfloat16), ("fsdp", "ctx"), scatter_dimension=0, tiled=True
        ).astype(jnp.float32),
        lax.psum_scatter(
            gain_two_grad.astype(jnp.bfloat16), ("fsdp", "ctx"), scatter_dimension=0, tiled=True
        ).astype(jnp.float32),
        lax.psum_scatter(
            router_grad.astype(jnp.bfloat16), ("fsdp", "ctx"), scatter_dimension=0, tiled=True
        ).astype(jnp.float32),
        lax.psum_scatter(
            shared_gate_grad.astype(jnp.bfloat16), ("fsdp", "ctx"), scatter_dimension=0, tiled=True
        ).astype(jnp.float32),
        lax.psum_scatter(
            shared_up_grad.astype(jnp.bfloat16), ("fsdp", "ctx"), scatter_dimension=0, tiled=True
        ).astype(jnp.float32),
        lax.psum_scatter(
            wo_grad.astype(jnp.bfloat16), ("fsdp", "ctx"), scatter_dimension=1, tiled=True
        ).astype(jnp.float32),
        lax.psum_scatter(
            shared_down_grad.astype(jnp.bfloat16), ("fsdp", "ctx"), scatter_dimension=1, tiled=True
        ).astype(jnp.float32),
    )
    experts_done = (
        lax.psum_scatter(
            egate_grad.astype(jnp.bfloat16), "fsdp", scatter_dimension=1, tiled=True
        ).astype(jnp.float32),
        lax.psum_scatter(
            expert_up_weight_grad.astype(jnp.bfloat16), "fsdp", scatter_dimension=1, tiled=True
        ).astype(jnp.float32),
        lax.psum_scatter(
            edown_grad.astype(jnp.bfloat16), "fsdp", scatter_dimension=2, tiled=True
        ).astype(jnp.float32),
    )
    return (
        layer_out,
        input_grad,
        dense[0],
        dense[1],
        dense[2],
        dense[3],
        dense[8],
        dense[4],
        dense[5],
        dense[6],
        dense[7],
        dense[9],
        experts_done[0],
        experts_done[1],
        experts_done[2],
    )


MESH = pl.DeviceIdType.MESH
HBM = pl.BlockSpec(memory_space=pl.ANY)
VMEM = pl.BlockSpec(memory_space=pltpu.VMEM)
DMA = pltpu.SemaphoreType.DMA
BF, F32 = jnp.bfloat16, jnp.float32
BIG = 60 * 1024 * 1024


def dot_nt(left, right):
    return lax.dot_general(left, right, (((1,), (1,)), ((), ())), preferred_element_type=F32)


def dot_tn(left, right):
    return lax.dot_general(left, right, (((0,), (0,)), ((), ())), preferred_element_type=F32)


def dot_nn(left, right):
    return jnp.dot(left, right, preferred_element_type=F32)


def ranks():
    return lax.axis_index("fsdp"), lax.axis_index("ctx"), lax.axis_index("tp")


def sibling(t):
    return t + 1 - 2 * lax.rem(t, 2)


def opposite(t):
    return lax.rem(t + 2, 4)


def remote(src, dst, send, recv, to):
    return pltpu.make_async_remote_copy(
        src_ref=src, dst_ref=dst, send_sem=send, recv_sem=recv, device_id=to, device_id_type=MESH
    )


def greet(peers):
    barrier = pltpu.get_barrier_semaphore()
    for peer in peers:
        pl.semaphore_signal(barrier, inc=1, device_id=peer, device_id_type=MESH)
    pl.semaphore_wait(barrier, len(peers))


def line_peers(c, n_c):
    return [{"ctx": lax.rem(c + step, n_c)} for step in range(1, n_c)]


def piece(index, size):
    return pl.ds(pl.multiple_of(index * size, size), size)


def nearest(c, n_c, act):
    act(c)
    for step in range(1, n_c):
        for side in (-1, 1):
            place = c + side * step

            @pl.when((place >= 0) & (place < n_c))
            def _():
                act(place)


def spread_sems(n_c):
    return [
        DMA((n_c + 2,)),
        DMA((n_c,)),
        DMA((n_c,)),
        DMA((n_c,)),
        DMA((2 * n_c,)),
        DMA((2 * n_c,)),
        DMA((4 * n_c,)),
        DMA((4 * n_c,)),
        DMA(()),
    ]


class Spread:
    def __init__(self, own, place, n_c, both, sems):
        self.own, self.place, self.n_c, self.both = own, place, n_c, both
        self.zs, self.zr, self.xs, self.xr, self.ys, self.yr, self.ks, self.kr, self.ls = sems
        self.f, self.c, self.t = ranks()
        self.other_t = opposite(self.t)
        self.groups = ((self.f, 0), (1 - self.f, n_c))[: 2 if both else 1]

    def local(self):
        return pltpu.make_async_copy(self.own, self.place(self.f, self.c, self.t), self.ls)

    def far_copy(self, src, i, g, cc, col):
        return remote(src, self.place(g, cc, col), self.ys.at[i], self.yr.at[i], {"tp": self.other_t})

    def sib_copy(self, src, i, which, g, cc, col):
        at = 2 * i + which
        return remote(src, self.place(g, cc, col), self.ks.at[at], self.kr.at[at], {"tp": sibling(self.t)})

    def other_copy(self, src, g, cc):
        return remote(src, self.place(g, cc, self.t), self.xs.at[cc], self.xr.at[cc], {"fsdp": 1 - self.f})

    def line_copy(self, src, cc, sem, to):
        return remote(src, self.place(self.f, cc, self.t), self.zs.at[sem], self.zr.at[cc], {"ctx": to})

    def pass_on(self, src, i, g, cc):
        self.far_copy(src, i, g, cc, self.t).start()
        self.sib_copy(src, i, 0, g, cc, self.t).start()

    def start(self):
        self.local().start()
        n_c, c, own = self.n_c, self.c, self.own

        @pl.when(c < n_c - 1)
        def _():
            self.line_copy(own, c, n_c, c + 1).start()

        @pl.when(c > 0)
        def _():
            self.line_copy(own, c, n_c + 1, c - 1).start()

        if self.both:
            self.other_copy(own, self.f, c).start()
        self.pass_on(own, c, self.f, c)

    def each_other(self, act):
        for step in range(1, self.n_c):
            for side in (-1, 1):
                cc = self.c + side * step

                @pl.when((cc >= 0) & (cc < self.n_c))
                def _():
                    act(cc, self.c - side)

    def line(self):
        n_c = self.n_c

        def arrive(cc, onward):
            block = self.place(self.f, cc, self.t)
            self.line_copy(block, cc, cc, self.c).wait_recv()

            @pl.when((onward >= 0) & (onward < n_c))
            def _():
                self.line_copy(block, cc, cc, onward).start()

            if self.both:
                self.other_copy(block, self.f, cc).start()
            self.pass_on(block, cc, self.f, cc)

        self.each_other(arrive)

    def other(self):
        def arrive(cc):
            block = self.place(1 - self.f, cc, self.t)
            self.other_copy(block, 1 - self.f, cc).wait_recv()
            self.pass_on(block, self.n_c + cc, 1 - self.f, cc)

        nearest(self.c, self.n_c, arrive)

    def far(self, which):
        g, base = self.groups[which]

        def arrive(cc):
            i = base + cc
            block = self.place(g, cc, self.other_t)
            self.far_copy(block, i, g, cc, self.other_t).wait_recv()
            self.sib_copy(block, i, 1, g, cc, self.other_t).start()

        nearest(self.c, self.n_c, arrive)

    def arrived(self, which):
        g, base = self.groups[which]
        for cc in range(self.n_c):
            block = self.place(g, cc, self.t)
            for half in range(2):
                self.sib_copy(block, base + cc, half, g, cc, self.t).wait_recv()

    def finish(self):
        n_c, c, f, t, own = self.n_c, self.c, self.f, self.t, self.own
        for g, base in self.groups:
            for cc in range(n_c):
                block = self.place(g, cc, t)
                for half in range(2):
                    self.sib_copy(block, base + cc, half, g, cc, t).wait_send()
                self.far_copy(block, base + cc, g, cc, t).wait_send()
        if self.both:
            for cc in range(n_c):
                self.other_copy(self.place(f, cc, t), f, cc).wait_send()
        block = self.place(f, c, t)

        @pl.when(c < n_c - 1)
        def _():
            self.line_copy(block, c, n_c, c).wait_send()

        @pl.when(c > 0)
        def _():
            self.line_copy(block, c, n_c + 1, c).wait_send()

        def sent(cc, onward):
            @pl.when((onward >= 0) & (onward < n_c))
            def _():
                self.line_copy(block, cc, cc, c).wait_send()

        self.each_other(sent)


def to_each(src_of, dst, n_f, n_c, sems, act):
    send, recv, own = sems
    f, c, _ = ranks()
    here = f * n_c + c
    for df in range(n_f):
        for dc in range(n_c):
            i = df * n_c + dc
            if i == 0:
                copy = pltpu.make_async_copy(src_of(here), dst.at[here], own)
                copy.start() if act == "start" else copy.wait()
                continue
            to_f, to_c = lax.rem(f + df, n_f), lax.rem(c + dc, n_c)
            copy = remote(
                src_of(to_f * n_c + to_c), dst.at[here], send.at[i], recv.at[i], {"fsdp": to_f, "ctx": to_c}
            )
            copy.start() if act == "start" else copy.wait()


def each_peers(f, c, n_f, n_c):
    return [
        {"fsdp": lax.rem(f + df, n_f), "ctx": lax.rem(c + dc, n_c)}
        for df in range(n_f)
        for dc in range(n_c)
        if df or dc
    ]


def reduce_seq_scratch(n_c, rows, quarter):
    return [
        pltpu.VMEM((n_c, 2, rows, quarter), BF),
        pltpu.VMEM((n_c, 2, rows, quarter), BF),
        pltpu.VMEM((n_c, 2, rows, quarter), F32),
        pltpu.VMEM((n_c, rows, quarter), BF),
        pltpu.VMEM((n_c, rows, quarter), BF),
        pltpu.VMEM((n_c, rows, quarter), BF),
        pltpu.VMEM((n_c, rows, quarter), BF),
        DMA((n_c,)),
        DMA((n_c,)),
        DMA((n_c,)),
        DMA((n_c,)),
        DMA((n_c,)),
        DMA((n_c,)),
    ]


def reduce_seq(part_of, n_c, scratch, middle=None, before_last=None):
    out1, in1, own, out2, in2, out3, in3, s1, r1, s2, r2, s3, r3 = scratch
    f, c, t = ranks()
    far, sib = opposite(t), sibling(t)
    to_sib, to_far = {"tp": sib}, {"tp": far}
    order = [2, 1, 3, 0] if n_c == 4 else list(range(1, n_c)) + [0]
    for d in order:
        cc = lax.rem(c + d, n_c)
        out1[d, 0] = part_of(cc, sib).astype(BF)
        out1[d, 1] = part_of(cc, opposite(sib)).astype(BF)
        remote(out1.at[d], in1.at[d], s1.at[d], r1.at[d], to_sib).start()
        own[d, 0] = part_of(cc, t)
        own[d, 1] = part_of(cc, far)
    for d in order:
        remote(out1.at[d], in1.at[d], s1.at[d], r1.at[d], to_sib).wait()
        out2[d] = (own[d, 1] + in1[d, 1].astype(F32)).astype(BF)
        remote(out2.at[d], in2.at[d], s2.at[d], r2.at[d], to_far).start()
    if middle is not None:
        middle()
    for d in order:
        remote(out2.at[d], in2.at[d], s2.at[d], r2.at[d], to_far).wait()
        total = own[d, 0] + in1[d, 0].astype(F32) + in2[d].astype(F32)
        if d:
            out3[d] = total.astype(BF)
            cc = lax.rem(c + d, n_c)
            remote(out3.at[d], in3.at[d], s3.at[d], r3.at[d], {"ctx": cc}).start()
    if before_last is not None:
        before_last()
    for d in order[:-1]:
        remote(out3.at[d], in3.at[d], s3.at[d], r3.at[d], {"ctx": c}).wait()
        total = total + in3[d].astype(F32)
    return total


def first_kernel(
    n_c, n_f, n_exp, mine, hidden, wq, wk, wv, wo, og, gate_t, up_t, down, router_in, chosen, lines, sg, su, sd, angle,
    normed, q_out, k_out, v_out, hf_out, lse_out, r_out, cos_out, sin_out, resid_out,
    wqkv_out, wo_out, small_out, all_out, og_out, shared_out, gg_out, gu_out, gd_out,
    seq, wqkv, wo_all, small_all, hb, blk, own_og, small, shared,
    ws, wr, ls, xs, xr, ss, sr, sl, es, er, os, *scratch,
):
    f, c, t = ranks()
    rows, quarter = blk.shape
    part = wo.shape[1]
    tokens, width = seq.shape
    n_s = len(spread_sems(n_c))
    named = lax.broadcasted_iota(jnp.int32, (n_exp, part), 0)
    mask = jnp.zeros((n_exp, part), F32)
    for k in range(chosen.shape[0]):
        mask = mask + jnp.where(chosen[k : k + 1, :] == named, 1.0, 0.0)
    small[:n_exp, :] = router_in[...]
    small[n_exp : 2 * n_exp, :] = mask.astype(BF)
    small[2 * n_exp :, :] = lines[...]
    n_b = n_f * n_c
    own_rows, srows = sg.shape[0] // n_b, shared.shape[1] // 3
    for i, src in enumerate((sg, su, sd)):
        for b in range(n_b):
            shared[b, i * srows : i * srows + own_rows, :] = src[b * own_rows : (b + 1) * own_rows, :]
            if srows > own_rows:
                shared[b, i * srows + own_rows : (i + 1) * srows, :] = jnp.zeros((srows - own_rows, part), BF)
    greet([{"tp": sibling(t)}, {"tp": opposite(t)}] + each_peers(f, c, n_f, n_c))
    seq_place = lambda g, cc, tt: seq.at[piece(cc, rows), piece(tt, quarter)]
    og_place = lambda g, cc, tt: og_out.at[g * n_c + cc, tt]
    all_place = lambda g, cc, tt: all_out.at[piece(g * n_c + cc, rows), piece(tt, quarter)]
    hid = Spread(hidden, seq_place, n_c, False, scratch[:n_s])
    grad = Spread(og, og_place, n_c, True, scratch[n_s : 2 * n_s])
    res = Spread(blk, all_place, n_c, True, scratch[2 * n_s : 3 * n_s])

    def targets(g, cc):
        block = piece(g * n_c + cc, part)
        return [wqkv.at[block, pl.ds(i * HD, HD)] for i in range(3)] + [
            wo_all.at[:, block],
            small_all.at[:, block],
        ]

    def sources(head):
        cols = piece(head, HD)
        return [wq.at[:, cols], wk.at[:, cols], wv.at[:, cols], wo.at[cols, :], small]

    def slabs(g, cc):
        block = piece(g * n_c + cc, part)
        return [wqkv.at[block, :], wo_all.at[:, block], small_all.at[:, block]]

    def across(step, g, cc):
        return [
            remote(slab, slab, xs.at[step, i], xr.at[step, i], {"fsdp": 1 - f})
            for i, slab in enumerate(slabs(g, cc))
        ]

    def swap(weight, out, k):
        return [
            remote(weight.at[(1 - f) * mine + e], out.at[e], es.at[k, e], er.at[k, e], {"fsdp": 1 - f})
            for e in range(mine)
        ]

    more = swap(down, gd_out, 2)
    for copy in more:
        copy.start()
    hid.start()
    for step in range(1, n_c):
        to = lax.rem(c + step, n_c)
        for i, (src, dst) in enumerate(zip(sources(to), targets(f, c))):
            remote(src, dst, ws.at[step, i], wr.at[step, i], {"ctx": to}).start()
    own = [
        pltpu.make_async_copy(src, dst, ls.at[i])
        for i, (src, dst) in enumerate(zip(sources(c), targets(f, c)))
    ]
    for copy in own:
        copy.start()
    for copy in own:
        copy.wait()
    for copy in across(0, f, c):
        copy.start()
    grad.start()
    hid.line()
    for step in range(1, n_c):
        cc = lax.rem(c - step + n_c, n_c)
        for i, dst in enumerate(targets(f, cc)):
            remote(dst, dst, ws.at[step, i], wr.at[step, i], {"ctx": cc}).wait_recv()
        for copy in across(step, f, cc):
            copy.start()
    grad.line()
    swaps = swap(gate_t, gg_out, 0) + swap(up_t, gu_out, 1)
    for copy in swaps:
        copy.start()
    hid.far(0)
    hid.arrived(0)
    hid.local().wait()
    for step in range(n_c):
        for copy in across(step, 1 - f, lax.rem(c - step + n_c, n_c)):
            copy.wait_recv()
    outs = [
        pltpu.make_async_copy(src, dst, os.at[i])
        for i, (src, dst) in enumerate(((wqkv, wqkv_out), (wo_all, wo_out), (small_all, small_out)))
    ]
    for copy in outs:
        copy.start()
    grad.other()

    scale_att = HD ** (-0.5)
    gain = small_all[2 * n_exp : 2 * n_exp + 1, :].astype(F32)
    place_row = 2 * n_exp + 2
    for start in range(0, tokens, rows):
        at = pl.ds(start, rows)
        h = seq[at, :].astype(F32)
        r = lax.rsqrt(jnp.sum(h * h, axis=1, keepdims=True) / width + EPS)
        n = (h * r * gain).astype(BF)
        normed[at, :] = n
        r_out[at, :] = jnp.broadcast_to(r, (rows, HD))
        cols = pl.ds(pl.multiple_of(f * tokens + start, rows), rows)
        pos = small_all[place_row : place_row + 2, cols].astype(F32)
        pos = pos[0:1] * 64.0 + pos[1:2]
        turn = jnp.broadcast_to(pos, (HD, rows)).T * angle[0:1, :]
        cos, sin = jnp.cos(turn), jnp.sin(turn) * angle[1:2, :]
        cos_out[at, :] = cos
        sin_out[at, :] = sin
        qkv = dot_nn(n, wqkv[...])

        def rotate(values):
            return (values * cos + pltpu.roll(values, HD // 2, 1) * sin).astype(BF)

        q_out[at, :] = rotate(qkv[:, :HD])
        k_out[at, :] = rotate(qkv[:, HD : 2 * HD])
        v_out[at, :] = qkv[:, 2 * HD :].astype(BF)
    for start in range(0, tokens, rows):
        at = pl.ds(start, rows)
        seen = start + rows
        s = dot_nt(q_out[at, :], k_out[:seen, :]) * scale_att
        row = lax.broadcasted_iota(jnp.int32, (rows, seen), 0) + start
        col = lax.broadcasted_iota(jnp.int32, (rows, seen), 1)
        s = jnp.where(col <= row, s, NEG_BIG)
        top = jnp.max(s, axis=1, keepdims=True)
        e = jnp.exp(s - top)
        total = jnp.sum(e, axis=1, keepdims=True)
        out = dot_nn((e / total).astype(BF), v_out[:seen, :])
        hf_out[at, :] = out
        hb[at, :] = out.astype(BF)
        lse_out[at, :] = jnp.broadcast_to(top + jnp.log(total), (rows, HD))

    exchange = lambda act: to_each(lambda b: shared.at[b], shared_out, n_f, n_c, (ss, sr, sl), act)

    def part_of(cc, q):
        return dot_nn(hb[piece(cc, rows), :], wo_all[:, piece(q, quarter)])

    fetch = pltpu.make_async_copy(hidden, own_og, os.at[3])
    fetch.start()
    total = reduce_seq(part_of, n_c, scratch[3 * n_s :])
    fetch.wait()
    resid = own_og[...].astype(F32) + total
    resid_out[...] = resid
    blk[...] = resid.astype(BF)
    res.start()
    res.line()
    exchange("start")
    grad.far(0)
    grad.far(1)
    res.other()
    res.far(0)
    res.far(1)
    for which in range(2):
        grad.arrived(which)
        res.arrived(which)
    exchange("wait")
    for copy in swaps + more:
        copy.wait()
    for step in range(1, n_c):
        for i, (src, dst) in enumerate(zip(sources(c), targets(f, c))):
            remote(src, dst, ws.at[step, i], wr.at[step, i], {"ctx": c}).wait_send()
    for step in range(n_c):
        for copy in across(step, f, lax.rem(c - step + n_c, n_c)):
            copy.wait_send()
    for item in (hid, grad, res):
        item.finish()
    grad.local().wait()
    res.local().wait()
    for copy in outs:
        copy.wait()


def first(n_c, n_f, n_t, mine, srows, hidden, wq, wk, wv, wo, og, weights, router, chosen, lines, shared, angle):
    rows, quarter = hidden.shape
    width = quarter * n_t
    seq = rows * n_c
    n_exp = mine * n_f * n_c
    ffe, half = weights[0].shape[1:]
    sds = jax.ShapeDtypeStruct
    part = wo.shape[1]
    n_small = 2 * n_exp + lines.shape[0]
    head, head_f = sds((seq, HD), BF), sds((seq, HD), F32)
    got = sds((mine, ffe, half), BF)
    return pl.pallas_call(
        functools.partial(first_kernel, n_c, n_f, n_exp, mine),
        out_shape=(
            sds((seq, width), BF),
            head,
            head,
            head,
            head_f,
            head_f,
            head_f,
            head_f,
            head_f,
            sds((rows, quarter), F32),
            sds((width, 3 * HD), BF),
            sds((HD, width), BF),
            sds((n_small, width), BF),
            sds((seq * n_f, width), BF),
            sds((n_f * n_c, n_t, rows, quarter), BF),
            sds((n_f * n_c, 3 * srows, part), BF),
            got,
            got,
            got,
        ),
        in_specs=[HBM] * 9 + [VMEM] * 7,
        out_specs=[VMEM] * 10 + [HBM] * 9,
        scratch_shapes=[
            pltpu.VMEM((seq, width), BF),
            pltpu.VMEM((width, 3 * HD), BF),
            pltpu.VMEM((HD, width), BF),
            pltpu.VMEM((n_small, width), BF),
            pltpu.VMEM((seq, HD), BF),
            pltpu.VMEM((rows, quarter), BF),
            pltpu.VMEM((rows, quarter), BF),
            pltpu.VMEM((n_small, part), BF),
            pltpu.VMEM((n_f * n_c, 3 * srows, part), BF),
            DMA((n_c, 5)),
            DMA((n_c, 5)),
            DMA((5,)),
            DMA((n_c, 3)),
            DMA((n_c, 3)),
            DMA((n_f * n_c,)),
            DMA((n_f * n_c,)),
            DMA(()),
            DMA((3, mine)),
            DMA((3, mine)),
            DMA((4,)),
        ]
        + spread_sems(n_c) * 3
        + reduce_seq_scratch(n_c, rows, quarter),
        compiler_params=pltpu.CompilerParams(
            collective_id=1, has_side_effects=True, vmem_limit_bytes=BIG
        ),
        cost_estimate=pl.CostEstimate(
            flops=5 << 30, bytes_accessed=300 << 20, transcendentals=1 << 20
        ),
        name="first",
    )(hidden, wq, wk, wv, wo, og, *weights, router, chosen, lines, *shared, angle)


def fetch_experts(n_c, n_f, mine, ffe, srows, hp, weights, shared, wgu, wd, sems):
    f = lax.axis_index("fsdp")
    wg0, wu0, wd0, wg1, wu1, wd1 = weights
    width = wd.shape[1]
    used = mine * ffe
    part = width // (n_f * n_c)
    half = width // n_f
    copies = []

    def add(src, dst):
        copies.append(pltpu.make_async_copy(src, dst, sems.at[len(copies)]))

    for i, (kept, got) in enumerate(((wg0, wg1), (wu0, wu1), (wd0, wd1))):
        dst, base = ((wgu, 0), (wgu, hp), (wd, 0))[i]
        for e in range(mine):
            at = pl.ds(base + e * ffe, ffe)
            add(kept.at[f * mine + e], dst.at[at, piece(f, half)])
            add(got.at[e], dst.at[at, piece(1 - f, half)])
        for b in range(n_f * n_c):
            add(
                shared.at[b, pl.ds(i * srows, srows), :],
                dst.at[pl.ds(base + used, srows), pl.ds(b * part, part)],
            )
    return copies


def blank_rows(rows_used, hp, wgu, wd):
    blank = jnp.zeros((hp - rows_used, wd.shape[1]), BF)
    wgu[rows_used:hp, :] = blank
    wgu[hp + rows_used :, :] = blank
    wd[rows_used:, :] = blank


def gates(prob, picked, first, mine, ffe, hp):
    block, n_exp = prob.shape
    lane = lax.broadcasted_iota(jnp.int32, (block, n_exp), 1)
    gated = prob * picked
    col = lax.broadcasted_iota(jnp.int32, (block, hp), 1)
    gate = jnp.ones((block, hp), F32)
    for k in range(mine):
        g = jnp.sum(jnp.where(lane == first + k, gated, 0.0), axis=1, keepdims=True)
        gate = jnp.where((col >= k * ffe) & (col < (k + 1) * ffe), g, gate)
    return gate, lane, col


def reducer_scratch(n_f, n_c, rows, quarter):
    n_b = n_f * n_c
    blocks = lambda *lead: pltpu.VMEM(lead + (rows, quarter), BF)
    return [
        blocks(n_b, 2),
        blocks(n_b, 2),
        blocks(n_b, 2),
        blocks(n_b),
        blocks(n_b),
        blocks(n_c),
        blocks(n_c),
        pltpu.VMEM((n_c, rows, quarter), F32),
        blocks(n_c),
        blocks(n_c),
    ] + [DMA((n_b,))] * 4 + [DMA((n_c,))] * 4


class Reducer:
    def __init__(self, n_c, scratch):
        self.n_c = n_c
        (self.out1, self.in1, self.own, self.out2, self.in2, self.out3, self.in3, self.acc,
         self.out4, self.in4, self.s1, self.r1, self.s2, self.r2, self.s3, self.r3, self.s4, self.r4) = scratch
        self.f, self.c, self.t = ranks()
        self.far, self.sib = opposite(self.t), sibling(self.t)

    def row_block(self, i):
        n_c = self.n_c
        group = jnp.where(i < n_c, 1 - self.f, self.f)
        return group * n_c + lax.rem(self.c + lax.rem(i, n_c) + 1, n_c)

    def core_copy(self, i):
        return remote(self.out1.at[i], self.in1.at[i], self.s1.at[i], self.r1.at[i], {"tp": self.sib})

    def far_copy(self, i):
        return remote(self.out2.at[i], self.in2.at[i], self.s2.at[i], self.r2.at[i], {"tp": self.far})

    def other_copy(self, j):
        return remote(self.out3.at[j], self.in3.at[j], self.s3.at[j], self.r3.at[j], {"fsdp": 1 - self.f})

    def line_copy(self, j, to):
        return remote(self.out4.at[j], self.in4.at[j], self.s4.at[j], self.r4.at[j], {"ctx": to})

    def put(self, i, part_of):
        self.out1[i, 0] = part_of(opposite(self.sib)).astype(BF)
        self.out1[i, 1] = part_of(self.sib).astype(BF)
        self.core_copy(i).start()
        self.own[i, 0] = part_of(self.far).astype(BF)
        self.own[i, 1] = part_of(self.t).astype(BF)

    def over(self, i):
        self.core_copy(i).wait()
        self.out2[i] = (self.own[i, 0].astype(F32) + self.in1[i, 0].astype(F32)).astype(BF)
        self.far_copy(i).start()

    def _sum(self, i):
        self.far_copy(i).wait()
        return self.own[i, 1].astype(F32) + self.in1[i, 1].astype(F32) + self.in2[i].astype(F32)

    def after_other(self, i):
        self.out3[i] = self._sum(i).astype(BF)
        self.other_copy(i).start()

    def after_own(self, i):
        self.acc[i - self.n_c] = self._sum(i)

    def along(self, j):
        self.other_copy(j).wait()
        total = self.acc[j] + self.in3[j].astype(F32)
        if j < self.n_c - 1:
            self.out4[j] = total.astype(BF)
            self.line_copy(j, lax.rem(self.c + j + 1, self.n_c)).start()
        return total

    def total(self, total):
        for j in range(self.n_c - 1):
            self.line_copy(j, self.c).wait()
            total = total + self.in4[j].astype(F32)
        return total

    def loop(self, n_b, compute):
        n_c = self.n_c

        def step(i, carry):
            def between():
                @pl.when(i >= 1)
                def _():
                    self.over(i - 1)

                @pl.when((i >= 3) & (i < 3 + n_c))
                def _():
                    self.after_other(i - 3)

                @pl.when(i >= 3 + n_c)
                def _():
                    self.after_own(i - 3)

            compute(i, between)
            return carry

        lax.fori_loop(0, n_b, step, 0)

    def drain(self, n_b, works):
        works = list(works)
        self.over(n_b - 1)
        for i in range(n_b - 4, n_b):
            if i > n_b - 4:
                self.after_own(i) if i >= self.n_c else self.after_other(i)
            if i >= self.n_c:
                total = self.along(i - self.n_c)
            if works:
                works.pop(0)()
        for work in works:
            work()
        return self.total(total)


def forward_kernel(
    n_c, n_f, mine, ffe, srows, hp, rows_all, og_all, resid, small,
    wg0, wu0, wd0, wg1, wu1, wd1, shared,
    layer_out, in_out, act_out, silu_out, slope_out, r_out, prob_out, keep_out, send_out, shared_out,
    gt, wsem, xsem, nsem, asem, tsem, osem, *scratch,
):
    f, c, t = ranks()
    n_b = n_f * n_c
    rows, quarter = resid.shape
    width = rows_all.shape[1]
    routed = mine * ffe
    rows_used = routed + srows
    n_exp = mine * n_b
    red = Reducer(n_c, scratch)

    def blocks_phase(wgu, wd, xs, ns, acts):
        fetches = fetch_experts(
            n_c, n_f, mine, ffe, srows, hp, (wg0, wu0, wd0, wg1, wu1, wd1), shared, wgu, wd, wsem
        )
        for copy in fetches:
            copy.start()

        def load(i, slot):
            return pltpu.make_async_copy(
                rows_all.at[piece(red.row_block(i), rows), :], xs.at[slot], xsem.at[slot]
            )

        def stores(i, slot):
            at = piece(red.row_block(i), rows)
            return [pltpu.make_async_copy(ns.at[slot], in_out.at[at, :], nsem.at[slot])] + [
                pltpu.make_async_copy(acts.at[slot, k], out.at[at, :], asem.at[slot, k])
                for k, out in enumerate((act_out, silu_out, slope_out))
            ]

        load(0, 0).start()
        blank_rows(rows_used, hp, wgu, wd)
        greet([{"tp": red.sib}, {"tp": red.far}, {"fsdp": 1 - f}] + line_peers(c, n_c))
        for copy in fetches:
            copy.wait()

        def compute(i, between):
            slot = lax.rem(i, 2)
            b = red.row_block(i)
            at = piece(b, rows)
            load(i, slot).wait()

            @pl.when(i + 1 < n_b)
            def _():
                load(i + 1, 1 - slot).start()

            @pl.when(i >= 2)
            def _():
                for copy in stores(i - 2, slot):
                    copy.wait()

            h = xs[slot].astype(F32)
            r = lax.rsqrt(jnp.sum(h * h, axis=1, keepdims=True) / width + EPS)
            r_out[at, :] = jnp.broadcast_to(r, (rows, HD))
            gain = small[2 * n_exp + 1 : 2 * n_exp + 2, :].astype(F32)
            n = (h * r * gain).astype(BF)
            ns[slot] = n
            logits = dot_nt(n, small[:n_exp, :])
            e = jnp.exp(logits - jnp.max(logits, axis=1, keepdims=True))
            prob = e / jnp.sum(e, axis=1, keepdims=True)
            prob_out[at, :] = prob
            gate, _, _ = gates(prob, small[n_exp : 2 * n_exp, at].astype(F32).T, (c * n_f + f) * mine, mine, ffe, hp)
            ab = dot_nt(n, wgu[...])
            between()
            a, up = ab[:, :hp], ab[:, hp:]
            sig = 1.0 / (1.0 + jnp.exp(-a))
            silu = a * sig
            act = (silu * up).astype(BF)
            acts[slot, 0] = act
            acts[slot, 1] = silu.astype(BF)
            acts[slot, 2] = (up * (sig * (1.0 + a * (1.0 - sig)))).astype(BF)
            actg = (act.astype(F32) * gate).astype(BF)
            gt[:, at] = actg.T[:rows_used, :]
            for copy in stores(i, slot):
                copy.start()
            red.put(i, lambda q: dot_nn(actg, wd[:, piece(q, quarter)]))

        red.loop(n_b, compute)
        for i in range(n_b - 2, n_b):
            for copy in stores(i, i % 2):
                copy.wait()

    pl.run_scoped(
        blocks_phase,
        pltpu.VMEM((2 * hp, width), BF),
        pltpu.VMEM((hp, width), BF),
        pltpu.VMEM((2, rows, width), BF),
        pltpu.VMEM((2, rows, width), BF),
        pltpu.VMEM((2, 3, rows, hp), BF),
    )

    def grads_phase(tiles, keeps, sends, shs):
        def tile_of(s):
            return (1 - f) * 2 + s if s < 2 else f * 2 + s - 2

        def tile_load(s):
            return pltpu.make_async_copy(og_all.at[:, tile_of(s)], tiles.at[s % 2], tsem.at[s % 2])

        def out_copies(s):
            cols = pl.ds(s % 2 * quarter, quarter)
            if s < 2:
                src, dst = sends.at[s], send_out.at[:, :, cols]
            else:
                src, dst = keeps.at[s - 2], keep_out.at[:, :, cols]
            return [
                pltpu.make_async_copy(src, dst, osem.at[s, 0]),
                pltpu.make_async_copy(
                    shs.at[s], shared_out.at[:, piece(tile_of(s), quarter)], osem.at[s, 1]
                ),
            ]

        def work(s):
            def run():
                tile_load(s).wait()
                if s < 3:
                    tile_load(s + 1).start()
                g = dot_nn(gt[...], tiles[s % 2].reshape(n_b * rows, quarter))
                if s < 2:
                    sends[s] = g[:routed].astype(BF).reshape(mine, ffe, quarter)
                else:
                    keeps[s - 2] = g[:routed].astype(BF).reshape(mine, ffe, quarter)
                shs[s] = g[routed:].astype(BF)
                for copy in out_copies(s):
                    copy.start()

            return run

        tile_load(0).start()
        total = red.drain(n_b, [work(s) for s in range(4)])
        layer_out[...] = (resid[...] + total).astype(BF)
        for s in range(4):
            for copy in out_copies(s):
                copy.wait()

    pl.run_scoped(
        grads_phase,
        pltpu.VMEM((2, n_b, rows, quarter), BF),
        pltpu.VMEM((2, mine, ffe, quarter), BF),
        pltpu.VMEM((2, mine, ffe, quarter), BF),
        pltpu.VMEM((4, srows, quarter), BF),
    )


def expert_sizes(n_c, n_f, n_t, mine, ffe, srows, width):
    used = mine * ffe + srows
    return used, -(-used // HD) * HD, 3 * (2 * mine + n_f * n_c)


def forward(n_c, n_f, n_t, mine, ffe, srows, rows_all, og_all, resid, small, kept, got, shared):
    total, width = rows_all.shape
    rows, quarter = resid.shape
    n_b = n_f * n_c
    n_exp = mine * n_b
    used, hp, n_fetch = expert_sizes(n_c, n_f, n_t, mine, ffe, srows, width)
    sds = jax.ShapeDtypeStruct
    return pl.pallas_call(
        functools.partial(forward_kernel, n_c, n_f, mine, ffe, srows, hp),
        out_shape=(
            sds((rows, quarter), BF),
            sds((total, width), BF),
            sds((total, hp), BF),
            sds((total, hp), BF),
            sds((total, hp), BF),
            sds((total, HD), F32),
            sds((total, n_exp), F32),
            sds((mine, ffe, width // n_f), BF),
            sds((mine, ffe, width // n_f), BF),
            sds((srows, width), BF),
        ),
        in_specs=[HBM, HBM, VMEM, VMEM] + [HBM] * 7,
        out_specs=[VMEM, HBM, HBM, HBM, HBM, VMEM, VMEM, HBM, HBM, HBM],
        scratch_shapes=[
            pltpu.VMEM((used, total), BF),
            DMA((n_fetch,)),
            DMA((2,)),
            DMA((2,)),
            DMA((2, 3)),
            DMA((2,)),
            DMA((4, 2)),
        ]
        + reducer_scratch(n_f, n_c, rows, quarter),
        compiler_params=pltpu.CompilerParams(
            collective_id=5, has_side_effects=True, vmem_limit_bytes=BIG
        ),
        cost_estimate=pl.CostEstimate(
            flops=8 * total * width * used, bytes_accessed=80 << 20, transcendentals=total * used
        ),
        name="forward",
    )(rows_all, og_all, resid, small, *kept, *got, shared)


def backward_kernel(
    n_c, n_f, mine, ffe, srows, hp, og_all, act, silu, slope, moe_in, r_all, shared_d, prob_in, small,
    resid, og, wg0, wu0, wd0, wg1, wu1, wd1, shared,
    mid_out, gain_out, seq_out, shared_out, shs_out, kg_out, ku_out, gg_out, gu_out, lg_out, lu_out,
    gt, blk, r_own, sends, shs, wsem, xsem, tsem, ksem, ss, sr, rs, es, ds, dr, dl, *rest,
):
    f, c, t = ranks()
    n_b = n_f * n_c
    rows, quarter = resid.shape
    width = shared_d.shape[1]
    n_exp = mine * n_b
    routed = mine * ffe
    rows_used = routed + srows
    first = (c * n_f + f) * mine
    red = Reducer(n_c, rest[:18])

    cols = width // n_b

    def exchange(act):
        to_each(lambda b: shared_d.at[:, piece(b, cols)], shared_out, n_f, n_c, (ds, dr, dl), act)

    def blocks_phase(wgu, wd, ogs, acts):
        fetches = fetch_experts(
            n_c, n_f, mine, ffe, srows, hp, (wg0, wu0, wd0, wg1, wu1, wd1), shared, wgu, wd, wsem
        )
        for copy in fetches:
            copy.start()

        def loads(i, slot):
            b = red.row_block(i)
            return [
                pltpu.make_async_copy(
                    og_all.at[b, q], ogs.at[slot, :, pl.ds(q * quarter, quarter)], xsem.at[slot, q]
                )
                for q in range(4)
            ] + [
                pltpu.make_async_copy(src.at[piece(b, rows), :], acts.at[slot, k], xsem.at[slot, 4 + k])
                for k, src in enumerate((act, silu, slope))
            ]

        for copy in loads(0, 0):
            copy.start()
        blank_rows(rows_used, hp, wgu, wd)
        greet([{"tp": red.sib}, {"tp": red.far}, {"tp": opposite(red.sib)}] + each_peers(f, c, n_f, n_c))
        exchange("start")
        for copy in fetches:
            copy.wait()

        def compute(i, between):
            slot = lax.rem(i, 2)
            at = piece(red.row_block(i), rows)
            for copy in loads(i, slot):
                copy.wait()

            @pl.when(i + 1 < n_b)
            def _():
                for copy in loads(i + 1, 1 - slot):
                    copy.start()

            prob = prob_in[at, :]
            chosen = small[n_exp : 2 * n_exp, at].astype(F32).T
            gate, lane, col = gates(prob, chosen, first, mine, ffe, hp)
            dh = dot_nt(ogs[slot], wd[...])
            between()
            ad = acts[slot, 0].astype(F32) * dh
            p_grad = jnp.zeros(prob.shape, F32)
            for k in range(mine):
                s = jnp.sum(
                    jnp.where((col >= k * ffe) & (col < (k + 1) * ffe), ad, 0.0), axis=1, keepdims=True
                )
                p_grad = jnp.where(lane == first + k, s, p_grad)
            p_grad = p_grad * chosen
            logit_f = prob * (p_grad - jnp.sum(prob * p_grad, axis=1, keepdims=True))
            logit_grad = logit_f.astype(BF)
            dg = dh * gate
            da = (dg * acts[slot, 2].astype(F32)).astype(BF)
            db = (dg * acts[slot, 1].astype(F32)).astype(BF)
            gt[:rows_used, at] = da.T[:rows_used, :]
            gt[rows_used : 2 * rows_used, at] = db.T[:rows_used, :]
            gt[2 * rows_used :, at] = logit_f.T.astype(BF)
            dab = jnp.concatenate([da, db], axis=1)

            def part_of(q):
                cols = piece(q, quarter)
                return dot_nn(dab, wgu[:, cols]) + dot_nn(logit_grad, small[:n_exp, cols])

            red.put(i, part_of)

        red.loop(n_b, compute)

    pl.run_scoped(
        blocks_phase,
        pltpu.VMEM((2 * hp, width), BF),
        pltpu.VMEM((hp, width), BF),
        pltpu.VMEM((2, rows, width), BF),
        pltpu.VMEM((2, 3, rows, hp), BF),
    )

    def send_copy(s, m):
        if s:
            return pltpu.make_async_copy(sends.at[s, m], (lg_out, lu_out)[m], ss.at[s, m])
        return remote(sends.at[s, m], (gg_out, gu_out)[m], ss.at[s, m], sr.at[m], {"fsdp": 1 - f})

    def grads_phase(tiles, keeps):
        def tile_of(s):
            return (1 - f) * 2 + s if s < 2 else f * 2 + s - 2

        def tile_load(s):
            return pltpu.make_async_copy(
                moe_in.at[:, piece(tile_of(s), quarter)], tiles.at[s % 2], tsem.at[s % 2]
            )

        def keep_copy(s, m):
            dst = (kg_out, ku_out)[m].at[:, :, pl.ds((s - 2) * quarter, quarter)]
            return pltpu.make_async_copy(keeps.at[s - 2, m], dst, ksem.at[s - 2, m])

        def work(s):
            def run():
                tile_load(s).wait()
                if s < 3:
                    tile_load(s + 1).start()
                g = dot_nn(gt[...], tiles[s % 2])
                cols = piece(tile_of(s), quarter)
                for m in range(2):
                    base = m * rows_used
                    if s < 2:
                        sends[s, m] = g[base : base + routed].astype(BF).reshape(mine, ffe, quarter)
                        send_copy(s, m).start()
                    else:
                        keeps[s - 2, m] = g[base : base + routed].astype(BF).reshape(mine, ffe, quarter)
                        keep_copy(s, m).start()
                    shs[m * srows : (m + 1) * srows, cols] = g[base + routed : base + rows_used].astype(BF)
                shs[2 * srows :, cols] = g[2 * rows_used :].astype(BF)

            return run

        tile_load(0).start()
        blk[...] = red.drain(n_b, [work(s) for s in range(4)])
        for s in (2, 3):
            for m in range(2):
                keep_copy(s, m).wait()

    fetch = pltpu.make_async_copy(r_all.at[piece(f * n_c + c, rows), :], r_own, rs)
    fetch.start()
    pl.run_scoped(
        grads_phase,
        pltpu.VMEM((2, n_b * rows, quarter), BF),
        pltpu.VMEM((2, 2, mine, ffe, quarter), BF),
    )
    shs_copy = pltpu.make_async_copy(shs, shs_out, es)
    shs_copy.start()
    fetch.wait()
    gain = small[2 * n_exp + 1 : 2 * n_exp + 2, piece(t, quarter)].astype(F32)
    back, gain_part = norm_grad(resid[...], r_own[:, :1], gain, blk[...], width, *rest[18:22])
    gain_out[...] = jnp.broadcast_to(gain_part, gain_out.shape)
    grad = og[...].astype(F32) + back
    mid_out[...] = grad
    own = rest[22]
    own[...] = grad.astype(BF)

    def place(g, cc, tt):
        return seq_out.at[piece(cc, rows), piece(tt, quarter)]

    sequence = Spread(own, place, n_c, False, rest[23:])
    sequence.start()
    sequence.line()
    sequence.far(0)
    sequence.arrived(0)
    sequence.finish()
    sequence.local().wait()
    exchange("wait")
    shs_copy.wait()
    for s in range(2):
        for m in range(2):
            send_copy(s, m).wait()


def backward(
    n_c, n_f, n_t, mine, ffe, srows, og_all, act, silu, slope, moe_in, r_all, shared_d, prob, small,
    resid, og, kept, got, shared,
):
    total, width = moe_in.shape
    rows, quarter = resid.shape
    n_b = n_f * n_c
    n_exp = mine * n_b
    used, hp, n_fetch = expert_sizes(n_c, n_f, n_t, mine, ffe, srows, width)
    sds = jax.ShapeDtypeStruct
    kept_g = sds((mine, ffe, width // n_f), BF)
    sent_g = sds((mine, ffe, quarter), BF)
    return pl.pallas_call(
        functools.partial(backward_kernel, n_c, n_f, mine, ffe, srows, hp),
        out_shape=(
            sds((rows, quarter), F32),
            sds((8, quarter), F32),
            sds((rows * n_c, width), BF),
            sds((n_b, srows, width // n_b), BF),
            sds((2 * srows + n_exp, width), BF),
            kept_g,
            kept_g,
            sent_g,
            sent_g,
            sent_g,
            sent_g,
        ),
        in_specs=[HBM] * 7 + [VMEM] * 4 + [HBM] * 7,
        out_specs=[VMEM, VMEM] + [HBM] * 9,
        scratch_shapes=[
            pltpu.VMEM((2 * used + n_exp, total), BF),
            pltpu.VMEM((rows, quarter), F32),
            pltpu.VMEM((rows, HD), F32),
            pltpu.VMEM((2, 2, mine, ffe, quarter), BF),
            pltpu.VMEM((2 * srows + n_exp, width), BF),
            DMA((n_fetch,)),
            DMA((2, 7)),
            DMA((2,)),
            DMA((2, 2)),
            DMA((2, 2)),
            DMA((2,)),
            DMA(()),
            DMA(()),
            DMA((n_b,)),
            DMA((n_b,)),
            DMA(()),
        ]
        + reducer_scratch(n_f, n_c, rows, quarter)
        + norm_grad_scratch(rows)
        + [pltpu.VMEM((rows, quarter), BF)]
        + spread_sems(n_c),
        compiler_params=pltpu.CompilerParams(
            collective_id=3, has_side_effects=True, vmem_limit_bytes=BIG
        ),
        cost_estimate=pl.CostEstimate(
            flops=10 * total * width * used, bytes_accessed=200 << 20, transcendentals=0
        ),
        name="backward",
    )(
        og_all, act, silu, slope, moe_in, r_all, shared_d, prob, small, resid, og,
        *kept, *got, shared,
    )


def finish_kernel(n_plain, f_ref, *refs):
    ga, gb, ua, ub, d, kg, ku, kd, shared = refs[:9]
    plain = refs[9 : 9 + n_plain]
    og, ou, od, shared_out = refs[9 + n_plain : 13 + n_plain]
    step = pl.program_id(0)
    f = f_ref[0]
    n_e = kg.shape[0]

    def put(at):
        for keep, out in ((kg, og), (ku, ou), (kd, od)):
            out[at : at + n_e] = keep[...].astype(F32)
        for out, halves in ((og, (ga, gb)), (ou, (ua, ub))):
            @pl.when(step < 2)
            def _():
                out[n_e - at : 2 * n_e - at] = halves[0][...].astype(F32)

            @pl.when(step >= 2)
            def _():
                out[n_e - at : 2 * n_e - at] = halves[1][...].astype(F32)

        od[n_e - at : 2 * n_e - at] = d[...].astype(F32)

    @pl.when(f == 0)
    def _():
        put(0)

    @pl.when(f != 0)
    def _():
        put(n_e)

    own = shared_out.shape[0] // shared.shape[0]
    for b in range(shared.shape[0]):
        shared_out[b * own : (b + 1) * own, :] = shared[b, :own, :].astype(F32)
    for src, dst in zip(plain, refs[13 + n_plain :]):
        dst[...] = src[...]


def finish(f_rank, own_shared, arrived, kept, shared, plain):
    mine, ffe, quarter = arrived[0].shape
    half = kept[0].shape[2]
    tile = half // 4
    n_b, srows, part = shared.shape
    first = pl.BlockSpec((mine, ffe, tile), lambda i, f: (0, 0, jnp.minimum(i, 1)))
    second = pl.BlockSpec((mine, ffe, tile), lambda i, f: (0, 0, jnp.maximum(i - 2, 0)))
    every = pl.BlockSpec((mine, ffe, tile), lambda i, f: (0, 0, i))
    out = pl.BlockSpec((2 * mine, ffe, tile), lambda i, f: (0, 0, i))

    def rows_of(x):
        if x.shape[0] % 64:
            return pl.BlockSpec(x.shape, lambda i, f: (0, 0))
        return pl.BlockSpec((x.shape[0] // 4, x.shape[1]), lambda i, f: (i, 0))

    shared_grad = jax.ShapeDtypeStruct((n_b * own_shared, part), F32)
    return pl.pallas_call(
        functools.partial(finish_kernel, len(plain)),
        grid_spec=pltpu.PrefetchScalarGridSpec(
            num_scalar_prefetch=1,
            grid=(4,),
            in_specs=[first, second, first, second, every]
            + [every] * 3
            + [pl.BlockSpec((n_b // 4, srows, part), lambda i, f: (i, 0, 0))]
            + [rows_of(x) for x in plain],
            out_specs=[out] * 3 + [rows_of(shared_grad)] + [rows_of(x) for x in plain],
        ),
        out_shape=tuple(jax.ShapeDtypeStruct((2 * mine, ffe, half), F32) for k in kept)
        + (shared_grad,)
        + tuple(jax.ShapeDtypeStruct(x.shape, x.dtype) for x in plain),
        compiler_params=pltpu.CompilerParams(vmem_limit_bytes=BIG),
        name="finish",
    )(f_rank, *arrived, *kept, shared, *plain)


def norm_grad(values, r, gain, grad, width, out, into, send, recv):
    f, c, t = ranks()
    rows = values.shape[0]
    local = jnp.sum(grad * gain * values, axis=1, keepdims=True)
    out[...] = jnp.broadcast_to(local, (rows, HD)).T[:8, :]
    peers = [sibling(t), opposite(t), opposite(sibling(t))]
    copies = [
        remote(out, into.at[i], send.at[i], recv.at[i], {"tp": peer}) for i, peer in enumerate(peers)
    ]
    for copy in copies:
        copy.start()
    gain_part = jnp.sum(grad * values * r, axis=0, keepdims=True)
    total = out[...]
    for i, copy in enumerate(copies):
        copy.wait()
        total = total + into[i]
    total = jnp.broadcast_to(total[0:1, :], (HD, rows)).T[:, :1]
    return r * gain * grad - values * (r * r * r * (total / width)), gain_part


def norm_grad_scratch(rows):
    return [
        pltpu.VMEM((8, rows), F32),
        pltpu.VMEM((3, 8, rows), F32),
        DMA((3,)),
        DMA((3,)),
    ]


def attend_back(block, mid, wo, q, k, v, hf, lse, cosine, sine, dqkv, hg, dq, dk, dv):
    seq = mid.shape[0]
    scale_att = HD ** (-0.5)
    for start in range(0, seq, block):
        at = pl.ds(start, block)
        hg[at, :] = dot_nt(mid[at, :], wo[...]).astype(BF)
    dk[...] = jnp.zeros_like(dk)
    dv[...] = jnp.zeros_like(dv)
    for start in range(0, seq, block):
        at = pl.ds(start, block)
        seen = start + block
        qb, hb = q[at, :], hg[at, :]
        delta = jnp.sum(hb.astype(F32) * hf[at, :], axis=1, keepdims=True)
        s = dot_nt(qb, k[:seen, :]) * scale_att
        row = lax.broadcasted_iota(jnp.int32, (block, seen), 0) + start
        col = lax.broadcasted_iota(jnp.int32, (block, seen), 1)
        p = jnp.where(col <= row, jnp.exp(s - lse[at, :1]), 0.0)
        ds = (p * (dot_nt(hb, v[:seen, :]) - delta)).astype(BF)
        dq[at, :] = dot_nn(ds, k[:seen, :]) * scale_att
        dk[:seen, :] += dot_tn(ds, qb) * scale_att
        dv[:seen, :] += dot_tn(p.astype(BF), hb)

    def rotate(values, at):
        return (values * cosine[at, :] - pltpu.roll(values, HD // 2, 1) * sine[at, :]).astype(BF)

    for start in range(0, seq, block):
        at = pl.ds(start, block)
        dqkv[at, :HD] = rotate(dq[at, :], at)
        dqkv[at, HD : 2 * HD] = rotate(dk[at, :], at)
        dqkv[at, 2 * HD :] = dv[at, :].astype(BF)


def last_kernel(
    n_c, n_f, n_t, n_exp, own_shared, mid_seq, wo, q, k, v, hf, lse, cosine, sine, normed, wqkv, hidden, r_all,
    small, mid_grad, gain2, shs, lg, lu,
    in_out, gq, gk, gv, go, gains_out, router_out, sg_out, su_out, lg_out, lu_out,
    dqkv, hg, dq, dk, dv, gattn, shs_in, rpart, hs, hr, hl, es, er, rin, rss, rsr, r_own, mine, inx, own, outz, inz, gsend, gin, rs, sx, rx, lx, sz, rz, gs, gr, *rest,
):
    f, c, t = ranks()
    rows, quarter = hidden.shape
    tokens, width = normed.shape
    part = width // (n_f * n_c)
    here = f * n_c + c
    srows = (shs.shape[0] - n_exp) // 2
    others = []
    for df in range(n_f):
        for dc in range(n_c):
            for dt in range(n_t):
                if df or dc or dt:
                    others.append(
                        {
                            "fsdp": lax.rem(f + df, n_f),
                            "ctx": lax.rem(c + dc, n_c),
                            "tp": lax.rem(t + dt, n_t),
                        }
                    )
    gin[...] = jnp.zeros_like(gin)
    greet(others)
    order = [2, 1, 3, 0] if n_c == 4 else list(range(1, n_c)) + [0]

    def cross(d):
        cc = lax.rem(c + d, n_c)
        return remote(
            gattn.at[:, piece((1 - f) * n_c + cc, part)], inx.at[d], sx.at[d], rx.at[d], {"fsdp": 1 - f}
        )

    def keep(d):
        cc = lax.rem(c + d, n_c)
        return pltpu.make_async_copy(gattn.at[:, piece(f * n_c + cc, part)], own.at[d], lx.at[d])

    def line(d, to):
        return remote(outz.at[d], inz.at[d], sz.at[d], rz.at[d], {"ctx": to})

    router_copies = [
        remote(rpart, rin.at[i], rss.at[i], rsr.at[i], {"tp": peer})
        for i, peer in enumerate([sibling(t), opposite(t), opposite(sibling(t))])
    ]
    shared = lambda act: to_each(lambda b: shs.at[:, piece(b, part)], shs_in, n_f, n_c, (hs, hr, hl), act)
    late = [
        remote(src, dst, es.at[i], er.at[i], {"fsdp": 1 - f})
        for i, (src, dst) in enumerate(((lg, lg_out), (lu, lu_out)))
    ]
    shared("start")
    fetch = pltpu.make_async_copy(r_all.at[piece(c, rows), :], r_own, rs)
    fetch.start()
    for copy in late:
        copy.start()
    attend_back(rows, mid_seq, wo, q, k, v, hf, lse, cosine, sine, dqkv, hg, dq, dk, dv)
    gattn[3 * HD :, :] = dot_tn(hf[...].astype(BF), mid_seq[...]).astype(BF)

    def weights():
        gattn[: 3 * HD, :] = dot_tn(dqkv[...], normed[...]).astype(BF)
        for d in order:
            cross(d).start()
            keep(d).start()


    def part_of(cc, q):
        return dot_nt(dqkv[piece(cc, rows), :], wqkv[piece(q, quarter), :])

    def pass_weights():
        for d in order:
            cross(d).wait()
            keep(d).wait()
            both = own[d].astype(F32) + inx[d].astype(F32)
            if d:
                outz[d] = both.astype(BF)
                line(d, lax.rem(c + d, n_c)).start()
            else:
                mine[...] = both

    total = reduce_seq(part_of, n_c, rest[:13], weights, pass_weights)
    fetch.wait()
    gain = small[2 * n_exp : 2 * n_exp + 1, piece(t, quarter)].astype(F32)
    back, gain_part = norm_grad(
        hidden[...].astype(F32), r_own[:, :1], gain, total, width, *rest[13:17]
    )
    in_out[...] = mid_grad[...] + back

    gsend[0:1, :] = gain_part
    gsend[1:2, :] = gain2[0:1, :]
    gsend[2:, :] = jnp.zeros((6, quarter), F32)
    per = quarter // part
    holder = here // per
    def gain_copy(h, tt):
        b = t * per + h
        return remote(
            gsend.at[:, pl.ds(h * part, part)],
            gin.at[here],
            gs.at[h * n_t + tt],
            gr.at[here],
            {"fsdp": b // n_c, "ctx": lax.rem(b, n_c), "tp": jnp.int32(tt)},
        )

    def is_me(h, tt):
        return (t * per + h == here) & (t == tt)

    for h in range(per):
        for tt in range(n_t):

            @pl.when(jnp.logical_not(is_me(h, tt)))
            def _():
                gain_copy(h, tt).start()

    def put(src, block):
        at = piece(src, HD)
        for i, ref in enumerate((gq, gk, gv)):
            ref[:, at] = block[i * HD : (i + 1) * HD, :].T
        go[at, :] = block[3 * HD :, :]

    shared("wait")
    rpart[...] = jnp.sum(shs_in[:, 2 * srows :, :].astype(F32), axis=0)
    for copy in router_copies:
        copy.start()
    for b in range(n_f * n_c):
        at = pl.ds(b * own_shared, own_shared)
        sg_out[at, :] = shs_in[b, :own_shared, :].astype(F32)
        su_out[at, :] = shs_in[b, srows : srows + own_shared, :].astype(F32)
    put(c, mine[...])
    for d in order[:-1]:
        line(d, c).wait()
        put(lax.rem(c - d + n_c, n_c), inz[d].astype(F32))
    for h in range(per):
        for tt in range(n_t):

            @pl.when(jnp.logical_not(is_me(h, tt)))
            def _():
                gain_copy(h, tt).wait_send()

    for b in range(n_f * n_c):

        @pl.when((b != here) | (holder != t))
        def _():
            remote(gin.at[b], gin.at[b], gs.at[0], gr.at[b], {"tp": sibling(t)}).wait_recv()

    own_part = jnp.where(
        holder == t,
        gsend[:, piece(lax.rem(here, per), part)],
        jnp.zeros((8, part), F32),
    )
    gains_out[...] = own_part + jnp.sum(gin[...], axis=0)
    for copy in router_copies + late:
        copy.wait()
    router_out[...] = rpart[...] + jnp.sum(rin[...], axis=0)


def last(
    n_c, n_f, n_t, n_exp, own_shared, mid_seq, wo, q, k, v, hf, lse, cosine, sine, normed, wqkv, hidden, r_all,
    small, mid_grad, gain2, shs, lg, lu,
):
    rows, quarter = hidden.shape
    seq, width = normed.shape
    part = width // (n_f * n_c)
    sds = jax.ShapeDtypeStruct
    slab = pltpu.VMEM((n_c, 4 * HD, part), BF)
    head_f = pltpu.VMEM((seq, HD), F32)
    shared_grad = sds((n_f * n_c * own_shared, part), F32)
    return pl.pallas_call(
        functools.partial(last_kernel, n_c, n_f, n_t, n_exp, own_shared),
        out_shape=(
            sds((rows, quarter), F32),
            sds((part, n_c * HD), F32),
            sds((part, n_c * HD), F32),
            sds((part, n_c * HD), F32),
            sds((n_c * HD, part), F32),
            sds((8, part), F32),
            sds((n_exp, part), F32),
            shared_grad,
            shared_grad,
            sds(lg.shape, BF),
            sds(lu.shape, BF),
        ),
        in_specs=[VMEM] * 12 + [HBM] + [VMEM] * 3 + [HBM] * 3,
        out_specs=[VMEM] * 9 + [HBM] * 2,
        scratch_shapes=[
            pltpu.VMEM((seq, 3 * HD), BF),
            pltpu.VMEM((seq, HD), BF),
            head_f,
            head_f,
            head_f,
            pltpu.VMEM((4 * HD, width), BF),
            pltpu.VMEM((n_f * n_c, shs.shape[0], part), BF),
            pltpu.VMEM((n_exp, part), F32),
            DMA((n_f * n_c,)),
            DMA((n_f * n_c,)),
            DMA(()),
            DMA((2,)),
            DMA((2,)),
            pltpu.VMEM((3, n_exp, part), F32),
            DMA((3,)),
            DMA((3,)),
            pltpu.VMEM((rows, HD), F32),
            pltpu.VMEM((4 * HD, part), F32),
            slab,
            slab,
            slab,
            slab,
            pltpu.VMEM((8, quarter), F32),
            pltpu.VMEM((n_f * n_c, 8, part), F32),
            DMA(()),
            DMA((n_c,)),
            DMA((n_c,)),
            DMA((n_c,)),
            DMA((n_c,)),
            DMA((n_c,)),
            DMA((quarter // part * n_t,)),
            DMA((n_f * n_c,)),
        ]
        + reduce_seq_scratch(n_c, rows, quarter)
        + norm_grad_scratch(rows),
        compiler_params=pltpu.CompilerParams(
            collective_id=4, has_side_effects=True, vmem_limit_bytes=BIG
        ),
        cost_estimate=pl.CostEstimate(flops=8 << 30, bytes_accessed=150 << 20, transcendentals=1 << 20),
        name="last",
    )(
        mid_seq, wo, q, k, v, hf, lse, cosine, sine, normed, wqkv, hidden, r_all, small, mid_grad, gain2,
        shs, lg, lu,
    )


def per_device_seq(
    hidden_in,
    positions,
    chosen,
    out_grad,
    attn_gain,
    w_query,
    w_key,
    w_value,
    w_out,
    moe_gain,
    router,
    shared_gate,
    shared_up,
    shared_down,
    expert_gate,
    expert_up,
    expert_down,
):
    f_rank, c_rank, t_rank = ranks()
    n_f, n_c, n_t = (lax.axis_size(name) for name in ("fsdp", "ctx", "tp"))
    rows, quarter = hidden_in.shape
    width = quarter * n_t
    part = w_query.shape[0]
    seq = rows * n_c
    n_exp = router.shape[1]
    mine = n_exp // n_c // n_f
    ffe = expert_gate.shape[2]
    group = ("fsdp", "ctx")
    every = ("fsdp", "ctx", "tp")
    n_b = n_f * n_c
    own_shared = shared_gate.shape[1] // n_b
    srows = -(-own_shared // 16) * 16
    f_arr = f_rank.astype(jnp.int32).reshape(1)
    swap = [(i, n_f - 1 - i) for i in range(n_f)]
    weights = (expert_gate.swapaxes(1, 2), expert_up.swapaxes(1, 2), expert_down)

    line = jnp.arange(16)[:, None]
    lines = jnp.where(line == 0, attn_gain[None], jnp.zeros((), BF))
    lines = jnp.where(line == 1, moe_gain[None], lines)
    lines = jnp.where(line == 2, (positions // 64).astype(BF)[None], lines)
    lines = jnp.where(line == 3, (positions % 64).astype(BF)[None], lines)
    lane = np.arange(HD)
    inverse = 10000.0 ** (-(lane % (HD // 2)) * 2.0 / HD)
    angle = jnp.asarray(np.stack([inverse, np.where(lane < HD // 2, -1.0, 1.0)]).astype(np.float32))
    (
        normed, q, k, v, heads_f, lse, r_one, cosine, sine, resid_mid,
        wqkv, wo, small, resid_all, grad_all, shared, *got,
    ) = first(
        n_c, n_f, n_t, mine, srows, hidden_in, w_query, w_key, w_value, w_out, out_grad, weights,
        router.T, chosen.T, lines, (shared_gate.T, shared_up.T, shared_down), angle,
    )
    sizes = (n_c, n_f, n_t, mine, ffe, srows)
    layer_out, moe_in, act, silu, slope, r_two, prob, kd, sd, shared_d = forward(
        *sizes, resid_all, grad_all, resid_mid, small, weights, got, shared
    )
    arrived_d = lax.ppermute(sd, "fsdp", swap)
    mid_grad, gain_two_part, mid_seq, shared_back, shs, kg, ku, gg, gu, lg, lu = backward(
        *sizes, grad_all, act, silu, slope, moe_in, r_two, shared_d, prob, small,
        resid_mid, out_grad, weights, got, shared,
    )
    input_grad, gq, gk, gv, go, gains, router_grad, shared_g, shared_u, lg, lu = last(
        n_c, n_f, n_t, n_exp, own_shared, mid_seq, wo, q, k, v, heads_f, lse, cosine, sine, normed, wqkv,
        hidden_in, r_one, small, mid_grad, gain_two_part, shs, lg, lu,
    )
    plain = (layer_out, input_grad, gq, gk, gv, go, router_grad, shared_g, shared_u)
    eg, eu, ed, shared_d, layer_out, input_grad, gq, gk, gv, go, router_grad, shared_g, shared_u = finish(
        f_arr, own_shared, (gg, lg, gu, lu, arrived_d), (kg, ku, kd), shared_back, plain
    )

    return (
        layer_out,
        input_grad,
        gains[0],
        gq,
        gk,
        gv,
        go,
        gains[1],
        router_grad.T,
        shared_g.T,
        shared_u.T,
        shared_d,
        eg.swapaxes(1, 2),
        eu.swapaxes(1, 2),
        ed,
    )


def one_head_each(mesh, args):
    n_f, n_c, n_t = (mesh.shape[name] for name in ("fsdp", "ctx", "tp"))
    heads = args[5].shape[1] // HD
    experts = args[10].shape[1]
    return (
        n_f == 2
        and n_t == 4
        and heads == n_c * n_t
        and experts % (n_f * n_c) == 0
        and args[11].shape[1] % (8 * n_f * n_c * n_t) == 0
    )


def solution(mesh):
    placed = (
        P(("fsdp", "ctx"), "tp"),
        P(("fsdp", "ctx")),
        P(("fsdp", "ctx"), None),
        P(("fsdp", "ctx"), "tp"),
        P(("fsdp", "ctx")),
        P(("fsdp", "ctx"), "tp"),
        P(("fsdp", "ctx"), "tp"),
        P(("fsdp", "ctx"), "tp"),
        P("tp", ("fsdp", "ctx")),
        P(("fsdp", "ctx")),
        P(("fsdp", "ctx"), None),
        P(("fsdp", "ctx"), "tp"),
        P(("fsdp", "ctx"), "tp"),
        P("tp", ("fsdp", "ctx")),
        P("ctx", "fsdp", "tp"),
        P("ctx", "fsdp", "tp"),
        P("ctx", "tp", "fsdp"),
    )
    def run(*args):
        body = per_device_seq if one_head_each(mesh, args) else per_device
        return jax.shard_map(
        body,
        mesh=mesh,
        in_specs=placed,
        out_specs=(
            P(("fsdp", "ctx"), "tp"),
            P(("fsdp", "ctx"), "tp"),
            P(("fsdp", "ctx")),
            P(("fsdp", "ctx"), "tp"),
            P(("fsdp", "ctx"), "tp"),
            P(("fsdp", "ctx"), "tp"),
            P("tp", ("fsdp", "ctx")),
            P(("fsdp", "ctx")),
            P(("fsdp", "ctx"), None),
            P(("fsdp", "ctx"), "tp"),
            P(("fsdp", "ctx"), "tp"),
            P("tp", ("fsdp", "ctx")),
            P("ctx", "fsdp", "tp"),
            P("ctx", "fsdp", "tp"),
            P("ctx", "tp", "fsdp"),
        ),
        check_vma=False,
    )(*args)

    return run
```

```python
import functools

import jax
import jax.numpy as jnp
import numpy as np
from jax import lax
from jax.experimental import pallas as pl
from jax.experimental.pallas import tpu as pltpu
from jax.sharding import PartitionSpec as P

HD = 128
TOPK = 6


EPS = 1e-06
NEG_BIG = -1e30


def as_sent(value):
    return jax.tree.map(lambda a: a.astype(jnp.bfloat16) if a.dtype == jnp.float32 else a, value)


def features(local_part):
    return lax.all_gather(local_part, "tp", axis=1, tiled=True)


def row_stats(partial_terms):
    return lax.psum(partial_terms, "tp")


def partial_sums(partial_terms):
    return jax.tree.map(
        lambda part: part.astype(jnp.float32),
        lax.psum_scatter(as_sent(partial_terms), "tp", scatter_dimension=1, tiled=True),
    )


def to_owners(slot_rows):
    return lax.all_to_all(slot_rows, "ctx", split_axis=0, concat_axis=2, tiled=True)


def to_sources(slot_rows):
    return lax.all_to_all(
        slot_rows.astype(jnp.bfloat16), "ctx", split_axis=2, concat_axis=0, tiled=True
    ).astype(slot_rows.dtype)


def rotary(values, positions, rotate_sign):
    half_dim = values.shape[-1] // 2
    inverse = 10000.0 ** (-jnp.arange(half_dim, dtype=jnp.float32) * 2.0 / values.shape[-1])
    angles = positions.astype(jnp.float32)[:, None] * inverse[None, :]
    cosine = jnp.cos(angles)[:, None, :]
    sine_val = rotate_sign * jnp.sin(angles)[:, None, :]
    lower_half = values[..., :half_dim]
    upper_half = values[..., half_dim:]
    return jnp.concatenate(
        [lower_half * cosine - upper_half * sine_val, upper_half * cosine + lower_half * sine_val],
        axis=-1,
    )


def norm_rows(values, gain_part, model_width):
    square_sum = row_stats(jnp.sum(values * values, axis=1))
    row_scale = lax.rsqrt(square_sum / model_width + EPS)
    return (values * row_scale[:, None] * gain_part[None, :], row_scale)


def norm_back(values, row_scale, gain_part, grad_normed, model_width, tp_rank):
    quarter = values.shape[1]
    local_sum = jnp.sum(grad_normed * gain_part[None, :] * values, axis=1)
    gain_local = jnp.sum(grad_normed * values * row_scale[:, None], axis=0)
    gain_whole = lax.dynamic_update_slice_in_dim(
        jnp.zeros((model_width,), jnp.float32), gain_local, tp_rank * quarter, 0
    )
    row_total, gain_grad = row_stats((local_sum, gain_whole))
    back = (
        row_scale[:, None] * gain_part[None, :] * grad_normed
        - values * (row_scale**3 * row_total / model_width)[:, None]
    )
    return (back, gain_grad)


def scatter_slots(assign_rows, flat_exp, slot_of, n_exp, capacity):
    buffer = jnp.zeros((n_exp, capacity, assign_rows.shape[1]), assign_rows.dtype)
    return buffer.at[flat_exp, slot_of].set(assign_rows)


def silu_grad(pre_act):
    sigmoid_val = jax.nn.sigmoid(pre_act)
    return sigmoid_val * (1.0 + pre_act * (1.0 - sigmoid_val))


def keep_state(carried):
    return carried


def per_device(
    hidden_in,
    positions,
    chosen,
    out_grad,
    attn_gain,
    w_query,
    w_key,
    w_value,
    w_out,
    moe_gain,
    router,
    shared_gate,
    shared_up,
    shared_down,
    expert_gate,
    expert_up,
    expert_down,
):
    tp_rank = lax.axis_index("tp")
    ctx_rank = lax.axis_index("ctx")
    n_ctx = lax.axis_size("ctx")
    tok_rows, quarter = hidden_in.shape
    model_width = quarter * lax.axis_size("tp")
    gain_one, wq_all, wk_all, wv_all, gain_two, router_all, gate_all, up_all, wo_all, down_all = (
        lax.all_gather(attn_gain, ("fsdp", "ctx"), axis=0, tiled=True),
        lax.all_gather(w_query, ("fsdp", "ctx"), axis=0, tiled=True),
        lax.all_gather(w_key, ("fsdp", "ctx"), axis=0, tiled=True),
        lax.all_gather(w_value, ("fsdp", "ctx"), axis=0, tiled=True),
        lax.all_gather(moe_gain, ("fsdp", "ctx"), axis=0, tiled=True),
        lax.all_gather(router, ("fsdp", "ctx"), axis=0, tiled=True),
        lax.all_gather(shared_gate, ("fsdp", "ctx"), axis=0, tiled=True),
        lax.all_gather(shared_up, ("fsdp", "ctx"), axis=0, tiled=True),
        lax.all_gather(w_out, ("fsdp", "ctx"), axis=1, tiled=True),
        lax.all_gather(shared_down, ("fsdp", "ctx"), axis=1, tiled=True),
    )
    expert_gate_weights, expert_up_weights, expert_down_weights = (
        lax.all_gather(expert_gate, "fsdp", axis=1, tiled=True),
        lax.all_gather(expert_up, "fsdp", axis=1, tiled=True),
        lax.all_gather(expert_down, "fsdp", axis=2, tiled=True),
    )
    gain_q1 = lax.dynamic_slice_in_dim(gain_one, tp_rank * quarter, quarter).astype(jnp.float32)
    gain_q2 = lax.dynamic_slice_in_dim(gain_two, tp_rank * quarter, quarter).astype(jnp.float32)
    router_rows = lax.dynamic_slice_in_dim(router_all, tp_rank * quarter, quarter, 0)
    head_count = wq_all.shape[1] // HD
    scale_att = HD ** (-0.5)
    resid_in = hidden_in.astype(jnp.float32)
    normed_one, scale_one = norm_rows(resid_in, gain_q1, model_width)
    normed_in = features(normed_one.astype(jnp.bfloat16))
    query_pre = jnp.dot(normed_in, wq_all, preferred_element_type=jnp.float32).reshape(
        tok_rows, head_count, HD
    )
    key_pre = jnp.dot(normed_in, wk_all, preferred_element_type=jnp.float32).reshape(
        tok_rows, head_count, HD
    )
    value_b = (
        jnp.dot(normed_in, wv_all, preferred_element_type=jnp.float32)
        .astype(jnp.bfloat16)
        .reshape(tok_rows, head_count, HD)
    )
    query_b = rotary(query_pre, positions, 1.0).astype(jnp.bfloat16)
    key_b = rotary(key_pre, positions, 1.0).astype(jnp.bfloat16)
    q_start = ctx_rank * tok_rows
    row_pos = q_start + jnp.arange(tok_rows)
    start_state = (
        jnp.full((tok_rows, head_count), NEG_BIG, jnp.float32),
        jnp.zeros((tok_rows, head_count), jnp.float32),
        jnp.zeros((tok_rows, head_count, HD), jnp.float32),
    )
    keys_blk = lax.all_gather(key_b, "ctx", axis=0, tiled=True)
    vals_blk = lax.all_gather(value_b, "ctx", axis=0, tiled=True)
    key_count = keys_blk.shape[0]

    def compute(state_in):
        run_max, run_sum, run_acc = state_in
        scores = (
            jnp.einsum("qhd,khd->qhk", query_b, keys_blk, preferred_element_type=jnp.float32)
            * scale_att
        )
        visible = jnp.arange(key_count)[None, :] <= row_pos[:, None]
        scores = jnp.where(visible[:, None, :], scores, NEG_BIG)
        new_max = jnp.maximum(run_max, jnp.max(scores, axis=2))
        weights = jnp.exp(scores - new_max[:, :, None])
        new_sum = jnp.sum(weights, axis=2)
        new_acc = jnp.einsum(
            "qhk,khd->qhd",
            weights.astype(jnp.bfloat16),
            vals_blk,
            preferred_element_type=jnp.float32,
        )
        return (new_max, new_sum, new_acc)

    run_max, run_sum, run_acc = lax.cond(
        jnp.int32(0) <= q_start + tok_rows - 1, compute, keep_state, start_state
    )
    heads_f = run_acc / run_sum[:, :, None]
    log_sum = run_max + jnp.log(run_sum)
    heads_b = heads_f.astype(jnp.bfloat16).reshape(tok_rows, head_count * HD)
    resid_mid = resid_in + partial_sums(
        jnp.dot(heads_b, wo_all, preferred_element_type=jnp.float32)
    )
    normed_two, scale_two = norm_rows(resid_mid, gain_q2, model_width)
    moe_part = normed_two.astype(jnp.bfloat16)
    moe_in = features(moe_part)
    n_exp = router_all.shape[1]
    exp_dev = n_exp // n_ctx
    capacity = min(tok_rows, 5 * TOPK * tok_rows // (3 * n_exp))
    logits = jnp.dot(moe_in, router_all, preferred_element_type=jnp.float32)
    probs_all = jax.nn.softmax(logits, axis=1)
    picked = (chosen[:, :, None] == jnp.arange(n_exp)[None, None, :]).astype(jnp.float32)
    gate_vals = jnp.sum(picked * probs_all[:, None, :], axis=2)
    shared_a = jnp.dot(moe_in, gate_all, preferred_element_type=jnp.float32)
    shared_b = jnp.dot(moe_in, up_all, preferred_element_type=jnp.float32)
    shared_act = (jax.nn.silu(shared_a) * shared_b).astype(jnp.bfloat16)
    shared_out = jnp.dot(shared_act, down_all, preferred_element_type=jnp.float32)
    flat_exp = chosen.reshape(-1)
    flat_hot = (flat_exp[:, None] == jnp.arange(n_exp)[None, :]).astype(jnp.int32)
    slot_of = jnp.sum((jnp.cumsum(flat_hot, axis=0) - flat_hot) * flat_hot, axis=1)
    token_of = jnp.arange(tok_rows * TOPK) // TOPK
    slot_count = n_ctx * capacity
    outgoing = scatter_slots(moe_in[token_of], flat_exp, slot_of, n_exp, capacity)
    received_rows = to_owners(outgoing.reshape(n_ctx, exp_dev, capacity, model_width)).reshape(
        exp_dev, slot_count, model_width
    )
    expert_a = jnp.einsum(
        "bmw,bwv->bmv", received_rows, expert_gate_weights, preferred_element_type=jnp.float32
    )
    expert_up_proj = jnp.einsum(
        "bmw,bwv->bmv", received_rows, expert_up_weights, preferred_element_type=jnp.float32
    )
    expert_act = (jax.nn.silu(expert_a) * expert_up_proj).astype(jnp.bfloat16)
    expert_out = jnp.einsum(
        "erf,efd->erd", expert_act, expert_down_weights, preferred_element_type=jnp.float32
    )
    returned = to_sources(expert_out.reshape(1, exp_dev, slot_count, model_width))
    shared_q, slot_q = partial_sums((shared_out, returned.reshape(n_exp * capacity, model_width)))
    slot_rows = slot_q.reshape(n_exp, capacity, quarter)[flat_exp, slot_of].reshape(
        tok_rows, TOPK, quarter
    )
    result = resid_mid + shared_q + jnp.sum(gate_vals[:, :, None] * slot_rows, axis=1)
    layer_out = result.astype(jnp.bfloat16)
    grad_out = out_grad.astype(jnp.float32)
    gate_grad = row_stats(jnp.sum(grad_out[:, None, :] * slot_rows, axis=2))
    prob_grad = jnp.sum(gate_grad[:, :, None] * picked, axis=1)
    logit_grad = (
        probs_all * (prob_grad - jnp.sum(probs_all * prob_grad, axis=1, keepdims=True))
    ).astype(jnp.bfloat16)
    router_grad = jnp.einsum("td,te->de", moe_in, logit_grad, preferred_element_type=jnp.float32)
    router_back_q = jnp.einsum(
        "te,de->td", logit_grad, router_rows, preferred_element_type=jnp.float32
    )
    grad_full = features(out_grad)
    shared_dact = jnp.einsum("td,fd->tf", grad_full, down_all, preferred_element_type=jnp.float32)
    shared_da = (shared_dact * shared_b * silu_grad(shared_a)).astype(jnp.bfloat16)
    shared_db = (shared_dact * jax.nn.silu(shared_a)).astype(jnp.bfloat16)
    shared_down_grad = jnp.einsum(
        "tf,td->fd", shared_act, grad_full, preferred_element_type=jnp.float32
    )
    shared_gate_grad = jnp.einsum(
        "td,tf->df", moe_in, shared_da, preferred_element_type=jnp.float32
    )
    shared_up_grad = jnp.einsum("td,tf->df", moe_in, shared_db, preferred_element_type=jnp.float32)
    shared_back = jnp.einsum(
        "tf,df->td", shared_da, gate_all, preferred_element_type=jnp.float32
    ) + jnp.einsum("tf,df->td", shared_db, up_all, preferred_element_type=jnp.float32)
    assign_grad = (
        (gate_vals[:, :, None] * grad_full[:, None, :])
        .astype(jnp.bfloat16)
        .reshape(tok_rows * TOPK, model_width)
    )
    grad_slots = scatter_slots(assign_grad, flat_exp, slot_of, n_exp, capacity)
    grad_arrived = to_owners(grad_slots.reshape(n_ctx, exp_dev, capacity, model_width)).reshape(
        exp_dev, slot_count, model_width
    )
    expert_dact = jnp.einsum(
        "erd,efd->erf", grad_arrived, expert_down_weights, preferred_element_type=jnp.float32
    )
    expert_da = (expert_dact * expert_up_proj * silu_grad(expert_a)).astype(jnp.bfloat16)
    expert_up_proj_grad = (expert_dact * jax.nn.silu(expert_a)).astype(jnp.bfloat16)
    edown_grad = jnp.einsum(
        "erf,erd->efd", expert_act, grad_arrived, preferred_element_type=jnp.float32
    )
    egate_grad = jnp.einsum(
        "qgo,qgz->qoz", received_rows, expert_da, preferred_element_type=jnp.float32
    )
    expert_up_weight_grad = jnp.einsum(
        "qgo,qgz->qoz", received_rows, expert_up_proj_grad, preferred_element_type=jnp.float32
    )
    expert_back = jnp.einsum(
        "iac,igc->iag", expert_da, expert_gate_weights, preferred_element_type=jnp.float32
    ) + jnp.einsum(
        "iac,igc->iag", expert_up_proj_grad, expert_up_weights, preferred_element_type=jnp.float32
    )
    back_slots = to_sources(expert_back.reshape(1, exp_dev, slot_count, model_width)).reshape(
        n_exp, capacity, model_width
    )
    token_back = jnp.sum(back_slots[flat_exp, slot_of].reshape(tok_rows, TOPK, model_width), axis=1)
    moe_back_q = partial_sums(shared_back + token_back)
    mid_back, gain_two_grad = norm_back(
        resid_mid, scale_two, gain_q2, moe_back_q + router_back_q, model_width, tp_rank
    )
    mid_grad = grad_out + mid_back
    branch_full = features(mid_grad.astype(jnp.bfloat16))
    wo_grad = jnp.einsum("tf,td->fd", heads_b, branch_full, preferred_element_type=jnp.float32)
    heads_grad = (
        jnp.einsum("td,fd->tf", branch_full, wo_all, preferred_element_type=jnp.float32)
        .astype(jnp.bfloat16)
        .reshape(tok_rows, head_count, HD)
    )
    row_delta = jnp.sum(heads_grad.astype(jnp.float32) * heads_f, axis=2)
    seq_len = tok_rows * n_ctx
    back_state = (
        jnp.zeros((tok_rows, head_count, HD), jnp.float32),
        jnp.zeros((seq_len, head_count, HD), jnp.float32),
        jnp.zeros((seq_len, head_count, HD), jnp.float32),
    )
    attend_keys_blk = lax.all_gather(key_b, "ctx", axis=0, tiled=True)
    attend_vals_blk = lax.all_gather(value_b, "ctx", axis=0, tiled=True)
    attend_key_count = attend_keys_blk.shape[0]

    def compute(state_in):
        scores = (
            jnp.einsum("qhd,khd->qhk", query_b, attend_keys_blk, preferred_element_type=jnp.float32)
            * scale_att
        )
        visible = jnp.arange(attend_key_count)[None, :] <= row_pos[:, None]
        probs_blk = jnp.where(visible[:, None, :], jnp.exp(scores - log_sum[:, :, None]), 0.0)
        value_part = jnp.einsum(
            "qhk,qhd->khd",
            probs_blk.astype(jnp.bfloat16),
            heads_grad,
            preferred_element_type=jnp.float32,
        )
        dot_grad = jnp.einsum(
            "qhd,khd->qhk", heads_grad, attend_vals_blk, preferred_element_type=jnp.float32
        )
        score_grad = (probs_blk * (dot_grad - row_delta[:, :, None])).astype(jnp.bfloat16)
        query_acc = (
            jnp.einsum(
                "qhk,khd->qhd", score_grad, attend_keys_blk, preferred_element_type=jnp.float32
            )
            * scale_att
        )
        key_part = (
            jnp.einsum("qhk,qhd->khd", score_grad, query_b, preferred_element_type=jnp.float32)
            * scale_att
        )
        return (query_acc, key_part, value_part)

    query_grad, key_grad_all, value_grad_all = lax.cond(
        jnp.int32(0) <= q_start + tok_rows - 1, compute, keep_state, back_state
    )
    key_grad, value_grad = (
        lax.psum_scatter(
            key_grad_all.astype(jnp.bfloat16), "ctx", scatter_dimension=0, tiled=True
        ).astype(jnp.float32),
        lax.psum_scatter(
            value_grad_all.astype(jnp.bfloat16), "ctx", scatter_dimension=0, tiled=True
        ).astype(jnp.float32),
    )
    query_pre_grad = (
        rotary(query_grad, positions, -1.0).astype(jnp.bfloat16).reshape(tok_rows, head_count * HD)
    )
    key_pre_grad = (
        rotary(key_grad, positions, -1.0).astype(jnp.bfloat16).reshape(tok_rows, head_count * HD)
    )
    value_pre_grad = value_grad.astype(jnp.bfloat16).reshape(tok_rows, head_count * HD)
    wq_grad = jnp.einsum("td,tf->df", normed_in, query_pre_grad, preferred_element_type=jnp.float32)
    wk_grad = jnp.einsum("td,tf->df", normed_in, key_pre_grad, preferred_element_type=jnp.float32)
    wv_grad = jnp.einsum("td,tf->df", normed_in, value_pre_grad, preferred_element_type=jnp.float32)
    in_back = jnp.einsum("tf,df->td", query_pre_grad, wq_all, preferred_element_type=jnp.float32)
    in_back = in_back + jnp.einsum(
        "tf,df->td", key_pre_grad, wk_all, preferred_element_type=jnp.float32
    )
    in_back = in_back + jnp.einsum(
        "tf,df->td", value_pre_grad, wv_all, preferred_element_type=jnp.float32
    )
    first_back, gain_one_grad = norm_back(
        resid_in, scale_one, gain_q1, partial_sums(in_back), model_width, tp_rank
    )
    input_grad = mid_grad + first_back
    dense = (
        lax.psum_scatter(
            gain_one_grad.astype(jnp.bfloat16), ("fsdp", "ctx"), scatter_dimension=0, tiled=True
        ).astype(jnp.float32),
        lax.psum_scatter(
            wq_grad.astype(jnp.bfloat16), ("fsdp", "ctx"), scatter_dimension=0, tiled=True
        ).astype(jnp.float32),
        lax.psum_scatter(
            wk_grad.astype(jnp.bfloat16), ("fsdp", "ctx"), scatter_dimension=0, tiled=True
        ).astype(jnp.float32),
        lax.psum_scatter(
            wv_grad.astype(jnp.bfloat16), ("fsdp", "ctx"), scatter_dimension=0, tiled=True
        ).astype(jnp.float32),
        lax.psum_scatter(
            gain_two_grad.astype(jnp.bfloat16), ("fsdp", "ctx"), scatter_dimension=0, tiled=True
        ).astype(jnp.float32),
        lax.psum_scatter(
            router_grad.astype(jnp.bfloat16), ("fsdp", "ctx"), scatter_dimension=0, tiled=True
        ).astype(jnp.float32),
        lax.psum_scatter(
            shared_gate_grad.astype(jnp.bfloat16), ("fsdp", "ctx"), scatter_dimension=0, tiled=True
        ).astype(jnp.float32),
        lax.psum_scatter(
            shared_up_grad.astype(jnp.bfloat16), ("fsdp", "ctx"), scatter_dimension=0, tiled=True
        ).astype(jnp.float32),
        lax.psum_scatter(
            wo_grad.astype(jnp.bfloat16), ("fsdp", "ctx"), scatter_dimension=1, tiled=True
        ).astype(jnp.float32),
        lax.psum_scatter(
            shared_down_grad.astype(jnp.bfloat16), ("fsdp", "ctx"), scatter_dimension=1, tiled=True
        ).astype(jnp.float32),
    )
    experts_done = (
        lax.psum_scatter(
            egate_grad.astype(jnp.bfloat16), "fsdp", scatter_dimension=1, tiled=True
        ).astype(jnp.float32),
        lax.psum_scatter(
            expert_up_weight_grad.astype(jnp.bfloat16), "fsdp", scatter_dimension=1, tiled=True
        ).astype(jnp.float32),
        lax.psum_scatter(
            edown_grad.astype(jnp.bfloat16), "fsdp", scatter_dimension=2, tiled=True
        ).astype(jnp.float32),
    )
    return (
        layer_out,
        input_grad,
        dense[0],
        dense[1],
        dense[2],
        dense[3],
        dense[8],
        dense[4],
        dense[5],
        dense[6],
        dense[7],
        dense[9],
        experts_done[0],
        experts_done[1],
        experts_done[2],
    )


MESH = pl.DeviceIdType.MESH
HBM = pl.BlockSpec(memory_space=pl.ANY)
VMEM = pl.BlockSpec(memory_space=pltpu.VMEM)
DMA = pltpu.SemaphoreType.DMA
BF, F32 = jnp.bfloat16, jnp.float32
BIG = 60 * 1024 * 1024


def dot_nt(left, right):
    return lax.dot_general(left, right, (((1,), (1,)), ((), ())), preferred_element_type=F32)


def dot_tn(left, right):
    return lax.dot_general(left, right, (((0,), (0,)), ((), ())), preferred_element_type=F32)


def dot_nn(left, right):
    return jnp.dot(left, right, preferred_element_type=F32)


def ranks():
    return lax.axis_index("fsdp"), lax.axis_index("ctx"), lax.axis_index("tp")


def sibling(t):
    return t + 1 - 2 * lax.rem(t, 2)


def opposite(t):
    return lax.rem(t + 2, 4)


def remote(src, dst, send, recv, to):
    return pltpu.make_async_remote_copy(
        src_ref=src, dst_ref=dst, send_sem=send, recv_sem=recv, device_id=to, device_id_type=MESH
    )


def greet(peers):
    barrier = pltpu.get_barrier_semaphore()
    for peer in peers:
        pl.semaphore_signal(barrier, inc=1, device_id=peer, device_id_type=MESH)
    pl.semaphore_wait(barrier, len(peers))


def line_peers(c, n_c):
    return [{"ctx": lax.rem(c + step, n_c)} for step in range(1, n_c)]


def piece(index, size):
    return pl.ds(pl.multiple_of(index * size, size), size)


def nearest(c, n_c, act):
    act(c)
    for step in range(1, n_c):
        for side in (-1, 1):
            place = c + side * step

            @pl.when((place >= 0) & (place < n_c))
            def _():
                act(place)


def spread_sems(n_c):
    return [
        DMA((n_c + 2,)),
        DMA((n_c,)),
        DMA((n_c,)),
        DMA((n_c,)),
        DMA((2 * n_c,)),
        DMA((2 * n_c,)),
        DMA((4 * n_c,)),
        DMA((4 * n_c,)),
        DMA(()),
    ]


class Spread:
    def __init__(self, own, place, n_c, both, sems):
        self.own, self.place, self.n_c, self.both = own, place, n_c, both
        self.zs, self.zr, self.xs, self.xr, self.ys, self.yr, self.ks, self.kr, self.ls = sems
        self.f, self.c, self.t = ranks()
        self.other_t = opposite(self.t)
        self.groups = ((self.f, 0), (1 - self.f, n_c))[: 2 if both else 1]

    def local(self):
        return pltpu.make_async_copy(self.own, self.place(self.f, self.c, self.t), self.ls)

    def far_copy(self, src, i, g, cc, col):
        return remote(src, self.place(g, cc, col), self.ys.at[i], self.yr.at[i], {"tp": self.other_t})

    def sib_copy(self, src, i, which, g, cc, col):
        at = 2 * i + which
        return remote(src, self.place(g, cc, col), self.ks.at[at], self.kr.at[at], {"tp": sibling(self.t)})

    def other_copy(self, src, g, cc):
        return remote(src, self.place(g, cc, self.t), self.xs.at[cc], self.xr.at[cc], {"fsdp": 1 - self.f})

    def line_copy(self, src, cc, sem, to):
        return remote(src, self.place(self.f, cc, self.t), self.zs.at[sem], self.zr.at[cc], {"ctx": to})

    def pass_on(self, src, i, g, cc):
        self.far_copy(src, i, g, cc, self.t).start()
        self.sib_copy(src, i, 0, g, cc, self.t).start()

    def start(self):
        self.local().start()
        n_c, c, own = self.n_c, self.c, self.own

        @pl.when(c < n_c - 1)
        def _():
            self.line_copy(own, c, n_c, c + 1).start()

        @pl.when(c > 0)
        def _():
            self.line_copy(own, c, n_c + 1, c - 1).start()

        if self.both:
            self.other_copy(own, self.f, c).start()
        self.pass_on(own, c, self.f, c)

    def each_other(self, act):
        for step in range(1, self.n_c):
            for side in (-1, 1):
                cc = self.c + side * step

                @pl.when((cc >= 0) & (cc < self.n_c))
                def _():
                    act(cc, self.c - side)

    def line(self):
        n_c = self.n_c

        def arrive(cc, onward):
            block = self.place(self.f, cc, self.t)
            self.line_copy(block, cc, cc, self.c).wait_recv()

            @pl.when((onward >= 0) & (onward < n_c))
            def _():
                self.line_copy(block, cc, cc, onward).start()

            if self.both:
                self.other_copy(block, self.f, cc).start()
            self.pass_on(block, cc, self.f, cc)

        self.each_other(arrive)

    def other(self):
        def arrive(cc):
            block = self.place(1 - self.f, cc, self.t)
            self.other_copy(block, 1 - self.f, cc).wait_recv()
            self.pass_on(block, self.n_c + cc, 1 - self.f, cc)

        nearest(self.c, self.n_c, arrive)

    def far(self, which):
        g, base = self.groups[which]

        def arrive(cc):
            i = base + cc
            block = self.place(g, cc, self.other_t)
            self.far_copy(block, i, g, cc, self.other_t).wait_recv()
            self.sib_copy(block, i, 1, g, cc, self.other_t).start()

        nearest(self.c, self.n_c, arrive)

    def arrived(self, which):
        g, base = self.groups[which]
        for cc in range(self.n_c):
            block = self.place(g, cc, self.t)
            for half in range(2):
                self.sib_copy(block, base + cc, half, g, cc, self.t).wait_recv()

    def finish(self):
        n_c, c, f, t, own = self.n_c, self.c, self.f, self.t, self.own
        for g, base in self.groups:
            for cc in range(n_c):
                block = self.place(g, cc, t)
                for half in range(2):
                    self.sib_copy(block, base + cc, half, g, cc, t).wait_send()
                self.far_copy(block, base + cc, g, cc, t).wait_send()
        if self.both:
            for cc in range(n_c):
                self.other_copy(self.place(f, cc, t), f, cc).wait_send()
        block = self.place(f, c, t)

        @pl.when(c < n_c - 1)
        def _():
            self.line_copy(block, c, n_c, c).wait_send()

        @pl.when(c > 0)
        def _():
            self.line_copy(block, c, n_c + 1, c).wait_send()

        def sent(cc, onward):
            @pl.when((onward >= 0) & (onward < n_c))
            def _():
                self.line_copy(block, cc, cc, c).wait_send()

        self.each_other(sent)


def to_each(src_of, dst, n_f, n_c, sems, act):
    send, recv, own = sems
    f, c, _ = ranks()
    here = f * n_c + c
    for df in range(n_f):
        for dc in range(n_c):
            i = df * n_c + dc
            if i == 0:
                copy = pltpu.make_async_copy(src_of(here), dst.at[here], own)
                copy.start() if act == "start" else copy.wait()
                continue
            to_f, to_c = lax.rem(f + df, n_f), lax.rem(c + dc, n_c)
            copy = remote(
                src_of(to_f * n_c + to_c), dst.at[here], send.at[i], recv.at[i], {"fsdp": to_f, "ctx": to_c}
            )
            copy.start() if act == "start" else copy.wait()


def each_peers(f, c, n_f, n_c):
    return [
        {"fsdp": lax.rem(f + df, n_f), "ctx": lax.rem(c + dc, n_c)}
        for df in range(n_f)
        for dc in range(n_c)
        if df or dc
    ]


def reduce_seq_scratch(n_c, rows, quarter):
    return [
        pltpu.VMEM((n_c, 2, rows, quarter), BF),
        pltpu.VMEM((n_c, 2, rows, quarter), BF),
        pltpu.VMEM((n_c, 2, rows, quarter), F32),
        pltpu.VMEM((n_c, rows, quarter), BF),
        pltpu.VMEM((n_c, rows, quarter), BF),
        pltpu.VMEM((n_c, rows, quarter), BF),
        pltpu.VMEM((n_c, rows, quarter), BF),
        DMA((n_c,)),
        DMA((n_c,)),
        DMA((n_c,)),
        DMA((n_c,)),
        DMA((n_c,)),
        DMA((n_c,)),
    ]


def reduce_seq(part_of, n_c, scratch, middle=None, before_last=None):
    out1, in1, own, out2, in2, out3, in3, s1, r1, s2, r2, s3, r3 = scratch
    f, c, t = ranks()
    far, sib = opposite(t), sibling(t)
    to_sib, to_far = {"tp": sib}, {"tp": far}
    order = [2, 1, 3, 0] if n_c == 4 else list(range(1, n_c)) + [0]
    for d in order:
        cc = lax.rem(c + d, n_c)
        out1[d, 0] = part_of(cc, sib).astype(BF)
        out1[d, 1] = part_of(cc, opposite(sib)).astype(BF)
        remote(out1.at[d], in1.at[d], s1.at[d], r1.at[d], to_sib).start()
        own[d, 0] = part_of(cc, t)
        own[d, 1] = part_of(cc, far)
    for d in order:
        remote(out1.at[d], in1.at[d], s1.at[d], r1.at[d], to_sib).wait()
        out2[d] = (own[d, 1] + in1[d, 1].astype(F32)).astype(BF)
        remote(out2.at[d], in2.at[d], s2.at[d], r2.at[d], to_far).start()
    if middle is not None:
        middle()
    for d in order:
        remote(out2.at[d], in2.at[d], s2.at[d], r2.at[d], to_far).wait()
        total = own[d, 0] + in1[d, 0].astype(F32) + in2[d].astype(F32)
        if d:
            out3[d] = total.astype(BF)
            cc = lax.rem(c + d, n_c)
            remote(out3.at[d], in3.at[d], s3.at[d], r3.at[d], {"ctx": cc}).start()
    if before_last is not None:
        before_last()
    for d in order[:-1]:
        remote(out3.at[d], in3.at[d], s3.at[d], r3.at[d], {"ctx": c}).wait()
        total = total + in3[d].astype(F32)
    return total


def first_kernel(
    n_c, n_f, n_exp, mine, hidden, wq, wk, wv, wo, og, gate_t, up_t, down, router_in, chosen, lines, sg, su, sd, angle,
    normed_out, q_out, k_out, v_out, hf_out, lse_out, r_out, cos_out, sin_out, resid_out,
    wqkv_out, wo_out, small_out, all_out, og_out, shared_out, gg_out, gu_out, gd_out,
    seq, wqkv, wo_all, small_all, hb, blk, own_og, small, shared, normed,
    ws, wr, ls, xs, xr, ss, sr, sl, es, er, os, *scratch,
):
    f, c, t = ranks()
    rows, quarter = blk.shape
    part = wo.shape[1]
    tokens, width = seq.shape
    n_s = len(spread_sems(n_c))
    named = lax.broadcasted_iota(jnp.int32, (n_exp, part), 0)
    mask = jnp.zeros((n_exp, part), F32)
    for k in range(chosen.shape[0]):
        mask = mask + jnp.where(chosen[k : k + 1, :] == named, 1.0, 0.0)
    small[:n_exp, :] = router_in[...]
    small[n_exp : 2 * n_exp, :] = mask.astype(BF)
    small[2 * n_exp :, :] = lines[...]
    n_b = n_f * n_c
    own_rows, srows = sg.shape[0] // n_b, shared.shape[1] // 3
    for i, src in enumerate((sg, su, sd)):
        for b in range(n_b):
            shared[b, i * srows : i * srows + own_rows, :] = src[b * own_rows : (b + 1) * own_rows, :]
            if srows > own_rows:
                shared[b, i * srows + own_rows : (i + 1) * srows, :] = jnp.zeros((srows - own_rows, part), BF)
    greet([{"tp": sibling(t)}, {"tp": opposite(t)}] + each_peers(f, c, n_f, n_c))
    seq_place = lambda g, cc, tt: seq.at[piece(cc, rows), piece(tt, quarter)]
    og_place = lambda g, cc, tt: og_out.at[g * n_c + cc, tt]
    all_place = lambda g, cc, tt: all_out.at[piece(g * n_c + cc, rows), piece(tt, quarter)]
    hid = Spread(hidden, seq_place, n_c, False, scratch[:n_s])
    grad = Spread(og, og_place, n_c, True, scratch[n_s : 2 * n_s])
    res = Spread(blk, all_place, n_c, True, scratch[2 * n_s : 3 * n_s])

    def targets(g, cc):
        block = piece(g * n_c + cc, part)
        return [wqkv.at[block, pl.ds(i * HD, HD)] for i in range(3)] + [
            wo_all.at[:, block],
            small_all.at[:, block],
        ]

    def sources(head):
        cols = piece(head, HD)
        return [wq.at[:, cols], wk.at[:, cols], wv.at[:, cols], wo.at[cols, :], small]

    def slabs(g, cc):
        block = piece(g * n_c + cc, part)
        return [wqkv.at[block, :], wo_all.at[:, block], small_all.at[:, block]]

    def across(step, g, cc):
        return [
            remote(slab, slab, xs.at[step, i], xr.at[step, i], {"fsdp": 1 - f})
            for i, slab in enumerate(slabs(g, cc))
        ]

    def swap(weight, out, k):
        return [
            remote(weight.at[(1 - f) * mine + e], out.at[e], es.at[k, e], er.at[k, e], {"fsdp": 1 - f})
            for e in range(mine)
        ]

    more = swap(down, gd_out, 2)
    for copy in more:
        copy.start()
    hid.start()
    def weights_out(step):
        to = lax.rem(c + step, n_c)
        for i, (src, dst) in enumerate(zip(sources(to), targets(f, c))):
            remote(src, dst, ws.at[step, i], wr.at[step, i], {"ctx": to}).start()

    def weights_on(step):
        cc = lax.rem(c - step + n_c, n_c)
        for i, dst in enumerate(targets(f, cc)):
            remote(dst, dst, ws.at[step, i], wr.at[step, i], {"ctx": cc}).wait_recv()
        for copy in across(step, f, cc):
            copy.start()

    steps = ([2, 1, 3] if n_c == 4 else list(range(1, n_c))) + [None]
    weights_out(steps[0])
    own = [
        pltpu.make_async_copy(src, dst, ls.at[i])
        for i, (src, dst) in enumerate(zip(sources(c), targets(f, c)))
    ]
    for copy in own:
        copy.start()
    for copy in own:
        copy.wait()
    for copy in across(0, f, c):
        copy.start()
    grad.start()
    hid.line()
    for step, following in zip(steps, steps[1:]):
        if following is not None:
            weights_out(following)
        weights_on(step)
    grad.line()
    swaps = swap(gate_t, gg_out, 0) + swap(up_t, gu_out, 1)
    for copy in swaps[: mine + 1]:
        copy.start()
    hid.far(0)
    hid.arrived(0)
    hid.local().wait()
    for step in range(n_c):
        for copy in across(step, 1 - f, lax.rem(c - step + n_c, n_c)):
            copy.wait_recv()
    outs = [
        pltpu.make_async_copy(src, dst, os.at[i])
        for i, (src, dst) in enumerate(((wqkv, wqkv_out), (wo_all, wo_out), (small_all, small_out)))
    ]
    for copy in outs:
        copy.start()

    scale_att = HD ** (-0.5)
    gain = small_all[2 * n_exp : 2 * n_exp + 1, :].astype(F32)
    place_row = 2 * n_exp + 2
    for start in range(0, tokens, rows):
        at = pl.ds(start, rows)
        h = seq[at, :].astype(F32)
        r = lax.rsqrt(jnp.sum(h * h, axis=1, keepdims=True) / width + EPS)
        n = (h * r * gain).astype(BF)
        normed[at, :] = n
        r_out[at, :] = jnp.broadcast_to(r, (rows, HD))
        cols = pl.ds(pl.multiple_of(f * tokens + start, rows), rows)
        pos = small_all[place_row : place_row + 2, cols].astype(F32)
        pos = pos[0:1] * 64.0 + pos[1:2]
        turn = jnp.broadcast_to(pos, (HD, rows)).T * angle[0:1, :]
        cos, sin = jnp.cos(turn), jnp.sin(turn) * angle[1:2, :]
        cos_out[at, :] = cos
        sin_out[at, :] = sin
        qkv = dot_nn(n, wqkv[...])

        def rotate(values):
            return (values * cos + pltpu.roll(values, HD // 2, 1) * sin).astype(BF)

        q_out[at, :] = rotate(qkv[:, :HD])
        k_out[at, :] = rotate(qkv[:, HD : 2 * HD])
        v_out[at, :] = qkv[:, 2 * HD :].astype(BF)
    outs.append(pltpu.make_async_copy(normed, normed_out, os.at[4]))
    outs[-1].start()
    for start in range(0, tokens, rows):
        at = pl.ds(start, rows)
        seen = start + rows
        s = dot_nt(q_out[at, :], k_out[:seen, :]) * scale_att
        row = lax.broadcasted_iota(jnp.int32, (rows, seen), 0) + start
        col = lax.broadcasted_iota(jnp.int32, (rows, seen), 1)
        s = jnp.where(col <= row, s, NEG_BIG)
        top = jnp.max(s, axis=1, keepdims=True)
        e = jnp.exp(s - top)
        total = jnp.sum(e, axis=1, keepdims=True)
        out = dot_nn((e * (1.0 / total)).astype(BF), v_out[:seen, :])
        hf_out[at, :] = out
        hb[at, :] = out.astype(BF)
        lse_out[at, :] = jnp.broadcast_to(top + jnp.log(total), (rows, HD))

    exchange = lambda act: to_each(lambda b: shared.at[b], shared_out, n_f, n_c, (ss, sr, sl), act)

    def part_of(cc, q):
        return dot_nn(hb[piece(cc, rows), :], wo_all[:, piece(q, quarter)])

    grad.other()
    fetch = pltpu.make_async_copy(hidden, own_og, os.at[3])
    fetch.start()
    total = reduce_seq(part_of, n_c, scratch[3 * n_s :])
    fetch.wait()
    resid = own_og[...].astype(F32) + total
    resid_out[...] = resid
    blk[...] = resid.astype(BF)
    res.start()
    res.line()
    for copy in swaps[mine + 1 :]:
        copy.start()
    exchange("start")
    grad.far(0)
    grad.far(1)
    res.other()
    res.far(0)
    res.far(1)
    for which in range(2):
        grad.arrived(which)
        res.arrived(which)
    exchange("wait")
    for copy in swaps + more:
        copy.wait()
    for step in range(1, n_c):
        for i, (src, dst) in enumerate(zip(sources(c), targets(f, c))):
            remote(src, dst, ws.at[step, i], wr.at[step, i], {"ctx": c}).wait_send()
    for step in range(n_c):
        for copy in across(step, f, lax.rem(c - step + n_c, n_c)):
            copy.wait_send()
    for item in (hid, grad, res):
        item.finish()
    grad.local().wait()
    res.local().wait()
    for copy in outs:
        copy.wait()


def first(n_c, n_f, n_t, mine, srows, hidden, wq, wk, wv, wo, og, weights, router, chosen, lines, shared, angle):
    rows, quarter = hidden.shape
    width = quarter * n_t
    seq = rows * n_c
    n_exp = mine * n_f * n_c
    ffe, half = weights[0].shape[1:]
    sds = jax.ShapeDtypeStruct
    part = wo.shape[1]
    n_small = 2 * n_exp + lines.shape[0]
    head, head_f = sds((seq, HD), BF), sds((seq, HD), F32)
    got = sds((mine, ffe, half), BF)
    return pl.pallas_call(
        functools.partial(first_kernel, n_c, n_f, n_exp, mine),
        out_shape=(
            sds((seq, width), BF),
            head,
            head,
            head,
            head_f,
            head_f,
            head_f,
            head_f,
            head_f,
            sds((rows, quarter), F32),
            sds((width, 3 * HD), BF),
            sds((HD, width), BF),
            sds((n_small, width), BF),
            sds((seq * n_f, width), BF),
            sds((n_f * n_c, n_t, rows, quarter), BF),
            sds((n_f * n_c, 3 * srows, part), BF),
            got,
            got,
            got,
        ),
        in_specs=[HBM] * 9 + [VMEM] * 7,
        out_specs=[HBM] + [VMEM] * 9 + [HBM] * 9,
        scratch_shapes=[
            pltpu.VMEM((seq, width), BF),
            pltpu.VMEM((width, 3 * HD), BF),
            pltpu.VMEM((HD, width), BF),
            pltpu.VMEM((n_small, width), BF),
            pltpu.VMEM((seq, HD), BF),
            pltpu.VMEM((rows, quarter), BF),
            pltpu.VMEM((rows, quarter), BF),
            pltpu.VMEM((n_small, part), BF),
            pltpu.VMEM((n_f * n_c, 3 * srows, part), BF),
            pltpu.VMEM((seq, width), BF),
            DMA((n_c, 5)),
            DMA((n_c, 5)),
            DMA((5,)),
            DMA((n_c, 3)),
            DMA((n_c, 3)),
            DMA((n_f * n_c,)),
            DMA((n_f * n_c,)),
            DMA(()),
            DMA((3, mine)),
            DMA((3, mine)),
            DMA((5,)),
        ]
        + spread_sems(n_c) * 3
        + reduce_seq_scratch(n_c, rows, quarter),
        compiler_params=pltpu.CompilerParams(
            collective_id=1, has_side_effects=True, vmem_limit_bytes=BIG
        ),
        cost_estimate=pl.CostEstimate(
            flops=5 << 30, bytes_accessed=300 << 20, transcendentals=1 << 20
        ),
        name="first",
    )(hidden, wq, wk, wv, wo, og, *weights, router, chosen, lines, *shared, angle)


def fetch_experts(n_c, n_f, mine, ffe, srows, hp, weights, shared, wgu, wd, sems):
    f = lax.axis_index("fsdp")
    wg0, wu0, wd0, wg1, wu1, wd1 = weights
    width = wd.shape[1]
    used = mine * ffe
    part = width // (n_f * n_c)
    half = width // n_f
    copies = []

    def add(src, dst):
        copies.append(pltpu.make_async_copy(src, dst, sems.at[len(copies)]))

    groups = []
    for i, (kept, got) in enumerate(((wg0, wg1), (wu0, wu1), (wd0, wd1))):
        dst, base = ((wgu, 0), (wgu, hp), (wd, 0))[i]
        for e in range(mine):
            at = pl.ds(base + e * ffe, ffe)
            add(kept.at[f * mine + e], dst.at[at, piece(f, half)])
            add(got.at[e], dst.at[at, piece(1 - f, half)])
        for b in range(n_f * n_c):
            add(
                shared.at[b, pl.ds(i * srows, srows), :],
                dst.at[pl.ds(base + used, srows), pl.ds(b * part, part)],
            )
        groups.append(copies[sum(map(len, groups)) :])
    return groups[0] + groups[1], groups[2]


def blank_rows(rows_used, hp, wgu, wd):
    blank = jnp.zeros((hp - rows_used, wd.shape[1]), BF)
    wgu[rows_used:hp, :] = blank
    wgu[hp + rows_used :, :] = blank
    wd[rows_used:, :] = blank


def gates(prob, picked, first, mine, ffe, hp):
    block, n_exp = prob.shape
    lane = lax.broadcasted_iota(jnp.int32, (block, n_exp), 1)
    gated = prob * picked
    col = lax.broadcasted_iota(jnp.int32, (block, hp), 1)
    gate = jnp.ones((block, hp), F32)
    for k in range(mine):
        g = jnp.sum(jnp.where(lane == first + k, gated, 0.0), axis=1, keepdims=True)
        gate = jnp.where((col >= k * ffe) & (col < (k + 1) * ffe), g, gate)
    return gate, lane, col


def reducer_scratch(n_f, n_c, rows, quarter, split):
    n_b = n_f * n_c
    upper = rows // 2 if split else rows
    lower = rows // 2 if split else 16
    blocks = lambda *lead: pltpu.VMEM(lead + (rows, quarter), BF)
    return [
        blocks(n_b, 2),
        blocks(n_b, 2),
        blocks(n_b, 2),
        blocks(n_b),
        blocks(n_b),
        pltpu.VMEM((n_c, upper, quarter), BF),
        pltpu.VMEM((n_c, upper, quarter), BF),
        pltpu.VMEM((n_c, rows, quarter), F32),
        blocks(n_c),
        blocks(n_c),
        pltpu.VMEM((n_c, 2, lower, quarter), BF),
        pltpu.VMEM((n_c, 2, lower, quarter), BF),
    ] + [DMA((n_b,))] * 4 + [DMA((n_c,))] * 6


N_REDUCER = 22


def when(condition, act):
    if isinstance(condition, bool):
        if condition:
            act()
    else:
        pl.when(condition)(act)


class Reducer:
    def __init__(self, n_c, scratch):
        self.n_c = n_c
        (self.out1, self.in1, self.own, self.out2, self.in2, self.out3, self.in3, self.acc,
         self.out4, self.in4, self.out5, self.in5, self.s1, self.r1, self.s2, self.r2, self.s3, self.r3,
         self.s4, self.r4, self.s5, self.r5) = scratch
        self.half = self.out3.shape[1]
        self.split = self.half < self.out4.shape[1]
        self.f, self.c, self.t = ranks()
        self.far, self.sib = opposite(self.t), sibling(self.t)

    def row_block(self, i):
        n_c = self.n_c
        group = jnp.where(i < n_c, 1 - self.f, self.f)
        return group * n_c + lax.rem(self.c + lax.rem(i, n_c) + 1, n_c)

    def core_copy(self, i):
        return remote(self.out1.at[i], self.in1.at[i], self.s1.at[i], self.r1.at[i], {"tp": self.sib})

    def far_copy(self, i, upper=False):
        src, dst = self.out2.at[i], self.in2.at[i]
        if upper:
            src, dst = src.at[pl.ds(0, self.half)], dst.at[pl.ds(0, self.half)]
        return remote(src, dst, self.s2.at[i], self.r2.at[i], {"tp": self.far})

    def other_copy(self, j):
        return remote(self.out3.at[j], self.in3.at[j], self.s3.at[j], self.r3.at[j], {"fsdp": 1 - self.f})

    def lower_copy(self, j):
        return remote(self.out5.at[j], self.in5.at[j], self.s5.at[j], self.r5.at[j], {"fsdp": 1 - self.f})

    def line_copy(self, j, to):
        return remote(self.out4.at[j], self.in4.at[j], self.s4.at[j], self.r4.at[j], {"ctx": to})

    def put(self, i, part_of):
        self.out1[i, 0] = part_of(opposite(self.sib)).astype(BF)
        self.out1[i, 1] = part_of(self.sib).astype(BF)
        self.core_copy(i).start()
        self.own[i, 0] = part_of(self.far).astype(BF)
        self.own[i, 1] = part_of(self.t).astype(BF)

    def core_sum(self, i, which):
        return self.own[i, which].astype(F32) + self.in1[i, which].astype(F32)

    def over(self, i):
        self.core_copy(i).wait()
        half, n_c = self.half, self.n_c

        def of_other():
            far = self.core_sum(i, 0)
            if self.split:
                self.out5[i, 0] = far[half:].astype(BF)
                self.out5[i, 1] = self.core_sum(i, 1)[half:].astype(BF)
                self.lower_copy(i).start()
            self.out2[i, :half] = far[:half].astype(BF)
            self.far_copy(i, True).start()

        def of_own():
            j = i - n_c
            if self.split:
                self.lower_copy(j).wait_recv()
            far = self.core_sum(i, 0)
            self.out2[i, :half] = far[:half].astype(BF)
            if self.split:
                self.out2[i, half:] = (far[half:] + self.in5[j, 0].astype(F32)).astype(BF)
            self.far_copy(i).start()

        when(i < n_c, of_other)
        when(i >= n_c, of_own)

    def after_other(self, i):
        half = self.half
        self.far_copy(i, True).wait()
        self.out3[i] = (self.core_sum(i, 1)[:half] + self.in2[i, :half].astype(F32)).astype(BF)
        self.other_copy(i).start()

    def after_own(self, i):
        j, half = i - self.n_c, self.half
        self.far_copy(i).wait()
        total = self.core_sum(i, 1) + self.in2[i].astype(F32)
        self.acc[j, :half] = total[:half]
        if self.split:
            self.acc[j, half:] = total[half:] + self.in5[j, 1].astype(F32)

    def along(self, j):
        half = self.half
        if self.split:
            self.lower_copy(j).wait_send()
        self.other_copy(j).wait()
        self.acc[j, :half] = self.acc[j, :half] + self.in3[j].astype(F32)
        total = self.acc[j]
        if j < self.n_c - 1:
            self.out4[j] = total.astype(BF)
            self.line_copy(j, lax.rem(self.c + j + 1, self.n_c)).start()
        return total

    def total(self, total):
        for j in range(self.n_c - 1):
            self.line_copy(j, self.c).wait()
            total = total + self.in4[j].astype(F32)
        return total

    def loop(self, n_b, compute):
        n_c = self.n_c

        def step(i, carry):
            def between():
                @pl.when(i >= 1)
                def _():
                    self.over(i - 1)

                @pl.when((i >= 3) & (i < 3 + n_c))
                def _():
                    self.after_other(i - 3)

                @pl.when(i >= 3 + n_c)
                def _():
                    self.after_own(i - 3)

            compute(i, between)
            return carry

        lax.fori_loop(0, n_b, step, 0)

    def drain(self, n_b, works):
        works = list(works)
        self.over(n_b - 1)
        for i in range(n_b - 4, n_b):
            if i > n_b - 4:
                self.after_own(i) if i >= self.n_c else self.after_other(i)
            if i >= self.n_c:
                total = self.along(i - self.n_c)
            if works:
                works.pop(0)()
        for work in works:
            work()
        return self.total(total)


def forward_kernel(
    n_c, n_f, mine, ffe, srows, hp, rows_all, og_all, resid, small,
    wg0, wu0, wd0, wg1, wu1, wd1, shared,
    layer_out, in_out, act_out, silu_out, slope_out, r_out, prob_out, keep_out, send_out, shared_out,
    gt, wsem, xsem, nsem, asem, tsem, osem, *scratch,
):
    f, c, t = ranks()
    n_b = n_f * n_c
    rows, quarter = resid.shape
    width = rows_all.shape[1]
    routed = mine * ffe
    rows_used = routed + srows
    n_exp = mine * n_b
    red = Reducer(n_c, scratch)

    def blocks_phase(wgu, wd, xs, ns, acts):
        gate_up, down = fetch_experts(
            n_c, n_f, mine, ffe, srows, hp, (wg0, wu0, wd0, wg1, wu1, wd1), shared, wgu, wd, wsem
        )
        for copy in gate_up + down:
            copy.start()

        def load(i, slot):
            return pltpu.make_async_copy(
                rows_all.at[piece(red.row_block(i), rows), :], xs.at[slot], xsem.at[slot]
            )

        def stores(i, slot):
            at = piece(red.row_block(i), rows)
            return [pltpu.make_async_copy(ns.at[slot], in_out.at[at, :], nsem.at[slot])] + [
                pltpu.make_async_copy(acts.at[slot, k], out.at[at, :], asem.at[slot, k])
                for k, out in enumerate((act_out, silu_out, slope_out))
            ]

        load(0, 0).start()
        blank_rows(rows_used, hp, wgu, wd)
        greet([{"tp": red.sib}, {"tp": red.far}, {"fsdp": 1 - f}] + line_peers(c, n_c))
        for copy in gate_up:
            copy.wait()

        def compute(i, between):
            slot = lax.rem(i, 2)
            b = red.row_block(i)
            at = piece(b, rows)
            load(i, slot).wait()

            @pl.when(i + 1 < n_b)
            def _():
                load(i + 1, 1 - slot).start()

            @pl.when(i >= 2)
            def _():
                for copy in stores(i - 2, slot):
                    copy.wait()

            h = xs[slot].astype(F32)
            r = lax.rsqrt(jnp.sum(h * h, axis=1, keepdims=True) / width + EPS)
            r_out[at, :] = jnp.broadcast_to(r, (rows, HD))
            gain = small[2 * n_exp + 1 : 2 * n_exp + 2, :].astype(F32)
            n = (h * r * gain).astype(BF)
            ns[slot] = n
            logits = dot_nt(n, small[:n_exp, :])
            e = jnp.exp(logits - jnp.max(logits, axis=1, keepdims=True))
            prob = e / jnp.sum(e, axis=1, keepdims=True)
            prob_out[at, :] = prob
            gate, _, _ = gates(prob, small[n_exp : 2 * n_exp, at].astype(F32).T, (c * n_f + f) * mine, mine, ffe, hp)
            ab = dot_nt(n, wgu[...])
            between()
            a, up = ab[:, :hp], ab[:, hp:]
            sig = 1.0 / (1.0 + jnp.exp(-a))
            silu = a * sig
            act = (silu * up).astype(BF)
            acts[slot, 0] = act
            acts[slot, 1] = silu.astype(BF)
            acts[slot, 2] = (up * (sig * (1.0 + a * (1.0 - sig)))).astype(BF)
            actg = (act.astype(F32) * gate).astype(BF)
            gt[:, at] = actg.T[:rows_used, :]
            for copy in stores(i, slot):
                copy.start()

            @pl.when(i == 0)
            def _():
                for copy in down:
                    copy.wait()

            red.put(i, lambda q: dot_nn(actg, wd[:, piece(q, quarter)]))

        red.loop(n_b, compute)
        for i in range(n_b - 2, n_b):
            for copy in stores(i, i % 2):
                copy.wait()

    pl.run_scoped(
        blocks_phase,
        pltpu.VMEM((2 * hp, width), BF),
        pltpu.VMEM((hp, width), BF),
        pltpu.VMEM((2, rows, width), BF),
        pltpu.VMEM((2, rows, width), BF),
        pltpu.VMEM((2, 3, rows, hp), BF),
    )

    def grads_phase(tiles, keeps, sends, shs):
        def tile_of(s):
            return (1 - f) * 2 + s if s < 2 else f * 2 + s - 2

        def tile_load(s):
            return pltpu.make_async_copy(og_all.at[:, tile_of(s)], tiles.at[s % 2], tsem.at[s % 2])

        def out_copies(s):
            cols = pl.ds(s % 2 * quarter, quarter)
            if s < 2:
                src, dst = sends.at[s], send_out.at[:, :, cols]
            else:
                src, dst = keeps.at[s - 2], keep_out.at[:, :, cols]
            return [
                pltpu.make_async_copy(src, dst, osem.at[s, 0]),
                pltpu.make_async_copy(
                    shs.at[s], shared_out.at[:, piece(tile_of(s), quarter)], osem.at[s, 1]
                ),
            ]

        def work(s):
            def run():
                tile_load(s).wait()
                if s < 3:
                    tile_load(s + 1).start()
                g = dot_nn(gt[...], tiles[s % 2].reshape(n_b * rows, quarter))
                if s < 2:
                    sends[s] = g[:routed].astype(BF).reshape(mine, ffe, quarter)
                else:
                    keeps[s - 2] = g[:routed].astype(BF).reshape(mine, ffe, quarter)
                shs[s] = g[routed:].astype(BF)
                for copy in out_copies(s):
                    copy.start()

            return run

        tile_load(0).start()
        total = red.drain(n_b, [work(s) for s in range(4)])
        layer_out[...] = (resid[...] + total).astype(BF)
        for s in range(4):
            for copy in out_copies(s):
                copy.wait()

    pl.run_scoped(
        grads_phase,
        pltpu.VMEM((2, n_b, rows, quarter), BF),
        pltpu.VMEM((2, mine, ffe, quarter), BF),
        pltpu.VMEM((2, mine, ffe, quarter), BF),
        pltpu.VMEM((4, srows, quarter), BF),
    )


def expert_sizes(n_c, n_f, n_t, mine, ffe, srows, width):
    used = mine * ffe + srows
    return used, -(-used // HD) * HD, 3 * (2 * mine + n_f * n_c)


def forward(n_c, n_f, n_t, mine, ffe, srows, rows_all, og_all, resid, small, kept, got, shared):
    total, width = rows_all.shape
    rows, quarter = resid.shape
    n_b = n_f * n_c
    n_exp = mine * n_b
    used, hp, n_fetch = expert_sizes(n_c, n_f, n_t, mine, ffe, srows, width)
    sds = jax.ShapeDtypeStruct
    return pl.pallas_call(
        functools.partial(forward_kernel, n_c, n_f, mine, ffe, srows, hp),
        out_shape=(
            sds((rows, quarter), BF),
            sds((total, width), BF),
            sds((total, hp), BF),
            sds((total, hp), BF),
            sds((total, hp), BF),
            sds((total, HD), F32),
            sds((total, n_exp), F32),
            sds((mine, ffe, width // n_f), BF),
            sds((mine, ffe, width // n_f), BF),
            sds((srows, width), BF),
        ),
        in_specs=[HBM, HBM, VMEM, VMEM] + [HBM] * 7,
        out_specs=[VMEM, HBM, HBM, HBM, HBM, VMEM, VMEM, HBM, HBM, HBM],
        scratch_shapes=[
            pltpu.VMEM((used, total), BF),
            DMA((n_fetch,)),
            DMA((2,)),
            DMA((2,)),
            DMA((2, 3)),
            DMA((2,)),
            DMA((4, 2)),
        ]
        + reducer_scratch(n_f, n_c, rows, quarter, True),
        compiler_params=pltpu.CompilerParams(
            collective_id=5, has_side_effects=True, vmem_limit_bytes=BIG
        ),
        cost_estimate=pl.CostEstimate(
            flops=8 * total * width * used, bytes_accessed=80 << 20, transcendentals=total * used
        ),
        name="forward",
    )(rows_all, og_all, resid, small, *kept, *got, shared)


def backward_kernel(
    n_c, n_f, mine, ffe, srows, hp, og_all, act, silu, slope, moe_in, r_all, shared_d, prob_in, small,
    resid, og, wg0, wu0, wd0, wg1, wu1, wd1, shared,
    mid_out, gain_out, seq_out, shared_out, shs_out, kg_out, ku_out, gg_out, gu_out, lg_out, lu_out,
    gt, blk, r_own, sends, shs, wsem, xsem, tsem, ksem, ss, sr, rs, es, ds, dr, dl, *rest,
):
    f, c, t = ranks()
    n_b = n_f * n_c
    rows, quarter = resid.shape
    width = shared_d.shape[1]
    n_exp = mine * n_b
    routed = mine * ffe
    rows_used = routed + srows
    first = (c * n_f + f) * mine
    reduce_scratch, rest = rest[:N_REDUCER], rest[N_REDUCER:]
    red = Reducer(n_c, reduce_scratch)

    cols = width // n_b

    def exchange(act):
        to_each(lambda b: shared_d.at[:, piece(b, cols)], shared_out, n_f, n_c, (ds, dr, dl), act)

    def blocks_phase(wgu, wd, ogs, acts):
        gate_up, down = fetch_experts(
            n_c, n_f, mine, ffe, srows, hp, (wg0, wu0, wd0, wg1, wu1, wd1), shared, wgu, wd, wsem
        )
        for copy in down + gate_up:
            copy.start()

        def loads(i, slot):
            b = red.row_block(i)
            return [
                pltpu.make_async_copy(
                    og_all.at[b, q], ogs.at[slot, :, pl.ds(q * quarter, quarter)], xsem.at[slot, q]
                )
                for q in range(4)
            ] + [
                pltpu.make_async_copy(src.at[piece(b, rows), :], acts.at[slot, k], xsem.at[slot, 4 + k])
                for k, src in enumerate((act, silu, slope))
            ]

        for copy in loads(0, 0):
            copy.start()
        blank_rows(rows_used, hp, wgu, wd)
        greet([{"tp": red.sib}, {"tp": red.far}, {"tp": opposite(red.sib)}] + each_peers(f, c, n_f, n_c))
        exchange("start")
        for copy in down:
            copy.wait()

        def compute(i, between):
            slot = lax.rem(i, 2)
            at = piece(red.row_block(i), rows)
            for copy in loads(i, slot):
                copy.wait()

            @pl.when(i + 1 < n_b)
            def _():
                for copy in loads(i + 1, 1 - slot):
                    copy.start()

            prob = prob_in[at, :]
            chosen = small[n_exp : 2 * n_exp, at].astype(F32).T
            gate, lane, col = gates(prob, chosen, first, mine, ffe, hp)
            dh = dot_nt(ogs[slot], wd[...])
            between()
            ad = acts[slot, 0].astype(F32) * dh
            p_grad = jnp.zeros(prob.shape, F32)
            for k in range(mine):
                s = jnp.sum(
                    jnp.where((col >= k * ffe) & (col < (k + 1) * ffe), ad, 0.0), axis=1, keepdims=True
                )
                p_grad = jnp.where(lane == first + k, s, p_grad)
            p_grad = p_grad * chosen
            logit_f = prob * (p_grad - jnp.sum(prob * p_grad, axis=1, keepdims=True))
            logit_grad = logit_f.astype(BF)
            dg = dh * gate
            da = (dg * acts[slot, 2].astype(F32)).astype(BF)
            db = (dg * acts[slot, 1].astype(F32)).astype(BF)
            gt[:rows_used, at] = da.T[:rows_used, :]
            gt[rows_used : 2 * rows_used, at] = db.T[:rows_used, :]
            gt[2 * rows_used :, at] = logit_f.T.astype(BF)
            dab = jnp.concatenate([da, db], axis=1)

            @pl.when(i == 0)
            def _():
                for copy in gate_up:
                    copy.wait()

            def part_of(q):
                cols = piece(q, quarter)
                return dot_nn(dab, wgu[:, cols]) + dot_nn(logit_grad, small[:n_exp, cols])

            red.put(i, part_of)

        red.loop(n_b, compute)

    pl.run_scoped(
        blocks_phase,
        pltpu.VMEM((2 * hp, width), BF),
        pltpu.VMEM((hp, width), BF),
        pltpu.VMEM((2, rows, width), BF),
        pltpu.VMEM((2, 3, rows, hp), BF),
    )

    def send_copy(s, m):
        if s:
            return pltpu.make_async_copy(sends.at[s, m], (lg_out, lu_out)[m], ss.at[s, m])
        return remote(sends.at[s, m], (gg_out, gu_out)[m], ss.at[s, m], sr.at[m], {"fsdp": 1 - f})

    def grads_phase(tiles, keeps):
        def tile_of(s):
            return (1 - f) * 2 + s if s < 2 else f * 2 + s - 2

        def tile_load(s):
            return pltpu.make_async_copy(
                moe_in.at[:, piece(tile_of(s), quarter)], tiles.at[s % 2], tsem.at[s % 2]
            )

        def keep_copy(s, m):
            dst = (kg_out, ku_out)[m].at[:, :, pl.ds((s - 2) * quarter, quarter)]
            return pltpu.make_async_copy(keeps.at[s - 2, m], dst, ksem.at[s - 2, m])

        def work(s):
            def run():
                tile_load(s).wait()
                if s < 3:
                    tile_load(s + 1).start()
                g = dot_nn(gt[...], tiles[s % 2])
                cols = piece(tile_of(s), quarter)
                for m in range(2):
                    base = m * rows_used
                    if s < 2:
                        sends[s, m] = g[base : base + routed].astype(BF).reshape(mine, ffe, quarter)
                        send_copy(s, m).start()
                    else:
                        keeps[s - 2, m] = g[base : base + routed].astype(BF).reshape(mine, ffe, quarter)
                        keep_copy(s, m).start()
                    shs[m * srows : (m + 1) * srows, cols] = g[base + routed : base + rows_used].astype(BF)
                shs[2 * srows :, cols] = g[2 * rows_used :].astype(BF)

            return run

        tile_load(0).start()
        blk[...] = red.drain(n_b, [work(s) for s in range(4)])
        for s in (2, 3):
            for m in range(2):
                keep_copy(s, m).wait()

    fetch = pltpu.make_async_copy(r_all.at[piece(f * n_c + c, rows), :], r_own, rs)
    fetch.start()
    pl.run_scoped(
        grads_phase,
        pltpu.VMEM((2, n_b * rows, quarter), BF),
        pltpu.VMEM((2, 2, mine, ffe, quarter), BF),
    )
    shs_copy = pltpu.make_async_copy(shs, shs_out, es)
    shs_copy.start()
    fetch.wait()
    gain = small[2 * n_exp + 1 : 2 * n_exp + 2, piece(t, quarter)].astype(F32)
    back, gain_part = norm_grad(resid[...], r_own[:, :1], gain, blk[...], width, *rest[:4])
    gain_out[...] = jnp.broadcast_to(gain_part, gain_out.shape)
    grad = og[...].astype(F32) + back
    mid_out[...] = grad
    own = rest[4]
    own[...] = grad.astype(BF)

    def place(g, cc, tt):
        return seq_out.at[piece(cc, rows), piece(tt, quarter)]

    sequence = Spread(own, place, n_c, False, rest[5:])
    sequence.start()
    sequence.line()
    sequence.far(0)
    sequence.arrived(0)
    sequence.finish()
    sequence.local().wait()
    exchange("wait")
    shs_copy.wait()
    for s in range(2):
        for m in range(2):
            send_copy(s, m).wait()


def backward(
    n_c, n_f, n_t, mine, ffe, srows, og_all, act, silu, slope, moe_in, r_all, shared_d, prob, small,
    resid, og, kept, got, shared,
):
    total, width = moe_in.shape
    rows, quarter = resid.shape
    n_b = n_f * n_c
    n_exp = mine * n_b
    used, hp, n_fetch = expert_sizes(n_c, n_f, n_t, mine, ffe, srows, width)
    sds = jax.ShapeDtypeStruct
    kept_g = sds((mine, ffe, width // n_f), BF)
    sent_g = sds((mine, ffe, quarter), BF)
    return pl.pallas_call(
        functools.partial(backward_kernel, n_c, n_f, mine, ffe, srows, hp),
        out_shape=(
            sds((rows, quarter), F32),
            sds((8, quarter), F32),
            sds((rows * n_c, width), BF),
            sds((n_b, srows, width // n_b), BF),
            sds((2 * srows + n_exp, width), BF),
            kept_g,
            kept_g,
            sent_g,
            sent_g,
            sent_g,
            sent_g,
        ),
        in_specs=[HBM] * 7 + [VMEM] * 4 + [HBM] * 7,
        out_specs=[VMEM, VMEM] + [HBM] * 9,
        scratch_shapes=[
            pltpu.VMEM((2 * used + n_exp, total), BF),
            pltpu.VMEM((rows, quarter), F32),
            pltpu.VMEM((rows, HD), F32),
            pltpu.VMEM((2, 2, mine, ffe, quarter), BF),
            pltpu.VMEM((2 * srows + n_exp, width), BF),
            DMA((n_fetch,)),
            DMA((2, 7)),
            DMA((2,)),
            DMA((2, 2)),
            DMA((2, 2)),
            DMA((2,)),
            DMA(()),
            DMA(()),
            DMA((n_b,)),
            DMA((n_b,)),
            DMA(()),
        ]
        + reducer_scratch(n_f, n_c, rows, quarter, False)
        + norm_grad_scratch(rows)
        + [pltpu.VMEM((rows, quarter), BF)]
        + spread_sems(n_c),
        compiler_params=pltpu.CompilerParams(
            collective_id=3, has_side_effects=True, vmem_limit_bytes=BIG
        ),
        cost_estimate=pl.CostEstimate(
            flops=10 * total * width * used, bytes_accessed=200 << 20, transcendentals=0
        ),
        name="backward",
    )(
        og_all, act, silu, slope, moe_in, r_all, shared_d, prob, small, resid, og,
        *kept, *got, shared,
    )


def finish_kernel(n_plain, f_ref, *refs):
    ga, gb, ua, ub, d, kg, ku, kd, shared = refs[:9]
    plain = refs[9 : 9 + n_plain]
    og, ou, od, shared_out = refs[9 + n_plain : 13 + n_plain]
    step = pl.program_id(0)
    f = f_ref[0]
    n_e = kg.shape[0]

    def put(at):
        for keep, out in ((kg, og), (ku, ou), (kd, od)):
            out[at : at + n_e] = keep[...].astype(F32)
        for out, halves in ((og, (ga, gb)), (ou, (ua, ub))):
            @pl.when(step < 2)
            def _():
                out[n_e - at : 2 * n_e - at] = halves[0][...].astype(F32)

            @pl.when(step >= 2)
            def _():
                out[n_e - at : 2 * n_e - at] = halves[1][...].astype(F32)

        od[n_e - at : 2 * n_e - at] = d[...].astype(F32)

    @pl.when(f == 0)
    def _():
        put(0)

    @pl.when(f != 0)
    def _():
        put(n_e)

    own = shared_out.shape[0] // shared.shape[0]
    for b in range(shared.shape[0]):
        shared_out[b * own : (b + 1) * own, :] = shared[b, :own, :].astype(F32)
    for src, dst in zip(plain, refs[13 + n_plain :]):
        dst[...] = src[...]


def finish(f_rank, own_shared, arrived, kept, shared, plain):
    mine, ffe, quarter = arrived[0].shape
    half = kept[0].shape[2]
    tile = half // 4
    n_b, srows, part = shared.shape
    first = pl.BlockSpec((mine, ffe, tile), lambda i, f: (0, 0, jnp.minimum(i, 1)))
    second = pl.BlockSpec((mine, ffe, tile), lambda i, f: (0, 0, jnp.maximum(i - 2, 0)))
    every = pl.BlockSpec((mine, ffe, tile), lambda i, f: (0, 0, i))
    out = pl.BlockSpec((2 * mine, ffe, tile), lambda i, f: (0, 0, i))

    def rows_of(x):
        if x.shape[0] % 64:
            return pl.BlockSpec(x.shape, lambda i, f: (0, 0))
        return pl.BlockSpec((x.shape[0] // 4, x.shape[1]), lambda i, f: (i, 0))

    shared_grad = jax.ShapeDtypeStruct((n_b * own_shared, part), F32)
    return pl.pallas_call(
        functools.partial(finish_kernel, len(plain)),
        grid_spec=pltpu.PrefetchScalarGridSpec(
            num_scalar_prefetch=1,
            grid=(4,),
            in_specs=[first, second, first, second, every]
            + [every] * 3
            + [pl.BlockSpec((n_b // 4, srows, part), lambda i, f: (i, 0, 0))]
            + [rows_of(x) for x in plain],
            out_specs=[out] * 3 + [rows_of(shared_grad)] + [rows_of(x) for x in plain],
        ),
        out_shape=tuple(jax.ShapeDtypeStruct((2 * mine, ffe, half), F32) for k in kept)
        + (shared_grad,)
        + tuple(jax.ShapeDtypeStruct(x.shape, x.dtype) for x in plain),
        compiler_params=pltpu.CompilerParams(vmem_limit_bytes=BIG),
        name="finish",
    )(f_rank, *arrived, *kept, shared, *plain)


def norm_grad(values, r, gain, grad, width, out, into, send, recv):
    f, c, t = ranks()
    rows = values.shape[0]
    local = jnp.sum(grad * gain * values, axis=1, keepdims=True)
    out[...] = jnp.broadcast_to(local, (rows, HD)).T[:8, :]
    peers = [sibling(t), opposite(t), opposite(sibling(t))]
    copies = [
        remote(out, into.at[i], send.at[i], recv.at[i], {"tp": peer}) for i, peer in enumerate(peers)
    ]
    for copy in copies:
        copy.start()
    gain_part = jnp.sum(grad * values * r, axis=0, keepdims=True)
    total = out[...]
    for i, copy in enumerate(copies):
        copy.wait()
        total = total + into[i]
    total = jnp.broadcast_to(total[0:1, :], (HD, rows)).T[:, :1]
    return r * gain * grad - values * (r * r * r * (total / width)), gain_part


def norm_grad_scratch(rows):
    return [
        pltpu.VMEM((8, rows), F32),
        pltpu.VMEM((3, 8, rows), F32),
        DMA((3,)),
        DMA((3,)),
    ]


def attend_back(block, mid, wo, q, k, v, hf, lse, cosine, sine, dqkv, hg, dq, dk, dv):
    seq = mid.shape[0]
    scale_att = HD ** (-0.5)
    for start in range(0, seq, block):
        at = pl.ds(start, block)
        hg[at, :] = dot_nt(mid[at, :], wo[...]).astype(BF)
    dk[...] = jnp.zeros_like(dk)
    dv[...] = jnp.zeros_like(dv)
    for start in range(0, seq, block):
        at = pl.ds(start, block)
        seen = start + block
        qb, hb = q[at, :], hg[at, :]
        delta = jnp.sum(hb.astype(F32) * hf[at, :], axis=1, keepdims=True)
        s = dot_nt(qb, k[:seen, :]) * scale_att
        row = lax.broadcasted_iota(jnp.int32, (block, seen), 0) + start
        col = lax.broadcasted_iota(jnp.int32, (block, seen), 1)
        p = jnp.where(col <= row, jnp.exp(s - lse[at, :1]), 0.0)
        ds = (p * (dot_nt(hb, v[:seen, :]) - delta)).astype(BF)
        dq[at, :] = dot_nn(ds, k[:seen, :]) * scale_att
        dk[:seen, :] += dot_tn(ds, qb) * scale_att
        dv[:seen, :] += dot_tn(p.astype(BF), hb)

    def rotate(values, at):
        return (values * cosine[at, :] - pltpu.roll(values, HD // 2, 1) * sine[at, :]).astype(BF)

    for start in range(0, seq, block):
        at = pl.ds(start, block)
        dqkv[at, :HD] = rotate(dq[at, :], at)
        dqkv[at, HD : 2 * HD] = rotate(dk[at, :], at)
        dqkv[at, 2 * HD :] = dv[at, :].astype(BF)


def last_kernel(
    n_c, n_f, n_t, n_exp, own_shared, mid_in, wo, q, k, v, hf, lse, cosine, sine, normed_in, wqkv_in, hidden, r_all,
    small, mid_grad, gain2, shs, lg, lu,
    in_out, gq, gk, gv, go, gains_out, router_out, sg_out, su_out, lg_out, lu_out,
    mid_seq, normed, wqkv, big, dqkv, hg, dq, dk, dv, gattn, shs_in, rpart, hs, hr, hl, es, er, rin, rss, rsr, r_own, mine, inx, own, outz, inz, gsend, gin, rs, sx, rx, lx, sz, rz, gs, gr, *rest,
):
    f, c, t = ranks()
    rows, quarter = hidden.shape
    tokens, width = normed.shape
    part = width // (n_f * n_c)
    here = f * n_c + c
    srows = (shs.shape[0] - n_exp) // 2
    others = []
    for df in range(n_f):
        for dc in range(n_c):
            for dt in range(n_t):
                if df or dc or dt:
                    others.append(
                        {
                            "fsdp": lax.rem(f + df, n_f),
                            "ctx": lax.rem(c + dc, n_c),
                            "tp": lax.rem(t + dt, n_t),
                        }
                    )
    large = [
        pltpu.make_async_copy(src, dst, big.at[i])
        for i, (src, dst) in enumerate(((mid_in, mid_seq), (wqkv_in, wqkv), (normed_in, normed)))
    ]
    for copy in large:
        copy.start()
    gin[...] = jnp.zeros_like(gin)
    greet(others)
    order = [2, 1, 3, 0] if n_c == 4 else list(range(1, n_c)) + [0]

    def cross(d):
        cc = lax.rem(c + d, n_c)
        return remote(
            gattn.at[:, piece((1 - f) * n_c + cc, part)], inx.at[d], sx.at[d], rx.at[d], {"fsdp": 1 - f}
        )

    def keep(d):
        cc = lax.rem(c + d, n_c)
        return pltpu.make_async_copy(gattn.at[:, piece(f * n_c + cc, part)], own.at[d], lx.at[d])

    def line(d, to):
        return remote(outz.at[d], inz.at[d], sz.at[d], rz.at[d], {"ctx": to})

    router_copies = [
        remote(rpart, rin.at[i], rss.at[i], rsr.at[i], {"tp": peer})
        for i, peer in enumerate([sibling(t), opposite(t), opposite(sibling(t))])
    ]
    shared = lambda act: to_each(lambda b: shs.at[:, piece(b, part)], shs_in, n_f, n_c, (hs, hr, hl), act)
    late = [
        remote(src, dst, es.at[i], er.at[i], {"fsdp": 1 - f})
        for i, (src, dst) in enumerate(((lg, lg_out), (lu, lu_out)))
    ]
    shared("start")
    fetch = pltpu.make_async_copy(r_all.at[piece(c, rows), :], r_own, rs)
    fetch.start()
    late[0].start()
    large[0].wait()
    attend_back(rows, mid_seq, wo, q, k, v, hf, lse, cosine, sine, dqkv, hg, dq, dk, dv)
    gattn[3 * HD :, :] = dot_tn(hf[...].astype(BF), mid_seq[...]).astype(BF)

    large[1].wait()

    def weights():
        large[2].wait()
        gattn[: 3 * HD, :] = dot_tn(dqkv[...], normed[...]).astype(BF)
        for d in order:
            cross(d).start()
            keep(d).start()
        late[1].start()


    def part_of(cc, q):
        return dot_nt(dqkv[piece(cc, rows), :], wqkv[piece(q, quarter), :])

    def pass_weights():
        for d in order:
            cross(d).wait()
            keep(d).wait()
            both = own[d].astype(F32) + inx[d].astype(F32)
            if d:
                outz[d] = both.astype(BF)
                line(d, lax.rem(c + d, n_c)).start()
            else:
                mine[...] = both

    total = reduce_seq(part_of, n_c, rest[:13], weights, pass_weights)
    fetch.wait()
    gain = small[2 * n_exp : 2 * n_exp + 1, piece(t, quarter)].astype(F32)
    back, gain_part = norm_grad(
        hidden[...].astype(F32), r_own[:, :1], gain, total, width, *rest[13:17]
    )
    in_out[...] = mid_grad[...] + back

    gsend[0:1, :] = gain_part
    gsend[1:2, :] = gain2[0:1, :]
    gsend[2:, :] = jnp.zeros((6, quarter), F32)
    per = quarter // part
    holder = here // per
    def gain_copy(h, tt):
        b = t * per + h
        return remote(
            gsend.at[:, pl.ds(h * part, part)],
            gin.at[here],
            gs.at[h * n_t + tt],
            gr.at[here],
            {"fsdp": b // n_c, "ctx": lax.rem(b, n_c), "tp": jnp.int32(tt)},
        )

    def is_me(h, tt):
        return (t * per + h == here) & (t == tt)

    for h in range(per):
        for tt in range(n_t):

            @pl.when(jnp.logical_not(is_me(h, tt)))
            def _():
                gain_copy(h, tt).start()

    def put(src, block):
        at = piece(src, HD)
        for i, ref in enumerate((gq, gk, gv)):
            ref[:, at] = block[i * HD : (i + 1) * HD, :].T
        go[at, :] = block[3 * HD :, :]

    shared("wait")
    rpart[...] = jnp.sum(shs_in[:, 2 * srows :, :].astype(F32), axis=0)
    for copy in router_copies:
        copy.start()
    for b in range(n_f * n_c):
        at = pl.ds(b * own_shared, own_shared)
        sg_out[at, :] = shs_in[b, :own_shared, :].astype(F32)
        su_out[at, :] = shs_in[b, srows : srows + own_shared, :].astype(F32)
    put(c, mine[...])
    for d in order[:-1]:
        line(d, c).wait()
        put(lax.rem(c - d + n_c, n_c), inz[d].astype(F32))
    for h in range(per):
        for tt in range(n_t):

            @pl.when(jnp.logical_not(is_me(h, tt)))
            def _():
                gain_copy(h, tt).wait_send()

    for b in range(n_f * n_c):

        @pl.when((b != here) | (holder != t))
        def _():
            remote(gin.at[b], gin.at[b], gs.at[0], gr.at[b], {"tp": sibling(t)}).wait_recv()

    own_part = jnp.where(
        holder == t,
        gsend[:, piece(lax.rem(here, per), part)],
        jnp.zeros((8, part), F32),
    )
    gains_out[...] = own_part + jnp.sum(gin[...], axis=0)
    for copy in router_copies + late:
        copy.wait()
    router_out[...] = rpart[...] + jnp.sum(rin[...], axis=0)


def last(
    n_c, n_f, n_t, n_exp, own_shared, mid_seq, wo, q, k, v, hf, lse, cosine, sine, normed, wqkv, hidden, r_all,
    small, mid_grad, gain2, shs, lg, lu,
):
    rows, quarter = hidden.shape
    seq, width = normed.shape
    part = width // (n_f * n_c)
    sds = jax.ShapeDtypeStruct
    slab = pltpu.VMEM((n_c, 4 * HD, part), BF)
    head_f = pltpu.VMEM((seq, HD), F32)
    shared_grad = sds((n_f * n_c * own_shared, part), F32)
    return pl.pallas_call(
        functools.partial(last_kernel, n_c, n_f, n_t, n_exp, own_shared),
        out_shape=(
            sds((rows, quarter), F32),
            sds((part, n_c * HD), F32),
            sds((part, n_c * HD), F32),
            sds((part, n_c * HD), F32),
            sds((n_c * HD, part), F32),
            sds((8, part), F32),
            sds((n_exp, part), F32),
            shared_grad,
            shared_grad,
            sds(lg.shape, BF),
            sds(lu.shape, BF),
        ),
        in_specs=[HBM] + [VMEM] * 8 + [HBM] * 2 + [VMEM, HBM] + [VMEM] * 3 + [HBM] * 3,
        out_specs=[VMEM] * 9 + [HBM] * 2,
        scratch_shapes=[
            pltpu.VMEM((seq, width), BF),
            pltpu.VMEM((seq, width), BF),
            pltpu.VMEM((width, 3 * HD), BF),
            DMA((3,)),
            pltpu.VMEM((seq, 3 * HD), BF),
            pltpu.VMEM((seq, HD), BF),
            head_f,
            head_f,
            head_f,
            pltpu.VMEM((4 * HD, width), BF),
            pltpu.VMEM((n_f * n_c, shs.shape[0], part), BF),
            pltpu.VMEM((n_exp, part), F32),
            DMA((n_f * n_c,)),
            DMA((n_f * n_c,)),
            DMA(()),
            DMA((2,)),
            DMA((2,)),
            pltpu.VMEM((3, n_exp, part), F32),
            DMA((3,)),
            DMA((3,)),
            pltpu.VMEM((rows, HD), F32),
            pltpu.VMEM((4 * HD, part), F32),
            slab,
            slab,
            slab,
            slab,
            pltpu.VMEM((8, quarter), F32),
            pltpu.VMEM((n_f * n_c, 8, part), F32),
            DMA(()),
            DMA((n_c,)),
            DMA((n_c,)),
            DMA((n_c,)),
            DMA((n_c,)),
            DMA((n_c,)),
            DMA((quarter // part * n_t,)),
            DMA((n_f * n_c,)),
        ]
        + reduce_seq_scratch(n_c, rows, quarter)
        + norm_grad_scratch(rows),
        compiler_params=pltpu.CompilerParams(
            collective_id=4, has_side_effects=True, vmem_limit_bytes=BIG
        ),
        cost_estimate=pl.CostEstimate(flops=8 << 30, bytes_accessed=150 << 20, transcendentals=1 << 20),
        name="last",
    )(
        mid_seq, wo, q, k, v, hf, lse, cosine, sine, normed, wqkv, hidden, r_all, small, mid_grad, gain2,
        shs, lg, lu,
    )


def per_device_seq(
    hidden_in,
    positions,
    chosen,
    out_grad,
    attn_gain,
    w_query,
    w_key,
    w_value,
    w_out,
    moe_gain,
    router,
    shared_gate,
    shared_up,
    shared_down,
    expert_gate,
    expert_up,
    expert_down,
):
    f_rank, c_rank, t_rank = ranks()
    n_f, n_c, n_t = (lax.axis_size(name) for name in ("fsdp", "ctx", "tp"))
    rows, quarter = hidden_in.shape
    width = quarter * n_t
    part = w_query.shape[0]
    seq = rows * n_c
    n_exp = router.shape[1]
    mine = n_exp // n_c // n_f
    ffe = expert_gate.shape[2]
    group = ("fsdp", "ctx")
    every = ("fsdp", "ctx", "tp")
    n_b = n_f * n_c
    own_shared = shared_gate.shape[1] // n_b
    srows = -(-own_shared // 16) * 16
    f_arr = f_rank.astype(jnp.int32).reshape(1)
    swap = [(i, n_f - 1 - i) for i in range(n_f)]
    weights = (expert_gate.swapaxes(1, 2), expert_up.swapaxes(1, 2), expert_down)

    line = jnp.arange(16)[:, None]
    lines = jnp.where(line == 0, attn_gain[None], jnp.zeros((), BF))
    lines = jnp.where(line == 1, moe_gain[None], lines)
    lines = jnp.where(line == 2, (positions // 64).astype(BF)[None], lines)
    lines = jnp.where(line == 3, (positions % 64).astype(BF)[None], lines)
    lane = np.arange(HD)
    inverse = 10000.0 ** (-(lane % (HD // 2)) * 2.0 / HD)
    angle = jnp.asarray(np.stack([inverse, np.where(lane < HD // 2, -1.0, 1.0)]).astype(np.float32))
    (
        normed, q, k, v, heads_f, lse, r_one, cosine, sine, resid_mid,
        wqkv, wo, small, resid_all, grad_all, shared, *got,
    ) = first(
        n_c, n_f, n_t, mine, srows, hidden_in, w_query, w_key, w_value, w_out, out_grad, weights,
        router.T, chosen.T, lines, (shared_gate.T, shared_up.T, shared_down), angle,
    )
    sizes = (n_c, n_f, n_t, mine, ffe, srows)
    layer_out, moe_in, act, silu, slope, r_two, prob, kd, sd, shared_d = forward(
        *sizes, resid_all, grad_all, resid_mid, small, weights, got, shared
    )
    arrived_d = lax.ppermute(sd, "fsdp", swap)
    mid_grad, gain_two_part, mid_seq, shared_back, shs, kg, ku, gg, gu, lg, lu = backward(
        *sizes, grad_all, act, silu, slope, moe_in, r_two, shared_d, prob, small,
        resid_mid, out_grad, weights, got, shared,
    )
    input_grad, gq, gk, gv, go, gains, router_grad, shared_g, shared_u, lg, lu = last(
        n_c, n_f, n_t, n_exp, own_shared, mid_seq, wo, q, k, v, heads_f, lse, cosine, sine, normed, wqkv,
        hidden_in, r_one, small, mid_grad, gain_two_part, shs, lg, lu,
    )
    plain = (layer_out, input_grad, gq, gk, gv, go, router_grad, shared_g, shared_u)
    eg, eu, ed, shared_d, layer_out, input_grad, gq, gk, gv, go, router_grad, shared_g, shared_u = finish(
        f_arr, own_shared, (gg, lg, gu, lu, arrived_d), (kg, ku, kd), shared_back, plain
    )

    return (
        layer_out,
        input_grad,
        gains[0],
        gq,
        gk,
        gv,
        go,
        gains[1],
        router_grad.T,
        shared_g.T,
        shared_u.T,
        shared_d,
        eg.swapaxes(1, 2),
        eu.swapaxes(1, 2),
        ed,
    )


def one_head_each(mesh, args):
    n_f, n_c, n_t = (mesh.shape[name] for name in ("fsdp", "ctx", "tp"))
    heads = args[5].shape[1] // HD
    experts = args[10].shape[1]
    return (
        n_f == 2
        and n_t == 4
        and heads == n_c * n_t
        and experts % (n_f * n_c) == 0
        and args[11].shape[1] % (8 * n_f * n_c * n_t) == 0
    )


def solution(mesh):
    placed = (
        P(("fsdp", "ctx"), "tp"),
        P(("fsdp", "ctx")),
        P(("fsdp", "ctx"), None),
        P(("fsdp", "ctx"), "tp"),
        P(("fsdp", "ctx")),
        P(("fsdp", "ctx"), "tp"),
        P(("fsdp", "ctx"), "tp"),
        P(("fsdp", "ctx"), "tp"),
        P("tp", ("fsdp", "ctx")),
        P(("fsdp", "ctx")),
        P(("fsdp", "ctx"), None),
        P(("fsdp", "ctx"), "tp"),
        P(("fsdp", "ctx"), "tp"),
        P("tp", ("fsdp", "ctx")),
        P("ctx", "fsdp", "tp"),
        P("ctx", "fsdp", "tp"),
        P("ctx", "tp", "fsdp"),
    )
    def run(*args):
        body = per_device_seq if one_head_each(mesh, args) else per_device
        return jax.shard_map(
        body,
        mesh=mesh,
        in_specs=placed,
        out_specs=(
            P(("fsdp", "ctx"), "tp"),
            P(("fsdp", "ctx"), "tp"),
            P(("fsdp", "ctx")),
            P(("fsdp", "ctx"), "tp"),
            P(("fsdp", "ctx"), "tp"),
            P(("fsdp", "ctx"), "tp"),
            P("tp", ("fsdp", "ctx")),
            P(("fsdp", "ctx")),
            P(("fsdp", "ctx"), None),
            P(("fsdp", "ctx"), "tp"),
            P(("fsdp", "ctx"), "tp"),
            P("tp", ("fsdp", "ctx")),
            P("ctx", "fsdp", "tp"),
            P("ctx", "fsdp", "tp"),
            P("ctx", "tp", "fsdp"),
        ),
        check_vma=False,
    )(*args)

    return run
```

```python
import functools

import jax
import jax.numpy as jnp
import numpy as np
from jax import lax
from jax.experimental import pallas as pl
from jax.experimental.pallas import tpu as pltpu
from jax.sharding import PartitionSpec as P

HD = 128
TOPK = 6


EPS = 1e-06
NEG_BIG = -1e30


def as_sent(value):
    return jax.tree.map(lambda a: a.astype(jnp.bfloat16) if a.dtype == jnp.float32 else a, value)


def features(local_part):
    return lax.all_gather(local_part, "tp", axis=1, tiled=True)


def row_stats(partial_terms):
    return lax.psum(partial_terms, "tp")


def partial_sums(partial_terms):
    return jax.tree.map(
        lambda part: part.astype(jnp.float32),
        lax.psum_scatter(as_sent(partial_terms), "tp", scatter_dimension=1, tiled=True),
    )


def to_owners(slot_rows):
    return lax.all_to_all(slot_rows, "ctx", split_axis=0, concat_axis=2, tiled=True)


def to_sources(slot_rows):
    return lax.all_to_all(
        slot_rows.astype(jnp.bfloat16), "ctx", split_axis=2, concat_axis=0, tiled=True
    ).astype(slot_rows.dtype)


def rotary(values, positions, rotate_sign):
    half_dim = values.shape[-1] // 2
    inverse = 10000.0 ** (-jnp.arange(half_dim, dtype=jnp.float32) * 2.0 / values.shape[-1])
    angles = positions.astype(jnp.float32)[:, None] * inverse[None, :]
    cosine = jnp.cos(angles)[:, None, :]
    sine_val = rotate_sign * jnp.sin(angles)[:, None, :]
    lower_half = values[..., :half_dim]
    upper_half = values[..., half_dim:]
    return jnp.concatenate(
        [lower_half * cosine - upper_half * sine_val, upper_half * cosine + lower_half * sine_val],
        axis=-1,
    )


def norm_rows(values, gain_part, model_width):
    square_sum = row_stats(jnp.sum(values * values, axis=1))
    row_scale = lax.rsqrt(square_sum / model_width + EPS)
    return (values * row_scale[:, None] * gain_part[None, :], row_scale)


def norm_back(values, row_scale, gain_part, grad_normed, model_width, tp_rank):
    quarter = values.shape[1]
    local_sum = jnp.sum(grad_normed * gain_part[None, :] * values, axis=1)
    gain_local = jnp.sum(grad_normed * values * row_scale[:, None], axis=0)
    gain_whole = lax.dynamic_update_slice_in_dim(
        jnp.zeros((model_width,), jnp.float32), gain_local, tp_rank * quarter, 0
    )
    row_total, gain_grad = row_stats((local_sum, gain_whole))
    back = (
        row_scale[:, None] * gain_part[None, :] * grad_normed
        - values * (row_scale**3 * row_total / model_width)[:, None]
    )
    return (back, gain_grad)


def scatter_slots(assign_rows, flat_exp, slot_of, n_exp, capacity):
    buffer = jnp.zeros((n_exp, capacity, assign_rows.shape[1]), assign_rows.dtype)
    return buffer.at[flat_exp, slot_of].set(assign_rows)


def silu_grad(pre_act):
    sigmoid_val = jax.nn.sigmoid(pre_act)
    return sigmoid_val * (1.0 + pre_act * (1.0 - sigmoid_val))


def keep_state(carried):
    return carried


def per_device(
    hidden_in,
    positions,
    chosen,
    out_grad,
    attn_gain,
    w_query,
    w_key,
    w_value,
    w_out,
    moe_gain,
    router,
    shared_gate,
    shared_up,
    shared_down,
    expert_gate,
    expert_up,
    expert_down,
):
    tp_rank = lax.axis_index("tp")
    ctx_rank = lax.axis_index("ctx")
    n_ctx = lax.axis_size("ctx")
    tok_rows, quarter = hidden_in.shape
    model_width = quarter * lax.axis_size("tp")
    gain_one, wq_all, wk_all, wv_all, gain_two, router_all, gate_all, up_all, wo_all, down_all = (
        lax.all_gather(attn_gain, ("fsdp", "ctx"), axis=0, tiled=True),
        lax.all_gather(w_query, ("fsdp", "ctx"), axis=0, tiled=True),
        lax.all_gather(w_key, ("fsdp", "ctx"), axis=0, tiled=True),
        lax.all_gather(w_value, ("fsdp", "ctx"), axis=0, tiled=True),
        lax.all_gather(moe_gain, ("fsdp", "ctx"), axis=0, tiled=True),
        lax.all_gather(router, ("fsdp", "ctx"), axis=0, tiled=True),
        lax.all_gather(shared_gate, ("fsdp", "ctx"), axis=0, tiled=True),
        lax.all_gather(shared_up, ("fsdp", "ctx"), axis=0, tiled=True),
        lax.all_gather(w_out, ("fsdp", "ctx"), axis=1, tiled=True),
        lax.all_gather(shared_down, ("fsdp", "ctx"), axis=1, tiled=True),
    )
    expert_gate_weights, expert_up_weights, expert_down_weights = (
        lax.all_gather(expert_gate, "fsdp", axis=1, tiled=True),
        lax.all_gather(expert_up, "fsdp", axis=1, tiled=True),
        lax.all_gather(expert_down, "fsdp", axis=2, tiled=True),
    )
    gain_q1 = lax.dynamic_slice_in_dim(gain_one, tp_rank * quarter, quarter).astype(jnp.float32)
    gain_q2 = lax.dynamic_slice_in_dim(gain_two, tp_rank * quarter, quarter).astype(jnp.float32)
    router_rows = lax.dynamic_slice_in_dim(router_all, tp_rank * quarter, quarter, 0)
    head_count = wq_all.shape[1] // HD
    scale_att = HD ** (-0.5)
    resid_in = hidden_in.astype(jnp.float32)
    normed_one, scale_one = norm_rows(resid_in, gain_q1, model_width)
    normed_in = features(normed_one.astype(jnp.bfloat16))
    query_pre = jnp.dot(normed_in, wq_all, preferred_element_type=jnp.float32).reshape(
        tok_rows, head_count, HD
    )
    key_pre = jnp.dot(normed_in, wk_all, preferred_element_type=jnp.float32).reshape(
        tok_rows, head_count, HD
    )
    value_b = (
        jnp.dot(normed_in, wv_all, preferred_element_type=jnp.float32)
        .astype(jnp.bfloat16)
        .reshape(tok_rows, head_count, HD)
    )
    query_b = rotary(query_pre, positions, 1.0).astype(jnp.bfloat16)
    key_b = rotary(key_pre, positions, 1.0).astype(jnp.bfloat16)
    q_start = ctx_rank * tok_rows
    row_pos = q_start + jnp.arange(tok_rows)
    start_state = (
        jnp.full((tok_rows, head_count), NEG_BIG, jnp.float32),
        jnp.zeros((tok_rows, head_count), jnp.float32),
        jnp.zeros((tok_rows, head_count, HD), jnp.float32),
    )
    keys_blk = lax.all_gather(key_b, "ctx", axis=0, tiled=True)
    vals_blk = lax.all_gather(value_b, "ctx", axis=0, tiled=True)
    key_count = keys_blk.shape[0]

    def compute(state_in):
        run_max, run_sum, run_acc = state_in
        scores = (
            jnp.einsum("qhd,khd->qhk", query_b, keys_blk, preferred_element_type=jnp.float32)
            * scale_att
        )
        visible = jnp.arange(key_count)[None, :] <= row_pos[:, None]
        scores = jnp.where(visible[:, None, :], scores, NEG_BIG)
        new_max = jnp.maximum(run_max, jnp.max(scores, axis=2))
        weights = jnp.exp(scores - new_max[:, :, None])
        new_sum = jnp.sum(weights, axis=2)
        new_acc = jnp.einsum(
            "qhk,khd->qhd",
            weights.astype(jnp.bfloat16),
            vals_blk,
            preferred_element_type=jnp.float32,
        )
        return (new_max, new_sum, new_acc)

    run_max, run_sum, run_acc = lax.cond(
        jnp.int32(0) <= q_start + tok_rows - 1, compute, keep_state, start_state
    )
    heads_f = run_acc / run_sum[:, :, None]
    log_sum = run_max + jnp.log(run_sum)
    heads_b = heads_f.astype(jnp.bfloat16).reshape(tok_rows, head_count * HD)
    resid_mid = resid_in + partial_sums(
        jnp.dot(heads_b, wo_all, preferred_element_type=jnp.float32)
    )
    normed_two, scale_two = norm_rows(resid_mid, gain_q2, model_width)
    moe_part = normed_two.astype(jnp.bfloat16)
    moe_in = features(moe_part)
    n_exp = router_all.shape[1]
    exp_dev = n_exp // n_ctx
    capacity = min(tok_rows, 5 * TOPK * tok_rows // (3 * n_exp))
    logits = jnp.dot(moe_in, router_all, preferred_element_type=jnp.float32)
    probs_all = jax.nn.softmax(logits, axis=1)
    picked = (chosen[:, :, None] == jnp.arange(n_exp)[None, None, :]).astype(jnp.float32)
    gate_vals = jnp.sum(picked * probs_all[:, None, :], axis=2)
    shared_a = jnp.dot(moe_in, gate_all, preferred_element_type=jnp.float32)
    shared_b = jnp.dot(moe_in, up_all, preferred_element_type=jnp.float32)
    shared_act = (jax.nn.silu(shared_a) * shared_b).astype(jnp.bfloat16)
    shared_out = jnp.dot(shared_act, down_all, preferred_element_type=jnp.float32)
    flat_exp = chosen.reshape(-1)
    flat_hot = (flat_exp[:, None] == jnp.arange(n_exp)[None, :]).astype(jnp.int32)
    slot_of = jnp.sum((jnp.cumsum(flat_hot, axis=0) - flat_hot) * flat_hot, axis=1)
    token_of = jnp.arange(tok_rows * TOPK) // TOPK
    slot_count = n_ctx * capacity
    outgoing = scatter_slots(moe_in[token_of], flat_exp, slot_of, n_exp, capacity)
    received_rows = to_owners(outgoing.reshape(n_ctx, exp_dev, capacity, model_width)).reshape(
        exp_dev, slot_count, model_width
    )
    expert_a = jnp.einsum(
        "bmw,bwv->bmv", received_rows, expert_gate_weights, preferred_element_type=jnp.float32
    )
    expert_up_proj = jnp.einsum(
        "bmw,bwv->bmv", received_rows, expert_up_weights, preferred_element_type=jnp.float32
    )
    expert_act = (jax.nn.silu(expert_a) * expert_up_proj).astype(jnp.bfloat16)
    expert_out = jnp.einsum(
        "erf,efd->erd", expert_act, expert_down_weights, preferred_element_type=jnp.float32
    )
    returned = to_sources(expert_out.reshape(1, exp_dev, slot_count, model_width))
    shared_q, slot_q = partial_sums((shared_out, returned.reshape(n_exp * capacity, model_width)))
    slot_rows = slot_q.reshape(n_exp, capacity, quarter)[flat_exp, slot_of].reshape(
        tok_rows, TOPK, quarter
    )
    result = resid_mid + shared_q + jnp.sum(gate_vals[:, :, None] * slot_rows, axis=1)
    layer_out = result.astype(jnp.bfloat16)
    grad_out = out_grad.astype(jnp.float32)
    gate_grad = row_stats(jnp.sum(grad_out[:, None, :] * slot_rows, axis=2))
    prob_grad = jnp.sum(gate_grad[:, :, None] * picked, axis=1)
    logit_grad = (
        probs_all * (prob_grad - jnp.sum(probs_all * prob_grad, axis=1, keepdims=True))
    ).astype(jnp.bfloat16)
    router_grad = jnp.einsum("td,te->de", moe_in, logit_grad, preferred_element_type=jnp.float32)
    router_back_q = jnp.einsum(
        "te,de->td", logit_grad, router_rows, preferred_element_type=jnp.float32
    )
    grad_full = features(out_grad)
    shared_dact = jnp.einsum("td,fd->tf", grad_full, down_all, preferred_element_type=jnp.float32)
    shared_da = (shared_dact * shared_b * silu_grad(shared_a)).astype(jnp.bfloat16)
    shared_db = (shared_dact * jax.nn.silu(shared_a)).astype(jnp.bfloat16)
    shared_down_grad = jnp.einsum(
        "tf,td->fd", shared_act, grad_full, preferred_element_type=jnp.float32
    )
    shared_gate_grad = jnp.einsum(
        "td,tf->df", moe_in, shared_da, preferred_element_type=jnp.float32
    )
    shared_up_grad = jnp.einsum("td,tf->df", moe_in, shared_db, preferred_element_type=jnp.float32)
    shared_back = jnp.einsum(
        "tf,df->td", shared_da, gate_all, preferred_element_type=jnp.float32
    ) + jnp.einsum("tf,df->td", shared_db, up_all, preferred_element_type=jnp.float32)
    assign_grad = (
        (gate_vals[:, :, None] * grad_full[:, None, :])
        .astype(jnp.bfloat16)
        .reshape(tok_rows * TOPK, model_width)
    )
    grad_slots = scatter_slots(assign_grad, flat_exp, slot_of, n_exp, capacity)
    grad_arrived = to_owners(grad_slots.reshape(n_ctx, exp_dev, capacity, model_width)).reshape(
        exp_dev, slot_count, model_width
    )
    expert_dact = jnp.einsum(
        "erd,efd->erf", grad_arrived, expert_down_weights, preferred_element_type=jnp.float32
    )
    expert_da = (expert_dact * expert_up_proj * silu_grad(expert_a)).astype(jnp.bfloat16)
    expert_up_proj_grad = (expert_dact * jax.nn.silu(expert_a)).astype(jnp.bfloat16)
    edown_grad = jnp.einsum(
        "erf,erd->efd", expert_act, grad_arrived, preferred_element_type=jnp.float32
    )
    egate_grad = jnp.einsum(
        "qgo,qgz->qoz", received_rows, expert_da, preferred_element_type=jnp.float32
    )
    expert_up_weight_grad = jnp.einsum(
        "qgo,qgz->qoz", received_rows, expert_up_proj_grad, preferred_element_type=jnp.float32
    )
    expert_back = jnp.einsum(
        "iac,igc->iag", expert_da, expert_gate_weights, preferred_element_type=jnp.float32
    ) + jnp.einsum(
        "iac,igc->iag", expert_up_proj_grad, expert_up_weights, preferred_element_type=jnp.float32
    )
    back_slots = to_sources(expert_back.reshape(1, exp_dev, slot_count, model_width)).reshape(
        n_exp, capacity, model_width
    )
    token_back = jnp.sum(back_slots[flat_exp, slot_of].reshape(tok_rows, TOPK, model_width), axis=1)
    moe_back_q = partial_sums(shared_back + token_back)
    mid_back, gain_two_grad = norm_back(
        resid_mid, scale_two, gain_q2, moe_back_q + router_back_q, model_width, tp_rank
    )
    mid_grad = grad_out + mid_back
    branch_full = features(mid_grad.astype(jnp.bfloat16))
    wo_grad = jnp.einsum("tf,td->fd", heads_b, branch_full, preferred_element_type=jnp.float32)
    heads_grad = (
        jnp.einsum("td,fd->tf", branch_full, wo_all, preferred_element_type=jnp.float32)
        .astype(jnp.bfloat16)
        .reshape(tok_rows, head_count, HD)
    )
    row_delta = jnp.sum(heads_grad.astype(jnp.float32) * heads_f, axis=2)
    seq_len = tok_rows * n_ctx
    back_state = (
        jnp.zeros((tok_rows, head_count, HD), jnp.float32),
        jnp.zeros((seq_len, head_count, HD), jnp.float32),
        jnp.zeros((seq_len, head_count, HD), jnp.float32),
    )
    attend_keys_blk = lax.all_gather(key_b, "ctx", axis=0, tiled=True)
    attend_vals_blk = lax.all_gather(value_b, "ctx", axis=0, tiled=True)
    attend_key_count = attend_keys_blk.shape[0]

    def compute(state_in):
        scores = (
            jnp.einsum("qhd,khd->qhk", query_b, attend_keys_blk, preferred_element_type=jnp.float32)
            * scale_att
        )
        visible = jnp.arange(attend_key_count)[None, :] <= row_pos[:, None]
        probs_blk = jnp.where(visible[:, None, :], jnp.exp(scores - log_sum[:, :, None]), 0.0)
        value_part = jnp.einsum(
            "qhk,qhd->khd",
            probs_blk.astype(jnp.bfloat16),
            heads_grad,
            preferred_element_type=jnp.float32,
        )
        dot_grad = jnp.einsum(
            "qhd,khd->qhk", heads_grad, attend_vals_blk, preferred_element_type=jnp.float32
        )
        score_grad = (probs_blk * (dot_grad - row_delta[:, :, None])).astype(jnp.bfloat16)
        query_acc = (
            jnp.einsum(
                "qhk,khd->qhd", score_grad, attend_keys_blk, preferred_element_type=jnp.float32
            )
            * scale_att
        )
        key_part = (
            jnp.einsum("qhk,qhd->khd", score_grad, query_b, preferred_element_type=jnp.float32)
            * scale_att
        )
        return (query_acc, key_part, value_part)

    query_grad, key_grad_all, value_grad_all = lax.cond(
        jnp.int32(0) <= q_start + tok_rows - 1, compute, keep_state, back_state
    )
    key_grad, value_grad = (
        lax.psum_scatter(
            key_grad_all.astype(jnp.bfloat16), "ctx", scatter_dimension=0, tiled=True
        ).astype(jnp.float32),
        lax.psum_scatter(
            value_grad_all.astype(jnp.bfloat16), "ctx", scatter_dimension=0, tiled=True
        ).astype(jnp.float32),
    )
    query_pre_grad = (
        rotary(query_grad, positions, -1.0).astype(jnp.bfloat16).reshape(tok_rows, head_count * HD)
    )
    key_pre_grad = (
        rotary(key_grad, positions, -1.0).astype(jnp.bfloat16).reshape(tok_rows, head_count * HD)
    )
    value_pre_grad = value_grad.astype(jnp.bfloat16).reshape(tok_rows, head_count * HD)
    wq_grad = jnp.einsum("td,tf->df", normed_in, query_pre_grad, preferred_element_type=jnp.float32)
    wk_grad = jnp.einsum("td,tf->df", normed_in, key_pre_grad, preferred_element_type=jnp.float32)
    wv_grad = jnp.einsum("td,tf->df", normed_in, value_pre_grad, preferred_element_type=jnp.float32)
    in_back = jnp.einsum("tf,df->td", query_pre_grad, wq_all, preferred_element_type=jnp.float32)
    in_back = in_back + jnp.einsum(
        "tf,df->td", key_pre_grad, wk_all, preferred_element_type=jnp.float32
    )
    in_back = in_back + jnp.einsum(
        "tf,df->td", value_pre_grad, wv_all, preferred_element_type=jnp.float32
    )
    first_back, gain_one_grad = norm_back(
        resid_in, scale_one, gain_q1, partial_sums(in_back), model_width, tp_rank
    )
    input_grad = mid_grad + first_back
    dense = (
        lax.psum_scatter(
            gain_one_grad.astype(jnp.bfloat16), ("fsdp", "ctx"), scatter_dimension=0, tiled=True
        ).astype(jnp.float32),
        lax.psum_scatter(
            wq_grad.astype(jnp.bfloat16), ("fsdp", "ctx"), scatter_dimension=0, tiled=True
        ).astype(jnp.float32),
        lax.psum_scatter(
            wk_grad.astype(jnp.bfloat16), ("fsdp", "ctx"), scatter_dimension=0, tiled=True
        ).astype(jnp.float32),
        lax.psum_scatter(
            wv_grad.astype(jnp.bfloat16), ("fsdp", "ctx"), scatter_dimension=0, tiled=True
        ).astype(jnp.float32),
        lax.psum_scatter(
            gain_two_grad.astype(jnp.bfloat16), ("fsdp", "ctx"), scatter_dimension=0, tiled=True
        ).astype(jnp.float32),
        lax.psum_scatter(
            router_grad.astype(jnp.bfloat16), ("fsdp", "ctx"), scatter_dimension=0, tiled=True
        ).astype(jnp.float32),
        lax.psum_scatter(
            shared_gate_grad.astype(jnp.bfloat16), ("fsdp", "ctx"), scatter_dimension=0, tiled=True
        ).astype(jnp.float32),
        lax.psum_scatter(
            shared_up_grad.astype(jnp.bfloat16), ("fsdp", "ctx"), scatter_dimension=0, tiled=True
        ).astype(jnp.float32),
        lax.psum_scatter(
            wo_grad.astype(jnp.bfloat16), ("fsdp", "ctx"), scatter_dimension=1, tiled=True
        ).astype(jnp.float32),
        lax.psum_scatter(
            shared_down_grad.astype(jnp.bfloat16), ("fsdp", "ctx"), scatter_dimension=1, tiled=True
        ).astype(jnp.float32),
    )
    experts_done = (
        lax.psum_scatter(
            egate_grad.astype(jnp.bfloat16), "fsdp", scatter_dimension=1, tiled=True
        ).astype(jnp.float32),
        lax.psum_scatter(
            expert_up_weight_grad.astype(jnp.bfloat16), "fsdp", scatter_dimension=1, tiled=True
        ).astype(jnp.float32),
        lax.psum_scatter(
            edown_grad.astype(jnp.bfloat16), "fsdp", scatter_dimension=2, tiled=True
        ).astype(jnp.float32),
    )
    return (
        layer_out,
        input_grad,
        dense[0],
        dense[1],
        dense[2],
        dense[3],
        dense[8],
        dense[4],
        dense[5],
        dense[6],
        dense[7],
        dense[9],
        experts_done[0],
        experts_done[1],
        experts_done[2],
    )


MESH = pl.DeviceIdType.MESH
HBM = pl.BlockSpec(memory_space=pl.ANY)
VMEM = pl.BlockSpec(memory_space=pltpu.VMEM)
DMA = pltpu.SemaphoreType.DMA
BF, F32 = jnp.bfloat16, jnp.float32
BIG = 60 * 1024 * 1024


def dot_nt(left, right):
    return lax.dot_general(left, right, (((1,), (1,)), ((), ())), preferred_element_type=F32)


def dot_tn(left, right):
    return lax.dot_general(left, right, (((0,), (0,)), ((), ())), preferred_element_type=F32)


def dot_nn(left, right):
    return jnp.dot(left, right, preferred_element_type=F32)


def ranks():
    return lax.axis_index("fsdp"), lax.axis_index("ctx"), lax.axis_index("tp")


def sibling(t):
    return t + 1 - 2 * lax.rem(t, 2)


def opposite(t):
    return lax.rem(t + 2, 4)


def remote(src, dst, send, recv, to):
    return pltpu.make_async_remote_copy(
        src_ref=src, dst_ref=dst, send_sem=send, recv_sem=recv, device_id=to, device_id_type=MESH
    )


def greet(peers):
    barrier = pltpu.get_barrier_semaphore()
    for peer in peers:
        pl.semaphore_signal(barrier, inc=1, device_id=peer, device_id_type=MESH)
    pl.semaphore_wait(barrier, len(peers))


def line_peers(c, n_c):
    return [{"ctx": lax.rem(c + step, n_c)} for step in range(1, n_c)]


def piece(index, size):
    return pl.ds(pl.multiple_of(index * size, size), size)


def nearest(c, n_c, act):
    act(c)
    for step in range(1, n_c):
        for side in (-1, 1):
            place = c + side * step

            @pl.when((place >= 0) & (place < n_c))
            def _():
                act(place)


def spread_sems(n_c):
    return [
        DMA((n_c + 2,)),
        DMA((n_c,)),
        DMA((n_c,)),
        DMA((n_c,)),
        DMA((2 * n_c,)),
        DMA((2 * n_c,)),
        DMA((4 * n_c,)),
        DMA((4 * n_c,)),
        DMA(()),
    ]


class Spread:
    def __init__(self, own, place, n_c, both, sems):
        self.own, self.place, self.n_c, self.both = own, place, n_c, both
        self.zs, self.zr, self.xs, self.xr, self.ys, self.yr, self.ks, self.kr, self.ls = sems
        self.f, self.c, self.t = ranks()
        self.other_t = opposite(self.t)
        self.groups = ((self.f, 0), (1 - self.f, n_c))[: 2 if both else 1]

    def local(self):
        return pltpu.make_async_copy(self.own, self.place(self.f, self.c, self.t), self.ls)

    def far_copy(self, src, i, g, cc, col):
        return remote(src, self.place(g, cc, col), self.ys.at[i], self.yr.at[i], {"tp": self.other_t})

    def sib_copy(self, src, i, which, g, cc, col):
        at = 2 * i + which
        return remote(src, self.place(g, cc, col), self.ks.at[at], self.kr.at[at], {"tp": sibling(self.t)})

    def other_copy(self, src, g, cc):
        return remote(src, self.place(g, cc, self.t), self.xs.at[cc], self.xr.at[cc], {"fsdp": 1 - self.f})

    def line_copy(self, src, cc, sem, to):
        return remote(src, self.place(self.f, cc, self.t), self.zs.at[sem], self.zr.at[cc], {"ctx": to})

    def pass_on(self, src, i, g, cc):
        self.far_copy(src, i, g, cc, self.t).start()
        self.sib_copy(src, i, 0, g, cc, self.t).start()

    def start(self):
        self.local().start()
        n_c, c, own = self.n_c, self.c, self.own

        @pl.when(c < n_c - 1)
        def _():
            self.line_copy(own, c, n_c, c + 1).start()

        @pl.when(c > 0)
        def _():
            self.line_copy(own, c, n_c + 1, c - 1).start()

        if self.both:
            self.other_copy(own, self.f, c).start()
        self.pass_on(own, c, self.f, c)

    def each_other(self, act):
        for step in range(1, self.n_c):
            for side in (-1, 1):
                cc = self.c + side * step

                @pl.when((cc >= 0) & (cc < self.n_c))
                def _():
                    act(cc, self.c - side)

    def line(self):
        n_c = self.n_c

        def arrive(cc, onward):
            block = self.place(self.f, cc, self.t)
            self.line_copy(block, cc, cc, self.c).wait_recv()

            @pl.when((onward >= 0) & (onward < n_c))
            def _():
                self.line_copy(block, cc, cc, onward).start()

            if self.both:
                self.other_copy(block, self.f, cc).start()
            self.pass_on(block, cc, self.f, cc)

        self.each_other(arrive)

    def other(self):
        def arrive(cc):
            block = self.place(1 - self.f, cc, self.t)
            self.other_copy(block, 1 - self.f, cc).wait_recv()
            self.pass_on(block, self.n_c + cc, 1 - self.f, cc)

        nearest(self.c, self.n_c, arrive)

    def far(self, which):
        g, base = self.groups[which]

        def arrive(cc):
            i = base + cc
            block = self.place(g, cc, self.other_t)
            self.far_copy(block, i, g, cc, self.other_t).wait_recv()
            self.sib_copy(block, i, 1, g, cc, self.other_t).start()

        nearest(self.c, self.n_c, arrive)

    def arrived(self, which):
        g, base = self.groups[which]
        for cc in range(self.n_c):
            block = self.place(g, cc, self.t)
            for half in range(2):
                self.sib_copy(block, base + cc, half, g, cc, self.t).wait_recv()

    def finish(self):
        n_c, c, f, t, own = self.n_c, self.c, self.f, self.t, self.own
        for g, base in self.groups:
            for cc in range(n_c):
                block = self.place(g, cc, t)
                for half in range(2):
                    self.sib_copy(block, base + cc, half, g, cc, t).wait_send()
                self.far_copy(block, base + cc, g, cc, t).wait_send()
        if self.both:
            for cc in range(n_c):
                self.other_copy(self.place(f, cc, t), f, cc).wait_send()
        block = self.place(f, c, t)

        @pl.when(c < n_c - 1)
        def _():
            self.line_copy(block, c, n_c, c).wait_send()

        @pl.when(c > 0)
        def _():
            self.line_copy(block, c, n_c + 1, c).wait_send()

        def sent(cc, onward):
            @pl.when((onward >= 0) & (onward < n_c))
            def _():
                self.line_copy(block, cc, cc, c).wait_send()

        self.each_other(sent)


def to_each(src_of, dst, n_f, n_c, sems, act):
    send, recv, own = sems
    f, c, _ = ranks()
    here = f * n_c + c
    for df in range(n_f):
        for dc in range(n_c):
            i = df * n_c + dc
            if i == 0:
                copy = pltpu.make_async_copy(src_of(here), dst.at[here], own)
                copy.start() if act == "start" else copy.wait()
                continue
            to_f, to_c = lax.rem(f + df, n_f), lax.rem(c + dc, n_c)
            copy = remote(
                src_of(to_f * n_c + to_c), dst.at[here], send.at[i], recv.at[i], {"fsdp": to_f, "ctx": to_c}
            )
            copy.start() if act == "start" else copy.wait()


def each_peers(f, c, n_f, n_c):
    return [
        {"fsdp": lax.rem(f + df, n_f), "ctx": lax.rem(c + dc, n_c)}
        for df in range(n_f)
        for dc in range(n_c)
        if df or dc
    ]


def reduce_seq_scratch(n_c, rows, quarter):
    return [
        pltpu.VMEM((n_c, 2, rows, quarter), BF),
        pltpu.VMEM((n_c, 2, rows, quarter), BF),
        pltpu.VMEM((n_c, 2, rows, quarter), F32),
        pltpu.VMEM((n_c, rows, quarter), BF),
        pltpu.VMEM((n_c, rows, quarter), BF),
        pltpu.VMEM((n_c, rows, quarter), BF),
        pltpu.VMEM((n_c, rows, quarter), BF),
        DMA((n_c,)),
        DMA((n_c,)),
        DMA((n_c,)),
        DMA((n_c,)),
        DMA((n_c,)),
        DMA((n_c,)),
    ]


def reduce_seq(part_of, n_c, scratch, middle=None, before_last=None):
    out1, in1, own, out2, in2, out3, in3, s1, r1, s2, r2, s3, r3 = scratch
    f, c, t = ranks()
    far, sib = opposite(t), sibling(t)
    to_sib, to_far = {"tp": sib}, {"tp": far}
    order = [2, 1, 3, 0] if n_c == 4 else list(range(1, n_c)) + [0]
    for d in order:
        cc = lax.rem(c + d, n_c)
        out1[d, 0] = part_of(cc, sib).astype(BF)
        out1[d, 1] = part_of(cc, opposite(sib)).astype(BF)
        remote(out1.at[d], in1.at[d], s1.at[d], r1.at[d], to_sib).start()
        own[d, 0] = part_of(cc, t)
        own[d, 1] = part_of(cc, far)
    for d in order:
        remote(out1.at[d], in1.at[d], s1.at[d], r1.at[d], to_sib).wait()
        out2[d] = (own[d, 1] + in1[d, 1].astype(F32)).astype(BF)
        remote(out2.at[d], in2.at[d], s2.at[d], r2.at[d], to_far).start()
    if middle is not None:
        middle()
    for d in order:
        remote(out2.at[d], in2.at[d], s2.at[d], r2.at[d], to_far).wait()
        total = own[d, 0] + in1[d, 0].astype(F32) + in2[d].astype(F32)
        if d:
            out3[d] = total.astype(BF)
            cc = lax.rem(c + d, n_c)
            remote(out3.at[d], in3.at[d], s3.at[d], r3.at[d], {"ctx": cc}).start()
    if before_last is not None:
        before_last()
    for d in order[:-1]:
        remote(out3.at[d], in3.at[d], s3.at[d], r3.at[d], {"ctx": c}).wait()
        total = total + in3[d].astype(F32)
    return total


def first_kernel(
    n_c, n_f, n_exp, mine, hidden, wq, wk, wv, wo, og, gate_t, up_t, down, router_in, chosen, lines, sg, su, sd, angle,
    normed_out, q_out, k_out, v_out, hf_out, lse_out, r_out, cos_out, sin_out, resid_out,
    wqkv_out, wo_out, small_out, all_out, og_out, shared_out, gg_out, gu_out, gd_out,
    seq, wqkv, wo_all, small_all, hb, blk, own_og, small, shared, normed,
    ws, wr, ls, xs, xr, ss, sr, sl, es, er, os, *scratch,
):
    f, c, t = ranks()
    rows, quarter = blk.shape
    part = wo.shape[1]
    tokens, width = seq.shape
    n_s = len(spread_sems(n_c))
    named = lax.broadcasted_iota(jnp.int32, (n_exp, part), 0)
    mask = jnp.zeros((n_exp, part), F32)
    for k in range(chosen.shape[0]):
        mask = mask + jnp.where(chosen[k : k + 1, :] == named, 1.0, 0.0)
    small[:n_exp, :] = router_in[...]
    small[n_exp : 2 * n_exp, :] = mask.astype(BF)
    small[2 * n_exp :, :] = lines[...]
    n_b = n_f * n_c
    own_rows, srows = sg.shape[0] // n_b, shared.shape[1] // 3
    for i, src in enumerate((sg, su, sd)):
        for b in range(n_b):
            shared[b, i * srows : i * srows + own_rows, :] = src[b * own_rows : (b + 1) * own_rows, :]
            if srows > own_rows:
                shared[b, i * srows + own_rows : (i + 1) * srows, :] = jnp.zeros((srows - own_rows, part), BF)
    greet([{"tp": sibling(t)}, {"tp": opposite(t)}] + each_peers(f, c, n_f, n_c))
    seq_place = lambda g, cc, tt: seq.at[piece(cc, rows), piece(tt, quarter)]
    og_place = lambda g, cc, tt: og_out.at[g * n_c + cc, tt]
    all_place = lambda g, cc, tt: all_out.at[piece(g * n_c + cc, rows), piece(tt, quarter)]
    hid = Spread(hidden, seq_place, n_c, False, scratch[:n_s])
    grad = Spread(og, og_place, n_c, True, scratch[n_s : 2 * n_s])
    res = Spread(blk, all_place, n_c, True, scratch[2 * n_s : 3 * n_s])

    def targets(g, cc):
        block = piece(g * n_c + cc, part)
        return [wqkv.at[block, pl.ds(i * HD, HD)] for i in range(3)] + [
            wo_all.at[:, block],
            small_all.at[:, block],
        ]

    def sources(head):
        cols = piece(head, HD)
        return [wq.at[:, cols], wk.at[:, cols], wv.at[:, cols], wo.at[cols, :], small]

    def slabs(g, cc):
        block = piece(g * n_c + cc, part)
        return [wqkv.at[block, :], wo_all.at[:, block], small_all.at[:, block]]

    def across(step, g, cc):
        return [
            remote(slab, slab, xs.at[step, i], xr.at[step, i], {"fsdp": 1 - f})
            for i, slab in enumerate(slabs(g, cc))
        ]

    def swap(weight, out, k):
        return [
            remote(weight.at[(1 - f) * mine + e], out.at[e], es.at[k, e], er.at[k, e], {"fsdp": 1 - f})
            for e in range(mine)
        ]

    more = swap(down, gd_out, 2)
    for copy in more:
        copy.start()
    hid.start()
    def weights_out(step):
        to = lax.rem(c + step, n_c)
        for i, (src, dst) in enumerate(zip(sources(to), targets(f, c))):
            remote(src, dst, ws.at[step, i], wr.at[step, i], {"ctx": to}).start()

    def weights_on(step):
        cc = lax.rem(c - step + n_c, n_c)
        for i, dst in enumerate(targets(f, cc)):
            remote(dst, dst, ws.at[step, i], wr.at[step, i], {"ctx": cc}).wait_recv()
        for copy in across(step, f, cc):
            copy.start()

    steps = ([2, 1, 3] if n_c == 4 else list(range(1, n_c))) + [None]
    weights_out(steps[0])
    own = [
        pltpu.make_async_copy(src, dst, ls.at[i])
        for i, (src, dst) in enumerate(zip(sources(c), targets(f, c)))
    ]
    for copy in own:
        copy.start()
    for copy in own:
        copy.wait()
    for copy in across(0, f, c):
        copy.start()
    grad.start()
    hid.line()
    for step, following in zip(steps, steps[1:]):
        if following is not None:
            weights_out(following)
        weights_on(step)
    grad.line()
    swaps = swap(gate_t, gg_out, 0) + swap(up_t, gu_out, 1)
    for copy in swaps[: mine + 1]:
        copy.start()
    hid.far(0)
    hid.arrived(0)
    hid.local().wait()
    for step in range(n_c):
        for copy in across(step, 1 - f, lax.rem(c - step + n_c, n_c)):
            copy.wait_recv()
    outs = [
        pltpu.make_async_copy(src, dst, os.at[i])
        for i, (src, dst) in enumerate(((wqkv, wqkv_out), (wo_all, wo_out), (small_all, small_out)))
    ]
    for copy in outs:
        copy.start()

    exchange = lambda act: to_each(lambda b: shared.at[b], shared_out, n_f, n_c, (ss, sr, sl), act)
    exchange("start")

    scale_att = HD ** (-0.5)
    gain = small_all[2 * n_exp : 2 * n_exp + 1, :].astype(F32)
    place_row = 2 * n_exp + 2
    for start in range(0, tokens, rows):
        at = pl.ds(start, rows)
        h = seq[at, :].astype(F32)
        r = lax.rsqrt(jnp.sum(h * h, axis=1, keepdims=True) / width + EPS)
        n = (h * r * gain).astype(BF)
        normed[at, :] = n
        r_out[at, :] = jnp.broadcast_to(r, (rows, HD))
        cols = pl.ds(pl.multiple_of(f * tokens + start, rows), rows)
        pos = small_all[place_row : place_row + 2, cols].astype(F32)
        pos = pos[0:1] * 64.0 + pos[1:2]
        turn = jnp.broadcast_to(pos, (HD, rows)).T * angle[0:1, :]
        cos, sin = jnp.cos(turn), jnp.sin(turn) * angle[1:2, :]
        cos_out[at, :] = cos
        sin_out[at, :] = sin
        qkv = dot_nn(n, wqkv[...])

        def rotate(values):
            return (values * cos + pltpu.roll(values, HD // 2, 1) * sin).astype(BF)

        q_out[at, :] = rotate(qkv[:, :HD])
        k_out[at, :] = rotate(qkv[:, HD : 2 * HD])
        v_out[at, :] = qkv[:, 2 * HD :].astype(BF)
    outs.append(pltpu.make_async_copy(normed, normed_out, os.at[4]))
    outs[-1].start()
    for start in range(0, tokens, rows):
        at = pl.ds(start, rows)
        seen = start + rows
        s = dot_nt(q_out[at, :], k_out[:seen, :]) * scale_att
        row = lax.broadcasted_iota(jnp.int32, (rows, seen), 0) + start
        col = lax.broadcasted_iota(jnp.int32, (rows, seen), 1)
        s = jnp.where(col <= row, s, NEG_BIG)
        top = jnp.max(s, axis=1, keepdims=True)
        e = jnp.exp(s - top)
        total = jnp.sum(e, axis=1, keepdims=True)
        out = dot_nn((e * (1.0 / total)).astype(BF), v_out[:seen, :])
        hf_out[at, :] = out
        hb[at, :] = out.astype(BF)
        lse_out[at, :] = jnp.broadcast_to(top + jnp.log(total), (rows, HD))

    def part_of(cc, q):
        return dot_nn(hb[piece(cc, rows), :], wo_all[:, piece(q, quarter)])

    fetch = pltpu.make_async_copy(hidden, own_og, os.at[3])
    fetch.start()
    total = reduce_seq(part_of, n_c, scratch[3 * n_s :], grad.other)
    fetch.wait()
    resid = own_og[...].astype(F32) + total
    resid_out[...] = resid
    blk[...] = resid.astype(BF)
    res.start()
    res.line()
    for copy in swaps[mine + 1 :]:
        copy.start()
    grad.far(0)
    grad.far(1)
    res.other()
    res.far(0)
    res.far(1)
    for which in range(2):
        grad.arrived(which)
        res.arrived(which)
    exchange("wait")
    for copy in swaps + more:
        copy.wait()
    for step in range(1, n_c):
        for i, (src, dst) in enumerate(zip(sources(c), targets(f, c))):
            remote(src, dst, ws.at[step, i], wr.at[step, i], {"ctx": c}).wait_send()
    for step in range(n_c):
        for copy in across(step, f, lax.rem(c - step + n_c, n_c)):
            copy.wait_send()
    for item in (hid, grad, res):
        item.finish()
    grad.local().wait()
    res.local().wait()
    for copy in outs:
        copy.wait()


def first(n_c, n_f, n_t, mine, srows, hidden, wq, wk, wv, wo, og, weights, router, chosen, lines, shared, angle):
    rows, quarter = hidden.shape
    width = quarter * n_t
    seq = rows * n_c
    n_exp = mine * n_f * n_c
    ffe, half = weights[0].shape[1:]
    sds = jax.ShapeDtypeStruct
    part = wo.shape[1]
    n_small = 2 * n_exp + lines.shape[0]
    head, head_f = sds((seq, HD), BF), sds((seq, HD), F32)
    got = sds((mine, ffe, half), BF)
    return pl.pallas_call(
        functools.partial(first_kernel, n_c, n_f, n_exp, mine),
        out_shape=(
            sds((seq, width), BF),
            head,
            head,
            head,
            head_f,
            head_f,
            head_f,
            head_f,
            head_f,
            sds((rows, quarter), F32),
            sds((width, 3 * HD), BF),
            sds((HD, width), BF),
            sds((n_small, width), BF),
            sds((seq * n_f, width), BF),
            sds((n_f * n_c, n_t, rows, quarter), BF),
            sds((n_f * n_c, 3 * srows, part), BF),
            got,
            got,
            got,
        ),
        in_specs=[HBM] * 9 + [VMEM] * 7,
        out_specs=[HBM] + [VMEM] * 9 + [HBM] * 9,
        scratch_shapes=[
            pltpu.VMEM((seq, width), BF),
            pltpu.VMEM((width, 3 * HD), BF),
            pltpu.VMEM((HD, width), BF),
            pltpu.VMEM((n_small, width), BF),
            pltpu.VMEM((seq, HD), BF),
            pltpu.VMEM((rows, quarter), BF),
            pltpu.VMEM((rows, quarter), BF),
            pltpu.VMEM((n_small, part), BF),
            pltpu.VMEM((n_f * n_c, 3 * srows, part), BF),
            pltpu.VMEM((seq, width), BF),
            DMA((n_c, 5)),
            DMA((n_c, 5)),
            DMA((5,)),
            DMA((n_c, 3)),
            DMA((n_c, 3)),
            DMA((n_f * n_c,)),
            DMA((n_f * n_c,)),
            DMA(()),
            DMA((3, mine)),
            DMA((3, mine)),
            DMA((5,)),
        ]
        + spread_sems(n_c) * 3
        + reduce_seq_scratch(n_c, rows, quarter),
        compiler_params=pltpu.CompilerParams(
            collective_id=1, has_side_effects=True, vmem_limit_bytes=BIG
        ),
        cost_estimate=pl.CostEstimate(
            flops=5 << 30, bytes_accessed=300 << 20, transcendentals=1 << 20
        ),
        name="first",
    )(hidden, wq, wk, wv, wo, og, *weights, router, chosen, lines, *shared, angle)


def fetch_experts(n_c, n_f, mine, ffe, srows, hp, weights, shared, wgu, wd, sems):
    f = lax.axis_index("fsdp")
    wg0, wu0, wd0, wg1, wu1, wd1 = weights
    width = wd.shape[1]
    used = mine * ffe
    part = width // (n_f * n_c)
    half = width // n_f
    copies = []

    def add(src, dst):
        copies.append(pltpu.make_async_copy(src, dst, sems.at[len(copies)]))

    groups = []
    for i, (kept, got) in enumerate(((wg0, wg1), (wu0, wu1), (wd0, wd1))):
        dst, base = ((wgu, 0), (wgu, hp), (wd, 0))[i]
        for e in range(mine):
            at = pl.ds(base + e * ffe, ffe)
            add(kept.at[f * mine + e], dst.at[at, piece(f, half)])
            add(got.at[e], dst.at[at, piece(1 - f, half)])
        for b in range(n_f * n_c):
            add(
                shared.at[b, pl.ds(i * srows, srows), :],
                dst.at[pl.ds(base + used, srows), pl.ds(b * part, part)],
            )
        groups.append(copies[sum(map(len, groups)) :])
    return groups[0] + groups[1], groups[2]


def blank_rows(rows_used, hp, wgu, wd):
    blank = jnp.zeros((hp - rows_used, wd.shape[1]), BF)
    wgu[rows_used:hp, :] = blank
    wgu[hp + rows_used :, :] = blank
    wd[rows_used:, :] = blank


def gates(prob, picked, first, mine, ffe, hp):
    block, n_exp = prob.shape
    lane = lax.broadcasted_iota(jnp.int32, (block, n_exp), 1)
    gated = prob * picked
    col = lax.broadcasted_iota(jnp.int32, (block, hp), 1)
    gate = jnp.ones((block, hp), F32)
    for k in reversed(range(mine)):
        g = jnp.sum(jnp.where(lane == first + k, gated, 0.0), axis=1, keepdims=True)
        gate = jnp.where(col < (k + 1) * ffe, g, gate)
    return gate, lane, col


def reducer_scratch(n_f, n_c, rows, quarter, split):
    n_b = n_f * n_c
    upper = rows // 2 if split else rows
    lower = rows // 2 if split else 16
    blocks = lambda *lead: pltpu.VMEM(lead + (rows, quarter), BF)
    return [
        blocks(n_b, 2),
        blocks(n_b, 2),
        blocks(n_b, 2),
        blocks(n_b),
        blocks(n_b),
        pltpu.VMEM((n_c, upper, quarter), BF),
        pltpu.VMEM((n_c, upper, quarter), BF),
        pltpu.VMEM((n_c, rows, quarter), F32),
        blocks(n_c),
        blocks(n_c),
        pltpu.VMEM((n_c, 2, lower, quarter), BF),
        pltpu.VMEM((n_c, 2, lower, quarter), BF),
    ] + [DMA((n_b,))] * 4 + [DMA((n_c,))] * 6


N_REDUCER = 22


def when(condition, act):
    if isinstance(condition, bool):
        if condition:
            act()
    else:
        pl.when(condition)(act)


class Reducer:
    def __init__(self, n_c, scratch):
        self.n_c = n_c
        (self.out1, self.in1, self.own, self.out2, self.in2, self.out3, self.in3, self.acc,
         self.out4, self.in4, self.out5, self.in5, self.s1, self.r1, self.s2, self.r2, self.s3, self.r3,
         self.s4, self.r4, self.s5, self.r5) = scratch
        self.half = self.out3.shape[1]
        self.split = self.half < self.out4.shape[1]
        self.f, self.c, self.t = ranks()
        self.far, self.sib = opposite(self.t), sibling(self.t)

    def row_block(self, i):
        n_c = self.n_c
        group = jnp.where(i < n_c, 1 - self.f, self.f)
        return group * n_c + lax.rem(self.c + lax.rem(i, n_c) + 1, n_c)

    def core_copy(self, i):
        return remote(self.out1.at[i], self.in1.at[i], self.s1.at[i], self.r1.at[i], {"tp": self.sib})

    def far_copy(self, i, upper=False):
        src, dst = self.out2.at[i], self.in2.at[i]
        if upper:
            src, dst = src.at[pl.ds(0, self.half)], dst.at[pl.ds(0, self.half)]
        return remote(src, dst, self.s2.at[i], self.r2.at[i], {"tp": self.far})

    def other_copy(self, j):
        return remote(self.out3.at[j], self.in3.at[j], self.s3.at[j], self.r3.at[j], {"fsdp": 1 - self.f})

    def lower_copy(self, j):
        return remote(self.out5.at[j], self.in5.at[j], self.s5.at[j], self.r5.at[j], {"fsdp": 1 - self.f})

    def line_copy(self, j, to):
        return remote(self.out4.at[j], self.in4.at[j], self.s4.at[j], self.r4.at[j], {"ctx": to})

    def put(self, i, part_of):
        self.out1[i, 0] = part_of(opposite(self.sib)).astype(BF)
        self.out1[i, 1] = part_of(self.sib).astype(BF)
        self.core_copy(i).start()
        self.own[i, 0] = part_of(self.far).astype(BF)
        self.own[i, 1] = part_of(self.t).astype(BF)

    def core_sum(self, i, which):
        return self.own[i, which].astype(F32) + self.in1[i, which].astype(F32)

    def over(self, i):
        self.core_copy(i).wait()
        half, n_c = self.half, self.n_c

        def of_other():
            far = self.core_sum(i, 0)
            if self.split:
                self.out5[i, 0] = far[half:].astype(BF)
                self.out5[i, 1] = self.core_sum(i, 1)[half:].astype(BF)
                self.lower_copy(i).start()
            self.out2[i, :half] = far[:half].astype(BF)
            self.far_copy(i, True).start()

        def of_own():
            j = i - n_c
            if self.split:
                self.lower_copy(j).wait_recv()
            far = self.core_sum(i, 0)
            self.out2[i, :half] = far[:half].astype(BF)
            if self.split:
                self.out2[i, half:] = (far[half:] + self.in5[j, 0].astype(F32)).astype(BF)
            self.far_copy(i).start()

        when(i < n_c, of_other)
        when(i >= n_c, of_own)

    def after_other(self, i):
        half = self.half
        self.far_copy(i, True).wait()
        self.out3[i] = (self.core_sum(i, 1)[:half] + self.in2[i, :half].astype(F32)).astype(BF)
        self.other_copy(i).start()

    def after_own(self, i):
        j, half = i - self.n_c, self.half
        self.far_copy(i).wait()
        total = self.core_sum(i, 1) + self.in2[i].astype(F32)
        self.acc[j, :half] = total[:half]
        if self.split:
            self.acc[j, half:] = total[half:] + self.in5[j, 1].astype(F32)

    def along(self, j):
        half = self.half
        if self.split:
            self.lower_copy(j).wait_send()
        self.other_copy(j).wait()
        self.acc[j, :half] = self.acc[j, :half] + self.in3[j].astype(F32)
        total = self.acc[j]
        if j < self.n_c - 1:
            self.out4[j] = total.astype(BF)
            self.line_copy(j, lax.rem(self.c + j + 1, self.n_c)).start()
        return total

    def total(self, total):
        for j in range(self.n_c - 1):
            self.line_copy(j, self.c).wait()
            total = total + self.in4[j].astype(F32)
        return total

    def loop(self, n_b, compute):
        n_c = self.n_c

        def step(i, carry):
            def between():
                @pl.when(i >= 1)
                def _():
                    self.over(i - 1)

                @pl.when((i >= 3) & (i < 3 + n_c))
                def _():
                    self.after_other(i - 3)

                @pl.when(i >= 3 + n_c)
                def _():
                    self.after_own(i - 3)

            compute(i, between)
            return carry

        lax.fori_loop(0, n_b, step, 0)

    def drain(self, n_b, works):
        works = list(works)
        self.over(n_b - 1)
        for i in range(n_b - 4, n_b):
            if i > n_b - 4:
                self.after_own(i) if i >= self.n_c else self.after_other(i)
            if i >= self.n_c:
                total = self.along(i - self.n_c)
            if works:
                works.pop(0)()
        for work in works:
            work()
        return self.total(total)


def forward_kernel(
    n_c, n_f, mine, ffe, srows, hp, rows_all, og_all, resid, small,
    wg0, wu0, wd0, wg1, wu1, wd1, shared,
    layer_out, in_out, act_out, silu_out, slope_out, r_out, prob_out, keep_out, send_out, shared_out,
    gt, wsem, xsem, nsem, asem, tsem, osem, *scratch,
):
    f, c, t = ranks()
    n_b = n_f * n_c
    rows, quarter = resid.shape
    width = rows_all.shape[1]
    routed = mine * ffe
    rows_used = routed + srows
    n_exp = mine * n_b
    red = Reducer(n_c, scratch)

    def blocks_phase(wgu, wd, xs, ns, acts):
        gate_up, down = fetch_experts(
            n_c, n_f, mine, ffe, srows, hp, (wg0, wu0, wd0, wg1, wu1, wd1), shared, wgu, wd, wsem
        )
        for copy in gate_up + down:
            copy.start()

        def load(i, slot):
            return pltpu.make_async_copy(
                rows_all.at[piece(red.row_block(i), rows), :], xs.at[slot], xsem.at[slot]
            )

        def stores(i, slot):
            at = piece(red.row_block(i), rows)
            return [pltpu.make_async_copy(ns.at[slot], in_out.at[at, :], nsem.at[slot])] + [
                pltpu.make_async_copy(acts.at[slot, k], out.at[at, :], asem.at[slot, k])
                for k, out in enumerate((act_out, silu_out, slope_out))
            ]

        load(0, 0).start()
        blank_rows(rows_used, hp, wgu, wd)
        greet([{"tp": red.sib}, {"tp": red.far}, {"fsdp": 1 - f}] + line_peers(c, n_c))
        for copy in gate_up:
            copy.wait()

        def compute(i, between):
            slot = lax.rem(i, 2)
            b = red.row_block(i)
            at = piece(b, rows)
            load(i, slot).wait()

            @pl.when(i + 1 < n_b)
            def _():
                load(i + 1, 1 - slot).start()

            @pl.when(i >= 2)
            def _():
                for copy in stores(i - 2, slot):
                    copy.wait()

            h = xs[slot].astype(F32)
            r = lax.rsqrt(jnp.sum(h * h, axis=1, keepdims=True) / width + EPS)
            r_out[at, :] = jnp.broadcast_to(r, (rows, HD))
            gain = small[2 * n_exp + 1 : 2 * n_exp + 2, :].astype(F32)
            n = (h * r * gain).astype(BF)
            ns[slot] = n
            logits = dot_nt(n, small[:n_exp, :])
            e = jnp.exp(logits - jnp.max(logits, axis=1, keepdims=True))
            prob = e / jnp.sum(e, axis=1, keepdims=True)
            prob_out[at, :] = prob
            gate, _, _ = gates(prob, small[n_exp : 2 * n_exp, at].astype(F32).T, (c * n_f + f) * mine, mine, ffe, hp)
            ab = dot_nt(n, wgu[...])
            between()
            a, up = ab[:, :hp], ab[:, hp:]
            sig = 0.5 * jnp.tanh(0.5 * a) + 0.5
            silu = a * sig
            act = (silu * up).astype(BF)
            acts[slot, 0] = act
            acts[slot, 1] = silu.astype(BF)
            acts[slot, 2] = (up * (sig * (1.0 + a * (1.0 - sig)))).astype(BF)
            actg = (act.astype(F32) * gate).astype(BF)
            gt[:, at] = actg.T[:rows_used, :]
            for copy in stores(i, slot):
                copy.start()

            @pl.when(i == 0)
            def _():
                for copy in down:
                    copy.wait()

            red.put(i, lambda q: dot_nn(actg, wd[:, piece(q, quarter)]))

        red.loop(n_b, compute)
        for i in range(n_b - 2, n_b):
            for copy in stores(i, i % 2):
                copy.wait()

    pl.run_scoped(
        blocks_phase,
        pltpu.VMEM((2 * hp, width), BF),
        pltpu.VMEM((hp, width), BF),
        pltpu.VMEM((2, rows, width), BF),
        pltpu.VMEM((2, rows, width), BF),
        pltpu.VMEM((2, 3, rows, hp), BF),
    )

    def grads_phase(tiles, keeps, sends, shs):
        def tile_of(s):
            return (1 - f) * 2 + s if s < 2 else f * 2 + s - 2

        def tile_load(s):
            return pltpu.make_async_copy(og_all.at[:, tile_of(s)], tiles.at[s % 2], tsem.at[s % 2])

        def out_copies(s):
            cols = pl.ds(s % 2 * quarter, quarter)
            if s < 2:
                src, dst = sends.at[s], send_out.at[:, :, cols]
            else:
                src, dst = keeps.at[s - 2], keep_out.at[:, :, cols]
            return [
                pltpu.make_async_copy(src, dst, osem.at[s, 0]),
                pltpu.make_async_copy(
                    shs.at[s], shared_out.at[:, piece(tile_of(s), quarter)], osem.at[s, 1]
                ),
            ]

        def work(s):
            def run():
                tile_load(s).wait()
                if s < 3:
                    tile_load(s + 1).start()
                g = dot_nn(gt[...], tiles[s % 2].reshape(n_b * rows, quarter))
                if s < 2:
                    sends[s] = g[:routed].astype(BF).reshape(mine, ffe, quarter)
                else:
                    keeps[s - 2] = g[:routed].astype(BF).reshape(mine, ffe, quarter)
                shs[s] = g[routed:].astype(BF)
                for copy in out_copies(s):
                    copy.start()

            return run

        tile_load(0).start()
        total = red.drain(n_b, [work(s) for s in range(4)])
        layer_out[...] = (resid[...] + total).astype(BF)
        for s in range(4):
            for copy in out_copies(s):
                copy.wait()

    pl.run_scoped(
        grads_phase,
        pltpu.VMEM((2, n_b, rows, quarter), BF),
        pltpu.VMEM((2, mine, ffe, quarter), BF),
        pltpu.VMEM((2, mine, ffe, quarter), BF),
        pltpu.VMEM((4, srows, quarter), BF),
    )


def expert_sizes(n_c, n_f, n_t, mine, ffe, srows, width):
    used = mine * ffe + srows
    return used, -(-used // HD) * HD, 3 * (2 * mine + n_f * n_c)


def forward(n_c, n_f, n_t, mine, ffe, srows, rows_all, og_all, resid, small, kept, got, shared):
    total, width = rows_all.shape
    rows, quarter = resid.shape
    n_b = n_f * n_c
    n_exp = mine * n_b
    used, hp, n_fetch = expert_sizes(n_c, n_f, n_t, mine, ffe, srows, width)
    sds = jax.ShapeDtypeStruct
    return pl.pallas_call(
        functools.partial(forward_kernel, n_c, n_f, mine, ffe, srows, hp),
        out_shape=(
            sds((rows, quarter), BF),
            sds((total, width), BF),
            sds((total, hp), BF),
            sds((total, hp), BF),
            sds((total, hp), BF),
            sds((total, HD), F32),
            sds((total, n_exp), F32),
            sds((mine, ffe, width // n_f), BF),
            sds((mine, ffe, width // n_f), BF),
            sds((srows, width), BF),
        ),
        in_specs=[HBM, HBM, VMEM, VMEM] + [HBM] * 7,
        out_specs=[VMEM, HBM, HBM, HBM, HBM, VMEM, VMEM, HBM, HBM, HBM],
        scratch_shapes=[
            pltpu.VMEM((used, total), BF),
            DMA((n_fetch,)),
            DMA((2,)),
            DMA((2,)),
            DMA((2, 3)),
            DMA((2,)),
            DMA((4, 2)),
        ]
        + reducer_scratch(n_f, n_c, rows, quarter, True),
        compiler_params=pltpu.CompilerParams(
            collective_id=5, has_side_effects=True, vmem_limit_bytes=BIG
        ),
        cost_estimate=pl.CostEstimate(
            flops=8 * total * width * used, bytes_accessed=80 << 20, transcendentals=total * used
        ),
        name="forward",
    )(rows_all, og_all, resid, small, *kept, *got, shared)


def backward_kernel(
    n_c, n_f, mine, ffe, srows, hp, og_all, act, silu, slope, moe_in, r_all, shared_d, prob_in, small,
    resid, og, wg0, wu0, wd0, wg1, wu1, wd1, shared,
    mid_out, gain_out, seq_out, shared_out, shs_out, kg_out, ku_out, gg_out, gu_out, lg_out, lu_out,
    gt, blk, r_own, sends, shs, wsem, xsem, tsem, ksem, ss, sr, rs, es, ds, dr, dl, *rest,
):
    f, c, t = ranks()
    n_b = n_f * n_c
    rows, quarter = resid.shape
    width = shared_d.shape[1]
    n_exp = mine * n_b
    routed = mine * ffe
    rows_used = routed + srows
    first = (c * n_f + f) * mine
    reduce_scratch, rest = rest[:N_REDUCER], rest[N_REDUCER:]
    red = Reducer(n_c, reduce_scratch)

    cols = width // n_b

    def exchange(act):
        to_each(lambda b: shared_d.at[:, piece(b, cols)], shared_out, n_f, n_c, (ds, dr, dl), act)

    def blocks_phase(wgu, wd, ogs, acts):
        gate_up, down = fetch_experts(
            n_c, n_f, mine, ffe, srows, hp, (wg0, wu0, wd0, wg1, wu1, wd1), shared, wgu, wd, wsem
        )
        for copy in down + gate_up:
            copy.start()

        def loads(i, slot):
            b = red.row_block(i)
            return [
                pltpu.make_async_copy(
                    og_all.at[b, q], ogs.at[slot, :, pl.ds(q * quarter, quarter)], xsem.at[slot, q]
                )
                for q in range(4)
            ] + [
                pltpu.make_async_copy(src.at[piece(b, rows), :], acts.at[slot, k], xsem.at[slot, 4 + k])
                for k, src in enumerate((act, silu, slope))
            ]

        for copy in loads(0, 0):
            copy.start()
        blank_rows(rows_used, hp, wgu, wd)
        greet([{"tp": red.sib}, {"tp": red.far}, {"tp": opposite(red.sib)}] + each_peers(f, c, n_f, n_c))
        exchange("start")
        for copy in down:
            copy.wait()

        def compute(i, between):
            slot = lax.rem(i, 2)
            at = piece(red.row_block(i), rows)
            for copy in loads(i, slot):
                copy.wait()

            @pl.when(i + 1 < n_b)
            def _():
                for copy in loads(i + 1, 1 - slot):
                    copy.start()

            prob = prob_in[at, :]
            chosen = small[n_exp : 2 * n_exp, at].astype(F32).T
            gate, lane, col = gates(prob, chosen, first, mine, ffe, hp)
            dh = dot_nt(ogs[slot], wd[...])
            between()
            ad = acts[slot, 0].astype(F32) * dh
            p_grad = jnp.zeros(prob.shape, F32)
            for k in reversed(range(mine)):
                below = jnp.where(col < k * ffe, ad, 0.0) if k else jnp.zeros_like(ad)
                ad = jnp.where(col < (k + 1) * ffe, ad, 0.0)
                s = jnp.sum(ad - below, axis=1, keepdims=True)
                p_grad = jnp.where(lane == first + k, s, p_grad)
                ad = below
            p_grad = p_grad * chosen
            logit_f = prob * (p_grad - jnp.sum(prob * p_grad, axis=1, keepdims=True))
            logit_grad = logit_f.astype(BF)
            dg = dh * gate
            da = (dg * acts[slot, 2].astype(F32)).astype(BF)
            db = (dg * acts[slot, 1].astype(F32)).astype(BF)
            gt[:rows_used, at] = da.T[:rows_used, :]
            gt[rows_used : 2 * rows_used, at] = db.T[:rows_used, :]
            gt[2 * rows_used :, at] = logit_f.T.astype(BF)
            dab = jnp.concatenate([da, db], axis=1)

            @pl.when(i == 0)
            def _():
                for copy in gate_up:
                    copy.wait()

            def part_of(q):
                cols = piece(q, quarter)
                return dot_nn(dab, wgu[:, cols]) + dot_nn(logit_grad, small[:n_exp, cols])

            red.put(i, part_of)

        red.loop(n_b, compute)

    pl.run_scoped(
        blocks_phase,
        pltpu.VMEM((2 * hp, width), BF),
        pltpu.VMEM((hp, width), BF),
        pltpu.VMEM((2, rows, width), BF),
        pltpu.VMEM((2, 3, rows, hp), BF),
    )

    def send_copy(s, m):
        if s:
            return pltpu.make_async_copy(sends.at[s, m], (lg_out, lu_out)[m], ss.at[s, m])
        return remote(sends.at[s, m], (gg_out, gu_out)[m], ss.at[s, m], sr.at[m], {"fsdp": 1 - f})

    def grads_phase(tiles, keeps):
        def tile_of(s):
            return (1 - f) * 2 + s if s < 2 else f * 2 + s - 2

        def tile_load(s):
            return pltpu.make_async_copy(
                moe_in.at[:, piece(tile_of(s), quarter)], tiles.at[s % 2], tsem.at[s % 2]
            )

        def keep_copy(s, m):
            dst = (kg_out, ku_out)[m].at[:, :, pl.ds((s - 2) * quarter, quarter)]
            return pltpu.make_async_copy(keeps.at[s - 2, m], dst, ksem.at[s - 2, m])

        def work(s):
            def run():
                tile_load(s).wait()
                if s < 3:
                    tile_load(s + 1).start()
                g = dot_nn(gt[...], tiles[s % 2])
                cols = piece(tile_of(s), quarter)
                for m in range(2):
                    base = m * rows_used
                    if s < 2:
                        sends[s, m] = g[base : base + routed].astype(BF).reshape(mine, ffe, quarter)
                        send_copy(s, m).start()
                    else:
                        keeps[s - 2, m] = g[base : base + routed].astype(BF).reshape(mine, ffe, quarter)
                        keep_copy(s, m).start()
                    shs[m * srows : (m + 1) * srows, cols] = g[base + routed : base + rows_used].astype(BF)
                shs[2 * srows :, cols] = g[2 * rows_used :].astype(BF)

            return run

        tile_load(0).start()
        blk[...] = red.drain(n_b, [work(s) for s in range(4)])
        for s in (2, 3):
            for m in range(2):
                keep_copy(s, m).wait()

    fetch = pltpu.make_async_copy(r_all.at[piece(f * n_c + c, rows), :], r_own, rs)
    fetch.start()
    pl.run_scoped(
        grads_phase,
        pltpu.VMEM((2, n_b * rows, quarter), BF),
        pltpu.VMEM((2, 2, mine, ffe, quarter), BF),
    )
    shs_copy = pltpu.make_async_copy(shs, shs_out, es)
    shs_copy.start()
    fetch.wait()
    gain = small[2 * n_exp + 1 : 2 * n_exp + 2, piece(t, quarter)].astype(F32)
    back, gain_part = norm_grad(resid[...], r_own[:, :1], gain, blk[...], width, *rest[:4])
    gain_out[...] = jnp.broadcast_to(gain_part, gain_out.shape)
    grad = og[...].astype(F32) + back
    mid_out[...] = grad
    own = rest[4]
    own[...] = grad.astype(BF)

    def place(g, cc, tt):
        return seq_out.at[piece(cc, rows), piece(tt, quarter)]

    sequence = Spread(own, place, n_c, False, rest[5:])
    sequence.start()
    sequence.line()
    sequence.far(0)
    sequence.arrived(0)
    sequence.finish()
    sequence.local().wait()
    exchange("wait")
    shs_copy.wait()
    for s in range(2):
        for m in range(2):
            send_copy(s, m).wait()


def backward(
    n_c, n_f, n_t, mine, ffe, srows, og_all, act, silu, slope, moe_in, r_all, shared_d, prob, small,
    resid, og, kept, got, shared,
):
    total, width = moe_in.shape
    rows, quarter = resid.shape
    n_b = n_f * n_c
    n_exp = mine * n_b
    used, hp, n_fetch = expert_sizes(n_c, n_f, n_t, mine, ffe, srows, width)
    sds = jax.ShapeDtypeStruct
    kept_g = sds((mine, ffe, width // n_f), BF)
    sent_g = sds((mine, ffe, quarter), BF)
    return pl.pallas_call(
        functools.partial(backward_kernel, n_c, n_f, mine, ffe, srows, hp),
        out_shape=(
            sds((rows, quarter), F32),
            sds((8, quarter), F32),
            sds((rows * n_c, width), BF),
            sds((n_b, srows, width // n_b), BF),
            sds((2 * srows + n_exp, width), BF),
            kept_g,
            kept_g,
            sent_g,
            sent_g,
            sent_g,
            sent_g,
        ),
        in_specs=[HBM] * 7 + [VMEM] * 4 + [HBM] * 7,
        out_specs=[VMEM, VMEM] + [HBM] * 9,
        scratch_shapes=[
            pltpu.VMEM((2 * used + n_exp, total), BF),
            pltpu.VMEM((rows, quarter), F32),
            pltpu.VMEM((rows, HD), F32),
            pltpu.VMEM((2, 2, mine, ffe, quarter), BF),
            pltpu.VMEM((2 * srows + n_exp, width), BF),
            DMA((n_fetch,)),
            DMA((2, 7)),
            DMA((2,)),
            DMA((2, 2)),
            DMA((2, 2)),
            DMA((2,)),
            DMA(()),
            DMA(()),
            DMA((n_b,)),
            DMA((n_b,)),
            DMA(()),
        ]
        + reducer_scratch(n_f, n_c, rows, quarter, False)
        + norm_grad_scratch(rows)
        + [pltpu.VMEM((rows, quarter), BF)]
        + spread_sems(n_c),
        compiler_params=pltpu.CompilerParams(
            collective_id=3, has_side_effects=True, vmem_limit_bytes=BIG
        ),
        cost_estimate=pl.CostEstimate(
            flops=10 * total * width * used, bytes_accessed=200 << 20, transcendentals=0
        ),
        name="backward",
    )(
        og_all, act, silu, slope, moe_in, r_all, shared_d, prob, small, resid, og,
        *kept, *got, shared,
    )


def finish_kernel(n_plain, f_ref, *refs):
    ga, gb, ua, ub, d, kg, ku, kd, shared = refs[:9]
    plain, gains, refs = refs[9 : 9 + n_plain], refs[9 + n_plain], refs[:9] + refs[10:]
    og, ou, od, shared_out = refs[9 + n_plain : 13 + n_plain]
    step = pl.program_id(0)
    f = f_ref[0]
    n_e = kg.shape[0]

    def put(at):
        for keep, out in ((kg, og), (ku, ou), (kd, od)):
            out[at : at + n_e] = keep[...].astype(F32)
        for out, halves in ((og, (ga, gb)), (ou, (ua, ub))):
            @pl.when(step < 2)
            def _():
                out[n_e - at : 2 * n_e - at] = halves[0][...].astype(F32)

            @pl.when(step >= 2)
            def _():
                out[n_e - at : 2 * n_e - at] = halves[1][...].astype(F32)

        od[n_e - at : 2 * n_e - at] = d[...].astype(F32)

    @pl.when(f == 0)
    def _():
        put(0)

    @pl.when(f != 0)
    def _():
        put(n_e)

    own = shared_out.shape[0] // shared.shape[0]
    for b in range(shared.shape[0]):
        shared_out[b * own : (b + 1) * own, :] = shared[b, :own, :].astype(F32)
    for src, dst in zip(plain, refs[13 + n_plain :]):
        dst[...] = src[...]
    for i, dst in enumerate(refs[13 + 2 * n_plain :]):
        dst[...] = gains[i : i + 1, :]


def finish(f_rank, own_shared, arrived, kept, shared, plain, gains):
    mine, ffe, quarter = arrived[0].shape
    half = kept[0].shape[2]
    tile = half // 4
    n_b, srows, part = shared.shape
    first = pl.BlockSpec((mine, ffe, tile), lambda i, f: (0, 0, jnp.minimum(i, 1)))
    second = pl.BlockSpec((mine, ffe, tile), lambda i, f: (0, 0, jnp.maximum(i - 2, 0)))
    every = pl.BlockSpec((mine, ffe, tile), lambda i, f: (0, 0, i))
    out = pl.BlockSpec((2 * mine, ffe, tile), lambda i, f: (0, 0, i))

    def rows_of(x):
        if x.shape[0] % 64:
            return pl.BlockSpec(x.shape, lambda i, f: (0, 0))
        return pl.BlockSpec((x.shape[0] // 4, x.shape[1]), lambda i, f: (i, 0))

    shared_grad = jax.ShapeDtypeStruct((n_b * own_shared, part), F32)
    return pl.pallas_call(
        functools.partial(finish_kernel, len(plain)),
        grid_spec=pltpu.PrefetchScalarGridSpec(
            num_scalar_prefetch=1,
            grid=(4,),
            in_specs=[first, second, first, second, every]
            + [every] * 3
            + [pl.BlockSpec((n_b // 4, srows, part), lambda i, f: (i, 0, 0))]
            + [rows_of(x) for x in plain]
            + [rows_of(gains)],
            out_specs=[out] * 3
            + [rows_of(shared_grad)]
            + [rows_of(x) for x in plain]
            + [pl.BlockSpec((1, part), lambda i, f: (0, 0))] * 2,
        ),
        out_shape=tuple(jax.ShapeDtypeStruct((2 * mine, ffe, half), F32) for k in kept)
        + (shared_grad,)
        + tuple(jax.ShapeDtypeStruct(x.shape, x.dtype) for x in plain)
        + (jax.ShapeDtypeStruct((1, part), F32),) * 2,
        compiler_params=pltpu.CompilerParams(vmem_limit_bytes=BIG),
        name="finish",
    )(f_rank, *arrived, *kept, shared, *plain, gains)


def norm_grad(values, r, gain, grad, width, out, into, send, recv):
    f, c, t = ranks()
    rows = values.shape[0]
    local = jnp.sum(grad * gain * values, axis=1, keepdims=True)
    out[...] = jnp.broadcast_to(local, (rows, HD)).T[:8, :]
    peers = [sibling(t), opposite(t), opposite(sibling(t))]
    copies = [
        remote(out, into.at[i], send.at[i], recv.at[i], {"tp": peer}) for i, peer in enumerate(peers)
    ]
    for copy in copies:
        copy.start()
    gain_part = jnp.sum(grad * values * r, axis=0, keepdims=True)
    total = out[...]
    for i, copy in enumerate(copies):
        copy.wait()
        total = total + into[i]
    total = jnp.broadcast_to(total[0:1, :], (HD, rows)).T[:, :1]
    return r * gain * grad - values * (r * r * r * (total / width)), gain_part


def norm_grad_scratch(rows):
    return [
        pltpu.VMEM((8, rows), F32),
        pltpu.VMEM((3, 8, rows), F32),
        DMA((3,)),
        DMA((3,)),
    ]


def attend_back(block, mid, wo, q, k, v, hf, lse, cosine, sine, dqkv, hg, dq, dk, dv):
    seq = mid.shape[0]
    scale_att = HD ** (-0.5)
    for start in range(0, seq, block):
        at = pl.ds(start, block)
        hg[at, :] = dot_nt(mid[at, :], wo[...]).astype(BF)
    dk[...] = jnp.zeros_like(dk)
    dv[...] = jnp.zeros_like(dv)
    for start in range(0, seq, block):
        at = pl.ds(start, block)
        seen = start + block
        qb, hb = q[at, :], hg[at, :]
        delta = jnp.sum(hb.astype(F32) * hf[at, :], axis=1, keepdims=True)
        s = dot_nt(qb, k[:seen, :]) * scale_att
        row = lax.broadcasted_iota(jnp.int32, (block, seen), 0) + start
        col = lax.broadcasted_iota(jnp.int32, (block, seen), 1)
        p = jnp.where(col <= row, jnp.exp(s - lse[at, :1]), 0.0)
        ds = (p * (dot_nt(hb, v[:seen, :]) - delta)).astype(BF)
        dq[at, :] = dot_nn(ds, k[:seen, :]) * scale_att
        dk[:seen, :] += dot_tn(ds, qb) * scale_att
        dv[:seen, :] += dot_tn(p.astype(BF), hb)

    def rotate(values, at):
        return (values * cosine[at, :] - pltpu.roll(values, HD // 2, 1) * sine[at, :]).astype(BF)

    for start in range(0, seq, block):
        at = pl.ds(start, block)
        dqkv[at, :HD] = rotate(dq[at, :], at)
        dqkv[at, HD : 2 * HD] = rotate(dk[at, :], at)
        dqkv[at, 2 * HD :] = dv[at, :].astype(BF)


def last_kernel(
    n_c, n_f, n_t, n_exp, own_shared, mid_in, wo, q, k, v, hf, lse, cosine, sine, normed_in, wqkv_in, hidden, r_all,
    small, mid_grad, gain2, shs, lg, lu,
    in_out, gq, gk, gv, go, gains_out, router_out, sg_out, su_out, lg_out, lu_out,
    mid_seq, normed, wqkv, big, dqkv, hg, dq, dk, dv, gattn, shs_in, rpart, hs, hr, hl, es, er, rin, rss, rsr, r_own, mine, inx, own, outz, inz, gsend, gin, rs, sx, rx, lx, sz, rz, gs, gr, *rest,
):
    f, c, t = ranks()
    rows, quarter = hidden.shape
    tokens, width = normed.shape
    part = width // (n_f * n_c)
    here = f * n_c + c
    srows = (shs.shape[0] - n_exp) // 2
    others = []
    for df in range(n_f):
        for dc in range(n_c):
            for dt in range(n_t):
                if df or dc or dt:
                    others.append(
                        {
                            "fsdp": lax.rem(f + df, n_f),
                            "ctx": lax.rem(c + dc, n_c),
                            "tp": lax.rem(t + dt, n_t),
                        }
                    )
    large = [
        pltpu.make_async_copy(src, dst, big.at[i])
        for i, (src, dst) in enumerate(((mid_in, mid_seq), (wqkv_in, wqkv), (normed_in, normed)))
    ]
    for copy in large:
        copy.start()
    gin[...] = jnp.zeros_like(gin)
    greet(others)
    order = [2, 1, 3, 0] if n_c == 4 else list(range(1, n_c)) + [0]

    def cross(d):
        cc = lax.rem(c + d, n_c)
        return remote(
            gattn.at[:, piece((1 - f) * n_c + cc, part)], inx.at[d], sx.at[d], rx.at[d], {"fsdp": 1 - f}
        )

    def keep(d):
        cc = lax.rem(c + d, n_c)
        return pltpu.make_async_copy(gattn.at[:, piece(f * n_c + cc, part)], own.at[d], lx.at[d])

    def line(d, to):
        return remote(outz.at[d], inz.at[d], sz.at[d], rz.at[d], {"ctx": to})

    router_copies = [
        remote(rpart, rin.at[i], rss.at[i], rsr.at[i], {"tp": peer})
        for i, peer in enumerate([sibling(t), opposite(t), opposite(sibling(t))])
    ]
    shared = lambda act: to_each(lambda b: shs.at[:, piece(b, part)], shs_in, n_f, n_c, (hs, hr, hl), act)
    late = [
        remote(src, dst, es.at[i], er.at[i], {"fsdp": 1 - f})
        for i, (src, dst) in enumerate(((lg, lg_out), (lu, lu_out)))
    ]
    shared("start")
    fetch = pltpu.make_async_copy(r_all.at[piece(c, rows), :], r_own, rs)
    fetch.start()
    late[0].start()
    large[0].wait()
    attend_back(rows, mid_seq, wo, q, k, v, hf, lse, cosine, sine, dqkv, hg, dq, dk, dv)
    gattn[3 * HD :, :] = dot_tn(hf[...].astype(BF), mid_seq[...]).astype(BF)

    large[1].wait()

    def weights():
        large[2].wait()
        gattn[: 3 * HD, :] = dot_tn(dqkv[...], normed[...]).astype(BF)
        for d in order:
            cross(d).start()
            keep(d).start()
        late[1].start()


    def part_of(cc, q):
        return dot_nt(dqkv[piece(cc, rows), :], wqkv[piece(q, quarter), :])

    def pass_weights():
        for d in order:
            cross(d).wait()
            keep(d).wait()
            both = own[d].astype(F32) + inx[d].astype(F32)
            if d:
                outz[d] = both.astype(BF)
                line(d, lax.rem(c + d, n_c)).start()
            else:
                mine[...] = both

    total = reduce_seq(part_of, n_c, rest[:13], weights, pass_weights)
    fetch.wait()
    gain = small[2 * n_exp : 2 * n_exp + 1, piece(t, quarter)].astype(F32)
    back, gain_part = norm_grad(
        hidden[...].astype(F32), r_own[:, :1], gain, total, width, *rest[13:17]
    )
    in_out[...] = mid_grad[...] + back

    gsend[0:1, :] = gain_part
    gsend[1:2, :] = gain2[0:1, :]
    gsend[2:, :] = jnp.zeros((6, quarter), F32)
    per = quarter // part
    holder = here // per
    def gain_copy(h, tt):
        b = t * per + h
        return remote(
            gsend.at[:, pl.ds(h * part, part)],
            gin.at[here],
            gs.at[h * n_t + tt],
            gr.at[here],
            {"fsdp": b // n_c, "ctx": lax.rem(b, n_c), "tp": jnp.int32(tt)},
        )

    def is_me(h, tt):
        return (t * per + h == here) & (t == tt)

    for h in range(per):
        for tt in range(n_t):

            @pl.when(jnp.logical_not(is_me(h, tt)))
            def _():
                gain_copy(h, tt).start()

    def put(src, block):
        at = piece(src, HD)
        for i, ref in enumerate((gq, gk, gv)):
            ref[:, at] = block[i * HD : (i + 1) * HD, :].T
        go[at, :] = block[3 * HD :, :]

    shared("wait")
    rpart[...] = jnp.sum(shs_in[:, 2 * srows :, :].astype(F32), axis=0)
    for copy in router_copies:
        copy.start()
    for b in range(n_f * n_c):
        at = pl.ds(b * own_shared, own_shared)
        sg_out[at, :] = shs_in[b, :own_shared, :].astype(F32)
        su_out[at, :] = shs_in[b, srows : srows + own_shared, :].astype(F32)
    put(c, mine[...])
    for d in order[:-1]:
        line(d, c).wait()
        put(lax.rem(c - d + n_c, n_c), inz[d].astype(F32))
    for h in range(per):
        for tt in range(n_t):

            @pl.when(jnp.logical_not(is_me(h, tt)))
            def _():
                gain_copy(h, tt).wait_send()

    for b in range(n_f * n_c):

        @pl.when((b != here) | (holder != t))
        def _():
            remote(gin.at[b], gin.at[b], gs.at[0], gr.at[b], {"tp": sibling(t)}).wait_recv()

    own_part = jnp.where(
        holder == t,
        gsend[:, piece(lax.rem(here, per), part)],
        jnp.zeros((8, part), F32),
    )
    gains_out[...] = own_part + jnp.sum(gin[...], axis=0)
    for copy in router_copies + late:
        copy.wait()
    router_out[...] = rpart[...] + jnp.sum(rin[...], axis=0)


def last(
    n_c, n_f, n_t, n_exp, own_shared, mid_seq, wo, q, k, v, hf, lse, cosine, sine, normed, wqkv, hidden, r_all,
    small, mid_grad, gain2, shs, lg, lu,
):
    rows, quarter = hidden.shape
    seq, width = normed.shape
    part = width // (n_f * n_c)
    sds = jax.ShapeDtypeStruct
    slab = pltpu.VMEM((n_c, 4 * HD, part), BF)
    head_f = pltpu.VMEM((seq, HD), F32)
    shared_grad = sds((n_f * n_c * own_shared, part), F32)
    return pl.pallas_call(
        functools.partial(last_kernel, n_c, n_f, n_t, n_exp, own_shared),
        out_shape=(
            sds((rows, quarter), F32),
            sds((part, n_c * HD), F32),
            sds((part, n_c * HD), F32),
            sds((part, n_c * HD), F32),
            sds((n_c * HD, part), F32),
            sds((8, part), F32),
            sds((n_exp, part), F32),
            shared_grad,
            shared_grad,
            sds(lg.shape, BF),
            sds(lu.shape, BF),
        ),
        in_specs=[HBM] + [VMEM] * 8 + [HBM] * 2 + [VMEM, HBM] + [VMEM] * 3 + [HBM] * 3,
        out_specs=[VMEM] * 9 + [HBM] * 2,
        scratch_shapes=[
            pltpu.VMEM((seq, width), BF),
            pltpu.VMEM((seq, width), BF),
            pltpu.VMEM((width, 3 * HD), BF),
            DMA((3,)),
            pltpu.VMEM((seq, 3 * HD), BF),
            pltpu.VMEM((seq, HD), BF),
            head_f,
            head_f,
            head_f,
            pltpu.VMEM((4 * HD, width), BF),
            pltpu.VMEM((n_f * n_c, shs.shape[0], part), BF),
            pltpu.VMEM((n_exp, part), F32),
            DMA((n_f * n_c,)),
            DMA((n_f * n_c,)),
            DMA(()),
            DMA((2,)),
            DMA((2,)),
            pltpu.VMEM((3, n_exp, part), F32),
            DMA((3,)),
            DMA((3,)),
            pltpu.VMEM((rows, HD), F32),
            pltpu.VMEM((4 * HD, part), F32),
            slab,
            slab,
            slab,
            slab,
            pltpu.VMEM((8, quarter), F32),
            pltpu.VMEM((n_f * n_c, 8, part), F32),
            DMA(()),
            DMA((n_c,)),
            DMA((n_c,)),
            DMA((n_c,)),
            DMA((n_c,)),
            DMA((n_c,)),
            DMA((quarter // part * n_t,)),
            DMA((n_f * n_c,)),
        ]
        + reduce_seq_scratch(n_c, rows, quarter)
        + norm_grad_scratch(rows),
        compiler_params=pltpu.CompilerParams(
            collective_id=4, has_side_effects=True, vmem_limit_bytes=BIG
        ),
        cost_estimate=pl.CostEstimate(flops=8 << 30, bytes_accessed=150 << 20, transcendentals=1 << 20),
        name="last",
    )(
        mid_seq, wo, q, k, v, hf, lse, cosine, sine, normed, wqkv, hidden, r_all, small, mid_grad, gain2,
        shs, lg, lu,
    )


def per_device_seq(
    hidden_in,
    positions,
    chosen,
    out_grad,
    attn_gain,
    w_query,
    w_key,
    w_value,
    w_out,
    moe_gain,
    router,
    shared_gate,
    shared_up,
    shared_down,
    expert_gate,
    expert_up,
    expert_down,
):
    f_rank, c_rank, t_rank = ranks()
    n_f, n_c, n_t = (lax.axis_size(name) for name in ("fsdp", "ctx", "tp"))
    rows, quarter = hidden_in.shape
    width = quarter * n_t
    part = w_query.shape[0]
    seq = rows * n_c
    n_exp = router.shape[1]
    mine = n_exp // n_c // n_f
    ffe = expert_gate.shape[2]
    group = ("fsdp", "ctx")
    every = ("fsdp", "ctx", "tp")
    n_b = n_f * n_c
    own_shared = shared_gate.shape[1] // n_b
    srows = -(-own_shared // 16) * 16
    f_arr = f_rank.astype(jnp.int32).reshape(1)
    swap = [(i, n_f - 1 - i) for i in range(n_f)]
    weights = (expert_gate.swapaxes(1, 2), expert_up.swapaxes(1, 2), expert_down)

    line = jnp.arange(16)[:, None]
    lines = jnp.where(line == 0, attn_gain[None], jnp.zeros((), BF))
    lines = jnp.where(line == 1, moe_gain[None], lines)
    lines = jnp.where(line == 2, (positions // 64).astype(BF)[None], lines)
    lines = jnp.where(line == 3, (positions % 64).astype(BF)[None], lines)
    lane = np.arange(HD)
    inverse = 10000.0 ** (-(lane % (HD // 2)) * 2.0 / HD)
    angle = jnp.asarray(np.stack([inverse, np.where(lane < HD // 2, -1.0, 1.0)]).astype(np.float32))
    (
        normed, q, k, v, heads_f, lse, r_one, cosine, sine, resid_mid,
        wqkv, wo, small, resid_all, grad_all, shared, *got,
    ) = first(
        n_c, n_f, n_t, mine, srows, hidden_in, w_query, w_key, w_value, w_out, out_grad, weights,
        router.T, chosen.T, lines, (shared_gate.T, shared_up.T, shared_down), angle,
    )
    sizes = (n_c, n_f, n_t, mine, ffe, srows)
    layer_out, moe_in, act, silu, slope, r_two, prob, kd, sd, shared_d = forward(
        *sizes, resid_all, grad_all, resid_mid, small, weights, got, shared
    )
    arrived_d = lax.ppermute(sd, "fsdp", swap)
    mid_grad, gain_two_part, mid_seq, shared_back, shs, kg, ku, gg, gu, lg, lu = backward(
        *sizes, grad_all, act, silu, slope, moe_in, r_two, shared_d, prob, small,
        resid_mid, out_grad, weights, got, shared,
    )
    input_grad, gq, gk, gv, go, gains, router_grad, shared_g, shared_u, lg, lu = last(
        n_c, n_f, n_t, n_exp, own_shared, mid_seq, wo, q, k, v, heads_f, lse, cosine, sine, normed, wqkv,
        hidden_in, r_one, small, mid_grad, gain_two_part, shs, lg, lu,
    )
    plain = (layer_out, input_grad, gq, gk, gv, go, router_grad, shared_g, shared_u)
    (
        eg, eu, ed, shared_d, layer_out, input_grad, gq, gk, gv, go, router_grad, shared_g, shared_u, gain_1, gain_2,
    ) = finish(f_arr, own_shared, (gg, lg, gu, lu, arrived_d), (kg, ku, kd), shared_back, plain, gains)

    return (
        layer_out,
        input_grad,
        gain_1[0],
        gq,
        gk,
        gv,
        go,
        gain_2[0],
        router_grad.T,
        shared_g.T,
        shared_u.T,
        shared_d,
        eg.swapaxes(1, 2),
        eu.swapaxes(1, 2),
        ed,
    )


def one_head_each(mesh, args):
    n_f, n_c, n_t = (mesh.shape[name] for name in ("fsdp", "ctx", "tp"))
    heads = args[5].shape[1] // HD
    experts = args[10].shape[1]
    return (
        n_f == 2
        and n_t == 4
        and heads == n_c * n_t
        and experts % (n_f * n_c) == 0
        and args[11].shape[1] % (8 * n_f * n_c * n_t) == 0
    )


def solution(mesh):
    placed = (
        P(("fsdp", "ctx"), "tp"),
        P(("fsdp", "ctx")),
        P(("fsdp", "ctx"), None),
        P(("fsdp", "ctx"), "tp"),
        P(("fsdp", "ctx")),
        P(("fsdp", "ctx"), "tp"),
        P(("fsdp", "ctx"), "tp"),
        P(("fsdp", "ctx"), "tp"),
        P("tp", ("fsdp", "ctx")),
        P(("fsdp", "ctx")),
        P(("fsdp", "ctx"), None),
        P(("fsdp", "ctx"), "tp"),
        P(("fsdp", "ctx"), "tp"),
        P("tp", ("fsdp", "ctx")),
        P("ctx", "fsdp", "tp"),
        P("ctx", "fsdp", "tp"),
        P("ctx", "tp", "fsdp"),
    )
    def run(*args):
        body = per_device_seq if one_head_each(mesh, args) else per_device
        return jax.shard_map(
        body,
        mesh=mesh,
        in_specs=placed,
        out_specs=(
            P(("fsdp", "ctx"), "tp"),
            P(("fsdp", "ctx"), "tp"),
            P(("fsdp", "ctx")),
            P(("fsdp", "ctx"), "tp"),
            P(("fsdp", "ctx"), "tp"),
            P(("fsdp", "ctx"), "tp"),
            P("tp", ("fsdp", "ctx")),
            P(("fsdp", "ctx")),
            P(("fsdp", "ctx"), None),
            P(("fsdp", "ctx"), "tp"),
            P(("fsdp", "ctx"), "tp"),
            P("tp", ("fsdp", "ctx")),
            P("ctx", "fsdp", "tp"),
            P("ctx", "fsdp", "tp"),
            P("ctx", "tp", "fsdp"),
        ),
        check_vma=False,
    )(*args)

    return run
```

```python
import functools

import jax
import jax.numpy as jnp
import numpy as np
from jax import lax
from jax.experimental import pallas as pl
from jax.experimental.pallas import tpu as pltpu
from jax.sharding import PartitionSpec as P

HD = 128
TOPK = 6


EPS = 1e-06
NEG_BIG = -1e30


def as_sent(value):
    return jax.tree.map(lambda a: a.astype(jnp.bfloat16) if a.dtype == jnp.float32 else a, value)


def features(local_part):
    return lax.all_gather(local_part, "tp", axis=1, tiled=True)


def row_stats(partial_terms):
    return lax.psum(partial_terms, "tp")


def partial_sums(partial_terms):
    return jax.tree.map(
        lambda part: part.astype(jnp.float32),
        lax.psum_scatter(as_sent(partial_terms), "tp", scatter_dimension=1, tiled=True),
    )


def to_owners(slot_rows):
    return lax.all_to_all(slot_rows, "ctx", split_axis=0, concat_axis=2, tiled=True)


def to_sources(slot_rows):
    return lax.all_to_all(
        slot_rows.astype(jnp.bfloat16), "ctx", split_axis=2, concat_axis=0, tiled=True
    ).astype(slot_rows.dtype)


def rotary(values, positions, rotate_sign):
    half_dim = values.shape[-1] // 2
    inverse = 10000.0 ** (-jnp.arange(half_dim, dtype=jnp.float32) * 2.0 / values.shape[-1])
    angles = positions.astype(jnp.float32)[:, None] * inverse[None, :]
    cosine = jnp.cos(angles)[:, None, :]
    sine_val = rotate_sign * jnp.sin(angles)[:, None, :]
    lower_half = values[..., :half_dim]
    upper_half = values[..., half_dim:]
    return jnp.concatenate(
        [lower_half * cosine - upper_half * sine_val, upper_half * cosine + lower_half * sine_val],
        axis=-1,
    )


def norm_rows(values, gain_part, model_width):
    square_sum = row_stats(jnp.sum(values * values, axis=1))
    row_scale = lax.rsqrt(square_sum / model_width + EPS)
    return (values * row_scale[:, None] * gain_part[None, :], row_scale)


def norm_back(values, row_scale, gain_part, grad_normed, model_width, tp_rank):
    quarter = values.shape[1]
    local_sum = jnp.sum(grad_normed * gain_part[None, :] * values, axis=1)
    gain_local = jnp.sum(grad_normed * values * row_scale[:, None], axis=0)
    gain_whole = lax.dynamic_update_slice_in_dim(
        jnp.zeros((model_width,), jnp.float32), gain_local, tp_rank * quarter, 0
    )
    row_total, gain_grad = row_stats((local_sum, gain_whole))
    back = (
        row_scale[:, None] * gain_part[None, :] * grad_normed
        - values * (row_scale**3 * row_total / model_width)[:, None]
    )
    return (back, gain_grad)


def scatter_slots(assign_rows, flat_exp, slot_of, n_exp, capacity):
    buffer = jnp.zeros((n_exp, capacity, assign_rows.shape[1]), assign_rows.dtype)
    return buffer.at[flat_exp, slot_of].set(assign_rows)


def silu_grad(pre_act):
    sigmoid_val = jax.nn.sigmoid(pre_act)
    return sigmoid_val * (1.0 + pre_act * (1.0 - sigmoid_val))


def keep_state(carried):
    return carried


def per_device(
    hidden_in,
    positions,
    chosen,
    out_grad,
    attn_gain,
    w_query,
    w_key,
    w_value,
    w_out,
    moe_gain,
    router,
    shared_gate,
    shared_up,
    shared_down,
    expert_gate,
    expert_up,
    expert_down,
):
    tp_rank = lax.axis_index("tp")
    ctx_rank = lax.axis_index("ctx")
    n_ctx = lax.axis_size("ctx")
    tok_rows, quarter = hidden_in.shape
    model_width = quarter * lax.axis_size("tp")
    gain_one, wq_all, wk_all, wv_all, gain_two, router_all, gate_all, up_all, wo_all, down_all = (
        lax.all_gather(attn_gain, ("fsdp", "ctx"), axis=0, tiled=True),
        lax.all_gather(w_query, ("fsdp", "ctx"), axis=0, tiled=True),
        lax.all_gather(w_key, ("fsdp", "ctx"), axis=0, tiled=True),
        lax.all_gather(w_value, ("fsdp", "ctx"), axis=0, tiled=True),
        lax.all_gather(moe_gain, ("fsdp", "ctx"), axis=0, tiled=True),
        lax.all_gather(router, ("fsdp", "ctx"), axis=0, tiled=True),
        lax.all_gather(shared_gate, ("fsdp", "ctx"), axis=0, tiled=True),
        lax.all_gather(shared_up, ("fsdp", "ctx"), axis=0, tiled=True),
        lax.all_gather(w_out, ("fsdp", "ctx"), axis=1, tiled=True),
        lax.all_gather(shared_down, ("fsdp", "ctx"), axis=1, tiled=True),
    )
    expert_gate_weights, expert_up_weights, expert_down_weights = (
        lax.all_gather(expert_gate, "fsdp", axis=1, tiled=True),
        lax.all_gather(expert_up, "fsdp", axis=1, tiled=True),
        lax.all_gather(expert_down, "fsdp", axis=2, tiled=True),
    )
    gain_q1 = lax.dynamic_slice_in_dim(gain_one, tp_rank * quarter, quarter).astype(jnp.float32)
    gain_q2 = lax.dynamic_slice_in_dim(gain_two, tp_rank * quarter, quarter).astype(jnp.float32)
    router_rows = lax.dynamic_slice_in_dim(router_all, tp_rank * quarter, quarter, 0)
    head_count = wq_all.shape[1] // HD
    scale_att = HD ** (-0.5)
    resid_in = hidden_in.astype(jnp.float32)
    normed_one, scale_one = norm_rows(resid_in, gain_q1, model_width)
    normed_in = features(normed_one.astype(jnp.bfloat16))
    query_pre = jnp.dot(normed_in, wq_all, preferred_element_type=jnp.float32).reshape(
        tok_rows, head_count, HD
    )
    key_pre = jnp.dot(normed_in, wk_all, preferred_element_type=jnp.float32).reshape(
        tok_rows, head_count, HD
    )
    value_b = (
        jnp.dot(normed_in, wv_all, preferred_element_type=jnp.float32)
        .astype(jnp.bfloat16)
        .reshape(tok_rows, head_count, HD)
    )
    query_b = rotary(query_pre, positions, 1.0).astype(jnp.bfloat16)
    key_b = rotary(key_pre, positions, 1.0).astype(jnp.bfloat16)
    q_start = ctx_rank * tok_rows
    row_pos = q_start + jnp.arange(tok_rows)
    start_state = (
        jnp.full((tok_rows, head_count), NEG_BIG, jnp.float32),
        jnp.zeros((tok_rows, head_count), jnp.float32),
        jnp.zeros((tok_rows, head_count, HD), jnp.float32),
    )
    keys_blk = lax.all_gather(key_b, "ctx", axis=0, tiled=True)
    vals_blk = lax.all_gather(value_b, "ctx", axis=0, tiled=True)
    key_count = keys_blk.shape[0]

    def compute(state_in):
        run_max, run_sum, run_acc = state_in
        scores = (
            jnp.einsum("qhd,khd->qhk", query_b, keys_blk, preferred_element_type=jnp.float32)
            * scale_att
        )
        visible = jnp.arange(key_count)[None, :] <= row_pos[:, None]
        scores = jnp.where(visible[:, None, :], scores, NEG_BIG)
        new_max = jnp.maximum(run_max, jnp.max(scores, axis=2))
        weights = jnp.exp(scores - new_max[:, :, None])
        new_sum = jnp.sum(weights, axis=2)
        new_acc = jnp.einsum(
            "qhk,khd->qhd",
            weights.astype(jnp.bfloat16),
            vals_blk,
            preferred_element_type=jnp.float32,
        )
        return (new_max, new_sum, new_acc)

    run_max, run_sum, run_acc = lax.cond(
        jnp.int32(0) <= q_start + tok_rows - 1, compute, keep_state, start_state
    )
    heads_f = run_acc / run_sum[:, :, None]
    log_sum = run_max + jnp.log(run_sum)
    heads_b = heads_f.astype(jnp.bfloat16).reshape(tok_rows, head_count * HD)
    resid_mid = resid_in + partial_sums(
        jnp.dot(heads_b, wo_all, preferred_element_type=jnp.float32)
    )
    normed_two, scale_two = norm_rows(resid_mid, gain_q2, model_width)
    moe_part = normed_two.astype(jnp.bfloat16)
    moe_in = features(moe_part)
    n_exp = router_all.shape[1]
    exp_dev = n_exp // n_ctx
    capacity = min(tok_rows, 5 * TOPK * tok_rows // (3 * n_exp))
    logits = jnp.dot(moe_in, router_all, preferred_element_type=jnp.float32)
    probs_all = jax.nn.softmax(logits, axis=1)
    picked = (chosen[:, :, None] == jnp.arange(n_exp)[None, None, :]).astype(jnp.float32)
    gate_vals = jnp.sum(picked * probs_all[:, None, :], axis=2)
    shared_a = jnp.dot(moe_in, gate_all, preferred_element_type=jnp.float32)
    shared_b = jnp.dot(moe_in, up_all, preferred_element_type=jnp.float32)
    shared_act = (jax.nn.silu(shared_a) * shared_b).astype(jnp.bfloat16)
    shared_out = jnp.dot(shared_act, down_all, preferred_element_type=jnp.float32)
    flat_exp = chosen.reshape(-1)
    flat_hot = (flat_exp[:, None] == jnp.arange(n_exp)[None, :]).astype(jnp.int32)
    slot_of = jnp.sum((jnp.cumsum(flat_hot, axis=0) - flat_hot) * flat_hot, axis=1)
    token_of = jnp.arange(tok_rows * TOPK) // TOPK
    slot_count = n_ctx * capacity
    outgoing = scatter_slots(moe_in[token_of], flat_exp, slot_of, n_exp, capacity)
    received_rows = to_owners(outgoing.reshape(n_ctx, exp_dev, capacity, model_width)).reshape(
        exp_dev, slot_count, model_width
    )
    expert_a = jnp.einsum(
        "bmw,bwv->bmv", received_rows, expert_gate_weights, preferred_element_type=jnp.float32
    )
    expert_up_proj = jnp.einsum(
        "bmw,bwv->bmv", received_rows, expert_up_weights, preferred_element_type=jnp.float32
    )
    expert_act = (jax.nn.silu(expert_a) * expert_up_proj).astype(jnp.bfloat16)
    expert_out = jnp.einsum(
        "erf,efd->erd", expert_act, expert_down_weights, preferred_element_type=jnp.float32
    )
    returned = to_sources(expert_out.reshape(1, exp_dev, slot_count, model_width))
    shared_q, slot_q = partial_sums((shared_out, returned.reshape(n_exp * capacity, model_width)))
    slot_rows = slot_q.reshape(n_exp, capacity, quarter)[flat_exp, slot_of].reshape(
        tok_rows, TOPK, quarter
    )
    result = resid_mid + shared_q + jnp.sum(gate_vals[:, :, None] * slot_rows, axis=1)
    layer_out = result.astype(jnp.bfloat16)
    grad_out = out_grad.astype(jnp.float32)
    gate_grad = row_stats(jnp.sum(grad_out[:, None, :] * slot_rows, axis=2))
    prob_grad = jnp.sum(gate_grad[:, :, None] * picked, axis=1)
    logit_grad = (
        probs_all * (prob_grad - jnp.sum(probs_all * prob_grad, axis=1, keepdims=True))
    ).astype(jnp.bfloat16)
    router_grad = jnp.einsum("td,te->de", moe_in, logit_grad, preferred_element_type=jnp.float32)
    router_back_q = jnp.einsum(
        "te,de->td", logit_grad, router_rows, preferred_element_type=jnp.float32
    )
    grad_full = features(out_grad)
    shared_dact = jnp.einsum("td,fd->tf", grad_full, down_all, preferred_element_type=jnp.float32)
    shared_da = (shared_dact * shared_b * silu_grad(shared_a)).astype(jnp.bfloat16)
    shared_db = (shared_dact * jax.nn.silu(shared_a)).astype(jnp.bfloat16)
    shared_down_grad = jnp.einsum(
        "tf,td->fd", shared_act, grad_full, preferred_element_type=jnp.float32
    )
    shared_gate_grad = jnp.einsum(
        "td,tf->df", moe_in, shared_da, preferred_element_type=jnp.float32
    )
    shared_up_grad = jnp.einsum("td,tf->df", moe_in, shared_db, preferred_element_type=jnp.float32)
    shared_back = jnp.einsum(
        "tf,df->td", shared_da, gate_all, preferred_element_type=jnp.float32
    ) + jnp.einsum("tf,df->td", shared_db, up_all, preferred_element_type=jnp.float32)
    assign_grad = (
        (gate_vals[:, :, None] * grad_full[:, None, :])
        .astype(jnp.bfloat16)
        .reshape(tok_rows * TOPK, model_width)
    )
    grad_slots = scatter_slots(assign_grad, flat_exp, slot_of, n_exp, capacity)
    grad_arrived = to_owners(grad_slots.reshape(n_ctx, exp_dev, capacity, model_width)).reshape(
        exp_dev, slot_count, model_width
    )
    expert_dact = jnp.einsum(
        "erd,efd->erf", grad_arrived, expert_down_weights, preferred_element_type=jnp.float32
    )
    expert_da = (expert_dact * expert_up_proj * silu_grad(expert_a)).astype(jnp.bfloat16)
    expert_up_proj_grad = (expert_dact * jax.nn.silu(expert_a)).astype(jnp.bfloat16)
    edown_grad = jnp.einsum(
        "erf,erd->efd", expert_act, grad_arrived, preferred_element_type=jnp.float32
    )
    egate_grad = jnp.einsum(
        "qgo,qgz->qoz", received_rows, expert_da, preferred_element_type=jnp.float32
    )
    expert_up_weight_grad = jnp.einsum(
        "qgo,qgz->qoz", received_rows, expert_up_proj_grad, preferred_element_type=jnp.float32
    )
    expert_back = jnp.einsum(
        "iac,igc->iag", expert_da, expert_gate_weights, preferred_element_type=jnp.float32
    ) + jnp.einsum(
        "iac,igc->iag", expert_up_proj_grad, expert_up_weights, preferred_element_type=jnp.float32
    )
    back_slots = to_sources(expert_back.reshape(1, exp_dev, slot_count, model_width)).reshape(
        n_exp, capacity, model_width
    )
    token_back = jnp.sum(back_slots[flat_exp, slot_of].reshape(tok_rows, TOPK, model_width), axis=1)
    moe_back_q = partial_sums(shared_back + token_back)
    mid_back, gain_two_grad = norm_back(
        resid_mid, scale_two, gain_q2, moe_back_q + router_back_q, model_width, tp_rank
    )
    mid_grad = grad_out + mid_back
    branch_full = features(mid_grad.astype(jnp.bfloat16))
    wo_grad = jnp.einsum("tf,td->fd", heads_b, branch_full, preferred_element_type=jnp.float32)
    heads_grad = (
        jnp.einsum("td,fd->tf", branch_full, wo_all, preferred_element_type=jnp.float32)
        .astype(jnp.bfloat16)
        .reshape(tok_rows, head_count, HD)
    )
    row_delta = jnp.sum(heads_grad.astype(jnp.float32) * heads_f, axis=2)
    seq_len = tok_rows * n_ctx
    back_state = (
        jnp.zeros((tok_rows, head_count, HD), jnp.float32),
        jnp.zeros((seq_len, head_count, HD), jnp.float32),
        jnp.zeros((seq_len, head_count, HD), jnp.float32),
    )
    attend_keys_blk = lax.all_gather(key_b, "ctx", axis=0, tiled=True)
    attend_vals_blk = lax.all_gather(value_b, "ctx", axis=0, tiled=True)
    attend_key_count = attend_keys_blk.shape[0]

    def compute(state_in):
        scores = (
            jnp.einsum("qhd,khd->qhk", query_b, attend_keys_blk, preferred_element_type=jnp.float32)
            * scale_att
        )
        visible = jnp.arange(attend_key_count)[None, :] <= row_pos[:, None]
        probs_blk = jnp.where(visible[:, None, :], jnp.exp(scores - log_sum[:, :, None]), 0.0)
        value_part = jnp.einsum(
            "qhk,qhd->khd",
            probs_blk.astype(jnp.bfloat16),
            heads_grad,
            preferred_element_type=jnp.float32,
        )
        dot_grad = jnp.einsum(
            "qhd,khd->qhk", heads_grad, attend_vals_blk, preferred_element_type=jnp.float32
        )
        score_grad = (probs_blk * (dot_grad - row_delta[:, :, None])).astype(jnp.bfloat16)
        query_acc = (
            jnp.einsum(
                "qhk,khd->qhd", score_grad, attend_keys_blk, preferred_element_type=jnp.float32
            )
            * scale_att
        )
        key_part = (
            jnp.einsum("qhk,qhd->khd", score_grad, query_b, preferred_element_type=jnp.float32)
            * scale_att
        )
        return (query_acc, key_part, value_part)

    query_grad, key_grad_all, value_grad_all = lax.cond(
        jnp.int32(0) <= q_start + tok_rows - 1, compute, keep_state, back_state
    )
    key_grad, value_grad = (
        lax.psum_scatter(
            key_grad_all.astype(jnp.bfloat16), "ctx", scatter_dimension=0, tiled=True
        ).astype(jnp.float32),
        lax.psum_scatter(
            value_grad_all.astype(jnp.bfloat16), "ctx", scatter_dimension=0, tiled=True
        ).astype(jnp.float32),
    )
    query_pre_grad = (
        rotary(query_grad, positions, -1.0).astype(jnp.bfloat16).reshape(tok_rows, head_count * HD)
    )
    key_pre_grad = (
        rotary(key_grad, positions, -1.0).astype(jnp.bfloat16).reshape(tok_rows, head_count * HD)
    )
    value_pre_grad = value_grad.astype(jnp.bfloat16).reshape(tok_rows, head_count * HD)
    wq_grad = jnp.einsum("td,tf->df", normed_in, query_pre_grad, preferred_element_type=jnp.float32)
    wk_grad = jnp.einsum("td,tf->df", normed_in, key_pre_grad, preferred_element_type=jnp.float32)
    wv_grad = jnp.einsum("td,tf->df", normed_in, value_pre_grad, preferred_element_type=jnp.float32)
    in_back = jnp.einsum("tf,df->td", query_pre_grad, wq_all, preferred_element_type=jnp.float32)
    in_back = in_back + jnp.einsum(
        "tf,df->td", key_pre_grad, wk_all, preferred_element_type=jnp.float32
    )
    in_back = in_back + jnp.einsum(
        "tf,df->td", value_pre_grad, wv_all, preferred_element_type=jnp.float32
    )
    first_back, gain_one_grad = norm_back(
        resid_in, scale_one, gain_q1, partial_sums(in_back), model_width, tp_rank
    )
    input_grad = mid_grad + first_back
    dense = (
        lax.psum_scatter(
            gain_one_grad.astype(jnp.bfloat16), ("fsdp", "ctx"), scatter_dimension=0, tiled=True
        ).astype(jnp.float32),
        lax.psum_scatter(
            wq_grad.astype(jnp.bfloat16), ("fsdp", "ctx"), scatter_dimension=0, tiled=True
        ).astype(jnp.float32),
        lax.psum_scatter(
            wk_grad.astype(jnp.bfloat16), ("fsdp", "ctx"), scatter_dimension=0, tiled=True
        ).astype(jnp.float32),
        lax.psum_scatter(
            wv_grad.astype(jnp.bfloat16), ("fsdp", "ctx"), scatter_dimension=0, tiled=True
        ).astype(jnp.float32),
        lax.psum_scatter(
            gain_two_grad.astype(jnp.bfloat16), ("fsdp", "ctx"), scatter_dimension=0, tiled=True
        ).astype(jnp.float32),
        lax.psum_scatter(
            router_grad.astype(jnp.bfloat16), ("fsdp", "ctx"), scatter_dimension=0, tiled=True
        ).astype(jnp.float32),
        lax.psum_scatter(
            shared_gate_grad.astype(jnp.bfloat16), ("fsdp", "ctx"), scatter_dimension=0, tiled=True
        ).astype(jnp.float32),
        lax.psum_scatter(
            shared_up_grad.astype(jnp.bfloat16), ("fsdp", "ctx"), scatter_dimension=0, tiled=True
        ).astype(jnp.float32),
        lax.psum_scatter(
            wo_grad.astype(jnp.bfloat16), ("fsdp", "ctx"), scatter_dimension=1, tiled=True
        ).astype(jnp.float32),
        lax.psum_scatter(
            shared_down_grad.astype(jnp.bfloat16), ("fsdp", "ctx"), scatter_dimension=1, tiled=True
        ).astype(jnp.float32),
    )
    experts_done = (
        lax.psum_scatter(
            egate_grad.astype(jnp.bfloat16), "fsdp", scatter_dimension=1, tiled=True
        ).astype(jnp.float32),
        lax.psum_scatter(
            expert_up_weight_grad.astype(jnp.bfloat16), "fsdp", scatter_dimension=1, tiled=True
        ).astype(jnp.float32),
        lax.psum_scatter(
            edown_grad.astype(jnp.bfloat16), "fsdp", scatter_dimension=2, tiled=True
        ).astype(jnp.float32),
    )
    return (
        layer_out,
        input_grad,
        dense[0],
        dense[1],
        dense[2],
        dense[3],
        dense[8],
        dense[4],
        dense[5],
        dense[6],
        dense[7],
        dense[9],
        experts_done[0],
        experts_done[1],
        experts_done[2],
    )


MESH = pl.DeviceIdType.MESH
HBM = pl.BlockSpec(memory_space=pl.ANY)
VMEM = pl.BlockSpec(memory_space=pltpu.VMEM)
DMA = pltpu.SemaphoreType.DMA
BF, F32 = jnp.bfloat16, jnp.float32
BIG = 60 * 1024 * 1024


def dot_nt(left, right):
    return lax.dot_general(left, right, (((1,), (1,)), ((), ())), preferred_element_type=F32)


def dot_tn(left, right):
    return lax.dot_general(left, right, (((0,), (0,)), ((), ())), preferred_element_type=F32)


def dot_nn(left, right):
    return jnp.dot(left, right, preferred_element_type=F32)


def ranks():
    return lax.axis_index("fsdp"), lax.axis_index("ctx"), lax.axis_index("tp")


def sibling(t):
    return t + 1 - 2 * lax.rem(t, 2)


def opposite(t):
    return lax.rem(t + 2, 4)


def remote(src, dst, send, recv, to):
    return pltpu.make_async_remote_copy(
        src_ref=src, dst_ref=dst, send_sem=send, recv_sem=recv, device_id=to, device_id_type=MESH
    )


def greet(peers):
    barrier = pltpu.get_barrier_semaphore()
    for peer in peers:
        pl.semaphore_signal(barrier, inc=1, device_id=peer, device_id_type=MESH)
    pl.semaphore_wait(barrier, len(peers))


def line_peers(c, n_c):
    return [{"ctx": lax.rem(c + step, n_c)} for step in range(1, n_c)]


def piece(index, size):
    return pl.ds(pl.multiple_of(index * size, size), size)


def nearest(c, n_c, act):
    act(c)
    for step in range(1, n_c):
        for side in (-1, 1):
            place = c + side * step

            @pl.when((place >= 0) & (place < n_c))
            def _():
                act(place)


def spread_sems(n_c):
    return [
        DMA((n_c + 2,)),
        DMA((n_c,)),
        DMA((n_c,)),
        DMA((n_c,)),
        DMA((2 * n_c,)),
        DMA((2 * n_c,)),
        DMA((4 * n_c,)),
        DMA((4 * n_c,)),
        DMA(()),
    ]


class Spread:
    def __init__(self, own, place, n_c, both, sems):
        self.own, self.place, self.n_c, self.both = own, place, n_c, both
        self.zs, self.zr, self.xs, self.xr, self.ys, self.yr, self.ks, self.kr, self.ls = sems
        self.f, self.c, self.t = ranks()
        self.other_t = opposite(self.t)
        self.groups = ((self.f, 0), (1 - self.f, n_c))[: 2 if both else 1]

    def local(self):
        return pltpu.make_async_copy(self.own, self.place(self.f, self.c, self.t), self.ls)

    def far_copy(self, src, i, g, cc, col):
        return remote(src, self.place(g, cc, col), self.ys.at[i], self.yr.at[i], {"tp": self.other_t})

    def sib_copy(self, src, i, which, g, cc, col):
        at = 2 * i + which
        return remote(src, self.place(g, cc, col), self.ks.at[at], self.kr.at[at], {"tp": sibling(self.t)})

    def other_copy(self, src, g, cc):
        return remote(src, self.place(g, cc, self.t), self.xs.at[cc], self.xr.at[cc], {"fsdp": 1 - self.f})

    def line_copy(self, src, cc, sem, to):
        return remote(src, self.place(self.f, cc, self.t), self.zs.at[sem], self.zr.at[cc], {"ctx": to})

    def pass_on(self, src, i, g, cc):
        self.far_copy(src, i, g, cc, self.t).start()
        self.sib_copy(src, i, 0, g, cc, self.t).start()

    def start(self):
        self.local().start()
        n_c, c, own = self.n_c, self.c, self.own

        @pl.when(c < n_c - 1)
        def _():
            self.line_copy(own, c, n_c, c + 1).start()

        @pl.when(c > 0)
        def _():
            self.line_copy(own, c, n_c + 1, c - 1).start()

        if self.both:
            self.other_copy(own, self.f, c).start()
        self.pass_on(own, c, self.f, c)

    def each_other(self, act):
        for step in range(1, self.n_c):
            for side in (-1, 1):
                cc = self.c + side * step

                @pl.when((cc >= 0) & (cc < self.n_c))
                def _():
                    act(cc, self.c - side)

    def line(self):
        n_c = self.n_c

        def arrive(cc, onward):
            block = self.place(self.f, cc, self.t)
            self.line_copy(block, cc, cc, self.c).wait_recv()

            @pl.when((onward >= 0) & (onward < n_c))
            def _():
                self.line_copy(block, cc, cc, onward).start()

            if self.both:
                self.other_copy(block, self.f, cc).start()
            self.pass_on(block, cc, self.f, cc)

        self.each_other(arrive)

    def other(self):
        def arrive(cc):
            block = self.place(1 - self.f, cc, self.t)
            self.other_copy(block, 1 - self.f, cc).wait_recv()
            self.pass_on(block, self.n_c + cc, 1 - self.f, cc)

        nearest(self.c, self.n_c, arrive)

    def far(self, which):
        g, base = self.groups[which]

        def arrive(cc):
            i = base + cc
            block = self.place(g, cc, self.other_t)
            self.far_copy(block, i, g, cc, self.other_t).wait_recv()
            self.sib_copy(block, i, 1, g, cc, self.other_t).start()

        nearest(self.c, self.n_c, arrive)

    def arrived(self, which):
        g, base = self.groups[which]
        for cc in range(self.n_c):
            block = self.place(g, cc, self.t)
            for half in range(2):
                self.sib_copy(block, base + cc, half, g, cc, self.t).wait_recv()

    def finish(self):
        n_c, c, f, t, own = self.n_c, self.c, self.f, self.t, self.own
        for g, base in self.groups:
            for cc in range(n_c):
                block = self.place(g, cc, t)
                for half in range(2):
                    self.sib_copy(block, base + cc, half, g, cc, t).wait_send()
                self.far_copy(block, base + cc, g, cc, t).wait_send()
        if self.both:
            for cc in range(n_c):
                self.other_copy(self.place(f, cc, t), f, cc).wait_send()
        block = self.place(f, c, t)

        @pl.when(c < n_c - 1)
        def _():
            self.line_copy(block, c, n_c, c).wait_send()

        @pl.when(c > 0)
        def _():
            self.line_copy(block, c, n_c + 1, c).wait_send()

        def sent(cc, onward):
            @pl.when((onward >= 0) & (onward < n_c))
            def _():
                self.line_copy(block, cc, cc, c).wait_send()

        self.each_other(sent)


def to_each(src_of, dst, n_f, n_c, sems, act):
    send, recv, own = sems
    f, c, _ = ranks()
    here = f * n_c + c
    for df in range(n_f):
        for dc in range(n_c):
            i = df * n_c + dc
            if i == 0:
                copy = pltpu.make_async_copy(src_of(here), dst.at[here], own)
                copy.start() if act == "start" else copy.wait()
                continue
            to_f, to_c = lax.rem(f + df, n_f), lax.rem(c + dc, n_c)
            copy = remote(
                src_of(to_f * n_c + to_c), dst.at[here], send.at[i], recv.at[i], {"fsdp": to_f, "ctx": to_c}
            )
            copy.start() if act == "start" else copy.wait()


def each_peers(f, c, n_f, n_c):
    return [
        {"fsdp": lax.rem(f + df, n_f), "ctx": lax.rem(c + dc, n_c)}
        for df in range(n_f)
        for dc in range(n_c)
        if df or dc
    ]


def reduce_seq_scratch(n_c, rows, quarter):
    return [
        pltpu.VMEM((n_c, 2, rows, quarter), BF),
        pltpu.VMEM((n_c, 2, rows, quarter), BF),
        pltpu.VMEM((n_c, 2, rows, quarter), F32),
        pltpu.VMEM((n_c, rows, quarter), BF),
        pltpu.VMEM((n_c, rows, quarter), BF),
        pltpu.VMEM((n_c, rows, quarter), BF),
        pltpu.VMEM((n_c, rows, quarter), BF),
        DMA((n_c,)),
        DMA((n_c,)),
        DMA((n_c,)),
        DMA((n_c,)),
        DMA((n_c,)),
        DMA((n_c,)),
    ]


def reduce_seq(part_of, n_c, scratch, middle=None, before_last=None):
    out1, in1, own, out2, in2, out3, in3, s1, r1, s2, r2, s3, r3 = scratch
    f, c, t = ranks()
    far, sib = opposite(t), sibling(t)
    to_sib, to_far = {"tp": sib}, {"tp": far}
    order = [2, 1, 3, 0] if n_c == 4 else list(range(1, n_c)) + [0]
    for d in order:
        cc = lax.rem(c + d, n_c)
        out1[d, 0] = part_of(cc, sib).astype(BF)
        out1[d, 1] = part_of(cc, opposite(sib)).astype(BF)
        remote(out1.at[d], in1.at[d], s1.at[d], r1.at[d], to_sib).start()
        own[d, 0] = part_of(cc, t)
        own[d, 1] = part_of(cc, far)
    for d in order:
        remote(out1.at[d], in1.at[d], s1.at[d], r1.at[d], to_sib).wait()
        out2[d] = (own[d, 1] + in1[d, 1].astype(F32)).astype(BF)
        remote(out2.at[d], in2.at[d], s2.at[d], r2.at[d], to_far).start()
    if middle is not None:
        middle()
    for d in order:
        remote(out2.at[d], in2.at[d], s2.at[d], r2.at[d], to_far).wait()
        total = own[d, 0] + in1[d, 0].astype(F32) + in2[d].astype(F32)
        if d:
            out3[d] = total.astype(BF)
            cc = lax.rem(c + d, n_c)
            remote(out3.at[d], in3.at[d], s3.at[d], r3.at[d], {"ctx": cc}).start()
    if before_last is not None:
        before_last()
    for d in order[:-1]:
        remote(out3.at[d], in3.at[d], s3.at[d], r3.at[d], {"ctx": c}).wait()
        total = total + in3[d].astype(F32)
    return total


def first_kernel(
    n_c, n_f, n_exp, mine, hidden, wq, wk, wv, wo, og, gate_t, up_t, down, router_in, chosen, lines, sg, su, sd, angle,
    normed_out, q_out, k_out, v_out, hf_out, lse_out, r_out, cos_out, sin_out, resid_out,
    wqkv_out, wo_out, small_out, all_out, og_out, shared_out, gg_out, gu_out, gd_out,
    seq, wqkv, wo_all, small_all, hb, blk, own_og, small, shared, normed,
    ws, wr, ls, xs, xr, ss, sr, sl, es, er, os, *scratch,
):
    f, c, t = ranks()
    rows, quarter = blk.shape
    part = wo.shape[1]
    tokens, width = seq.shape
    n_s = len(spread_sems(n_c))
    named = lax.broadcasted_iota(jnp.int32, (n_exp, part), 0)
    mask = jnp.zeros((n_exp, part), F32)
    for k in range(chosen.shape[0]):
        mask = mask + jnp.where(chosen[k : k + 1, :] == named, 1.0, 0.0)
    small[:n_exp, :] = router_in[...]
    small[n_exp : 2 * n_exp, :] = mask.astype(BF)
    small[2 * n_exp :, :] = lines[...]
    n_b = n_f * n_c
    own_rows, srows = sg.shape[0] // n_b, shared.shape[1] // 3
    for i, src in enumerate((sg, su, sd)):
        for b in range(n_b):
            shared[b, i * srows : i * srows + own_rows, :] = src[b * own_rows : (b + 1) * own_rows, :]
            if srows > own_rows:
                shared[b, i * srows + own_rows : (i + 1) * srows, :] = jnp.zeros((srows - own_rows, part), BF)
    greet([{"tp": sibling(t)}, {"tp": opposite(t)}] + each_peers(f, c, n_f, n_c))
    seq_place = lambda g, cc, tt: seq.at[piece(cc, rows), piece(tt, quarter)]
    og_place = lambda g, cc, tt: og_out.at[g * n_c + cc, tt]
    all_place = lambda g, cc, tt: all_out.at[piece(g * n_c + cc, rows), piece(tt, quarter)]
    hid = Spread(hidden, seq_place, n_c, False, scratch[:n_s])
    grad = Spread(og, og_place, n_c, True, scratch[n_s : 2 * n_s])
    res = Spread(blk, all_place, n_c, True, scratch[2 * n_s : 3 * n_s])

    def targets(g, cc):
        block = piece(g * n_c + cc, part)
        return [wqkv.at[block, pl.ds(i * HD, HD)] for i in range(3)] + [
            wo_all.at[:, block],
            small_all.at[:, block],
        ]

    def sources(head):
        cols = piece(head, HD)
        return [wq.at[:, cols], wk.at[:, cols], wv.at[:, cols], wo.at[cols, :], small]

    def slabs(g, cc):
        block = piece(g * n_c + cc, part)
        return [wqkv.at[block, :], wo_all.at[:, block], small_all.at[:, block]]

    def across(step, g, cc):
        return [
            remote(slab, slab, xs.at[step, i], xr.at[step, i], {"fsdp": 1 - f})
            for i, slab in enumerate(slabs(g, cc))
        ]

    def swap(weight, out, k):
        return [
            remote(weight.at[(1 - f) * mine + e], out.at[e], es.at[k, e], er.at[k, e], {"fsdp": 1 - f})
            for e in range(mine)
        ]

    more = swap(down, gd_out, 2)
    for copy in more:
        copy.start()
    hid.start()
    def weights_out(step):
        to = lax.rem(c + step, n_c)
        for i, (src, dst) in enumerate(zip(sources(to), targets(f, c))):
            remote(src, dst, ws.at[step, i], wr.at[step, i], {"ctx": to}).start()

    def weights_on(step):
        cc = lax.rem(c - step + n_c, n_c)
        for i, dst in enumerate(targets(f, cc)):
            remote(dst, dst, ws.at[step, i], wr.at[step, i], {"ctx": cc}).wait_recv()
        for copy in across(step, f, cc):
            copy.start()

    steps = ([2, 1, 3] if n_c == 4 else list(range(1, n_c))) + [None]
    weights_out(steps[0])
    own = [
        pltpu.make_async_copy(src, dst, ls.at[i])
        for i, (src, dst) in enumerate(zip(sources(c), targets(f, c)))
    ]
    for copy in own:
        copy.start()
    for copy in own:
        copy.wait()
    for copy in across(0, f, c):
        copy.start()
    grad.start()
    hid.line()
    for step, following in zip(steps, steps[1:]):
        if following is not None:
            weights_out(following)
        weights_on(step)
    grad.line()
    swaps = swap(gate_t, gg_out, 0) + swap(up_t, gu_out, 1)
    for copy in swaps[: mine + 1]:
        copy.start()
    hid.far(0)
    hid.arrived(0)
    hid.local().wait()
    for step in range(n_c):
        for copy in across(step, 1 - f, lax.rem(c - step + n_c, n_c)):
            copy.wait_recv()
    outs = [
        pltpu.make_async_copy(src, dst, os.at[i])
        for i, (src, dst) in enumerate(((wqkv, wqkv_out), (wo_all, wo_out), (small_all, small_out)))
    ]
    for copy in outs:
        copy.start()

    exchange = lambda act: to_each(lambda b: shared.at[b], shared_out, n_f, n_c, (ss, sr, sl), act)
    exchange("start")

    scale_att = HD ** (-0.5)
    gain = small_all[2 * n_exp : 2 * n_exp + 1, :].astype(F32)
    place_row = 2 * n_exp + 2
    for start in range(0, tokens, rows):
        at = pl.ds(start, rows)
        h = seq[at, :].astype(F32)
        r = lax.rsqrt(jnp.sum(h * h, axis=1, keepdims=True) / width + EPS)
        n = (h * r * gain).astype(BF)
        normed[at, :] = n
        r_out[at, :] = jnp.broadcast_to(r, (rows, HD))
        cols = pl.ds(pl.multiple_of(f * tokens + start, rows), rows)
        pos = small_all[place_row : place_row + 2, cols].astype(F32)
        pos = pos[0:1] * 64.0 + pos[1:2]
        turn = jnp.broadcast_to(pos, (HD, rows)).T * angle[0:1, :]
        cos, sin = jnp.cos(turn), jnp.sin(turn) * angle[1:2, :]
        cos_out[at, :] = cos
        sin_out[at, :] = sin
        qkv = dot_nn(n, wqkv[...])

        def rotate(values):
            return (values * cos + pltpu.roll(values, HD // 2, 1) * sin).astype(BF)

        q_out[at, :] = rotate(qkv[:, :HD])
        k_out[at, :] = rotate(qkv[:, HD : 2 * HD])
        v_out[at, :] = qkv[:, 2 * HD :].astype(BF)
    outs.append(pltpu.make_async_copy(normed, normed_out, os.at[4]))
    outs[-1].start()
    for start in range(0, tokens, rows):
        at = pl.ds(start, rows)
        seen = start + rows
        s = dot_nt(q_out[at, :], k_out[:seen, :]) * scale_att
        row = lax.broadcasted_iota(jnp.int32, (rows, seen), 0) + start
        col = lax.broadcasted_iota(jnp.int32, (rows, seen), 1)
        s = jnp.where(col <= row, s, NEG_BIG)
        top = jnp.max(s, axis=1, keepdims=True)
        e = jnp.exp(s - top)
        total = jnp.sum(e, axis=1, keepdims=True)
        out = dot_nn((e * (1.0 / total)).astype(BF), v_out[:seen, :])
        hf_out[at, :] = out
        hb[at, :] = out.astype(BF)
        lse_out[at, :] = jnp.broadcast_to(top + jnp.log(total), (rows, HD))

    def part_of(cc, q):
        return dot_nn(hb[piece(cc, rows), :], wo_all[:, piece(q, quarter)])

    fetch = pltpu.make_async_copy(hidden, own_og, os.at[3])
    fetch.start()
    total = reduce_seq(part_of, n_c, scratch[3 * n_s :], grad.other)
    fetch.wait()
    resid = own_og[...].astype(F32) + total
    resid_out[...] = resid
    blk[...] = resid.astype(BF)
    res.start()
    res.line()
    for copy in swaps[mine + 1 :]:
        copy.start()
    grad.far(0)
    grad.far(1)
    res.other()
    res.far(0)
    res.far(1)
    for which in range(2):
        grad.arrived(which)
        res.arrived(which)
    exchange("wait")
    for copy in swaps + more:
        copy.wait()
    for step in range(1, n_c):
        for i, (src, dst) in enumerate(zip(sources(c), targets(f, c))):
            remote(src, dst, ws.at[step, i], wr.at[step, i], {"ctx": c}).wait_send()
    for step in range(n_c):
        for copy in across(step, f, lax.rem(c - step + n_c, n_c)):
            copy.wait_send()
    for item in (hid, grad, res):
        item.finish()
    grad.local().wait()
    res.local().wait()
    for copy in outs:
        copy.wait()


def first(n_c, n_f, n_t, mine, srows, hidden, wq, wk, wv, wo, og, weights, router, chosen, lines, shared, angle):
    rows, quarter = hidden.shape
    width = quarter * n_t
    seq = rows * n_c
    n_exp = mine * n_f * n_c
    ffe, half = weights[0].shape[1:]
    sds = jax.ShapeDtypeStruct
    part = wo.shape[1]
    n_small = 2 * n_exp + lines.shape[0]
    head, head_f = sds((seq, HD), BF), sds((seq, HD), F32)
    got = sds((mine, ffe, half), BF)
    return pl.pallas_call(
        functools.partial(first_kernel, n_c, n_f, n_exp, mine),
        out_shape=(
            sds((seq, width), BF),
            head,
            head,
            head,
            head_f,
            head_f,
            head_f,
            head_f,
            head_f,
            sds((rows, quarter), F32),
            sds((width, 3 * HD), BF),
            sds((HD, width), BF),
            sds((n_small, width), BF),
            sds((seq * n_f, width), BF),
            sds((n_f * n_c, n_t, rows, quarter), BF),
            sds((n_f * n_c, 3 * srows, part), BF),
            got,
            got,
            got,
        ),
        in_specs=[HBM] * 9 + [VMEM] * 7,
        out_specs=[HBM] + [VMEM] * 9 + [HBM] * 9,
        scratch_shapes=[
            pltpu.VMEM((seq, width), BF),
            pltpu.VMEM((width, 3 * HD), BF),
            pltpu.VMEM((HD, width), BF),
            pltpu.VMEM((n_small, width), BF),
            pltpu.VMEM((seq, HD), BF),
            pltpu.VMEM((rows, quarter), BF),
            pltpu.VMEM((rows, quarter), BF),
            pltpu.VMEM((n_small, part), BF),
            pltpu.VMEM((n_f * n_c, 3 * srows, part), BF),
            pltpu.VMEM((seq, width), BF),
            DMA((n_c, 5)),
            DMA((n_c, 5)),
            DMA((5,)),
            DMA((n_c, 3)),
            DMA((n_c, 3)),
            DMA((n_f * n_c,)),
            DMA((n_f * n_c,)),
            DMA(()),
            DMA((3, mine)),
            DMA((3, mine)),
            DMA((5,)),
        ]
        + spread_sems(n_c) * 3
        + reduce_seq_scratch(n_c, rows, quarter),
        compiler_params=pltpu.CompilerParams(
            collective_id=1, has_side_effects=True, vmem_limit_bytes=BIG
        ),
        cost_estimate=pl.CostEstimate(
            flops=5 << 30, bytes_accessed=300 << 20, transcendentals=1 << 20
        ),
        name="first",
    )(hidden, wq, wk, wv, wo, og, *weights, router, chosen, lines, *shared, angle)


def fetch_experts(n_c, n_f, mine, ffe, srows, hp, weights, shared, wgu, wd, sems):
    f = lax.axis_index("fsdp")
    wg0, wu0, wd0, wg1, wu1, wd1 = weights
    width = wd.shape[1]
    used = mine * ffe
    part = width // (n_f * n_c)
    half = width // n_f
    copies = []

    def add(src, dst):
        copies.append(pltpu.make_async_copy(src, dst, sems.at[len(copies)]))

    groups = []
    for i, (kept, got) in enumerate(((wg0, wg1), (wu0, wu1), (wd0, wd1))):
        dst, base = ((wgu, 0), (wgu, hp), (wd, 0))[i]
        for e in range(mine):
            at = pl.ds(base + e * ffe, ffe)
            add(kept.at[f * mine + e], dst.at[at, piece(f, half)])
            add(got.at[e], dst.at[at, piece(1 - f, half)])
        for b in range(n_f * n_c):
            add(
                shared.at[b, pl.ds(i * srows, srows), :],
                dst.at[pl.ds(base + used, srows), pl.ds(b * part, part)],
            )
        groups.append(copies[sum(map(len, groups)) :])
    return groups[0] + groups[1], groups[2]


def blank_rows(rows_used, hp, wgu, wd):
    blank = jnp.zeros((hp - rows_used, wd.shape[1]), BF)
    wgu[rows_used:hp, :] = blank
    wgu[hp + rows_used :, :] = blank
    wd[rows_used:, :] = blank


def gates(prob, picked, first, mine, ffe, hp):
    block, n_exp = prob.shape
    lane = lax.broadcasted_iota(jnp.int32, (block, n_exp), 1)
    gated = prob * picked
    col = lax.broadcasted_iota(jnp.int32, (block, hp), 1)
    gate = jnp.ones((block, hp), F32)
    for k in reversed(range(mine)):
        g = jnp.sum(jnp.where(lane == first + k, gated, 0.0), axis=1, keepdims=True)
        gate = jnp.where(col < (k + 1) * ffe, g, gate)
    return gate, lane, col


def reducer_scratch(n_f, n_c, rows, quarter, split):
    n_b = n_f * n_c
    upper = rows // 2 if split else rows
    lower = rows // 2 if split else 16
    blocks = lambda *lead: pltpu.VMEM(lead + (rows, quarter), BF)
    return [
        blocks(n_b, 2),
        blocks(n_b, 2),
        blocks(n_b, 2),
        blocks(n_b),
        blocks(n_b),
        pltpu.VMEM((n_c, upper, quarter), BF),
        pltpu.VMEM((n_c, upper, quarter), BF),
        pltpu.VMEM((n_c, rows, quarter), F32),
        blocks(n_c),
        blocks(n_c),
        pltpu.VMEM((n_c, 2, lower, quarter), BF),
        pltpu.VMEM((n_c, 2, lower, quarter), BF),
    ] + [DMA((n_b,))] * 4 + [DMA((n_c,))] * 6


N_REDUCER = 22


def when(condition, act):
    if isinstance(condition, bool):
        if condition:
            act()
    else:
        pl.when(condition)(act)


class Reducer:
    def __init__(self, n_c, scratch):
        self.n_c = n_c
        (self.out1, self.in1, self.own, self.out2, self.in2, self.out3, self.in3, self.acc,
         self.out4, self.in4, self.out5, self.in5, self.s1, self.r1, self.s2, self.r2, self.s3, self.r3,
         self.s4, self.r4, self.s5, self.r5) = scratch
        self.half = self.out3.shape[1]
        self.split = self.half < self.out4.shape[1]
        self.f, self.c, self.t = ranks()
        self.far, self.sib = opposite(self.t), sibling(self.t)

    def row_block(self, i):
        n_c = self.n_c
        group = jnp.where(i < n_c, 1 - self.f, self.f)
        return group * n_c + lax.rem(self.c + lax.rem(i, n_c) + 1, n_c)

    def core_copy(self, i):
        return remote(self.out1.at[i], self.in1.at[i], self.s1.at[i], self.r1.at[i], {"tp": self.sib})

    def far_copy(self, i, upper=False):
        src, dst = self.out2.at[i], self.in2.at[i]
        if upper:
            src, dst = src.at[pl.ds(0, self.half)], dst.at[pl.ds(0, self.half)]
        return remote(src, dst, self.s2.at[i], self.r2.at[i], {"tp": self.far})

    def other_copy(self, j):
        return remote(self.out3.at[j], self.in3.at[j], self.s3.at[j], self.r3.at[j], {"fsdp": 1 - self.f})

    def lower_copy(self, j):
        return remote(self.out5.at[j], self.in5.at[j], self.s5.at[j], self.r5.at[j], {"fsdp": 1 - self.f})

    def line_copy(self, j, to):
        return remote(self.out4.at[j], self.in4.at[j], self.s4.at[j], self.r4.at[j], {"ctx": to})

    def put(self, i, part_of):
        self.out1[i, 0] = part_of(opposite(self.sib)).astype(BF)
        self.out1[i, 1] = part_of(self.sib).astype(BF)
        self.core_copy(i).start()
        self.own[i, 0] = part_of(self.far).astype(BF)
        self.own[i, 1] = part_of(self.t).astype(BF)

    def core_sum(self, i, which):
        return self.own[i, which].astype(F32) + self.in1[i, which].astype(F32)

    def over(self, i):
        self.core_copy(i).wait()
        half, n_c = self.half, self.n_c

        def of_other():
            far = self.core_sum(i, 0)
            if self.split:
                self.out5[i, 0] = far[half:].astype(BF)
                self.out5[i, 1] = self.core_sum(i, 1)[half:].astype(BF)
                self.lower_copy(i).start()
            self.out2[i, :half] = far[:half].astype(BF)
            self.far_copy(i, True).start()

        def of_own():
            j = i - n_c
            if self.split:
                self.lower_copy(j).wait_recv()
            far = self.core_sum(i, 0)
            self.out2[i, :half] = far[:half].astype(BF)
            if self.split:
                self.out2[i, half:] = (far[half:] + self.in5[j, 0].astype(F32)).astype(BF)
            self.far_copy(i).start()

        when(i < n_c, of_other)
        when(i >= n_c, of_own)

    def after_other(self, i):
        half = self.half
        self.far_copy(i, True).wait()
        self.out3[i] = (self.core_sum(i, 1)[:half] + self.in2[i, :half].astype(F32)).astype(BF)
        self.other_copy(i).start()

    def after_own(self, i):
        j, half = i - self.n_c, self.half
        self.far_copy(i).wait()
        total = self.core_sum(i, 1) + self.in2[i].astype(F32)
        self.acc[j, :half] = total[:half]
        if self.split:
            self.acc[j, half:] = total[half:] + self.in5[j, 1].astype(F32)

    def along(self, j):
        half = self.half
        if self.split:
            self.lower_copy(j).wait_send()
        self.other_copy(j).wait()
        self.acc[j, :half] = self.acc[j, :half] + self.in3[j].astype(F32)
        total = self.acc[j]
        if j < self.n_c - 1:
            self.out4[j] = total.astype(BF)
            self.line_copy(j, lax.rem(self.c + j + 1, self.n_c)).start()
        return total

    def total(self, total):
        for j in range(self.n_c - 1):
            self.line_copy(j, self.c).wait()
            total = total + self.in4[j].astype(F32)
        return total

    def loop(self, n_b, lag, compute):
        n_c = self.n_c
        assert lag >= n_b - n_c

        def step(i, carry):
            def between():
                @pl.when(i >= 1)
                def _():
                    self.over(i - 1)

                @pl.when((i >= lag) & (i < lag + n_c))
                def _():
                    self.after_other(i - lag)

            compute(i, between)
            return carry

        lax.fori_loop(0, n_b, step, 0)

    def drain(self, n_b, lag, works):
        works = list(works)
        self.over(n_b - 1)
        for i in range(n_b - lag, n_b):
            if i < self.n_c:
                self.after_other(i)
                continue
            self.after_own(i)
            total = self.along(i - self.n_c)
            if works:
                works.pop(0)()
        for work in works:
            work()
        return self.total(total)


def forward_kernel(
    n_c, n_f, mine, ffe, srows, hp, rows_all, og_all, resid, small,
    wg0, wu0, wd0, wg1, wu1, wd1, shared,
    layer_out, in_out, act_out, silu_out, slope_out, r_out, prob_out, keep_out, send_out, shared_out,
    gt, wsem, xsem, nsem, asem, tsem, osem, *scratch,
):
    f, c, t = ranks()
    n_b = n_f * n_c
    rows, quarter = resid.shape
    width = rows_all.shape[1]
    routed = mine * ffe
    rows_used = routed + srows
    n_exp = mine * n_b
    red = Reducer(n_c, scratch)

    def blocks_phase(wgu, wd, xs, ns, acts):
        gate_up, down = fetch_experts(
            n_c, n_f, mine, ffe, srows, hp, (wg0, wu0, wd0, wg1, wu1, wd1), shared, wgu, wd, wsem
        )
        for copy in gate_up + down:
            copy.start()

        def load(i, slot):
            return pltpu.make_async_copy(
                rows_all.at[piece(red.row_block(i), rows), :], xs.at[slot], xsem.at[slot]
            )

        def stores(i, slot):
            at = piece(red.row_block(i), rows)
            return [pltpu.make_async_copy(ns.at[slot], in_out.at[at, :], nsem.at[slot])] + [
                pltpu.make_async_copy(acts.at[slot, k], out.at[at, :], asem.at[slot, k])
                for k, out in enumerate((act_out, silu_out, slope_out))
            ]

        load(0, 0).start()
        blank_rows(rows_used, hp, wgu, wd)
        greet([{"tp": red.sib}, {"tp": red.far}, {"fsdp": 1 - f}] + line_peers(c, n_c))
        for copy in gate_up:
            copy.wait()

        def compute(i, between):
            slot = lax.rem(i, 2)
            b = red.row_block(i)
            at = piece(b, rows)
            load(i, slot).wait()

            @pl.when(i + 1 < n_b)
            def _():
                load(i + 1, 1 - slot).start()

            @pl.when(i >= 2)
            def _():
                for copy in stores(i - 2, slot):
                    copy.wait()

            h = xs[slot].astype(F32)
            r = lax.rsqrt(jnp.sum(h * h, axis=1, keepdims=True) / width + EPS)
            r_out[at, :] = jnp.broadcast_to(r, (rows, HD))
            gain = small[2 * n_exp + 1 : 2 * n_exp + 2, :].astype(F32)
            n = (h * r * gain).astype(BF)
            ns[slot] = n
            logits = dot_nt(n, small[:n_exp, :])
            e = jnp.exp(logits - jnp.max(logits, axis=1, keepdims=True))
            prob = e / jnp.sum(e, axis=1, keepdims=True)
            prob_out[at, :] = prob
            gate, _, _ = gates(prob, small[n_exp : 2 * n_exp, at].astype(F32).T, (c * n_f + f) * mine, mine, ffe, hp)
            ab = dot_nt(n, wgu[...])
            between()
            a, up = ab[:, :hp], ab[:, hp:]
            sig = 0.5 * jnp.tanh(0.5 * a) + 0.5
            silu = a * sig
            act = (silu * up).astype(BF)
            acts[slot, 0] = act
            acts[slot, 1] = silu.astype(BF)
            acts[slot, 2] = (up * (sig * (1.0 + a * (1.0 - sig)))).astype(BF)
            actg = (act.astype(F32) * gate).astype(BF)
            gt[:, at] = actg.T[:rows_used, :]
            for copy in stores(i, slot):
                copy.start()

            @pl.when(i == 0)
            def _():
                for copy in down:
                    copy.wait()

            red.put(i, lambda q: dot_nn(actg, wd[:, piece(q, quarter)]))

        red.loop(n_b, n_c, compute)
        for i in range(n_b - 2, n_b):
            for copy in stores(i, i % 2):
                copy.wait()

    pl.run_scoped(
        blocks_phase,
        pltpu.VMEM((2 * hp, width), BF),
        pltpu.VMEM((hp, width), BF),
        pltpu.VMEM((2, rows, width), BF),
        pltpu.VMEM((2, rows, width), BF),
        pltpu.VMEM((2, 3, rows, hp), BF),
    )

    def grads_phase(tiles, keeps, sends, shs):
        def tile_of(s):
            return (1 - f) * 2 + s if s < 2 else f * 2 + s - 2

        def tile_load(s):
            return pltpu.make_async_copy(og_all.at[:, tile_of(s)], tiles.at[s % 2], tsem.at[s % 2])

        def out_copies(s):
            cols = pl.ds(s % 2 * quarter, quarter)
            if s < 2:
                src, dst = sends.at[s], send_out.at[:, :, cols]
            else:
                src, dst = keeps.at[s - 2], keep_out.at[:, :, cols]
            return [
                pltpu.make_async_copy(src, dst, osem.at[s, 0]),
                pltpu.make_async_copy(
                    shs.at[s], shared_out.at[:, piece(tile_of(s), quarter)], osem.at[s, 1]
                ),
            ]

        def work(s):
            def run():
                tile_load(s).wait()
                if s < 3:
                    tile_load(s + 1).start()
                g = dot_nn(gt[...], tiles[s % 2].reshape(n_b * rows, quarter))
                if s < 2:
                    sends[s] = g[:routed].astype(BF).reshape(mine, ffe, quarter)
                else:
                    keeps[s - 2] = g[:routed].astype(BF).reshape(mine, ffe, quarter)
                shs[s] = g[routed:].astype(BF)
                for copy in out_copies(s):
                    copy.start()

            return run

        tile_load(0).start()
        total = red.drain(n_b, n_c, [work(s) for s in range(4)])
        layer_out[...] = (resid[...] + total).astype(BF)
        for s in range(4):
            for copy in out_copies(s):
                copy.wait()

    pl.run_scoped(
        grads_phase,
        pltpu.VMEM((2, n_b, rows, quarter), BF),
        pltpu.VMEM((2, mine, ffe, quarter), BF),
        pltpu.VMEM((2, mine, ffe, quarter), BF),
        pltpu.VMEM((4, srows, quarter), BF),
    )


def expert_sizes(n_c, n_f, n_t, mine, ffe, srows, width):
    used = mine * ffe + srows
    return used, -(-used // HD) * HD, 3 * (2 * mine + n_f * n_c)


def forward(n_c, n_f, n_t, mine, ffe, srows, rows_all, og_all, resid, small, kept, got, shared):
    total, width = rows_all.shape
    rows, quarter = resid.shape
    n_b = n_f * n_c
    n_exp = mine * n_b
    used, hp, n_fetch = expert_sizes(n_c, n_f, n_t, mine, ffe, srows, width)
    sds = jax.ShapeDtypeStruct
    return pl.pallas_call(
        functools.partial(forward_kernel, n_c, n_f, mine, ffe, srows, hp),
        out_shape=(
            sds((rows, quarter), BF),
            sds((total, width), BF),
            sds((total, hp), BF),
            sds((total, hp), BF),
            sds((total, hp), BF),
            sds((total, HD), F32),
            sds((total, n_exp), F32),
            sds((mine, ffe, width // n_f), BF),
            sds((mine, ffe, width // n_f), BF),
            sds((srows, width), BF),
        ),
        in_specs=[HBM, HBM, VMEM, VMEM] + [HBM] * 7,
        out_specs=[VMEM, HBM, HBM, HBM, HBM, VMEM, VMEM, HBM, HBM, HBM],
        scratch_shapes=[
            pltpu.VMEM((used, total), BF),
            DMA((n_fetch,)),
            DMA((2,)),
            DMA((2,)),
            DMA((2, 3)),
            DMA((2,)),
            DMA((4, 2)),
        ]
        + reducer_scratch(n_f, n_c, rows, quarter, True),
        compiler_params=pltpu.CompilerParams(
            collective_id=5, has_side_effects=True, vmem_limit_bytes=BIG
        ),
        cost_estimate=pl.CostEstimate(
            flops=8 * total * width * used, bytes_accessed=80 << 20, transcendentals=total * used
        ),
        name="forward",
    )(rows_all, og_all, resid, small, *kept, *got, shared)


def backward_kernel(
    n_c, n_f, mine, ffe, srows, hp, og_all, act, silu, slope, moe_in, r_all, shared_d, prob_in, small,
    resid, og, wg0, wu0, wd0, wg1, wu1, wd1, shared,
    mid_out, gain_out, seq_out, shared_out, shs_out, kg_out, ku_out, gg_out, gu_out, lg_out, lu_out,
    gt, blk, r_own, sends, shs, wsem, xsem, tsem, ksem, ss, sr, rs, es, ds, dr, dl, *rest,
):
    f, c, t = ranks()
    n_b = n_f * n_c
    rows, quarter = resid.shape
    width = shared_d.shape[1]
    n_exp = mine * n_b
    routed = mine * ffe
    rows_used = routed + srows
    first = (c * n_f + f) * mine
    reduce_scratch, rest = rest[:N_REDUCER], rest[N_REDUCER:]
    red = Reducer(n_c, reduce_scratch)

    cols = width // n_b

    def exchange(act):
        to_each(lambda b: shared_d.at[:, piece(b, cols)], shared_out, n_f, n_c, (ds, dr, dl), act)

    def blocks_phase(wgu, wd, ogs, acts):
        gate_up, down = fetch_experts(
            n_c, n_f, mine, ffe, srows, hp, (wg0, wu0, wd0, wg1, wu1, wd1), shared, wgu, wd, wsem
        )
        for copy in down + gate_up:
            copy.start()

        def loads(i, slot):
            b = red.row_block(i)
            return [
                pltpu.make_async_copy(
                    og_all.at[b, q], ogs.at[slot, :, pl.ds(q * quarter, quarter)], xsem.at[slot, q]
                )
                for q in range(4)
            ] + [
                pltpu.make_async_copy(src.at[piece(b, rows), :], acts.at[slot, k], xsem.at[slot, 4 + k])
                for k, src in enumerate((act, silu, slope))
            ]

        for copy in loads(0, 0):
            copy.start()
        blank_rows(rows_used, hp, wgu, wd)
        greet([{"tp": red.sib}, {"tp": red.far}, {"tp": opposite(red.sib)}] + each_peers(f, c, n_f, n_c))
        exchange("start")
        for copy in down:
            copy.wait()

        def compute(i, between):
            slot = lax.rem(i, 2)
            at = piece(red.row_block(i), rows)
            for copy in loads(i, slot):
                copy.wait()

            @pl.when(i + 1 < n_b)
            def _():
                for copy in loads(i + 1, 1 - slot):
                    copy.start()

            prob = prob_in[at, :]
            chosen = small[n_exp : 2 * n_exp, at].astype(F32).T
            gate, lane, col = gates(prob, chosen, first, mine, ffe, hp)
            dh = dot_nt(ogs[slot], wd[...])
            between()
            ad = acts[slot, 0].astype(F32) * dh
            p_grad = jnp.zeros(prob.shape, F32)
            for k in reversed(range(mine)):
                below = jnp.where(col < k * ffe, ad, 0.0) if k else jnp.zeros_like(ad)
                ad = jnp.where(col < (k + 1) * ffe, ad, 0.0)
                s = jnp.sum(ad - below, axis=1, keepdims=True)
                p_grad = jnp.where(lane == first + k, s, p_grad)
                ad = below
            p_grad = p_grad * chosen
            logit_f = prob * (p_grad - jnp.sum(prob * p_grad, axis=1, keepdims=True))
            logit_grad = logit_f.astype(BF)
            dg = dh * gate
            da = (dg * acts[slot, 2].astype(F32)).astype(BF)
            db = (dg * acts[slot, 1].astype(F32)).astype(BF)
            gt[:rows_used, at] = da.T[:rows_used, :]
            gt[rows_used : 2 * rows_used, at] = db.T[:rows_used, :]
            gt[2 * rows_used :, at] = logit_f.T.astype(BF)
            dab = jnp.concatenate([da, db], axis=1)

            @pl.when(i == 0)
            def _():
                for copy in gate_up:
                    copy.wait()

            def part_of(q):
                cols = piece(q, quarter)
                return dot_nn(dab, wgu[:, cols]) + dot_nn(logit_grad, small[:n_exp, cols])

            red.put(i, part_of)

        red.loop(n_b, n_c + 1, compute)

    pl.run_scoped(
        blocks_phase,
        pltpu.VMEM((2 * hp, width), BF),
        pltpu.VMEM((hp, width), BF),
        pltpu.VMEM((2, rows, width), BF),
        pltpu.VMEM((2, 3, rows, hp), BF),
    )

    def send_copy(s, m):
        if s:
            return pltpu.make_async_copy(sends.at[s, m], (lg_out, lu_out)[m], ss.at[s, m])
        return remote(sends.at[s, m], (gg_out, gu_out)[m], ss.at[s, m], sr.at[m], {"fsdp": 1 - f})

    def grads_phase(tiles, keeps):
        def tile_of(s):
            return (1 - f) * 2 + s if s < 2 else f * 2 + s - 2

        def tile_load(s):
            return pltpu.make_async_copy(
                moe_in.at[:, piece(tile_of(s), quarter)], tiles.at[s % 2], tsem.at[s % 2]
            )

        def keep_copy(s, m):
            dst = (kg_out, ku_out)[m].at[:, :, pl.ds((s - 2) * quarter, quarter)]
            return pltpu.make_async_copy(keeps.at[s - 2, m], dst, ksem.at[s - 2, m])

        def work(s):
            def run():
                tile_load(s).wait()
                if s < 3:
                    tile_load(s + 1).start()
                g = dot_nn(gt[...], tiles[s % 2])
                cols = piece(tile_of(s), quarter)
                for m in range(2):
                    base = m * rows_used
                    if s < 2:
                        sends[s, m] = g[base : base + routed].astype(BF).reshape(mine, ffe, quarter)
                        send_copy(s, m).start()
                    else:
                        keeps[s - 2, m] = g[base : base + routed].astype(BF).reshape(mine, ffe, quarter)
                        keep_copy(s, m).start()
                    shs[m * srows : (m + 1) * srows, cols] = g[base + routed : base + rows_used].astype(BF)
                shs[2 * srows :, cols] = g[2 * rows_used :].astype(BF)

            return run

        tile_load(0).start()
        blk[...] = red.drain(n_b, n_c + 1, [work(s) for s in range(4)])
        for s in (2, 3):
            for m in range(2):
                keep_copy(s, m).wait()

    fetch = pltpu.make_async_copy(r_all.at[piece(f * n_c + c, rows), :], r_own, rs)
    fetch.start()
    pl.run_scoped(
        grads_phase,
        pltpu.VMEM((2, n_b * rows, quarter), BF),
        pltpu.VMEM((2, 2, mine, ffe, quarter), BF),
    )
    shs_copy = pltpu.make_async_copy(shs, shs_out, es)
    shs_copy.start()
    fetch.wait()
    gain = small[2 * n_exp + 1 : 2 * n_exp + 2, piece(t, quarter)].astype(F32)
    back, gain_part = norm_grad(resid[...], r_own[:, :1], gain, blk[...], width, *rest[:4])
    gain_out[...] = jnp.broadcast_to(gain_part, gain_out.shape)
    grad = og[...].astype(F32) + back
    mid_out[...] = grad
    own = rest[4]
    own[...] = grad.astype(BF)

    def place(g, cc, tt):
        return seq_out.at[piece(cc, rows), piece(tt, quarter)]

    sequence = Spread(own, place, n_c, False, rest[5:])
    sequence.start()
    sequence.line()
    sequence.far(0)
    sequence.arrived(0)
    sequence.finish()
    sequence.local().wait()
    exchange("wait")
    shs_copy.wait()
    for s in range(2):
        for m in range(2):
            send_copy(s, m).wait()


def backward(
    n_c, n_f, n_t, mine, ffe, srows, og_all, act, silu, slope, moe_in, r_all, shared_d, prob, small,
    resid, og, kept, got, shared,
):
    total, width = moe_in.shape
    rows, quarter = resid.shape
    n_b = n_f * n_c
    n_exp = mine * n_b
    used, hp, n_fetch = expert_sizes(n_c, n_f, n_t, mine, ffe, srows, width)
    sds = jax.ShapeDtypeStruct
    kept_g = sds((mine, ffe, width // n_f), BF)
    sent_g = sds((mine, ffe, quarter), BF)
    return pl.pallas_call(
        functools.partial(backward_kernel, n_c, n_f, mine, ffe, srows, hp),
        out_shape=(
            sds((rows, quarter), F32),
            sds((8, quarter), F32),
            sds((rows * n_c, width), BF),
            sds((n_b, srows, width // n_b), BF),
            sds((2 * srows + n_exp, width), BF),
            kept_g,
            kept_g,
            sent_g,
            sent_g,
            sent_g,
            sent_g,
        ),
        in_specs=[HBM] * 7 + [VMEM] * 4 + [HBM] * 7,
        out_specs=[VMEM, VMEM] + [HBM] * 9,
        scratch_shapes=[
            pltpu.VMEM((2 * used + n_exp, total), BF),
            pltpu.VMEM((rows, quarter), F32),
            pltpu.VMEM((rows, HD), F32),
            pltpu.VMEM((2, 2, mine, ffe, quarter), BF),
            pltpu.VMEM((2 * srows + n_exp, width), BF),
            DMA((n_fetch,)),
            DMA((2, 7)),
            DMA((2,)),
            DMA((2, 2)),
            DMA((2, 2)),
            DMA((2,)),
            DMA(()),
            DMA(()),
            DMA((n_b,)),
            DMA((n_b,)),
            DMA(()),
        ]
        + reducer_scratch(n_f, n_c, rows, quarter, False)
        + norm_grad_scratch(rows)
        + [pltpu.VMEM((rows, quarter), BF)]
        + spread_sems(n_c),
        compiler_params=pltpu.CompilerParams(
            collective_id=3, has_side_effects=True, vmem_limit_bytes=BIG
        ),
        cost_estimate=pl.CostEstimate(
            flops=10 * total * width * used, bytes_accessed=200 << 20, transcendentals=0
        ),
        name="backward",
    )(
        og_all, act, silu, slope, moe_in, r_all, shared_d, prob, small, resid, og,
        *kept, *got, shared,
    )


def finish_kernel(n_plain, f_ref, *refs):
    ga, gb, ua, ub, d, kg, ku, kd, shared = refs[:9]
    plain, gains, refs = refs[9 : 9 + n_plain], refs[9 + n_plain], refs[:9] + refs[10:]
    og, ou, od, shared_out = refs[9 + n_plain : 13 + n_plain]
    step = pl.program_id(0)
    f = f_ref[0]
    n_e = kg.shape[0]

    def put(at):
        for keep, out in ((kg, og), (ku, ou), (kd, od)):
            out[at : at + n_e] = keep[...].astype(F32)
        for out, halves in ((og, (ga, gb)), (ou, (ua, ub))):
            @pl.when(step < 2)
            def _():
                out[n_e - at : 2 * n_e - at] = halves[0][...].astype(F32)

            @pl.when(step >= 2)
            def _():
                out[n_e - at : 2 * n_e - at] = halves[1][...].astype(F32)

        od[n_e - at : 2 * n_e - at] = d[...].astype(F32)

    @pl.when(f == 0)
    def _():
        put(0)

    @pl.when(f != 0)
    def _():
        put(n_e)

    own = shared_out.shape[0] // shared.shape[0]
    for b in range(shared.shape[0]):
        shared_out[b * own : (b + 1) * own, :] = shared[b, :own, :].astype(F32)
    for src, dst in zip(plain, refs[13 + n_plain :]):
        dst[...] = src[...]
    for i, dst in enumerate(refs[13 + 2 * n_plain :]):
        dst[...] = gains[i : i + 1, :]


def finish(f_rank, own_shared, arrived, kept, shared, plain, gains):
    mine, ffe, quarter = arrived[0].shape
    half = kept[0].shape[2]
    tile = half // 4
    n_b, srows, part = shared.shape
    first = pl.BlockSpec((mine, ffe, tile), lambda i, f: (0, 0, jnp.minimum(i, 1)))
    second = pl.BlockSpec((mine, ffe, tile), lambda i, f: (0, 0, jnp.maximum(i - 2, 0)))
    every = pl.BlockSpec((mine, ffe, tile), lambda i, f: (0, 0, i))
    out = pl.BlockSpec((2 * mine, ffe, tile), lambda i, f: (0, 0, i))

    def rows_of(x):
        if x.shape[0] % 64:
            return pl.BlockSpec(x.shape, lambda i, f: (0, 0))
        return pl.BlockSpec((x.shape[0] // 4, x.shape[1]), lambda i, f: (i, 0))

    shared_grad = jax.ShapeDtypeStruct((n_b * own_shared, part), F32)
    return pl.pallas_call(
        functools.partial(finish_kernel, len(plain)),
        grid_spec=pltpu.PrefetchScalarGridSpec(
            num_scalar_prefetch=1,
            grid=(4,),
            in_specs=[first, second, first, second, every]
            + [every] * 3
            + [pl.BlockSpec((n_b // 4, srows, part), lambda i, f: (i, 0, 0))]
            + [rows_of(x) for x in plain]
            + [rows_of(gains)],
            out_specs=[out] * 3
            + [rows_of(shared_grad)]
            + [rows_of(x) for x in plain]
            + [pl.BlockSpec((1, part), lambda i, f: (0, 0))] * 2,
        ),
        out_shape=tuple(jax.ShapeDtypeStruct((2 * mine, ffe, half), F32) for k in kept)
        + (shared_grad,)
        + tuple(jax.ShapeDtypeStruct(x.shape, x.dtype) for x in plain)
        + (jax.ShapeDtypeStruct((1, part), F32),) * 2,
        compiler_params=pltpu.CompilerParams(vmem_limit_bytes=BIG),
        name="finish",
    )(f_rank, *arrived, *kept, shared, *plain, gains)


def norm_grad(values, r, gain, grad, width, out, into, send, recv):
    f, c, t = ranks()
    rows = values.shape[0]
    local = jnp.sum(grad * gain * values, axis=1, keepdims=True)
    out[...] = jnp.broadcast_to(local, (rows, HD)).T[:8, :]
    peers = [sibling(t), opposite(t), opposite(sibling(t))]
    copies = [
        remote(out, into.at[i], send.at[i], recv.at[i], {"tp": peer}) for i, peer in enumerate(peers)
    ]
    for copy in copies:
        copy.start()
    gain_part = jnp.sum(grad * values * r, axis=0, keepdims=True)
    total = out[...]
    for i, copy in enumerate(copies):
        copy.wait()
        total = total + into[i]
    total = jnp.broadcast_to(total[0:1, :], (HD, rows)).T[:, :1]
    return r * gain * grad - values * (r * r * r * (total / width)), gain_part


def norm_grad_scratch(rows):
    return [
        pltpu.VMEM((8, rows), F32),
        pltpu.VMEM((3, 8, rows), F32),
        DMA((3,)),
        DMA((3,)),
    ]


def attend_back(block, mid, wo, q, k, v, hf, lse, cosine, sine, dqkv, hg, dq, dk, dv):
    seq = mid.shape[0]
    scale_att = HD ** (-0.5)
    for start in range(0, seq, block):
        at = pl.ds(start, block)
        hg[at, :] = dot_nt(mid[at, :], wo[...]).astype(BF)
    dk[...] = jnp.zeros_like(dk)
    dv[...] = jnp.zeros_like(dv)
    for start in range(0, seq, block):
        at = pl.ds(start, block)
        seen = start + block
        qb, hb = q[at, :], hg[at, :]
        delta = jnp.sum(hb.astype(F32) * hf[at, :], axis=1, keepdims=True)
        s = dot_nt(qb, k[:seen, :]) * scale_att
        row = lax.broadcasted_iota(jnp.int32, (block, seen), 0) + start
        col = lax.broadcasted_iota(jnp.int32, (block, seen), 1)
        p = jnp.where(col <= row, jnp.exp(s - lse[at, :1]), 0.0)
        ds = (p * (dot_nt(hb, v[:seen, :]) - delta)).astype(BF)
        dq[at, :] = dot_nn(ds, k[:seen, :]) * scale_att
        dk[:seen, :] += dot_tn(ds, qb) * scale_att
        dv[:seen, :] += dot_tn(p.astype(BF), hb)

    def rotate(values, at):
        return (values * cosine[at, :] - pltpu.roll(values, HD // 2, 1) * sine[at, :]).astype(BF)

    for start in range(0, seq, block):
        at = pl.ds(start, block)
        dqkv[at, :HD] = rotate(dq[at, :], at)
        dqkv[at, HD : 2 * HD] = rotate(dk[at, :], at)
        dqkv[at, 2 * HD :] = dv[at, :].astype(BF)


def last_kernel(
    n_c, n_f, n_t, n_exp, own_shared, mid_in, wo, q, k, v, hf, lse, cosine, sine, normed_in, wqkv_in, hidden, r_all,
    small, mid_grad, gain2, shs, lg, lu,
    in_out, gq, gk, gv, go, gains_out, router_out, sg_out, su_out, lg_out, lu_out,
    mid_seq, normed, wqkv, big, dqkv, hg, dq, dk, dv, gattn, shs_in, rpart, hs, hr, hl, es, er, rin, rss, rsr, r_own, mine, inx, own, outz, inz, gsend, gin, rs, sx, rx, lx, sz, rz, gs, gr, *rest,
):
    f, c, t = ranks()
    rows, quarter = hidden.shape
    tokens, width = normed.shape
    part = width // (n_f * n_c)
    here = f * n_c + c
    srows = (shs.shape[0] - n_exp) // 2
    others = []
    for df in range(n_f):
        for dc in range(n_c):
            for dt in range(n_t):
                if df or dc or dt:
                    others.append(
                        {
                            "fsdp": lax.rem(f + df, n_f),
                            "ctx": lax.rem(c + dc, n_c),
                            "tp": lax.rem(t + dt, n_t),
                        }
                    )
    large = [
        pltpu.make_async_copy(src, dst, big.at[i])
        for i, (src, dst) in enumerate(((mid_in, mid_seq), (wqkv_in, wqkv), (normed_in, normed)))
    ]
    for copy in large:
        copy.start()
    gin[...] = jnp.zeros_like(gin)
    greet(others)
    order = [2, 1, 3, 0] if n_c == 4 else list(range(1, n_c)) + [0]

    def cross(d):
        cc = lax.rem(c + d, n_c)
        return remote(
            gattn.at[:, piece((1 - f) * n_c + cc, part)], inx.at[d], sx.at[d], rx.at[d], {"fsdp": 1 - f}
        )

    def keep(d):
        cc = lax.rem(c + d, n_c)
        return pltpu.make_async_copy(gattn.at[:, piece(f * n_c + cc, part)], own.at[d], lx.at[d])

    def line(d, to):
        return remote(outz.at[d], inz.at[d], sz.at[d], rz.at[d], {"ctx": to})

    router_copies = [
        remote(rpart, rin.at[i], rss.at[i], rsr.at[i], {"tp": peer})
        for i, peer in enumerate([sibling(t), opposite(t), opposite(sibling(t))])
    ]
    shared = lambda act: to_each(lambda b: shs.at[:, piece(b, part)], shs_in, n_f, n_c, (hs, hr, hl), act)
    late = [
        remote(src, dst, es.at[i], er.at[i], {"fsdp": 1 - f})
        for i, (src, dst) in enumerate(((lg, lg_out), (lu, lu_out)))
    ]
    shared("start")
    fetch = pltpu.make_async_copy(r_all.at[piece(c, rows), :], r_own, rs)
    fetch.start()
    late[0].start()
    large[0].wait()
    attend_back(rows, mid_seq, wo, q, k, v, hf, lse, cosine, sine, dqkv, hg, dq, dk, dv)
    gattn[3 * HD :, :] = dot_tn(hf[...].astype(BF), mid_seq[...]).astype(BF)

    large[1].wait()

    def weights():
        large[2].wait()
        gattn[: 3 * HD, :] = dot_tn(dqkv[...], normed[...]).astype(BF)
        for d in order:
            cross(d).start()
            keep(d).start()
        late[1].start()


    def part_of(cc, q):
        return dot_nt(dqkv[piece(cc, rows), :], wqkv[piece(q, quarter), :])

    def pass_weights():
        for d in order:
            cross(d).wait()
            keep(d).wait()
            both = own[d].astype(F32) + inx[d].astype(F32)
            if d:
                outz[d] = both.astype(BF)
                line(d, lax.rem(c + d, n_c)).start()
            else:
                mine[...] = both

    total = reduce_seq(part_of, n_c, rest[:13], weights, pass_weights)
    fetch.wait()
    gain = small[2 * n_exp : 2 * n_exp + 1, piece(t, quarter)].astype(F32)
    back, gain_part = norm_grad(
        hidden[...].astype(F32), r_own[:, :1], gain, total, width, *rest[13:17]
    )
    in_out[...] = mid_grad[...] + back

    gsend[0:1, :] = gain_part
    gsend[1:2, :] = gain2[0:1, :]
    gsend[2:, :] = jnp.zeros((6, quarter), F32)
    per = quarter // part
    holder = here // per
    def gain_copy(h, tt):
        b = t * per + h
        return remote(
            gsend.at[:, pl.ds(h * part, part)],
            gin.at[here],
            gs.at[h * n_t + tt],
            gr.at[here],
            {"fsdp": b // n_c, "ctx": lax.rem(b, n_c), "tp": jnp.int32(tt)},
        )

    def is_me(h, tt):
        return (t * per + h == here) & (t == tt)

    for h in range(per):
        for tt in range(n_t):

            @pl.when(jnp.logical_not(is_me(h, tt)))
            def _():
                gain_copy(h, tt).start()

    def put(src, block):
        at = piece(src, HD)
        for i, ref in enumerate((gq, gk, gv)):
            ref[:, at] = block[i * HD : (i + 1) * HD, :].T
        go[at, :] = block[3 * HD :, :]

    shared("wait")
    rpart[...] = jnp.sum(shs_in[:, 2 * srows :, :].astype(F32), axis=0)
    for copy in router_copies:
        copy.start()
    for b in range(n_f * n_c):
        at = pl.ds(b * own_shared, own_shared)
        sg_out[at, :] = shs_in[b, :own_shared, :].astype(F32)
        su_out[at, :] = shs_in[b, srows : srows + own_shared, :].astype(F32)
    put(c, mine[...])
    for d in order[:-1]:
        line(d, c).wait()
        put(lax.rem(c - d + n_c, n_c), inz[d].astype(F32))
    for h in range(per):
        for tt in range(n_t):

            @pl.when(jnp.logical_not(is_me(h, tt)))
            def _():
                gain_copy(h, tt).wait_send()

    for b in range(n_f * n_c):

        @pl.when((b != here) | (holder != t))
        def _():
            remote(gin.at[b], gin.at[b], gs.at[0], gr.at[b], {"tp": sibling(t)}).wait_recv()

    own_part = jnp.where(
        holder == t,
        gsend[:, piece(lax.rem(here, per), part)],
        jnp.zeros((8, part), F32),
    )
    gains_out[...] = own_part + jnp.sum(gin[...], axis=0)
    for copy in router_copies + late:
        copy.wait()
    router_out[...] = rpart[...] + jnp.sum(rin[...], axis=0)


def last(
    n_c, n_f, n_t, n_exp, own_shared, mid_seq, wo, q, k, v, hf, lse, cosine, sine, normed, wqkv, hidden, r_all,
    small, mid_grad, gain2, shs, lg, lu,
):
    rows, quarter = hidden.shape
    seq, width = normed.shape
    part = width // (n_f * n_c)
    sds = jax.ShapeDtypeStruct
    slab = pltpu.VMEM((n_c, 4 * HD, part), BF)
    head_f = pltpu.VMEM((seq, HD), F32)
    shared_grad = sds((n_f * n_c * own_shared, part), F32)
    return pl.pallas_call(
        functools.partial(last_kernel, n_c, n_f, n_t, n_exp, own_shared),
        out_shape=(
            sds((rows, quarter), F32),
            sds((part, n_c * HD), F32),
            sds((part, n_c * HD), F32),
            sds((part, n_c * HD), F32),
            sds((n_c * HD, part), F32),
            sds((8, part), F32),
            sds((n_exp, part), F32),
            shared_grad,
            shared_grad,
            sds(lg.shape, BF),
            sds(lu.shape, BF),
        ),
        in_specs=[HBM] + [VMEM] * 8 + [HBM] * 2 + [VMEM, HBM] + [VMEM] * 3 + [HBM] * 3,
        out_specs=[VMEM] * 9 + [HBM] * 2,
        scratch_shapes=[
            pltpu.VMEM((seq, width), BF),
            pltpu.VMEM((seq, width), BF),
            pltpu.VMEM((width, 3 * HD), BF),
            DMA((3,)),
            pltpu.VMEM((seq, 3 * HD), BF),
            pltpu.VMEM((seq, HD), BF),
            head_f,
            head_f,
            head_f,
            pltpu.VMEM((4 * HD, width), BF),
            pltpu.VMEM((n_f * n_c, shs.shape[0], part), BF),
            pltpu.VMEM((n_exp, part), F32),
            DMA((n_f * n_c,)),
            DMA((n_f * n_c,)),
            DMA(()),
            DMA((2,)),
            DMA((2,)),
            pltpu.VMEM((3, n_exp, part), F32),
            DMA((3,)),
            DMA((3,)),
            pltpu.VMEM((rows, HD), F32),
            pltpu.VMEM((4 * HD, part), F32),
            slab,
            slab,
            slab,
            slab,
            pltpu.VMEM((8, quarter), F32),
            pltpu.VMEM((n_f * n_c, 8, part), F32),
            DMA(()),
            DMA((n_c,)),
            DMA((n_c,)),
            DMA((n_c,)),
            DMA((n_c,)),
            DMA((n_c,)),
            DMA((quarter // part * n_t,)),
            DMA((n_f * n_c,)),
        ]
        + reduce_seq_scratch(n_c, rows, quarter)
        + norm_grad_scratch(rows),
        compiler_params=pltpu.CompilerParams(
            collective_id=4, has_side_effects=True, vmem_limit_bytes=BIG
        ),
        cost_estimate=pl.CostEstimate(flops=8 << 30, bytes_accessed=150 << 20, transcendentals=1 << 20),
        name="last",
    )(
        mid_seq, wo, q, k, v, hf, lse, cosine, sine, normed, wqkv, hidden, r_all, small, mid_grad, gain2,
        shs, lg, lu,
    )


def per_device_seq(
    hidden_in,
    positions,
    chosen,
    out_grad,
    attn_gain,
    w_query,
    w_key,
    w_value,
    w_out,
    moe_gain,
    router,
    shared_gate,
    shared_up,
    shared_down,
    expert_gate,
    expert_up,
    expert_down,
):
    f_rank, c_rank, t_rank = ranks()
    n_f, n_c, n_t = (lax.axis_size(name) for name in ("fsdp", "ctx", "tp"))
    rows, quarter = hidden_in.shape
    width = quarter * n_t
    part = w_query.shape[0]
    seq = rows * n_c
    n_exp = router.shape[1]
    mine = n_exp // n_c // n_f
    ffe = expert_gate.shape[2]
    group = ("fsdp", "ctx")
    every = ("fsdp", "ctx", "tp")
    n_b = n_f * n_c
    own_shared = shared_gate.shape[1] // n_b
    srows = -(-own_shared // 16) * 16
    f_arr = f_rank.astype(jnp.int32).reshape(1)
    swap = [(i, n_f - 1 - i) for i in range(n_f)]
    weights = (expert_gate.swapaxes(1, 2), expert_up.swapaxes(1, 2), expert_down)

    line = jnp.arange(16)[:, None]
    lines = jnp.where(line == 0, attn_gain[None], jnp.zeros((), BF))
    lines = jnp.where(line == 1, moe_gain[None], lines)
    lines = jnp.where(line == 2, (positions // 64).astype(BF)[None], lines)
    lines = jnp.where(line == 3, (positions % 64).astype(BF)[None], lines)
    lane = np.arange(HD)
    inverse = 10000.0 ** (-(lane % (HD // 2)) * 2.0 / HD)
    angle = jnp.asarray(np.stack([inverse, np.where(lane < HD // 2, -1.0, 1.0)]).astype(np.float32))
    (
        normed, q, k, v, heads_f, lse, r_one, cosine, sine, resid_mid,
        wqkv, wo, small, resid_all, grad_all, shared, *got,
    ) = first(
        n_c, n_f, n_t, mine, srows, hidden_in, w_query, w_key, w_value, w_out, out_grad, weights,
        router.T, chosen.T, lines, (shared_gate.T, shared_up.T, shared_down), angle,
    )
    sizes = (n_c, n_f, n_t, mine, ffe, srows)
    layer_out, moe_in, act, silu, slope, r_two, prob, kd, sd, shared_d = forward(
        *sizes, resid_all, grad_all, resid_mid, small, weights, got, shared
    )
    arrived_d = lax.ppermute(sd, "fsdp", swap)
    mid_grad, gain_two_part, mid_seq, shared_back, shs, kg, ku, gg, gu, lg, lu = backward(
        *sizes, grad_all, act, silu, slope, moe_in, r_two, shared_d, prob, small,
        resid_mid, out_grad, weights, got, shared,
    )
    input_grad, gq, gk, gv, go, gains, router_grad, shared_g, shared_u, lg, lu = last(
        n_c, n_f, n_t, n_exp, own_shared, mid_seq, wo, q, k, v, heads_f, lse, cosine, sine, normed, wqkv,
        hidden_in, r_one, small, mid_grad, gain_two_part, shs, lg, lu,
    )
    plain = (layer_out, input_grad, gq, gk, gv, go, router_grad, shared_g, shared_u)
    (
        eg, eu, ed, shared_d, layer_out, input_grad, gq, gk, gv, go, router_grad, shared_g, shared_u, gain_1, gain_2,
    ) = finish(f_arr, own_shared, (gg, lg, gu, lu, arrived_d), (kg, ku, kd), shared_back, plain, gains)

    return (
        layer_out,
        input_grad,
        gain_1[0],
        gq,
        gk,
        gv,
        go,
        gain_2[0],
        router_grad.T,
        shared_g.T,
        shared_u.T,
        shared_d,
        eg.swapaxes(1, 2),
        eu.swapaxes(1, 2),
        ed,
    )


def one_head_each(mesh, args):
    n_f, n_c, n_t = (mesh.shape[name] for name in ("fsdp", "ctx", "tp"))
    heads = args[5].shape[1] // HD
    experts = args[10].shape[1]
    return (
        n_f == 2
        and n_t == 4
        and heads == n_c * n_t
        and experts % (n_f * n_c) == 0
        and args[11].shape[1] % (8 * n_f * n_c * n_t) == 0
    )


def solution(mesh):
    placed = (
        P(("fsdp", "ctx"), "tp"),
        P(("fsdp", "ctx")),
        P(("fsdp", "ctx"), None),
        P(("fsdp", "ctx"), "tp"),
        P(("fsdp", "ctx")),
        P(("fsdp", "ctx"), "tp"),
        P(("fsdp", "ctx"), "tp"),
        P(("fsdp", "ctx"), "tp"),
        P("tp", ("fsdp", "ctx")),
        P(("fsdp", "ctx")),
        P(("fsdp", "ctx"), None),
        P(("fsdp", "ctx"), "tp"),
        P(("fsdp", "ctx"), "tp"),
        P("tp", ("fsdp", "ctx")),
        P("ctx", "fsdp", "tp"),
        P("ctx", "fsdp", "tp"),
        P("ctx", "tp", "fsdp"),
    )
    def run(*args):
        body = per_device_seq if one_head_each(mesh, args) else per_device
        return jax.shard_map(
        body,
        mesh=mesh,
        in_specs=placed,
        out_specs=(
            P(("fsdp", "ctx"), "tp"),
            P(("fsdp", "ctx"), "tp"),
            P(("fsdp", "ctx")),
            P(("fsdp", "ctx"), "tp"),
            P(("fsdp", "ctx"), "tp"),
            P(("fsdp", "ctx"), "tp"),
            P("tp", ("fsdp", "ctx")),
            P(("fsdp", "ctx")),
            P(("fsdp", "ctx"), None),
            P(("fsdp", "ctx"), "tp"),
            P(("fsdp", "ctx"), "tp"),
            P("tp", ("fsdp", "ctx")),
            P("ctx", "fsdp", "tp"),
            P("ctx", "fsdp", "tp"),
            P("ctx", "tp", "fsdp"),
        ),
        check_vma=False,
    )(*args)

    return run
```

```python
import functools

import jax
import jax.numpy as jnp
import numpy as np
from jax import lax
from jax.experimental import pallas as pl
from jax.experimental.pallas import tpu as pltpu
from jax.sharding import PartitionSpec as P

FSDP, CTX, TP = "fsdp", "ctx", "tp"
HD = 128
TOPK = 6


EPS = 1e-06
NEG_BIG = -1e30


def as_sent(value):
    return jax.tree.map(lambda a: a.astype(jnp.bfloat16) if a.dtype == jnp.float32 else a, value)


def features(local_part):
    return lax.all_gather(local_part, TP, axis=1, tiled=True)


def row_stats(partial_terms):
    return lax.psum(partial_terms, TP)


def partial_sums(partial_terms):
    return jax.tree.map(
        lambda part: part.astype(jnp.float32),
        lax.psum_scatter(as_sent(partial_terms), TP, scatter_dimension=1, tiled=True),
    )


def to_owners(slot_rows):
    return lax.all_to_all(slot_rows, CTX, split_axis=0, concat_axis=2, tiled=True)


def to_sources(slot_rows):
    return lax.all_to_all(
        slot_rows.astype(jnp.bfloat16), CTX, split_axis=2, concat_axis=0, tiled=True
    ).astype(slot_rows.dtype)


def rotary(values, positions, rotate_sign):
    half_dim = values.shape[-1] // 2
    inverse = 10000.0 ** (-jnp.arange(half_dim, dtype=jnp.float32) * 2.0 / values.shape[-1])
    angles = positions.astype(jnp.float32)[:, None] * inverse[None, :]
    cosine = jnp.cos(angles)[:, None, :]
    sine_val = rotate_sign * jnp.sin(angles)[:, None, :]
    lower_half = values[..., :half_dim]
    upper_half = values[..., half_dim:]
    return jnp.concatenate(
        [lower_half * cosine - upper_half * sine_val, upper_half * cosine + lower_half * sine_val],
        axis=-1,
    )


def norm_rows(values, gain_part, model_width):
    square_sum = row_stats(jnp.sum(values * values, axis=1))
    row_scale = lax.rsqrt(square_sum / model_width + EPS)
    return (values * row_scale[:, None] * gain_part[None, :], row_scale)


def norm_back(values, row_scale, gain_part, grad_normed, model_width, tp_rank):
    quarter = values.shape[1]
    local_sum = jnp.sum(grad_normed * gain_part[None, :] * values, axis=1)
    gain_local = jnp.sum(grad_normed * values * row_scale[:, None], axis=0)
    gain_whole = lax.dynamic_update_slice_in_dim(
        jnp.zeros((model_width,), jnp.float32), gain_local, tp_rank * quarter, 0
    )
    row_total, gain_grad = row_stats((local_sum, gain_whole))
    back = (
        row_scale[:, None] * gain_part[None, :] * grad_normed
        - values * (row_scale**3 * row_total / model_width)[:, None]
    )
    return (back, gain_grad)


def scatter_slots(assign_rows, flat_exp, slot_of, n_exp, capacity):
    buffer = jnp.zeros((n_exp, capacity, assign_rows.shape[1]), assign_rows.dtype)
    return buffer.at[flat_exp, slot_of].set(assign_rows)


def silu_grad(pre_act):
    sigmoid_val = jax.nn.sigmoid(pre_act)
    return sigmoid_val * (1.0 + pre_act * (1.0 - sigmoid_val))


def keep_state(carried):
    return carried


def per_device(
    hidden_in,
    positions,
    chosen,
    out_grad,
    attn_gain,
    w_query,
    w_key,
    w_value,
    w_out,
    moe_gain,
    router,
    shared_gate,
    shared_up,
    shared_down,
    expert_gate,
    expert_up,
    expert_down,
):
    tp_rank = lax.axis_index(TP)
    ctx_rank = lax.axis_index(CTX)
    n_ctx = lax.axis_size(CTX)
    tok_rows, quarter = hidden_in.shape
    model_width = quarter * lax.axis_size(TP)
    gain_one, wq_all, wk_all, wv_all, gain_two, router_all, gate_all, up_all, wo_all, down_all = (
        lax.all_gather(attn_gain, (FSDP, CTX), axis=0, tiled=True),
        lax.all_gather(w_query, (FSDP, CTX), axis=0, tiled=True),
        lax.all_gather(w_key, (FSDP, CTX), axis=0, tiled=True),
        lax.all_gather(w_value, (FSDP, CTX), axis=0, tiled=True),
        lax.all_gather(moe_gain, (FSDP, CTX), axis=0, tiled=True),
        lax.all_gather(router, (FSDP, CTX), axis=0, tiled=True),
        lax.all_gather(shared_gate, (FSDP, CTX), axis=0, tiled=True),
        lax.all_gather(shared_up, (FSDP, CTX), axis=0, tiled=True),
        lax.all_gather(w_out, (FSDP, CTX), axis=1, tiled=True),
        lax.all_gather(shared_down, (FSDP, CTX), axis=1, tiled=True),
    )
    expert_gate_weights, expert_up_weights, expert_down_weights = (
        lax.all_gather(expert_gate, FSDP, axis=1, tiled=True),
        lax.all_gather(expert_up, FSDP, axis=1, tiled=True),
        lax.all_gather(expert_down, FSDP, axis=2, tiled=True),
    )
    gain_q1 = lax.dynamic_slice_in_dim(gain_one, tp_rank * quarter, quarter).astype(jnp.float32)
    gain_q2 = lax.dynamic_slice_in_dim(gain_two, tp_rank * quarter, quarter).astype(jnp.float32)
    router_rows = lax.dynamic_slice_in_dim(router_all, tp_rank * quarter, quarter, 0)
    head_count = wq_all.shape[1] // HD
    scale_att = HD ** (-0.5)
    resid_in = hidden_in.astype(jnp.float32)
    normed_one, scale_one = norm_rows(resid_in, gain_q1, model_width)
    normed_in = features(normed_one.astype(jnp.bfloat16))
    query_pre = jnp.dot(normed_in, wq_all, preferred_element_type=jnp.float32).reshape(
        tok_rows, head_count, HD
    )
    key_pre = jnp.dot(normed_in, wk_all, preferred_element_type=jnp.float32).reshape(
        tok_rows, head_count, HD
    )
    value_b = (
        jnp.dot(normed_in, wv_all, preferred_element_type=jnp.float32)
        .astype(jnp.bfloat16)
        .reshape(tok_rows, head_count, HD)
    )
    query_b = rotary(query_pre, positions, 1.0).astype(jnp.bfloat16)
    key_b = rotary(key_pre, positions, 1.0).astype(jnp.bfloat16)
    q_start = ctx_rank * tok_rows
    row_pos = q_start + jnp.arange(tok_rows)
    start_state = (
        jnp.full((tok_rows, head_count), NEG_BIG, jnp.float32),
        jnp.zeros((tok_rows, head_count), jnp.float32),
        jnp.zeros((tok_rows, head_count, HD), jnp.float32),
    )
    keys_blk = lax.all_gather(key_b, CTX, axis=0, tiled=True)
    vals_blk = lax.all_gather(value_b, CTX, axis=0, tiled=True)
    key_count = keys_blk.shape[0]

    def compute(state_in):
        run_max, run_sum, run_acc = state_in
        scores = (
            jnp.einsum("qhd,khd->qhk", query_b, keys_blk, preferred_element_type=jnp.float32)
            * scale_att
        )
        visible = jnp.arange(key_count)[None, :] <= row_pos[:, None]
        scores = jnp.where(visible[:, None, :], scores, NEG_BIG)
        new_max = jnp.maximum(run_max, jnp.max(scores, axis=2))
        weights = jnp.exp(scores - new_max[:, :, None])
        new_sum = jnp.sum(weights, axis=2)
        new_acc = jnp.einsum(
            "qhk,khd->qhd",
            weights.astype(jnp.bfloat16),
            vals_blk,
            preferred_element_type=jnp.float32,
        )
        return (new_max, new_sum, new_acc)

    run_max, run_sum, run_acc = lax.cond(
        jnp.int32(0) <= q_start + tok_rows - 1, compute, keep_state, start_state
    )
    heads_f = run_acc / run_sum[:, :, None]
    log_sum = run_max + jnp.log(run_sum)
    heads_b = heads_f.astype(jnp.bfloat16).reshape(tok_rows, head_count * HD)
    resid_mid = resid_in + partial_sums(
        jnp.dot(heads_b, wo_all, preferred_element_type=jnp.float32)
    )
    normed_two, scale_two = norm_rows(resid_mid, gain_q2, model_width)
    moe_part = normed_two.astype(jnp.bfloat16)
    moe_in = features(moe_part)
    n_exp = router_all.shape[1]
    exp_dev = n_exp // n_ctx
    capacity = min(tok_rows, 5 * TOPK * tok_rows // (3 * n_exp))
    logits = jnp.dot(moe_in, router_all, preferred_element_type=jnp.float32)
    probs_all = jax.nn.softmax(logits, axis=1)
    picked = (chosen[:, :, None] == jnp.arange(n_exp)[None, None, :]).astype(jnp.float32)
    gate_vals = jnp.sum(picked * probs_all[:, None, :], axis=2)
    shared_a = jnp.dot(moe_in, gate_all, preferred_element_type=jnp.float32)
    shared_b = jnp.dot(moe_in, up_all, preferred_element_type=jnp.float32)
    shared_act = (jax.nn.silu(shared_a) * shared_b).astype(jnp.bfloat16)
    shared_out = jnp.dot(shared_act, down_all, preferred_element_type=jnp.float32)
    flat_exp = chosen.reshape(-1)
    flat_hot = (flat_exp[:, None] == jnp.arange(n_exp)[None, :]).astype(jnp.int32)
    slot_of = jnp.sum((jnp.cumsum(flat_hot, axis=0) - flat_hot) * flat_hot, axis=1)
    token_of = jnp.arange(tok_rows * TOPK) // TOPK
    slot_count = n_ctx * capacity
    outgoing = scatter_slots(moe_in[token_of], flat_exp, slot_of, n_exp, capacity)
    received_rows = to_owners(outgoing.reshape(n_ctx, exp_dev, capacity, model_width)).reshape(
        exp_dev, slot_count, model_width
    )
    expert_a = jnp.einsum(
        "bmw,bwv->bmv", received_rows, expert_gate_weights, preferred_element_type=jnp.float32
    )
    expert_up_proj = jnp.einsum(
        "bmw,bwv->bmv", received_rows, expert_up_weights, preferred_element_type=jnp.float32
    )
    expert_act = (jax.nn.silu(expert_a) * expert_up_proj).astype(jnp.bfloat16)
    expert_out = jnp.einsum(
        "erf,efd->erd", expert_act, expert_down_weights, preferred_element_type=jnp.float32
    )
    returned = to_sources(expert_out.reshape(1, exp_dev, slot_count, model_width))
    shared_q, slot_q = partial_sums((shared_out, returned.reshape(n_exp * capacity, model_width)))
    slot_rows = slot_q.reshape(n_exp, capacity, quarter)[flat_exp, slot_of].reshape(
        tok_rows, TOPK, quarter
    )
    result = resid_mid + shared_q + jnp.sum(gate_vals[:, :, None] * slot_rows, axis=1)
    layer_out = result.astype(jnp.bfloat16)
    grad_out = out_grad.astype(jnp.float32)
    gate_grad = row_stats(jnp.sum(grad_out[:, None, :] * slot_rows, axis=2))
    prob_grad = jnp.sum(gate_grad[:, :, None] * picked, axis=1)
    logit_grad = (
        probs_all * (prob_grad - jnp.sum(probs_all * prob_grad, axis=1, keepdims=True))
    ).astype(jnp.bfloat16)
    router_grad = jnp.einsum("td,te->de", moe_in, logit_grad, preferred_element_type=jnp.float32)
    router_back_q = jnp.einsum(
        "te,de->td", logit_grad, router_rows, preferred_element_type=jnp.float32
    )
    grad_full = features(out_grad)
    shared_dact = jnp.einsum("td,fd->tf", grad_full, down_all, preferred_element_type=jnp.float32)
    shared_da = (shared_dact * shared_b * silu_grad(shared_a)).astype(jnp.bfloat16)
    shared_db = (shared_dact * jax.nn.silu(shared_a)).astype(jnp.bfloat16)
    shared_down_grad = jnp.einsum(
        "tf,td->fd", shared_act, grad_full, preferred_element_type=jnp.float32
    )
    shared_gate_grad = jnp.einsum(
        "td,tf->df", moe_in, shared_da, preferred_element_type=jnp.float32
    )
    shared_up_grad = jnp.einsum("td,tf->df", moe_in, shared_db, preferred_element_type=jnp.float32)
    shared_back = jnp.einsum(
        "tf,df->td", shared_da, gate_all, preferred_element_type=jnp.float32
    ) + jnp.einsum("tf,df->td", shared_db, up_all, preferred_element_type=jnp.float32)
    assign_grad = (
        (gate_vals[:, :, None] * grad_full[:, None, :])
        .astype(jnp.bfloat16)
        .reshape(tok_rows * TOPK, model_width)
    )
    grad_slots = scatter_slots(assign_grad, flat_exp, slot_of, n_exp, capacity)
    grad_arrived = to_owners(grad_slots.reshape(n_ctx, exp_dev, capacity, model_width)).reshape(
        exp_dev, slot_count, model_width
    )
    expert_dact = jnp.einsum(
        "erd,efd->erf", grad_arrived, expert_down_weights, preferred_element_type=jnp.float32
    )
    expert_da = (expert_dact * expert_up_proj * silu_grad(expert_a)).astype(jnp.bfloat16)
    expert_up_proj_grad = (expert_dact * jax.nn.silu(expert_a)).astype(jnp.bfloat16)
    edown_grad = jnp.einsum(
        "erf,erd->efd", expert_act, grad_arrived, preferred_element_type=jnp.float32
    )
    egate_grad = jnp.einsum(
        "qgo,qgz->qoz", received_rows, expert_da, preferred_element_type=jnp.float32
    )
    expert_up_weight_grad = jnp.einsum(
        "qgo,qgz->qoz", received_rows, expert_up_proj_grad, preferred_element_type=jnp.float32
    )
    expert_back = jnp.einsum(
        "iac,igc->iag", expert_da, expert_gate_weights, preferred_element_type=jnp.float32
    ) + jnp.einsum(
        "iac,igc->iag", expert_up_proj_grad, expert_up_weights, preferred_element_type=jnp.float32
    )
    back_slots = to_sources(expert_back.reshape(1, exp_dev, slot_count, model_width)).reshape(
        n_exp, capacity, model_width
    )
    token_back = jnp.sum(back_slots[flat_exp, slot_of].reshape(tok_rows, TOPK, model_width), axis=1)
    moe_back_q = partial_sums(shared_back + token_back)
    mid_back, gain_two_grad = norm_back(
        resid_mid, scale_two, gain_q2, moe_back_q + router_back_q, model_width, tp_rank
    )
    mid_grad = grad_out + mid_back
    branch_full = features(mid_grad.astype(jnp.bfloat16))
    wo_grad = jnp.einsum("tf,td->fd", heads_b, branch_full, preferred_element_type=jnp.float32)
    heads_grad = (
        jnp.einsum("td,fd->tf", branch_full, wo_all, preferred_element_type=jnp.float32)
        .astype(jnp.bfloat16)
        .reshape(tok_rows, head_count, HD)
    )
    row_delta = jnp.sum(heads_grad.astype(jnp.float32) * heads_f, axis=2)
    seq_len = tok_rows * n_ctx
    back_state = (
        jnp.zeros((tok_rows, head_count, HD), jnp.float32),
        jnp.zeros((seq_len, head_count, HD), jnp.float32),
        jnp.zeros((seq_len, head_count, HD), jnp.float32),
    )
    attend_keys_blk = lax.all_gather(key_b, CTX, axis=0, tiled=True)
    attend_vals_blk = lax.all_gather(value_b, CTX, axis=0, tiled=True)
    attend_key_count = attend_keys_blk.shape[0]

    def compute(state_in):
        scores = (
            jnp.einsum("qhd,khd->qhk", query_b, attend_keys_blk, preferred_element_type=jnp.float32)
            * scale_att
        )
        visible = jnp.arange(attend_key_count)[None, :] <= row_pos[:, None]
        probs_blk = jnp.where(visible[:, None, :], jnp.exp(scores - log_sum[:, :, None]), 0.0)
        value_part = jnp.einsum(
            "qhk,qhd->khd",
            probs_blk.astype(jnp.bfloat16),
            heads_grad,
            preferred_element_type=jnp.float32,
        )
        dot_grad = jnp.einsum(
            "qhd,khd->qhk", heads_grad, attend_vals_blk, preferred_element_type=jnp.float32
        )
        score_grad = (probs_blk * (dot_grad - row_delta[:, :, None])).astype(jnp.bfloat16)
        query_acc = (
            jnp.einsum(
                "qhk,khd->qhd", score_grad, attend_keys_blk, preferred_element_type=jnp.float32
            )
            * scale_att
        )
        key_part = (
            jnp.einsum("qhk,qhd->khd", score_grad, query_b, preferred_element_type=jnp.float32)
            * scale_att
        )
        return (query_acc, key_part, value_part)

    query_grad, key_grad_all, value_grad_all = lax.cond(
        jnp.int32(0) <= q_start + tok_rows - 1, compute, keep_state, back_state
    )
    key_grad, value_grad = (
        lax.psum_scatter(
            key_grad_all.astype(jnp.bfloat16), CTX, scatter_dimension=0, tiled=True
        ).astype(jnp.float32),
        lax.psum_scatter(
            value_grad_all.astype(jnp.bfloat16), CTX, scatter_dimension=0, tiled=True
        ).astype(jnp.float32),
    )
    query_pre_grad = (
        rotary(query_grad, positions, -1.0).astype(jnp.bfloat16).reshape(tok_rows, head_count * HD)
    )
    key_pre_grad = (
        rotary(key_grad, positions, -1.0).astype(jnp.bfloat16).reshape(tok_rows, head_count * HD)
    )
    value_pre_grad = value_grad.astype(jnp.bfloat16).reshape(tok_rows, head_count * HD)
    wq_grad = jnp.einsum("td,tf->df", normed_in, query_pre_grad, preferred_element_type=jnp.float32)
    wk_grad = jnp.einsum("td,tf->df", normed_in, key_pre_grad, preferred_element_type=jnp.float32)
    wv_grad = jnp.einsum("td,tf->df", normed_in, value_pre_grad, preferred_element_type=jnp.float32)
    in_back = jnp.einsum("tf,df->td", query_pre_grad, wq_all, preferred_element_type=jnp.float32)
    in_back = in_back + jnp.einsum(
        "tf,df->td", key_pre_grad, wk_all, preferred_element_type=jnp.float32
    )
    in_back = in_back + jnp.einsum(
        "tf,df->td", value_pre_grad, wv_all, preferred_element_type=jnp.float32
    )
    first_back, gain_one_grad = norm_back(
        resid_in, scale_one, gain_q1, partial_sums(in_back), model_width, tp_rank
    )
    input_grad = mid_grad + first_back
    dense = (
        lax.psum_scatter(
            gain_one_grad.astype(jnp.bfloat16), (FSDP, CTX), scatter_dimension=0, tiled=True
        ).astype(jnp.float32),
        lax.psum_scatter(
            wq_grad.astype(jnp.bfloat16), (FSDP, CTX), scatter_dimension=0, tiled=True
        ).astype(jnp.float32),
        lax.psum_scatter(
            wk_grad.astype(jnp.bfloat16), (FSDP, CTX), scatter_dimension=0, tiled=True
        ).astype(jnp.float32),
        lax.psum_scatter(
            wv_grad.astype(jnp.bfloat16), (FSDP, CTX), scatter_dimension=0, tiled=True
        ).astype(jnp.float32),
        lax.psum_scatter(
            gain_two_grad.astype(jnp.bfloat16), (FSDP, CTX), scatter_dimension=0, tiled=True
        ).astype(jnp.float32),
        lax.psum_scatter(
            router_grad.astype(jnp.bfloat16), (FSDP, CTX), scatter_dimension=0, tiled=True
        ).astype(jnp.float32),
        lax.psum_scatter(
            shared_gate_grad.astype(jnp.bfloat16), (FSDP, CTX), scatter_dimension=0, tiled=True
        ).astype(jnp.float32),
        lax.psum_scatter(
            shared_up_grad.astype(jnp.bfloat16), (FSDP, CTX), scatter_dimension=0, tiled=True
        ).astype(jnp.float32),
        lax.psum_scatter(
            wo_grad.astype(jnp.bfloat16), (FSDP, CTX), scatter_dimension=1, tiled=True
        ).astype(jnp.float32),
        lax.psum_scatter(
            shared_down_grad.astype(jnp.bfloat16), (FSDP, CTX), scatter_dimension=1, tiled=True
        ).astype(jnp.float32),
    )
    experts_done = (
        lax.psum_scatter(
            egate_grad.astype(jnp.bfloat16), FSDP, scatter_dimension=1, tiled=True
        ).astype(jnp.float32),
        lax.psum_scatter(
            expert_up_weight_grad.astype(jnp.bfloat16), FSDP, scatter_dimension=1, tiled=True
        ).astype(jnp.float32),
        lax.psum_scatter(
            edown_grad.astype(jnp.bfloat16), FSDP, scatter_dimension=2, tiled=True
        ).astype(jnp.float32),
    )
    return (
        layer_out,
        input_grad,
        dense[0],
        dense[1],
        dense[2],
        dense[3],
        dense[8],
        dense[4],
        dense[5],
        dense[6],
        dense[7],
        dense[9],
        experts_done[0],
        experts_done[1],
        experts_done[2],
    )


MESH = pl.DeviceIdType.MESH
HBM = pl.BlockSpec(memory_space=pl.ANY)
VMEM = pl.BlockSpec(memory_space=pltpu.VMEM)
DMA = pltpu.SemaphoreType.DMA
BF, F32 = jnp.bfloat16, jnp.float32
BIG = 60 * 1024 * 1024


def dot_nt(left, right):
    return lax.dot_general(left, right, (((1,), (1,)), ((), ())), preferred_element_type=F32)


def dot_tn(left, right):
    return lax.dot_general(left, right, (((0,), (0,)), ((), ())), preferred_element_type=F32)


def dot_nn(left, right):
    return jnp.dot(left, right, preferred_element_type=F32)


def ranks():
    return lax.axis_index(FSDP), lax.axis_index(CTX), lax.axis_index(TP)


def sibling(t):
    return t + 1 - 2 * lax.rem(t, 2)


def opposite(t):
    return lax.rem(t + 2, 4)


def remote(src, dst, send, recv, to):
    return pltpu.make_async_remote_copy(
        src_ref=src, dst_ref=dst, send_sem=send, recv_sem=recv, device_id=to, device_id_type=MESH
    )


def greet(peers):
    barrier = pltpu.get_barrier_semaphore()
    for peer in peers:
        pl.semaphore_signal(barrier, inc=1, device_id=peer, device_id_type=MESH)
    pl.semaphore_wait(barrier, len(peers))


def line_peers(c, n_c):
    return [{CTX: lax.rem(c + step, n_c)} for step in range(1, n_c)]


def piece(index, size):
    return pl.ds(pl.multiple_of(index * size, size), size)


def nearest(c, n_c, act):
    act(c)
    for step in range(1, n_c):
        for side in (-1, 1):
            place = c + side * step

            @pl.when((place >= 0) & (place < n_c))
            def _():
                act(place)


def spread_sems(n_c):
    return [
        DMA((n_c + 2,)),
        DMA((n_c,)),
        DMA((n_c,)),
        DMA((n_c,)),
        DMA((2 * n_c,)),
        DMA((2 * n_c,)),
        DMA((4 * n_c,)),
        DMA((4 * n_c,)),
        DMA(()),
    ]


class Spread:
    def __init__(self, own, place, n_c, both, sems):
        self.own, self.place, self.n_c, self.both = own, place, n_c, both
        self.zs, self.zr, self.xs, self.xr, self.ys, self.yr, self.ks, self.kr, self.ls = sems
        self.f, self.c, self.t = ranks()
        self.other_t = opposite(self.t)
        self.groups = ((self.f, 0), (1 - self.f, n_c))[: 2 if both else 1]

    def local(self):
        return pltpu.make_async_copy(self.own, self.place(self.f, self.c, self.t), self.ls)

    def far_copy(self, src, i, g, cc, col):
        return remote(src, self.place(g, cc, col), self.ys.at[i], self.yr.at[i], {TP: self.other_t})

    def sib_copy(self, src, i, which, g, cc, col):
        at = 2 * i + which
        return remote(src, self.place(g, cc, col), self.ks.at[at], self.kr.at[at], {TP: sibling(self.t)})

    def other_copy(self, src, g, cc):
        return remote(src, self.place(g, cc, self.t), self.xs.at[cc], self.xr.at[cc], {FSDP: 1 - self.f})

    def line_copy(self, src, cc, sem, to):
        return remote(src, self.place(self.f, cc, self.t), self.zs.at[sem], self.zr.at[cc], {CTX: to})

    def pass_on(self, src, i, g, cc):
        self.far_copy(src, i, g, cc, self.t).start()
        self.sib_copy(src, i, 0, g, cc, self.t).start()

    def start(self):
        self.local().start()
        n_c, c, own = self.n_c, self.c, self.own

        @pl.when(c < n_c - 1)
        def _():
            self.line_copy(own, c, n_c, c + 1).start()

        @pl.when(c > 0)
        def _():
            self.line_copy(own, c, n_c + 1, c - 1).start()

        if self.both:
            self.other_copy(own, self.f, c).start()
        self.pass_on(own, c, self.f, c)

    def each_other(self, act):
        for step in range(1, self.n_c):
            for side in (-1, 1):
                cc = self.c + side * step

                @pl.when((cc >= 0) & (cc < self.n_c))
                def _():
                    act(cc, self.c - side)

    def line(self):
        n_c = self.n_c

        def arrive(cc, onward):
            block = self.place(self.f, cc, self.t)
            self.line_copy(block, cc, cc, self.c).wait_recv()

            @pl.when((onward >= 0) & (onward < n_c))
            def _():
                self.line_copy(block, cc, cc, onward).start()

            if self.both:
                self.other_copy(block, self.f, cc).start()
            self.pass_on(block, cc, self.f, cc)

        self.each_other(arrive)

    def other(self):
        def arrive(cc):
            block = self.place(1 - self.f, cc, self.t)
            self.other_copy(block, 1 - self.f, cc).wait_recv()
            self.pass_on(block, self.n_c + cc, 1 - self.f, cc)

        nearest(self.c, self.n_c, arrive)

    def far(self, which):
        g, base = self.groups[which]

        def arrive(cc):
            i = base + cc
            block = self.place(g, cc, self.other_t)
            self.far_copy(block, i, g, cc, self.other_t).wait_recv()
            self.sib_copy(block, i, 1, g, cc, self.other_t).start()

        nearest(self.c, self.n_c, arrive)

    def arrived(self, which):
        g, base = self.groups[which]
        for cc in range(self.n_c):
            block = self.place(g, cc, self.t)
            for half in range(2):
                self.sib_copy(block, base + cc, half, g, cc, self.t).wait_recv()

    def finish(self):
        n_c, c, f, t, own = self.n_c, self.c, self.f, self.t, self.own
        for g, base in self.groups:
            for cc in range(n_c):
                block = self.place(g, cc, t)
                for half in range(2):
                    self.sib_copy(block, base + cc, half, g, cc, t).wait_send()
                self.far_copy(block, base + cc, g, cc, t).wait_send()
        if self.both:
            for cc in range(n_c):
                self.other_copy(self.place(f, cc, t), f, cc).wait_send()
        block = self.place(f, c, t)

        @pl.when(c < n_c - 1)
        def _():
            self.line_copy(block, c, n_c, c).wait_send()

        @pl.when(c > 0)
        def _():
            self.line_copy(block, c, n_c + 1, c).wait_send()

        def sent(cc, onward):
            @pl.when((onward >= 0) & (onward < n_c))
            def _():
                self.line_copy(block, cc, cc, c).wait_send()

        self.each_other(sent)


def to_each(src_of, dst, n_f, n_c, sems, act):
    send, recv, own = sems
    f, c, _ = ranks()
    here = f * n_c + c
    for df in range(n_f):
        for dc in range(n_c):
            i = df * n_c + dc
            if i == 0:
                copy = pltpu.make_async_copy(src_of(here), dst.at[here], own)
                copy.start() if act == "start" else copy.wait()
                continue
            to_f, to_c = lax.rem(f + df, n_f), lax.rem(c + dc, n_c)
            copy = remote(
                src_of(to_f * n_c + to_c), dst.at[here], send.at[i], recv.at[i], {FSDP: to_f, CTX: to_c}
            )
            copy.start() if act == "start" else copy.wait()


def each_peers(f, c, n_f, n_c):
    return [
        {FSDP: lax.rem(f + df, n_f), CTX: lax.rem(c + dc, n_c)}
        for df in range(n_f)
        for dc in range(n_c)
        if df or dc
    ]


def reduce_seq_scratch(n_c, rows, quarter):
    return [
        pltpu.VMEM((n_c, 2, rows, quarter), BF),
        pltpu.VMEM((n_c, 2, rows, quarter), BF),
        pltpu.VMEM((n_c, 2, rows, quarter), F32),
        pltpu.VMEM((n_c, rows, quarter), BF),
        pltpu.VMEM((n_c, rows, quarter), BF),
        pltpu.VMEM((n_c, rows, quarter), BF),
        pltpu.VMEM((n_c, rows, quarter), BF),
        DMA((n_c,)),
        DMA((n_c,)),
        DMA((n_c,)),
        DMA((n_c,)),
        DMA((n_c,)),
        DMA((n_c,)),
    ]


def reduce_seq(part_of, n_c, scratch, middle=None, before_last=None):
    out1, in1, own, out2, in2, out3, in3, s1, r1, s2, r2, s3, r3 = scratch
    f, c, t = ranks()
    far, sib = opposite(t), sibling(t)
    to_sib, to_far = {TP: sib}, {TP: far}
    order = [2, 1, 3, 0] if n_c == 4 else list(range(1, n_c)) + [0]
    for d in order:
        cc = lax.rem(c + d, n_c)
        out1[d, 0] = part_of(cc, sib).astype(BF)
        out1[d, 1] = part_of(cc, opposite(sib)).astype(BF)
        remote(out1.at[d], in1.at[d], s1.at[d], r1.at[d], to_sib).start()
        own[d, 0] = part_of(cc, t)
        own[d, 1] = part_of(cc, far)
    for d in order:
        remote(out1.at[d], in1.at[d], s1.at[d], r1.at[d], to_sib).wait()
        out2[d] = (own[d, 1] + in1[d, 1].astype(F32)).astype(BF)
        remote(out2.at[d], in2.at[d], s2.at[d], r2.at[d], to_far).start()
    if middle is not None:
        middle()
    for d in order:
        remote(out2.at[d], in2.at[d], s2.at[d], r2.at[d], to_far).wait()
        total = own[d, 0] + in1[d, 0].astype(F32) + in2[d].astype(F32)
        if d:
            out3[d] = total.astype(BF)
            cc = lax.rem(c + d, n_c)
            remote(out3.at[d], in3.at[d], s3.at[d], r3.at[d], {CTX: cc}).start()
    if before_last is not None:
        before_last()
    for d in order[:-1]:
        remote(out3.at[d], in3.at[d], s3.at[d], r3.at[d], {CTX: c}).wait()
        total = total + in3[d].astype(F32)
    return total


def first_kernel(
    n_c, n_f, n_exp, mine, hidden, wq, wk, wv, wo, og, gate_t, up_t, down, router_in, chosen, lines, sg, su, sd, angle,
    normed_out, q_out, k_out, v_out, hf_out, lse_out, r_out, cos_out, sin_out, resid_out,
    wqkv_out, wo_out, small_out, all_out, og_out, shared_out, gg_out, gu_out, gd_out,
    seq, wqkv, wo_all, small_all, hb, blk, own_og, small, shared, normed,
    ws, wr, ls, xs, xr, ss, sr, sl, es, er, os, *scratch,
):
    f, c, t = ranks()
    rows, quarter = blk.shape
    part = wo.shape[1]
    tokens, width = seq.shape
    n_s = len(spread_sems(n_c))
    named = lax.broadcasted_iota(jnp.int32, (n_exp, part), 0)
    mask = jnp.zeros((n_exp, part), F32)
    for k in range(chosen.shape[0]):
        mask = mask + jnp.where(chosen[k : k + 1, :] == named, 1.0, 0.0)
    small[:n_exp, :] = router_in[...]
    small[n_exp : 2 * n_exp, :] = mask.astype(BF)
    small[2 * n_exp :, :] = lines[...]
    n_b = n_f * n_c
    own_rows, srows = sg.shape[0] // n_b, shared.shape[1] // 3
    for i, src in enumerate((sg, su, sd)):
        for b in range(n_b):
            shared[b, i * srows : i * srows + own_rows, :] = src[b * own_rows : (b + 1) * own_rows, :]
            if srows > own_rows:
                shared[b, i * srows + own_rows : (i + 1) * srows, :] = jnp.zeros((srows - own_rows, part), BF)
    greet([{TP: sibling(t)}, {TP: opposite(t)}] + each_peers(f, c, n_f, n_c))
    seq_place = lambda g, cc, tt: seq.at[piece(cc, rows), piece(tt, quarter)]
    og_place = lambda g, cc, tt: og_out.at[g * n_c + cc, tt]
    all_place = lambda g, cc, tt: all_out.at[piece(g * n_c + cc, rows), piece(tt, quarter)]
    hid = Spread(hidden, seq_place, n_c, False, scratch[:n_s])
    grad = Spread(og, og_place, n_c, True, scratch[n_s : 2 * n_s])
    res = Spread(blk, all_place, n_c, True, scratch[2 * n_s : 3 * n_s])

    def targets(g, cc):
        block = piece(g * n_c + cc, part)
        return [wqkv.at[block, pl.ds(i * HD, HD)] for i in range(3)] + [
            wo_all.at[:, block],
            small_all.at[:, block],
        ]

    def sources(head):
        cols = piece(head, HD)
        return [wq.at[:, cols], wk.at[:, cols], wv.at[:, cols], wo.at[cols, :], small]

    def slabs(g, cc):
        block = piece(g * n_c + cc, part)
        return [wqkv.at[block, :], wo_all.at[:, block], small_all.at[:, block]]

    def across(step, g, cc):
        return [
            remote(slab, slab, xs.at[step, i], xr.at[step, i], {FSDP: 1 - f})
            for i, slab in enumerate(slabs(g, cc))
        ]

    def swap(weight, out, k):
        return [
            remote(weight.at[(1 - f) * mine + e], out.at[e], es.at[k, e], er.at[k, e], {FSDP: 1 - f})
            for e in range(mine)
        ]

    more = swap(down, gd_out, 2)
    for copy in more:
        copy.start()
    hid.start()
    def weights_out(step):
        to = lax.rem(c + step, n_c)
        for i, (src, dst) in enumerate(zip(sources(to), targets(f, c))):
            remote(src, dst, ws.at[step, i], wr.at[step, i], {CTX: to}).start()

    def weights_on(step):
        cc = lax.rem(c - step + n_c, n_c)
        for i, dst in enumerate(targets(f, cc)):
            remote(dst, dst, ws.at[step, i], wr.at[step, i], {CTX: cc}).wait_recv()
        for copy in across(step, f, cc):
            copy.start()

    steps = ([2, 1, 3] if n_c == 4 else list(range(1, n_c))) + [None]
    weights_out(steps[0])
    own = [
        pltpu.make_async_copy(src, dst, ls.at[i])
        for i, (src, dst) in enumerate(zip(sources(c), targets(f, c)))
    ]
    for copy in own:
        copy.start()
    for copy in own:
        copy.wait()
    for copy in across(0, f, c):
        copy.start()
    grad.start()
    hid.line()
    for step, following in zip(steps, steps[1:]):
        if following is not None:
            weights_out(following)
        weights_on(step)
    grad.line()
    swaps = swap(gate_t, gg_out, 0) + swap(up_t, gu_out, 1)
    for copy in swaps[: mine + 1]:
        copy.start()
    hid.far(0)
    hid.arrived(0)
    hid.local().wait()
    for step in range(n_c):
        for copy in across(step, 1 - f, lax.rem(c - step + n_c, n_c)):
            copy.wait_recv()
    outs = [
        pltpu.make_async_copy(src, dst, os.at[i])
        for i, (src, dst) in enumerate(((wqkv, wqkv_out), (wo_all, wo_out), (small_all, small_out)))
    ]
    for copy in outs:
        copy.start()

    exchange = lambda act: to_each(lambda b: shared.at[b], shared_out, n_f, n_c, (ss, sr, sl), act)
    exchange("start")

    scale_att = HD ** (-0.5)
    gain = small_all[2 * n_exp : 2 * n_exp + 1, :].astype(F32)
    place_row = 2 * n_exp + 2
    for start in range(0, tokens, rows):
        at = pl.ds(start, rows)
        h = seq[at, :].astype(F32)
        r = lax.rsqrt(jnp.sum(h * h, axis=1, keepdims=True) / width + EPS)
        n = (h * r * gain).astype(BF)
        normed[at, :] = n
        r_out[at, :] = jnp.broadcast_to(r, (rows, HD))
        cols = pl.ds(pl.multiple_of(f * tokens + start, rows), rows)
        pos = small_all[place_row : place_row + 2, cols].astype(F32)
        pos = pos[0:1] * 64.0 + pos[1:2]
        turn = jnp.broadcast_to(pos, (HD, rows)).T * angle[0:1, :]
        cos, sin = jnp.cos(turn), jnp.sin(turn) * angle[1:2, :]
        cos_out[at, :] = cos
        sin_out[at, :] = sin
        qkv = dot_nn(n, wqkv[...])

        def rotate(values):
            return (values * cos + pltpu.roll(values, HD // 2, 1) * sin).astype(BF)

        q_out[at, :] = rotate(qkv[:, :HD])
        k_out[at, :] = rotate(qkv[:, HD : 2 * HD])
        v_out[at, :] = qkv[:, 2 * HD :].astype(BF)
    outs.append(pltpu.make_async_copy(normed, normed_out, os.at[4]))
    outs[-1].start()
    for start in range(0, tokens, rows):
        at = pl.ds(start, rows)
        seen = start + rows
        s = dot_nt(q_out[at, :], k_out[:seen, :]) * scale_att
        row = lax.broadcasted_iota(jnp.int32, (rows, seen), 0) + start
        col = lax.broadcasted_iota(jnp.int32, (rows, seen), 1)
        s = jnp.where(col <= row, s, NEG_BIG)
        top = jnp.max(s, axis=1, keepdims=True)
        e = jnp.exp(s - top)
        total = jnp.sum(e, axis=1, keepdims=True)
        out = dot_nn((e * (1.0 / total)).astype(BF), v_out[:seen, :])
        hf_out[at, :] = out
        hb[at, :] = out.astype(BF)
        lse_out[at, :] = jnp.broadcast_to(top + jnp.log(total), (rows, HD))

    def part_of(cc, q):
        return dot_nn(hb[piece(cc, rows), :], wo_all[:, piece(q, quarter)])

    fetch = pltpu.make_async_copy(hidden, own_og, os.at[3])
    fetch.start()
    total = reduce_seq(part_of, n_c, scratch[3 * n_s :], grad.other)
    fetch.wait()
    resid = own_og[...].astype(F32) + total
    resid_out[...] = resid
    blk[...] = resid.astype(BF)
    res.start()
    res.line()
    for copy in swaps[mine + 1 :]:
        copy.start()
    grad.far(0)
    grad.far(1)
    res.other()
    res.far(0)
    res.far(1)
    for which in range(2):
        grad.arrived(which)
        res.arrived(which)
    exchange("wait")
    for copy in swaps + more:
        copy.wait()
    for step in range(1, n_c):
        for i, (src, dst) in enumerate(zip(sources(c), targets(f, c))):
            remote(src, dst, ws.at[step, i], wr.at[step, i], {CTX: c}).wait_send()
    for step in range(n_c):
        for copy in across(step, f, lax.rem(c - step + n_c, n_c)):
            copy.wait_send()
    for item in (hid, grad, res):
        item.finish()
    grad.local().wait()
    res.local().wait()
    for copy in outs:
        copy.wait()


def first(n_c, n_f, n_t, mine, srows, hidden, wq, wk, wv, wo, og, weights, router, chosen, lines, shared, angle):
    rows, quarter = hidden.shape
    width = quarter * n_t
    seq = rows * n_c
    n_exp = mine * n_f * n_c
    ffe, half = weights[0].shape[1:]
    sds = jax.ShapeDtypeStruct
    part = wo.shape[1]
    n_small = 2 * n_exp + lines.shape[0]
    head, head_f = sds((seq, HD), BF), sds((seq, HD), F32)
    got = sds((mine, ffe, half), BF)
    return pl.pallas_call(
        functools.partial(first_kernel, n_c, n_f, n_exp, mine),
        out_shape=(
            sds((seq, width), BF),
            head,
            head,
            head,
            head_f,
            head_f,
            head_f,
            head_f,
            head_f,
            sds((rows, quarter), F32),
            sds((width, 3 * HD), BF),
            sds((HD, width), BF),
            sds((n_small, width), BF),
            sds((seq * n_f, width), BF),
            sds((n_f * n_c, n_t, rows, quarter), BF),
            sds((n_f * n_c, 3 * srows, part), BF),
            got,
            got,
            got,
        ),
        in_specs=[HBM] * 9 + [VMEM] * 7,
        out_specs=[HBM] + [VMEM] * 9 + [HBM] * 9,
        scratch_shapes=[
            pltpu.VMEM((seq, width), BF),
            pltpu.VMEM((width, 3 * HD), BF),
            pltpu.VMEM((HD, width), BF),
            pltpu.VMEM((n_small, width), BF),
            pltpu.VMEM((seq, HD), BF),
            pltpu.VMEM((rows, quarter), BF),
            pltpu.VMEM((rows, quarter), BF),
            pltpu.VMEM((n_small, part), BF),
            pltpu.VMEM((n_f * n_c, 3 * srows, part), BF),
            pltpu.VMEM((seq, width), BF),
            DMA((n_c, 5)),
            DMA((n_c, 5)),
            DMA((5,)),
            DMA((n_c, 3)),
            DMA((n_c, 3)),
            DMA((n_f * n_c,)),
            DMA((n_f * n_c,)),
            DMA(()),
            DMA((3, mine)),
            DMA((3, mine)),
            DMA((5,)),
        ]
        + spread_sems(n_c) * 3
        + reduce_seq_scratch(n_c, rows, quarter),
        compiler_params=pltpu.CompilerParams(
            collective_id=1, has_side_effects=True, vmem_limit_bytes=BIG
        ),
        cost_estimate=pl.CostEstimate(
            flops=5 << 30, bytes_accessed=300 << 20, transcendentals=1 << 20
        ),
        name="first",
    )(hidden, wq, wk, wv, wo, og, *weights, router, chosen, lines, *shared, angle)


def fetch_experts(n_c, n_f, mine, ffe, srows, hp, weights, shared, wgu, wd, sems):
    f = lax.axis_index(FSDP)
    wg0, wu0, wd0, wg1, wu1, wd1 = weights
    width = wd.shape[1]
    used = mine * ffe
    part = width // (n_f * n_c)
    half = width // n_f
    copies = []

    def add(src, dst):
        copies.append(pltpu.make_async_copy(src, dst, sems.at[len(copies)]))

    groups = []
    for i, (kept, got) in enumerate(((wg0, wg1), (wu0, wu1), (wd0, wd1))):
        dst, base = ((wgu, 0), (wgu, hp), (wd, 0))[i]
        for e in range(mine):
            at = pl.ds(base + e * ffe, ffe)
            add(kept.at[f * mine + e], dst.at[at, piece(f, half)])
            add(got.at[e], dst.at[at, piece(1 - f, half)])
        for b in range(n_f * n_c):
            add(
                shared.at[b, pl.ds(i * srows, srows), :],
                dst.at[pl.ds(base + used, srows), pl.ds(b * part, part)],
            )
        groups.append(copies[sum(map(len, groups)) :])
    return groups[0] + groups[1], groups[2]


def blank_rows(rows_used, hp, wgu, wd):
    blank = jnp.zeros((hp - rows_used, wd.shape[1]), BF)
    wgu[rows_used:hp, :] = blank
    wgu[hp + rows_used :, :] = blank
    wd[rows_used:, :] = blank


def gates(prob, picked, first, mine, ffe, hp):
    block, n_exp = prob.shape
    lane = lax.broadcasted_iota(jnp.int32, (block, n_exp), 1)
    gated = prob * picked
    col = lax.broadcasted_iota(jnp.int32, (block, hp), 1)
    gate = jnp.ones((block, hp), F32)
    for k in reversed(range(mine)):
        g = jnp.sum(jnp.where(lane == first + k, gated, 0.0), axis=1, keepdims=True)
        gate = jnp.where(col < (k + 1) * ffe, g, gate)
    return gate, lane, col


def reducer_scratch(n_f, n_c, rows, quarter, split):
    n_b = n_f * n_c
    upper = rows // 2 if split else rows
    lower = rows // 2 if split else 16
    blocks = lambda *lead: pltpu.VMEM(lead + (rows, quarter), BF)
    return [
        blocks(n_b, 2),
        blocks(n_b, 2),
        blocks(n_b, 2),
        blocks(n_b),
        blocks(n_b),
        pltpu.VMEM((n_c, upper, quarter), BF),
        pltpu.VMEM((n_c, upper, quarter), BF),
        pltpu.VMEM((n_c, rows, quarter), F32),
        blocks(n_c),
        blocks(n_c),
        pltpu.VMEM((n_c, 2, lower, quarter), BF),
        pltpu.VMEM((n_c, 2, lower, quarter), BF),
    ] + [DMA((n_b,))] * 4 + [DMA((n_c,))] * 6


N_REDUCER = 22


def when(condition, act):
    if isinstance(condition, bool):
        if condition:
            act()
    else:
        pl.when(condition)(act)


class Reducer:
    def __init__(self, n_c, scratch):
        self.n_c = n_c
        (self.out1, self.in1, self.own, self.out2, self.in2, self.out3, self.in3, self.acc,
         self.out4, self.in4, self.out5, self.in5, self.s1, self.r1, self.s2, self.r2, self.s3, self.r3,
         self.s4, self.r4, self.s5, self.r5) = scratch
        self.half = self.out3.shape[1]
        self.split = self.half < self.out4.shape[1]
        self.f, self.c, self.t = ranks()
        self.far, self.sib = opposite(self.t), sibling(self.t)

    def row_block(self, i):
        n_c = self.n_c
        group = jnp.where(i < n_c, 1 - self.f, self.f)
        return group * n_c + lax.rem(self.c + lax.rem(i, n_c) + 1, n_c)

    def core_copy(self, i):
        return remote(self.out1.at[i], self.in1.at[i], self.s1.at[i], self.r1.at[i], {TP: self.sib})

    def far_copy(self, i, upper=False):
        src, dst = self.out2.at[i], self.in2.at[i]
        if upper:
            src, dst = src.at[pl.ds(0, self.half)], dst.at[pl.ds(0, self.half)]
        return remote(src, dst, self.s2.at[i], self.r2.at[i], {TP: self.far})

    def other_copy(self, j):
        return remote(self.out3.at[j], self.in3.at[j], self.s3.at[j], self.r3.at[j], {FSDP: 1 - self.f})

    def lower_copy(self, j):
        return remote(self.out5.at[j], self.in5.at[j], self.s5.at[j], self.r5.at[j], {FSDP: 1 - self.f})

    def line_copy(self, j, to):
        return remote(self.out4.at[j], self.in4.at[j], self.s4.at[j], self.r4.at[j], {CTX: to})

    def put(self, i, part_of):
        self.out1[i, 0] = part_of(opposite(self.sib)).astype(BF)
        self.out1[i, 1] = part_of(self.sib).astype(BF)
        self.core_copy(i).start()
        self.own[i, 0] = part_of(self.far).astype(BF)
        self.own[i, 1] = part_of(self.t).astype(BF)

    def core_sum(self, i, which):
        return self.own[i, which].astype(F32) + self.in1[i, which].astype(F32)

    def over(self, i):
        self.core_copy(i).wait()
        half, n_c = self.half, self.n_c

        def of_other():
            far = self.core_sum(i, 0)
            if self.split:
                self.out5[i, 0] = far[half:].astype(BF)
                self.out5[i, 1] = self.core_sum(i, 1)[half:].astype(BF)
                self.lower_copy(i).start()
            self.out2[i, :half] = far[:half].astype(BF)
            self.far_copy(i, True).start()

        def of_own():
            j = i - n_c
            if self.split:
                self.lower_copy(j).wait_recv()
            far = self.core_sum(i, 0)
            self.out2[i, :half] = far[:half].astype(BF)
            if self.split:
                self.out2[i, half:] = (far[half:] + self.in5[j, 0].astype(F32)).astype(BF)
            self.far_copy(i).start()

        when(i < n_c, of_other)
        when(i >= n_c, of_own)

    def after_other(self, i):
        half = self.half
        self.far_copy(i, True).wait()
        self.out3[i] = (self.core_sum(i, 1)[:half] + self.in2[i, :half].astype(F32)).astype(BF)
        self.other_copy(i).start()

    def after_own(self, i):
        j, half = i - self.n_c, self.half
        self.far_copy(i).wait()
        total = self.core_sum(i, 1) + self.in2[i].astype(F32)
        self.acc[j, :half] = total[:half]
        if self.split:
            self.acc[j, half:] = total[half:] + self.in5[j, 1].astype(F32)

    def along(self, j):
        half = self.half
        if self.split:
            self.lower_copy(j).wait_send()
        self.other_copy(j).wait()
        self.acc[j, :half] = self.acc[j, :half] + self.in3[j].astype(F32)
        total = self.acc[j]
        if j < self.n_c - 1:
            self.out4[j] = total.astype(BF)
            self.line_copy(j, lax.rem(self.c + j + 1, self.n_c)).start()
        return total

    def total(self, total):
        for j in range(self.n_c - 1):
            self.line_copy(j, self.c).wait()
            total = total + self.in4[j].astype(F32)
        return total

    def loop(self, n_b, lag, compute):
        n_c = self.n_c
        assert lag >= n_b - n_c

        def step(i, carry):
            def between():
                @pl.when(i >= 1)
                def _():
                    self.over(i - 1)

                @pl.when((i >= lag) & (i < lag + n_c))
                def _():
                    self.after_other(i - lag)

            compute(i, between)
            return carry

        lax.fori_loop(0, n_b, step, 0)

    def drain(self, n_b, lag, works):
        works = list(works)
        self.over(n_b - 1)
        for i in range(n_b - lag, n_b):
            if i < self.n_c:
                self.after_other(i)
                continue
            self.after_own(i)
            total = self.along(i - self.n_c)
            if works:
                works.pop(0)()
        for work in works:
            work()
        return self.total(total)


def forward_kernel(
    n_c, n_f, mine, ffe, srows, hp, rows_all, og_all, resid, small,
    wg0, wu0, wd0, wg1, wu1, wd1, shared,
    layer_out, in_out, act_out, silu_out, slope_out, r_out, prob_out, keep_out, send_out, shared_out,
    gt, wsem, xsem, nsem, asem, tsem, osem, *scratch,
):
    f, c, t = ranks()
    n_b = n_f * n_c
    rows, quarter = resid.shape
    width = rows_all.shape[1]
    routed = mine * ffe
    rows_used = routed + srows
    n_exp = mine * n_b
    red = Reducer(n_c, scratch)

    def blocks_phase(wgu, wd, xs, ns, acts):
        gate_up, down = fetch_experts(
            n_c, n_f, mine, ffe, srows, hp, (wg0, wu0, wd0, wg1, wu1, wd1), shared, wgu, wd, wsem
        )
        for copy in gate_up + down:
            copy.start()

        def load(i, slot):
            return pltpu.make_async_copy(
                rows_all.at[piece(red.row_block(i), rows), :], xs.at[slot], xsem.at[slot]
            )

        def stores(i, slot):
            at = piece(red.row_block(i), rows)
            return [pltpu.make_async_copy(ns.at[slot], in_out.at[at, :], nsem.at[slot])] + [
                pltpu.make_async_copy(acts.at[slot, k], out.at[at, :], asem.at[slot, k])
                for k, out in enumerate((act_out, silu_out, slope_out))
            ]

        load(0, 0).start()
        blank_rows(rows_used, hp, wgu, wd)
        greet([{TP: red.sib}, {TP: red.far}, {FSDP: 1 - f}] + line_peers(c, n_c))
        for copy in gate_up:
            copy.wait()

        def compute(i, between):
            slot = lax.rem(i, 2)
            b = red.row_block(i)
            at = piece(b, rows)
            load(i, slot).wait()

            @pl.when(i + 1 < n_b)
            def _():
                load(i + 1, 1 - slot).start()

            @pl.when(i >= 2)
            def _():
                for copy in stores(i - 2, slot):
                    copy.wait()

            h = xs[slot].astype(F32)
            r = lax.rsqrt(jnp.sum(h * h, axis=1, keepdims=True) / width + EPS)
            r_out[at, :] = jnp.broadcast_to(r, (rows, HD))
            gain = small[2 * n_exp + 1 : 2 * n_exp + 2, :].astype(F32)
            n = (h * r * gain).astype(BF)
            ns[slot] = n
            logits = dot_nt(n, small[:n_exp, :])
            e = jnp.exp(logits - jnp.max(logits, axis=1, keepdims=True))
            prob = e / jnp.sum(e, axis=1, keepdims=True)
            prob_out[at, :] = prob
            gate, _, _ = gates(prob, small[n_exp : 2 * n_exp, at].astype(F32).T, (c * n_f + f) * mine, mine, ffe, hp)
            ab = dot_nt(n, wgu[...])
            between()
            a, up = ab[:, :hp], ab[:, hp:]
            sig = 0.5 * jnp.tanh(0.5 * a) + 0.5
            silu = a * sig
            act = (silu * up).astype(BF)
            acts[slot, 0] = act
            acts[slot, 1] = silu.astype(BF)
            acts[slot, 2] = (up * (sig * (1.0 + a * (1.0 - sig)))).astype(BF)
            actg = (act.astype(F32) * gate).astype(BF)
            gt[:, at] = actg.T[:rows_used, :]
            for copy in stores(i, slot):
                copy.start()

            @pl.when(i == 0)
            def _():
                for copy in down:
                    copy.wait()

            red.put(i, lambda q: dot_nn(actg, wd[:, piece(q, quarter)]))

        red.loop(n_b, n_c, compute)
        for i in range(n_b - 2, n_b):
            for copy in stores(i, i % 2):
                copy.wait()

    pl.run_scoped(
        blocks_phase,
        pltpu.VMEM((2 * hp, width), BF),
        pltpu.VMEM((hp, width), BF),
        pltpu.VMEM((2, rows, width), BF),
        pltpu.VMEM((2, rows, width), BF),
        pltpu.VMEM((2, 3, rows, hp), BF),
    )

    def grads_phase(tiles, keeps, sends, shs):
        def tile_of(s):
            return (1 - f) * 2 + s if s < 2 else f * 2 + s - 2

        def tile_load(s):
            return pltpu.make_async_copy(og_all.at[:, tile_of(s)], tiles.at[s % 2], tsem.at[s % 2])

        def out_copies(s):
            cols = pl.ds(s % 2 * quarter, quarter)
            if s < 2:
                src, dst = sends.at[s], send_out.at[:, :, cols]
            else:
                src, dst = keeps.at[s - 2], keep_out.at[:, :, cols]
            return [
                pltpu.make_async_copy(src, dst, osem.at[s, 0]),
                pltpu.make_async_copy(
                    shs.at[s], shared_out.at[:, piece(tile_of(s), quarter)], osem.at[s, 1]
                ),
            ]

        def work(s):
            def run():
                tile_load(s).wait()
                if s < 3:
                    tile_load(s + 1).start()
                g = dot_nn(gt[...], tiles[s % 2].reshape(n_b * rows, quarter))
                if s < 2:
                    sends[s] = g[:routed].astype(BF).reshape(mine, ffe, quarter)
                else:
                    keeps[s - 2] = g[:routed].astype(BF).reshape(mine, ffe, quarter)
                shs[s] = g[routed:].astype(BF)
                for copy in out_copies(s):
                    copy.start()

            return run

        tile_load(0).start()
        total = red.drain(n_b, n_c, [work(s) for s in range(4)])
        layer_out[...] = (resid[...] + total).astype(BF)
        for s in range(4):
            for copy in out_copies(s):
                copy.wait()

    pl.run_scoped(
        grads_phase,
        pltpu.VMEM((2, n_b, rows, quarter), BF),
        pltpu.VMEM((2, mine, ffe, quarter), BF),
        pltpu.VMEM((2, mine, ffe, quarter), BF),
        pltpu.VMEM((4, srows, quarter), BF),
    )


def expert_sizes(n_c, n_f, n_t, mine, ffe, srows, width):
    used = mine * ffe + srows
    return used, -(-used // HD) * HD, 3 * (2 * mine + n_f * n_c)


def forward(n_c, n_f, n_t, mine, ffe, srows, rows_all, og_all, resid, small, kept, got, shared):
    total, width = rows_all.shape
    rows, quarter = resid.shape
    n_b = n_f * n_c
    n_exp = mine * n_b
    used, hp, n_fetch = expert_sizes(n_c, n_f, n_t, mine, ffe, srows, width)
    sds = jax.ShapeDtypeStruct
    return pl.pallas_call(
        functools.partial(forward_kernel, n_c, n_f, mine, ffe, srows, hp),
        out_shape=(
            sds((rows, quarter), BF),
            sds((total, width), BF),
            sds((total, hp), BF),
            sds((total, hp), BF),
            sds((total, hp), BF),
            sds((total, HD), F32),
            sds((total, n_exp), F32),
            sds((mine, ffe, width // n_f), BF),
            sds((mine, ffe, width // n_f), BF),
            sds((srows, width), BF),
        ),
        in_specs=[HBM, HBM, VMEM, VMEM] + [HBM] * 7,
        out_specs=[VMEM, HBM, HBM, HBM, HBM, VMEM, VMEM, HBM, HBM, HBM],
        scratch_shapes=[
            pltpu.VMEM((used, total), BF),
            DMA((n_fetch,)),
            DMA((2,)),
            DMA((2,)),
            DMA((2, 3)),
            DMA((2,)),
            DMA((4, 2)),
        ]
        + reducer_scratch(n_f, n_c, rows, quarter, True),
        compiler_params=pltpu.CompilerParams(
            collective_id=5, has_side_effects=True, vmem_limit_bytes=BIG
        ),
        cost_estimate=pl.CostEstimate(
            flops=8 * total * width * used, bytes_accessed=80 << 20, transcendentals=total * used
        ),
        name="forward",
    )(rows_all, og_all, resid, small, *kept, *got, shared)


def backward_kernel(
    n_c, n_f, mine, ffe, srows, hp, og_all, act, silu, slope, moe_in, r_all, shared_d, prob_in, small,
    resid, og, wg0, wu0, wd0, wg1, wu1, wd1, shared,
    mid_out, gain_out, seq_out, shared_out, shs_out, kg_out, ku_out, gg_out, gu_out, lg_out, lu_out,
    gt, blk, r_own, sends, shs, wsem, xsem, tsem, ksem, ss, sr, rs, es, ds, dr, dl, *rest,
):
    f, c, t = ranks()
    n_b = n_f * n_c
    rows, quarter = resid.shape
    width = shared_d.shape[1]
    n_exp = mine * n_b
    routed = mine * ffe
    rows_used = routed + srows
    first = (c * n_f + f) * mine
    reduce_scratch, rest = rest[:N_REDUCER], rest[N_REDUCER:]
    red = Reducer(n_c, reduce_scratch)

    cols = width // n_b

    def exchange(act):
        to_each(lambda b: shared_d.at[:, piece(b, cols)], shared_out, n_f, n_c, (ds, dr, dl), act)

    def blocks_phase(wgu, wd, ogs, acts):
        gate_up, down = fetch_experts(
            n_c, n_f, mine, ffe, srows, hp, (wg0, wu0, wd0, wg1, wu1, wd1), shared, wgu, wd, wsem
        )
        for copy in down + gate_up:
            copy.start()

        def loads(i, slot):
            b = red.row_block(i)
            return [
                pltpu.make_async_copy(
                    og_all.at[b, q], ogs.at[slot, :, pl.ds(q * quarter, quarter)], xsem.at[slot, q]
                )
                for q in range(4)
            ] + [
                pltpu.make_async_copy(src.at[piece(b, rows), :], acts.at[slot, k], xsem.at[slot, 4 + k])
                for k, src in enumerate((act, silu, slope))
            ]

        for copy in loads(0, 0):
            copy.start()
        blank_rows(rows_used, hp, wgu, wd)
        greet([{TP: red.sib}, {TP: red.far}, {TP: opposite(red.sib)}] + each_peers(f, c, n_f, n_c))
        exchange("start")
        for copy in down:
            copy.wait()

        def compute(i, between):
            slot = lax.rem(i, 2)
            at = piece(red.row_block(i), rows)
            for copy in loads(i, slot):
                copy.wait()

            @pl.when(i + 1 < n_b)
            def _():
                for copy in loads(i + 1, 1 - slot):
                    copy.start()

            prob = prob_in[at, :]
            chosen = small[n_exp : 2 * n_exp, at].astype(F32).T
            gate, lane, col = gates(prob, chosen, first, mine, ffe, hp)
            dh = dot_nt(ogs[slot], wd[...])
            between()
            ad = acts[slot, 0].astype(F32) * dh
            p_grad = jnp.zeros(prob.shape, F32)
            for k in reversed(range(mine)):
                below = jnp.where(col < k * ffe, ad, 0.0) if k else jnp.zeros_like(ad)
                ad = jnp.where(col < (k + 1) * ffe, ad, 0.0)
                s = jnp.sum(ad - below, axis=1, keepdims=True)
                p_grad = jnp.where(lane == first + k, s, p_grad)
                ad = below
            p_grad = p_grad * chosen
            logit_f = prob * (p_grad - jnp.sum(prob * p_grad, axis=1, keepdims=True))
            logit_grad = logit_f.astype(BF)
            dg = dh * gate
            da = (dg * acts[slot, 2].astype(F32)).astype(BF)
            db = (dg * acts[slot, 1].astype(F32)).astype(BF)
            gt[:rows_used, at] = da.T[:rows_used, :]
            gt[rows_used : 2 * rows_used, at] = db.T[:rows_used, :]
            gt[2 * rows_used :, at] = logit_f.T.astype(BF)
            dab = jnp.concatenate([da, db], axis=1)

            @pl.when(i == 0)
            def _():
                for copy in gate_up:
                    copy.wait()

            def part_of(q):
                cols = piece(q, quarter)
                return dot_nn(dab, wgu[:, cols]) + dot_nn(logit_grad, small[:n_exp, cols])

            red.put(i, part_of)

        red.loop(n_b, n_c + 1, compute)

    pl.run_scoped(
        blocks_phase,
        pltpu.VMEM((2 * hp, width), BF),
        pltpu.VMEM((hp, width), BF),
        pltpu.VMEM((2, rows, width), BF),
        pltpu.VMEM((2, 3, rows, hp), BF),
    )

    def send_copy(s, m):
        if s:
            return pltpu.make_async_copy(sends.at[s, m], (lg_out, lu_out)[m], ss.at[s, m])
        return remote(sends.at[s, m], (gg_out, gu_out)[m], ss.at[s, m], sr.at[m], {FSDP: 1 - f})

    def grads_phase(tiles, keeps):
        def tile_of(s):
            return (1 - f) * 2 + s if s < 2 else f * 2 + s - 2

        def tile_load(s):
            return pltpu.make_async_copy(
                moe_in.at[:, piece(tile_of(s), quarter)], tiles.at[s % 2], tsem.at[s % 2]
            )

        def keep_copy(s, m):
            dst = (kg_out, ku_out)[m].at[:, :, pl.ds((s - 2) * quarter, quarter)]
            return pltpu.make_async_copy(keeps.at[s - 2, m], dst, ksem.at[s - 2, m])

        def work(s):
            def run():
                tile_load(s).wait()
                if s < 3:
                    tile_load(s + 1).start()
                g = dot_nn(gt[...], tiles[s % 2])
                cols = piece(tile_of(s), quarter)
                for m in range(2):
                    base = m * rows_used
                    if s < 2:
                        sends[s, m] = g[base : base + routed].astype(BF).reshape(mine, ffe, quarter)
                        send_copy(s, m).start()
                    else:
                        keeps[s - 2, m] = g[base : base + routed].astype(BF).reshape(mine, ffe, quarter)
                        keep_copy(s, m).start()
                    shs[m * srows : (m + 1) * srows, cols] = g[base + routed : base + rows_used].astype(BF)
                shs[2 * srows :, cols] = g[2 * rows_used :].astype(BF)

            return run

        tile_load(0).start()
        blk[...] = red.drain(n_b, n_c + 1, [work(s) for s in range(4)])
        for s in (2, 3):
            for m in range(2):
                keep_copy(s, m).wait()

    fetch = pltpu.make_async_copy(r_all.at[piece(f * n_c + c, rows), :], r_own, rs)
    fetch.start()
    pl.run_scoped(
        grads_phase,
        pltpu.VMEM((2, n_b * rows, quarter), BF),
        pltpu.VMEM((2, 2, mine, ffe, quarter), BF),
    )
    shs_copy = pltpu.make_async_copy(shs, shs_out, es)
    shs_copy.start()
    fetch.wait()
    gain = small[2 * n_exp + 1 : 2 * n_exp + 2, piece(t, quarter)].astype(F32)
    back, gain_part = norm_grad(resid[...], r_own[:, :1], gain, blk[...], width, *rest[:4])
    gain_out[...] = jnp.broadcast_to(gain_part, gain_out.shape)
    grad = og[...].astype(F32) + back
    mid_out[...] = grad
    own = rest[4]
    own[...] = grad.astype(BF)

    def place(g, cc, tt):
        return seq_out.at[piece(cc, rows), piece(tt, quarter)]

    sequence = Spread(own, place, n_c, False, rest[5:])
    sequence.start()
    sequence.line()
    sequence.far(0)
    sequence.arrived(0)
    sequence.finish()
    sequence.local().wait()
    exchange("wait")
    shs_copy.wait()
    for s in range(2):
        for m in range(2):
            send_copy(s, m).wait()


def backward(
    n_c, n_f, n_t, mine, ffe, srows, og_all, act, silu, slope, moe_in, r_all, shared_d, prob, small,
    resid, og, kept, got, shared,
):
    total, width = moe_in.shape
    rows, quarter = resid.shape
    n_b = n_f * n_c
    n_exp = mine * n_b
    used, hp, n_fetch = expert_sizes(n_c, n_f, n_t, mine, ffe, srows, width)
    sds = jax.ShapeDtypeStruct
    kept_g = sds((mine, ffe, width // n_f), BF)
    sent_g = sds((mine, ffe, quarter), BF)
    return pl.pallas_call(
        functools.partial(backward_kernel, n_c, n_f, mine, ffe, srows, hp),
        out_shape=(
            sds((rows, quarter), F32),
            sds((8, quarter), F32),
            sds((rows * n_c, width), BF),
            sds((n_b, srows, width // n_b), BF),
            sds((2 * srows + n_exp, width), BF),
            kept_g,
            kept_g,
            sent_g,
            sent_g,
            sent_g,
            sent_g,
        ),
        in_specs=[HBM] * 7 + [VMEM] * 4 + [HBM] * 7,
        out_specs=[VMEM, VMEM] + [HBM] * 9,
        scratch_shapes=[
            pltpu.VMEM((2 * used + n_exp, total), BF),
            pltpu.VMEM((rows, quarter), F32),
            pltpu.VMEM((rows, HD), F32),
            pltpu.VMEM((2, 2, mine, ffe, quarter), BF),
            pltpu.VMEM((2 * srows + n_exp, width), BF),
            DMA((n_fetch,)),
            DMA((2, 7)),
            DMA((2,)),
            DMA((2, 2)),
            DMA((2, 2)),
            DMA((2,)),
            DMA(()),
            DMA(()),
            DMA((n_b,)),
            DMA((n_b,)),
            DMA(()),
        ]
        + reducer_scratch(n_f, n_c, rows, quarter, False)
        + norm_grad_scratch(rows)
        + [pltpu.VMEM((rows, quarter), BF)]
        + spread_sems(n_c),
        compiler_params=pltpu.CompilerParams(
            collective_id=3, has_side_effects=True, vmem_limit_bytes=BIG
        ),
        cost_estimate=pl.CostEstimate(
            flops=10 * total * width * used, bytes_accessed=200 << 20, transcendentals=0
        ),
        name="backward",
    )(
        og_all, act, silu, slope, moe_in, r_all, shared_d, prob, small, resid, og,
        *kept, *got, shared,
    )


def finish_kernel(n_plain, f_ref, *refs):
    ga, gb, ua, ub, d, kg, ku, kd, shared = refs[:9]
    plain, gains, refs = refs[9 : 9 + n_plain], refs[9 + n_plain], refs[:9] + refs[10:]
    og, ou, od, shared_out = refs[9 + n_plain : 13 + n_plain]
    step = pl.program_id(0)
    f = f_ref[0]
    n_e = kg.shape[0]

    def put(at):
        for keep, out in ((kg, og), (ku, ou), (kd, od)):
            out[at : at + n_e] = keep[...].astype(F32)
        for out, halves in ((og, (ga, gb)), (ou, (ua, ub))):
            @pl.when(step < 2)
            def _():
                out[n_e - at : 2 * n_e - at] = halves[0][...].astype(F32)

            @pl.when(step >= 2)
            def _():
                out[n_e - at : 2 * n_e - at] = halves[1][...].astype(F32)

        od[n_e - at : 2 * n_e - at] = d[...].astype(F32)

    @pl.when(f == 0)
    def _():
        put(0)

    @pl.when(f != 0)
    def _():
        put(n_e)

    own = shared_out.shape[0] // shared.shape[0]
    for b in range(shared.shape[0]):
        shared_out[b * own : (b + 1) * own, :] = shared[b, :own, :].astype(F32)
    for src, dst in zip(plain, refs[13 + n_plain :]):
        dst[...] = src[...]
    for i, dst in enumerate(refs[13 + 2 * n_plain :]):
        dst[...] = gains[i : i + 1, :]


def finish(f_rank, own_shared, arrived, kept, shared, plain, gains):
    mine, ffe, quarter = arrived[0].shape
    half = kept[0].shape[2]
    tile = half // 4
    n_b, srows, part = shared.shape
    first = pl.BlockSpec((mine, ffe, tile), lambda i, f: (0, 0, jnp.minimum(i, 1)))
    second = pl.BlockSpec((mine, ffe, tile), lambda i, f: (0, 0, jnp.maximum(i - 2, 0)))
    every = pl.BlockSpec((mine, ffe, tile), lambda i, f: (0, 0, i))
    out = pl.BlockSpec((2 * mine, ffe, tile), lambda i, f: (0, 0, i))

    def rows_of(x):
        if x.shape[0] % 64:
            return pl.BlockSpec(x.shape, lambda i, f: (0, 0))
        return pl.BlockSpec((x.shape[0] // 4, x.shape[1]), lambda i, f: (i, 0))

    shared_grad = jax.ShapeDtypeStruct((n_b * own_shared, part), F32)
    return pl.pallas_call(
        functools.partial(finish_kernel, len(plain)),
        grid_spec=pltpu.PrefetchScalarGridSpec(
            num_scalar_prefetch=1,
            grid=(4,),
            in_specs=[first, second, first, second, every]
            + [every] * 3
            + [pl.BlockSpec((n_b // 4, srows, part), lambda i, f: (i, 0, 0))]
            + [rows_of(x) for x in plain]
            + [rows_of(gains)],
            out_specs=[out] * 3
            + [rows_of(shared_grad)]
            + [rows_of(x) for x in plain]
            + [pl.BlockSpec((1, part), lambda i, f: (0, 0))] * 2,
        ),
        out_shape=tuple(jax.ShapeDtypeStruct((2 * mine, ffe, half), F32) for k in kept)
        + (shared_grad,)
        + tuple(jax.ShapeDtypeStruct(x.shape, x.dtype) for x in plain)
        + (jax.ShapeDtypeStruct((1, part), F32),) * 2,
        compiler_params=pltpu.CompilerParams(vmem_limit_bytes=BIG),
        name="finish",
    )(f_rank, *arrived, *kept, shared, *plain, gains)


def norm_grad(values, r, gain, grad, width, out, into, send, recv):
    f, c, t = ranks()
    rows = values.shape[0]
    local = jnp.sum(grad * gain * values, axis=1, keepdims=True)
    out[...] = jnp.broadcast_to(local, (rows, HD)).T[:8, :]
    peers = [sibling(t), opposite(t), opposite(sibling(t))]
    copies = [
        remote(out, into.at[i], send.at[i], recv.at[i], {TP: peer}) for i, peer in enumerate(peers)
    ]
    for copy in copies:
        copy.start()
    gain_part = jnp.sum(grad * values * r, axis=0, keepdims=True)
    total = out[...]
    for i, copy in enumerate(copies):
        copy.wait()
        total = total + into[i]
    total = jnp.broadcast_to(total[0:1, :], (HD, rows)).T[:, :1]
    return r * gain * grad - values * (r * r * r * (total / width)), gain_part


def norm_grad_scratch(rows):
    return [
        pltpu.VMEM((8, rows), F32),
        pltpu.VMEM((3, 8, rows), F32),
        DMA((3,)),
        DMA((3,)),
    ]


def attend_back(block, mid, wo, q, k, v, hf, lse, cosine, sine, dqkv, hg, dq, dk, dv):
    seq = mid.shape[0]
    scale_att = HD ** (-0.5)
    for start in range(0, seq, block):
        at = pl.ds(start, block)
        hg[at, :] = dot_nt(mid[at, :], wo[...]).astype(BF)
    dk[...] = jnp.zeros_like(dk)
    dv[...] = jnp.zeros_like(dv)
    for start in range(0, seq, block):
        at = pl.ds(start, block)
        seen = start + block
        qb, hb = q[at, :], hg[at, :]
        delta = jnp.sum(hb.astype(F32) * hf[at, :], axis=1, keepdims=True)
        s = dot_nt(qb, k[:seen, :]) * scale_att
        row = lax.broadcasted_iota(jnp.int32, (block, seen), 0) + start
        col = lax.broadcasted_iota(jnp.int32, (block, seen), 1)
        p = jnp.where(col <= row, jnp.exp(s - lse[at, :1]), 0.0)
        ds = (p * (dot_nt(hb, v[:seen, :]) - delta)).astype(BF)
        dq[at, :] = dot_nn(ds, k[:seen, :]) * scale_att
        dk[:seen, :] += dot_tn(ds, qb) * scale_att
        dv[:seen, :] += dot_tn(p.astype(BF), hb)

    def rotate(values, at):
        return (values * cosine[at, :] - pltpu.roll(values, HD // 2, 1) * sine[at, :]).astype(BF)

    for start in range(0, seq, block):
        at = pl.ds(start, block)
        dqkv[at, :HD] = rotate(dq[at, :], at)
        dqkv[at, HD : 2 * HD] = rotate(dk[at, :], at)
        dqkv[at, 2 * HD :] = dv[at, :].astype(BF)


def last_kernel(
    n_c, n_f, n_t, n_exp, own_shared, mid_in, wo, q, k, v, hf, lse, cosine, sine, normed_in, wqkv_in, hidden, r_all,
    small, mid_grad, gain2, shs, lg, lu,
    in_out, gq, gk, gv, go, gains_out, router_out, sg_out, su_out, lg_out, lu_out,
    mid_seq, normed, wqkv, big, dqkv, hg, dq, dk, dv, gattn, shs_in, rpart, hs, hr, hl, es, er, rin, rss, rsr, r_own, mine, inx, own, outz, inz, gsend, gin, rs, sx, rx, lx, sz, rz, gs, gr, *rest,
):
    f, c, t = ranks()
    rows, quarter = hidden.shape
    tokens, width = normed.shape
    part = width // (n_f * n_c)
    here = f * n_c + c
    srows = (shs.shape[0] - n_exp) // 2
    others = []
    for df in range(n_f):
        for dc in range(n_c):
            for dt in range(n_t):
                if df or dc or dt:
                    others.append(
                        {
                            FSDP: lax.rem(f + df, n_f),
                            CTX: lax.rem(c + dc, n_c),
                            TP: lax.rem(t + dt, n_t),
                        }
                    )
    large = [
        pltpu.make_async_copy(src, dst, big.at[i])
        for i, (src, dst) in enumerate(((mid_in, mid_seq), (wqkv_in, wqkv), (normed_in, normed)))
    ]
    for copy in large:
        copy.start()
    gin[...] = jnp.zeros_like(gin)
    greet(others)
    order = [2, 1, 3, 0] if n_c == 4 else list(range(1, n_c)) + [0]

    def cross(d):
        cc = lax.rem(c + d, n_c)
        return remote(
            gattn.at[:, piece((1 - f) * n_c + cc, part)], inx.at[d], sx.at[d], rx.at[d], {FSDP: 1 - f}
        )

    def keep(d):
        cc = lax.rem(c + d, n_c)
        return pltpu.make_async_copy(gattn.at[:, piece(f * n_c + cc, part)], own.at[d], lx.at[d])

    def line(d, to):
        return remote(outz.at[d], inz.at[d], sz.at[d], rz.at[d], {CTX: to})

    router_copies = [
        remote(rpart, rin.at[i], rss.at[i], rsr.at[i], {TP: peer})
        for i, peer in enumerate([sibling(t), opposite(t), opposite(sibling(t))])
    ]
    shared = lambda act: to_each(lambda b: shs.at[:, piece(b, part)], shs_in, n_f, n_c, (hs, hr, hl), act)
    late = [
        remote(src, dst, es.at[i], er.at[i], {FSDP: 1 - f})
        for i, (src, dst) in enumerate(((lg, lg_out), (lu, lu_out)))
    ]
    shared("start")
    fetch = pltpu.make_async_copy(r_all.at[piece(c, rows), :], r_own, rs)
    fetch.start()
    late[0].start()
    large[0].wait()
    attend_back(rows, mid_seq, wo, q, k, v, hf, lse, cosine, sine, dqkv, hg, dq, dk, dv)
    gattn[3 * HD :, :] = dot_tn(hf[...].astype(BF), mid_seq[...]).astype(BF)

    large[1].wait()

    def weights():
        large[2].wait()
        gattn[: 3 * HD, :] = dot_tn(dqkv[...], normed[...]).astype(BF)
        for d in order:
            cross(d).start()
            keep(d).start()
        late[1].start()


    def part_of(cc, q):
        return dot_nt(dqkv[piece(cc, rows), :], wqkv[piece(q, quarter), :])

    def pass_weights():
        for d in order:
            cross(d).wait()
            keep(d).wait()
            both = own[d].astype(F32) + inx[d].astype(F32)
            if d:
                outz[d] = both.astype(BF)
                line(d, lax.rem(c + d, n_c)).start()
            else:
                mine[...] = both

    total = reduce_seq(part_of, n_c, rest[:13], weights, pass_weights)
    fetch.wait()
    gain = small[2 * n_exp : 2 * n_exp + 1, piece(t, quarter)].astype(F32)
    back, gain_part = norm_grad(
        hidden[...].astype(F32), r_own[:, :1], gain, total, width, *rest[13:17]
    )
    in_out[...] = mid_grad[...] + back

    gsend[0:1, :] = gain_part
    gsend[1:2, :] = gain2[0:1, :]
    gsend[2:, :] = jnp.zeros((6, quarter), F32)
    per = quarter // part
    holder = here // per
    def gain_copy(h, tt):
        b = t * per + h
        return remote(
            gsend.at[:, pl.ds(h * part, part)],
            gin.at[here],
            gs.at[h * n_t + tt],
            gr.at[here],
            {FSDP: b // n_c, CTX: lax.rem(b, n_c), TP: jnp.int32(tt)},
        )

    def is_me(h, tt):
        return (t * per + h == here) & (t == tt)

    for h in range(per):
        for tt in range(n_t):

            @pl.when(jnp.logical_not(is_me(h, tt)))
            def _():
                gain_copy(h, tt).start()

    def put(src, block):
        at = piece(src, HD)
        for i, ref in enumerate((gq, gk, gv)):
            ref[:, at] = block[i * HD : (i + 1) * HD, :].T
        go[at, :] = block[3 * HD :, :]

    shared("wait")
    rpart[...] = jnp.sum(shs_in[:, 2 * srows :, :].astype(F32), axis=0)
    for copy in router_copies:
        copy.start()
    for b in range(n_f * n_c):
        at = pl.ds(b * own_shared, own_shared)
        sg_out[at, :] = shs_in[b, :own_shared, :].astype(F32)
        su_out[at, :] = shs_in[b, srows : srows + own_shared, :].astype(F32)
    put(c, mine[...])
    for d in order[:-1]:
        line(d, c).wait()
        put(lax.rem(c - d + n_c, n_c), inz[d].astype(F32))
    for h in range(per):
        for tt in range(n_t):

            @pl.when(jnp.logical_not(is_me(h, tt)))
            def _():
                gain_copy(h, tt).wait_send()

    for b in range(n_f * n_c):

        @pl.when((b != here) | (holder != t))
        def _():
            remote(gin.at[b], gin.at[b], gs.at[0], gr.at[b], {TP: sibling(t)}).wait_recv()

    own_part = jnp.where(
        holder == t,
        gsend[:, piece(lax.rem(here, per), part)],
        jnp.zeros((8, part), F32),
    )
    gains_out[...] = own_part + jnp.sum(gin[...], axis=0)
    for copy in router_copies + late:
        copy.wait()
    router_out[...] = rpart[...] + jnp.sum(rin[...], axis=0)


def last(
    n_c, n_f, n_t, n_exp, own_shared, mid_seq, wo, q, k, v, hf, lse, cosine, sine, normed, wqkv, hidden, r_all,
    small, mid_grad, gain2, shs, lg, lu,
):
    rows, quarter = hidden.shape
    seq, width = normed.shape
    part = width // (n_f * n_c)
    sds = jax.ShapeDtypeStruct
    slab = pltpu.VMEM((n_c, 4 * HD, part), BF)
    head_f = pltpu.VMEM((seq, HD), F32)
    shared_grad = sds((n_f * n_c * own_shared, part), F32)
    return pl.pallas_call(
        functools.partial(last_kernel, n_c, n_f, n_t, n_exp, own_shared),
        out_shape=(
            sds((rows, quarter), F32),
            sds((part, n_c * HD), F32),
            sds((part, n_c * HD), F32),
            sds((part, n_c * HD), F32),
            sds((n_c * HD, part), F32),
            sds((8, part), F32),
            sds((n_exp, part), F32),
            shared_grad,
            shared_grad,
            sds(lg.shape, BF),
            sds(lu.shape, BF),
        ),
        in_specs=[HBM] + [VMEM] * 8 + [HBM] * 2 + [VMEM, HBM] + [VMEM] * 3 + [HBM] * 3,
        out_specs=[VMEM] * 9 + [HBM] * 2,
        scratch_shapes=[
            pltpu.VMEM((seq, width), BF),
            pltpu.VMEM((seq, width), BF),
            pltpu.VMEM((width, 3 * HD), BF),
            DMA((3,)),
            pltpu.VMEM((seq, 3 * HD), BF),
            pltpu.VMEM((seq, HD), BF),
            head_f,
            head_f,
            head_f,
            pltpu.VMEM((4 * HD, width), BF),
            pltpu.VMEM((n_f * n_c, shs.shape[0], part), BF),
            pltpu.VMEM((n_exp, part), F32),
            DMA((n_f * n_c,)),
            DMA((n_f * n_c,)),
            DMA(()),
            DMA((2,)),
            DMA((2,)),
            pltpu.VMEM((3, n_exp, part), F32),
            DMA((3,)),
            DMA((3,)),
            pltpu.VMEM((rows, HD), F32),
            pltpu.VMEM((4 * HD, part), F32),
            slab,
            slab,
            slab,
            slab,
            pltpu.VMEM((8, quarter), F32),
            pltpu.VMEM((n_f * n_c, 8, part), F32),
            DMA(()),
            DMA((n_c,)),
            DMA((n_c,)),
            DMA((n_c,)),
            DMA((n_c,)),
            DMA((n_c,)),
            DMA((quarter // part * n_t,)),
            DMA((n_f * n_c,)),
        ]
        + reduce_seq_scratch(n_c, rows, quarter)
        + norm_grad_scratch(rows),
        compiler_params=pltpu.CompilerParams(
            collective_id=4, has_side_effects=True, vmem_limit_bytes=BIG
        ),
        cost_estimate=pl.CostEstimate(flops=8 << 30, bytes_accessed=150 << 20, transcendentals=1 << 20),
        name="last",
    )(
        mid_seq, wo, q, k, v, hf, lse, cosine, sine, normed, wqkv, hidden, r_all, small, mid_grad, gain2,
        shs, lg, lu,
    )


def per_device_seq(
    hidden_in,
    positions,
    chosen,
    out_grad,
    attn_gain,
    w_query,
    w_key,
    w_value,
    w_out,
    moe_gain,
    router,
    shared_gate,
    shared_up,
    shared_down,
    expert_gate,
    expert_up,
    expert_down,
):
    f_rank, c_rank, t_rank = ranks()
    n_f, n_c, n_t = (lax.axis_size(name) for name in (FSDP, CTX, TP))
    rows, quarter = hidden_in.shape
    width = quarter * n_t
    part = w_query.shape[0]
    seq = rows * n_c
    n_exp = router.shape[1]
    mine = n_exp // n_c // n_f
    ffe = expert_gate.shape[2]
    group = (FSDP, CTX)
    every = (FSDP, CTX, TP)
    n_b = n_f * n_c
    own_shared = shared_gate.shape[1] // n_b
    srows = -(-own_shared // 16) * 16
    f_arr = f_rank.astype(jnp.int32).reshape(1)
    swap = [(i, n_f - 1 - i) for i in range(n_f)]
    weights = (expert_gate.swapaxes(1, 2), expert_up.swapaxes(1, 2), expert_down)

    line = jnp.arange(16)[:, None]
    lines = jnp.where(line == 0, attn_gain[None], jnp.zeros((), BF))
    lines = jnp.where(line == 1, moe_gain[None], lines)
    lines = jnp.where(line == 2, (positions // 64).astype(BF)[None], lines)
    lines = jnp.where(line == 3, (positions % 64).astype(BF)[None], lines)
    lane = np.arange(HD)
    inverse = 10000.0 ** (-(lane % (HD // 2)) * 2.0 / HD)
    angle = jnp.asarray(np.stack([inverse, np.where(lane < HD // 2, -1.0, 1.0)]).astype(np.float32))
    (
        normed, q, k, v, heads_f, lse, r_one, cosine, sine, resid_mid,
        wqkv, wo, small, resid_all, grad_all, shared, *got,
    ) = first(
        n_c, n_f, n_t, mine, srows, hidden_in, w_query, w_key, w_value, w_out, out_grad, weights,
        router.T, chosen.T, lines, (shared_gate.T, shared_up.T, shared_down), angle,
    )
    sizes = (n_c, n_f, n_t, mine, ffe, srows)
    layer_out, moe_in, act, silu, slope, r_two, prob, kd, sd, shared_d = forward(
        *sizes, resid_all, grad_all, resid_mid, small, weights, got, shared
    )
    arrived_d = lax.ppermute(sd, FSDP, swap)
    mid_grad, gain_two_part, mid_seq, shared_back, shs, kg, ku, gg, gu, lg, lu = backward(
        *sizes, grad_all, act, silu, slope, moe_in, r_two, shared_d, prob, small,
        resid_mid, out_grad, weights, got, shared,
    )
    input_grad, gq, gk, gv, go, gains, router_grad, shared_g, shared_u, lg, lu = last(
        n_c, n_f, n_t, n_exp, own_shared, mid_seq, wo, q, k, v, heads_f, lse, cosine, sine, normed, wqkv,
        hidden_in, r_one, small, mid_grad, gain_two_part, shs, lg, lu,
    )
    plain = (layer_out, input_grad, gq, gk, gv, go, router_grad, shared_g, shared_u)
    (
        eg, eu, ed, shared_d, layer_out, input_grad, gq, gk, gv, go, router_grad, shared_g, shared_u, gain_1, gain_2,
    ) = finish(f_arr, own_shared, (gg, lg, gu, lu, arrived_d), (kg, ku, kd), shared_back, plain, gains)

    return (
        layer_out,
        input_grad,
        gain_1[0],
        gq,
        gk,
        gv,
        go,
        gain_2[0],
        router_grad.T,
        shared_g.T,
        shared_u.T,
        shared_d,
        eg.swapaxes(1, 2),
        eu.swapaxes(1, 2),
        ed,
    )


def one_head_each(mesh, args):
    n_f, n_c, n_t = (mesh.shape[name] for name in (FSDP, CTX, TP))
    heads = args[5].shape[1] // HD
    experts = args[10].shape[1]
    return (
        n_f == 2
        and n_t == 4
        and heads == n_c * n_t
        and experts % (n_f * n_c) == 0
        and args[11].shape[1] % (8 * n_f * n_c * n_t) == 0
    )


def solution(mesh):
    placed = (
        P((FSDP, CTX), TP),
        P((FSDP, CTX)),
        P((FSDP, CTX), None),
        P((FSDP, CTX), TP),
        P((FSDP, CTX)),
        P((FSDP, CTX), TP),
        P((FSDP, CTX), TP),
        P((FSDP, CTX), TP),
        P(TP, (FSDP, CTX)),
        P((FSDP, CTX)),
        P((FSDP, CTX), None),
        P((FSDP, CTX), TP),
        P((FSDP, CTX), TP),
        P(TP, (FSDP, CTX)),
        P(CTX, FSDP, TP),
        P(CTX, FSDP, TP),
        P(CTX, TP, FSDP),
    )
    def run(*args):
        body = per_device_seq if one_head_each(mesh, args) else per_device
        return jax.shard_map(
        body,
        mesh=mesh,
        in_specs=placed,
        out_specs=(
            P((FSDP, CTX), TP),
            P((FSDP, CTX), TP),
            P((FSDP, CTX)),
            P((FSDP, CTX), TP),
            P((FSDP, CTX), TP),
            P((FSDP, CTX), TP),
            P(TP, (FSDP, CTX)),
            P((FSDP, CTX)),
            P((FSDP, CTX), None),
            P((FSDP, CTX), TP),
            P((FSDP, CTX), TP),
            P(TP, (FSDP, CTX)),
            P(CTX, FSDP, TP),
            P(CTX, FSDP, TP),
            P(CTX, TP, FSDP),
        ),
        check_vma=False,
    )(*args)

    return run
```
